128 devices in a mesh: seq: 16 (over y_hi, z, core), wt: 8 (over x, y_lo).
Axes of the slice: x: 4, y: 4 (y_hi: 2, y_lo: 2; y = y_hi * 2 + y_lo), z: 4, core: 2. Of those that a mesh axis runs over, the one named last changes fastest.
Arguments:
- layer_in: bfloat16 [8, 2048, 2048], P('wt', 'seq'), may hold values from -6 to 6
- segment_ids: int32 [8, 2048], P('wt'), may hold values from 0 to 2, as said below
- norm_one_gain: float32 [2048], replicated, may hold values from 0.5 to 1.5
- norm_one_shift: float32 [2048], replicated, may hold values from -3 to 3
- qkv_weight: bfloat16 [2048, 6144], P(None, 'wt'), may hold values from -0.125 to 0.125
- qkv_bias: float32 [6144], replicated, may hold values from -3 to 3
- out_weight: bfloat16 [2048, 2048], P(None, 'wt'), may hold values from -0.5 to 0.5
- norm_two_gain: float32 [2048], replicated, may hold values from 0.5 to 1.5
- norm_two_shift: float32 [2048], replicated, may hold values from -3 to 3
- gate_up_weight: bfloat16 [2048, 2, 5632], P(None, None, 'wt'), may hold values from -0.125 to 0.125
- down_weight: bfloat16 [5632, 2048], P('wt'), may hold values from -0.078125 to 0.078125
- layer_grad: bfloat16 [8, 2048, 2048], P('wt', 'seq'), may hold values from -6 to 6
Outputs:
- layer_out: bfloat16 [8, 2048, 2048], P('wt', 'seq')
- input_grad: bfloat16 [8, 2048, 2048], P('wt', 'seq')
- norm_one_gain_grad: float32 [2048], P(('seq', 'wt'))
- norm_one_shift_grad: float32 [2048], P(('seq', 'wt'))
- qkv_weight_grad: float32 [2048, 6144], P('seq', 'wt')
- qkv_bias_grad: float32 [6144], P(('seq', 'wt'))
- out_weight_grad: float32 [2048, 2048], P('seq', 'wt')
- norm_two_gain_grad: float32 [2048], P(('seq', 'wt'))
- norm_two_shift_grad: float32 [2048], P(('seq', 'wt'))
- gate_up_grad: float32 [2048, 2, 5632], P('seq', None, 'wt')
- down_grad: float32 [5632, 2048], P('wt', 'seq')
The draws below stay inside these ranges and needn't reach their ends.
Inputs may be any that keep to these rules, and one draw needn't show every extreme that they name: `segment_ids`: in each row the segment ids never fall and form three documents; the middle one starts within the first 128 positions and ends within the last 128 positions.
All inputs are finite; a program needn't handle non-finite values.
Results may differ from the reference program's by a relative error of at most 0.025.
Values may be sent and summed in bfloat16 or wider, within the bound.
A program may use at most 320 MiB of HBM per device.

```python
import math
import jax
import jax.numpy as jnp
from jax import lax

D = 2048
HEADS = 32
HEAD_DIM = 64
ROT = 16
FF = 5632
TOK_DEV = 128
GROUPS = 8
LENGTH = 2048


def draw_segment_ids(key, part):
    key = jax.random.fold_in(key, 11)
    first_key, second_key = jax.random.split(key)
    opening = jax.random.randint(first_key, (GROUPS, 1), 1, TOK_DEV)
    closing = jax.random.randint(second_key, (GROUPS, 1), LENGTH - TOK_DEV + 1, LENGTH)
    positions = jnp.arange(LENGTH, dtype=jnp.int32)[None, :]
    return (positions >= opening).astype(jnp.int32) + (positions >= closing).astype(jnp.int32)


def level_of(key, shape, cuts, least, top_value):
    def one(axis_at, blocks):
        heights = jax.random.uniform(jax.random.fold_in(jax.random.fold_in(key, 6), axis_at), (blocks,), jnp.float32, least / len(cuts), top_value / len(cuts))
        return jnp.repeat(jnp.exp(heights), shape[axis_at] // blocks).reshape((-1,) + (1,) * (len(shape) - axis_at - 1))

    loudness = one(*cuts[0])
    for cut in cuts[1:]:
        loudness = loudness * one(*cut)
    return loudness


def noise(key, extent, deviation, reach, cuts=(), held_as=jnp.bfloat16):
    array = jax.random.normal(key, extent, jnp.float32) * deviation
    if len(cuts) > 0:
        array = level_of(key, extent, cuts, -0.22, 0.18) * array
    return jnp.clip(array, min=-reach, max=reach).astype(held_as)


def setup_inputs(seed: int = 0) -> dict:
    streams_of = jax.random.split(jax.random.key(seed), 13)
    layer_in = noise(streams_of[0], (GROUPS, LENGTH, D), 1.0, 6.0, ((0, 8), (1, 16)))
    segment_ids = draw_segment_ids(jax.random.fold_in(streams_of[12], 71), 0)
    norm_one_gain = jnp.clip(1.0 + 0.1 * jax.random.normal(streams_of[2], (D,), jnp.float32), 0.5, 1.5)
    norm_one_shift = noise(streams_of[3], (D,), 0.3, 3.0, (), jnp.float32)
    qkv_weight = noise(streams_of[4], (D, 3 * D), D ** -0.5, 0.125, ((1, 8),))
    qkv_bias = noise(streams_of[5], (3 * D,), 0.4, 3.0, (), jnp.float32)
    out_weight = noise(streams_of[6], (D, D), (D // 16) ** -0.5, 0.5, ((1, 8),))
    norm_two_gain = jnp.clip(1.0 + 0.1 * jax.random.normal(streams_of[7], (D,), jnp.float32), 0.5, 1.5)
    norm_two_shift = noise(streams_of[8], (D,), 0.3, 3.0, (), jnp.float32)
    gate_up_weight = noise(streams_of[9], (D, 2, FF), D ** -0.5, 0.125, ((2, 8),))
    down_weight = noise(streams_of[10], (FF, D), FF ** -0.5, 0.078125, ((0, 8),))
    layer_grad = noise(streams_of[11], (GROUPS, LENGTH, D), 1.0, 6.0, ((0, 8), (1, 16)))
    return dict(layer_in=layer_in, segment_ids=segment_ids, norm_one_gain=norm_one_gain, norm_one_shift=norm_one_shift, qkv_weight=qkv_weight, qkv_bias=qkv_bias, out_weight=out_weight, norm_two_gain=norm_two_gain, norm_two_shift=norm_two_shift, gate_up_weight=gate_up_weight, down_weight=down_weight, layer_grad=layer_grad)


@jax.custom_vjp
def low(v):
    return lax.optimization_barrier(v.astype(jnp.bfloat16)).astype(jnp.float32)

@jax.custom_vjp
def low_back(v):
    return v

def low_keep(v):
    return (low(v), None)

def low_pass(kept, grad):
    return (grad,)

def back_keep(v):
    return (v, None)

def back_low(kept, grad):
    return (low(grad),)
low.defvjp(low_keep, low_pass)
low_back.defvjp(back_keep, back_low)
norm_eps = 1e-05
theta_base = 10000.0

def layer_norm(values, gain, shift):
    average = lax.optimization_barrier(jnp.mean(values, axis=-1, keepdims=True))
    centred = values - average
    spread = lax.optimization_barrier(jnp.mean(centred * centred, axis=-1, keepdims=True))
    return centred * lax.rsqrt(spread + norm_eps) * gain + shift

def matmul(left, right):
    return jnp.dot(left, right, preferred_element_type=jnp.float32, precision=lax.Precision.HIGHEST)

def rotary_tables(segment_row):
    positions = jnp.arange(segment_row.shape[0], dtype=jnp.int32)
    doc_start = lax.optimization_barrier(jnp.sum((segment_row[None, :] < segment_row[:, None]).astype(jnp.int32), axis=1))
    offsets = (positions - doc_start).astype(jnp.float32)
    inv_freq = jnp.exp(jnp.arange(ROT // 2, dtype=jnp.float32) * (-2.0 * math.log(theta_base) / ROT))
    angles = offsets[:, None] * inv_freq[None, :]
    return (jnp.cos(angles), jnp.sin(angles))

def rotate(values, cosine, sine):
    half_rot = ROT // 2
    leading = values[..., :half_rot]
    trailing = values[..., half_rot:ROT]
    passive = values[..., ROT:]
    cos_wide = cosine[:, None, :]
    sin_wide = sine[:, None, :]
    return jnp.concatenate([leading * cos_wide - trailing * sin_wide, trailing * cos_wide + leading * sin_wide, passive], axis=-1)

def forward(inputs, gain_one, shift_one, weight_qkv, bias_qkv, weight_out, gain_two, shift_two, weight_gate, weight_down, cosine, sine, segment_row):
    length = inputs.shape[0]
    score_scale = 1.0 / math.sqrt(HEAD_DIM)
    normed_one = low(layer_norm(inputs, gain_one, shift_one))
    projected = low_back(matmul(normed_one, weight_qkv) + bias_qkv)
    projected = projected.reshape(length, 3, HEADS, HEAD_DIM)
    queries = low(low_back(rotate(projected[:, 0], cosine, sine) * score_scale))
    keys_all = low(low_back(rotate(projected[:, 1], cosine, sine)))
    values_all = low(low_back(projected[:, 2]))
    block_rows = min(512, length)
    places = jnp.arange(length, dtype=jnp.int32)

    def one_block(block_index):
        first_row = block_index * block_rows
        query_block = lax.dynamic_slice_in_dim(queries, first_row, block_rows, 0)
        query_place = lax.dynamic_slice_in_dim(places, first_row, block_rows, 0)
        query_segments = lax.dynamic_slice_in_dim(segment_row, first_row, block_rows, 0)
        scores = low_back(jnp.einsum('qhd,khd->hqk', query_block, keys_all, precision=lax.Precision.HIGHEST))
        allowed = (query_place[:, None] >= places[None, :]) & (query_segments[:, None] == segment_row[None, :])
        scores = jnp.where(allowed[None], scores, -jnp.inf)
        weights_soft = low(jax.nn.softmax(scores, axis=-1))
        return jnp.einsum('hqk,khd->qhd', weights_soft, values_all, precision=lax.Precision.HIGHEST)
    blocks = lax.map(jax.checkpoint(one_block), jnp.arange(length // block_rows, dtype=jnp.int32))
    attended = low(low_back(blocks.reshape(length, HEADS * HEAD_DIM)))
    branch = low_back(matmul(attended, weight_out))
    middle = inputs + branch
    normed_two = low(layer_norm(middle, gain_two, shift_two))
    gate_up = low_back(jnp.einsum('td,dcf->tcf', normed_two, weight_gate, precision=lax.Precision.HIGHEST))
    hidden = low(jax.nn.silu(gate_up[:, 0]) * gate_up[:, 1])
    return middle + matmul(hidden, weight_down)

def reference(layer_in, segment_ids, norm_one_gain, norm_one_shift, qkv_weight, qkv_bias, out_weight, norm_two_gain, norm_two_shift, gate_up_weight, down_weight, layer_grad):
    params = tuple((weight.astype(jnp.float32) for weight in (norm_one_gain, norm_one_shift, qkv_weight, qkv_bias, out_weight, norm_two_gain, norm_two_shift, gate_up_weight, down_weight)))

    def row_step(totals, row_data):
        row_input, segment_row, row_grad = row_data
        cosine, sine = rotary_tables(segment_row)

        def run_layer(input_value, *weights):
            return forward(input_value, *weights, cosine, sine, segment_row)
        row_output, pullback = jax.vjp(run_layer, row_input.astype(jnp.float32), *params)
        gradients = pullback(row_grad.astype(jnp.float32))
        new_totals = tuple((total + gradient for total, gradient in zip(totals, gradients[1:])))
        return (new_totals, (row_output.astype(jnp.bfloat16), gradients[0].astype(jnp.bfloat16)))
    zero_sums = tuple((jnp.zeros(weight.shape, jnp.float32) for weight in params))
    totals, (outputs, input_grads) = lax.scan(row_step, zero_sums, (layer_in, segment_ids, layer_grad))
    return (outputs, input_grads, totals[0], totals[1], totals[2], totals[3], totals[4], totals[5], totals[6], totals[7], totals[8])
```

```python
import functools, math
import jax, jax.numpy as jnp
from jax import lax
from jax.experimental import pallas as pl
from jax.experimental.pallas import tpu as pltpu
from jax.sharding import PartitionSpec as P

MESH = pl.DeviceIdType.MESH

def coords():
    s = lax.axis_index("seq")
    w = lax.axis_index("wt")
    return s // 8, lax.rem(s // 2, 4), lax.rem(s, 2), w // 2, lax.rem(w, 2)

def at(yh, z, c, x, yl):
    return {"seq": yh * 8 + z * 2 + c, "wt": x * 2 + yl}

class Plane:
    def __init__(self, axis):
        self.axis = axis
        yh, z, c, x, yl = coords()
        self.c = c
        if axis == "wt":
            self.a, self.b = x, yl
            move = lambda da, db: at(yh, z, c, lax.rem(x + da + 4, 4), lax.rem(yl + db, 2))
        else:
            self.a, self.b = z, yh
            move = lambda da, db: at(lax.rem(yh + db, 2), lax.rem(z + da + 4, 4), c, x, yl)
        self.left, self.right, self.pair = move(-1, 0), move(1, 0), move(0, 1)
        self.twin = at(yh, z, 1 - c, x, yl)

    def block(self, da, db):
        a, b = lax.rem(self.a + da + 4, 4), lax.rem(self.b + db, 2)
        return a * 2 + b if self.axis == "wt" else b * 4 + a

def remote(src, dst, ssem, rsem, k, target):
    return pltpu.make_async_remote_copy(src_ref=src, dst_ref=dst, send_sem=ssem.at[k], recv_sem=rsem.at[k], device_id=target, device_id_type=MESH)

def greet(targets):
    bar = pltpu.get_barrier_semaphore()
    for t in targets:
        pl.semaphore_signal(bar, inc=1, device_id=t, device_id_type=MESH)
    pl.semaphore_wait(bar, len(targets))

GATHER_MSGS = 18
def gather_steps(pn, own, buf, rows, ssem, rsem, index=lambda j: j):
    h, q = rows // 2, rows // 4
    P_, Q_ = (0, h), (h, h)
    P0, P1, Q0, Q1 = (0, q), (q, q), (h, q), (h + q, q)
    L, Rt, Y = pn.left, pn.right, pn.pair
    table = {
        0: (Y, (0, 0), P_, (0, 1)),
        1: (Rt, (0, 0), Q_, (-1, 0)),
        2: (L, (0, 0), Q_, (1, 0)),
        3: (Rt, (0, 0), P_, (-1, 0)),
        4: (L, (0, 0), P_, (1, 0)),
        5: (Y, (0, 0), Q_, (0, 1)),
        6: (Rt, (-1, 0), Q0, (2, 0)),
        7: (Y, (-1, 0), Q_, (-1, 1)),
        8: (L, (1, 0), Q1, (2, 0)),
        9: (Y, (1, 0), Q_, (1, 1)),
        10: (Rt, (0, 1), P_, (-1, 1)),
        11: (L, (0, 1), P_, (1, 1)),
        12: (Rt, (-1, 0), P0, (2, 0)),
        13: (L, (1, 0), P1, (2, 0)),
        14: (Y, (2, 0), Q0, (2, 1)),
        15: (Y, (2, 0), Q1, (2, 1)),
        16: (Rt, (-1, 1), P0, (2, 1)),
        17: (L, (1, 1), P1, (2, 1)),
    }
    def part(d, r):
        return buf.at[index(pn.block(*d)), pl.ds(*r)]
    def send(k):
        t, d, r, _ = table[k]
        src = own.at[pl.ds(*r)] if d == (0, 0) else part(d, r)
        remote(src, part(d, r), ssem, rsem, k, t).start()
    def got(k):
        t, _, r, d = table[k]
        remote(part(d, r), part(d, r), ssem, rsem, k, t).wait_recv()
    def sent(k):
        t, d, r, _ = table[k]
        remote(part(d, r), part(d, r), ssem, rsem, k, t).wait_send()
    def first():
        for k in (0, 1, 2, 3, 4, 5): send(k)
    def after(k, *next_):
        def f():
            got(k)
            for n in next_: send(n)
        return f
    steps = [first, after(1, 6, 7), after(2, 8, 9), after(0, 10, 11), after(3, 12), after(4, 13),
             after(6, 14), after(8, 15), after(10, 16), after(11, 17)]
    tail = [after(5), after(7), after(9), after(12), after(13), after(14), after(15), after(16), after(17)]
    def done():
        for k in range(18): sent(k)
    return steps, tail, done

SUM_MSGS = 17
def sum_steps(pn, buf, land, rows, ssem, rsem, out, index=lambda j: j, add=None):
    h, q = rows // 2, rows // 4
    P_, Q_ = (0, h), (h, h)
    P0, P1, Q0, Q1 = (0, q), (q, q), (h, q), (h + q, q)
    L, Rt, Y = pn.left, pn.right, pn.pair
    table = {}
    off = 0
    def msg(k, t, d, r, r_to):
        nonlocal off
        table[k] = (t, d, r, off, r_to)
        off += r[1]
    msg(0, L, (-2, 0), P0, (-1, 0)); msg(1, Rt, (2, 0), P1, (1, 0))
    msg(2, L, (-2, 1), P0, (-1, 1)); msg(3, Rt, (2, 1), P1, (1, 1))
    msg(4, Y, (2, 1), Q_, (2, 0)); msg(5, Y, (-1, 1), Q_, (-1, 0)); msg(6, Y, (1, 1), Q_, (1, 0)); msg(7, Y, (0, 1), Q_, (0, 0))
    msg(8, L, (-1, 1), P_, (0, 1)); msg(9, Rt, (1, 1), P_, (0, 1))
    msg(10, L, (-1, 0), P_, (0, 0)); msg(11, Rt, (1, 0), P_, (0, 0))
    msg(12, L, (-2, 0), Q0, (-1, 0)); msg(13, Rt, (2, 0), Q1, (1, 0))
    msg(14, L, (-1, 0), Q_, (0, 0)); msg(15, Rt, (1, 0), Q_, (0, 0))
    msg(16, Y, (0, 1), P_, (0, 0))
    assert off <= 7 * rows, off
    def part(d, r):
        return buf.at[index(pn.block(*d)), pl.ds(*r)]
    def landing(k):
        _, _, r, o, _ = table[k]
        return land.at[pl.ds(o, r[1])]
    def send(k):
        t, d, r, _, _ = table[k]
        remote(part(d, r), landing(k), ssem, rsem, k, t).start()
    def got(k):
        remote(landing(k), landing(k), ssem, rsem, k, table[k][0]).wait_recv()
    def sent(k):
        remote(landing(k), landing(k), ssem, rsem, k, table[k][0]).wait_send()
    def accumulate(d, r, ks, to=None):
        j = index(pn.block(*d))
        step = 16
        def body(i, _):
            at_ = pl.multiple_of(r[0] + i * step, step)
            v = buf[j, pl.ds(at_, step)].astype(jnp.float32)
            for k in ks:
                v = v + land[pl.ds(pl.multiple_of(table[k][3] + i * step, step), step)].astype(jnp.float32)
            if to is None:
                buf[j, pl.ds(at_, step)] = v.astype(buf.dtype)
            else:
                to[pl.ds(at_, step)] = v.astype(to.dtype)
            return 0
        lax.fori_loop(0, r[1] // step, body, 0)
    def s0():
        for k in range(8): send(k)
    def s1():
        got(2); accumulate((-1, 1), P0, [2]); send(8)
        got(3); accumulate((1, 1), P1, [3]); send(9)
    def s2():
        got(0); accumulate((-1, 0), P0, [0]); send(10)
        got(1); accumulate((1, 0), P1, [1]); send(11)
    def s3():
        got(4); accumulate((2, 0), Q_, [4]); send(12); send(13)
    def s4():
        got(5); accumulate((-1, 0), Q_, [5]); got(12); accumulate((-1, 0), Q0, [12]); send(14)
        got(6); accumulate((1, 0), Q_, [6]); got(13); accumulate((1, 0), Q1, [13]); send(15)
    def s5():
        got(8); got(9); accumulate((0, 1), P_, [8, 9]); send(16)
    def s6():
        got(7); got(14); got(15); accumulate((0, 0), Q_, [7, 14, 15], out)
        got(10); got(11); got(16); accumulate((0, 0), P_, [10, 11, 16], out)
    def done():
        for k in range(17): sent(k)
    return [s0, s1, s2, s3, s4, s5, s6], done
ANY = pl.BlockSpec(memory_space=pl.ANY)
QB, KB = 512, 256
MASKED = -1e30
NT = (((1,), (1,)), ((), ()))

def halves(ref, kept):
    lane = lax.broadcasted_iota(jnp.int32, (1, 128), 1)
    low = (lane < 64).astype(jnp.float32)
    v = ref[...].astype(jnp.float32)
    kept[0] = (v * low).astype(jnp.bfloat16)
    kept[1] = (v * (1.0 - low)).astype(jnp.bfloat16)

def allowed(i, j, start):
    key = j * KB + lax.broadcasted_iota(jnp.int32, (KB, QB), 0)
    query = i * QB + lax.broadcasted_iota(jnp.int32, (KB, QB), 1)
    return (key <= query) & (key >= start)

def attn_fwd(q_ref, k_ref, v_ref, start_ref, o_ref, ot_ref, lse_ref, kept, vt):
    halves(k_ref, kept)
    vt[...] = v_ref[...].astype(jnp.float32).T.astype(jnp.bfloat16)
    n = q_ref.shape[0] // QB
    for i in range(n):
        q = q_ref[QB * i:QB * (i + 1)]
        start = start_ref[:, QB * i:QB * (i + 1)]
        def step(masked, j, carry):
            r = pl.ds(pl.multiple_of(j * KB, KB), KB)
            out = []
            for h in range(2):
                m, l, acc = carry[h]
                s = lax.dot_general(kept[h, r], q, NT, preferred_element_type=jnp.float32)
                if masked:
                    s = jnp.where(allowed(i, j, start), s, MASKED)
                top = jnp.maximum(m, jnp.max(s, axis=0, keepdims=True))
                p = jnp.exp(s - top)
                fade = jnp.exp(m - top)
                l = l * fade + jnp.sum(p, axis=0, keepdims=True)
                acc = acc * fade + jnp.dot(vt[64 * h:64 * h + 64, r], p.astype(jnp.bfloat16), preferred_element_type=jnp.float32)
                out.append((top, l, acc))
            return tuple(out)
        one = (jnp.full((1, QB), MASKED, jnp.float32), jnp.zeros((1, QB), jnp.float32), jnp.zeros((64, QB), jnp.float32))
        carry = (one, one)
        if i == n - 1:
            carry = lax.fori_loop(0, 2 * i + 2, functools.partial(step, True), carry)
        else:
            if i:
                carry = step(True, 0, carry)
                carry = lax.fori_loop(1, 2 * i, functools.partial(step, False), carry)
            carry = lax.fori_loop(2 * i, 2 * i + 2, functools.partial(step, True), carry)
        cols = pl.ds(QB * i, QB)
        for h in range(2):
            m, l, acc = carry[h]
            ot_ref[64 * h:64 * h + 64, cols] = acc / l
            lse_ref[h:h + 1, cols] = m + jnp.log(l)
        o_ref[QB * i:QB * (i + 1)] = ot_ref[:, cols].T.astype(jnp.bfloat16)

def attn_bwd(q_ref, k_ref, v_ref, start_ref, ot_ref, lse_ref, do_ref, dq_ref, dk_ref, dv_ref, keptk, keptv, keptq, keptd, kt, dot_):
    halves(k_ref, keptk)
    halves(v_ref, keptv)
    halves(q_ref, keptq)
    halves(do_ref, keptd)
    kt[...] = k_ref[...].astype(jnp.float32).T.astype(jnp.bfloat16)
    dot_[...] = do_ref[...].astype(jnp.float32).T
    dk_ref[...] = jnp.zeros_like(dk_ref)
    dv_ref[...] = jnp.zeros_like(dv_ref)
    n = q_ref.shape[0] // QB
    for i in range(n):
        rows = pl.ds(QB * i, QB)
        q = q_ref[rows]
        do = do_ref[rows]
        start = start_ref[:, rows]
        both = ot_ref[:, rows] * dot_[:, rows]
        inner = [jnp.sum(both[64 * h:64 * h + 64], axis=0, keepdims=True) for h in range(2)]
        lse = [lse_ref[h:h + 1, rows] for h in range(2)]
        def step(masked, j, carry):
            r = pl.ds(pl.multiple_of(j * KB, KB), KB)
            out, ps, ds = [], [], []
            for h in range(2):
                s = lax.dot_general(keptk[h, r], q, NT, preferred_element_type=jnp.float32)
                if masked:
                    s = jnp.where(allowed(i, j, start), s, MASKED)
                p = jnp.exp(s - lse[h])
                dp = lax.dot_general(keptv[h, r], do, NT, preferred_element_type=jnp.float32)
                g = (p * (dp - inner[h])).astype(jnp.bfloat16)
                out.append(carry[h] + jnp.dot(kt[64 * h:64 * h + 64, r], g, preferred_element_type=jnp.float32))
                ps.append(p.astype(jnp.bfloat16))
                ds.append(g)
            dv_ref[r] += sum(jnp.dot(ps[h], keptd[h, rows], preferred_element_type=jnp.float32) for h in range(2))
            dk_ref[r] += sum(jnp.dot(ds[h], keptq[h, rows], preferred_element_type=jnp.float32) for h in range(2))
            return tuple(out)
        carry = (jnp.zeros((64, QB), jnp.float32),) * 2
        if i == n - 1:
            carry = lax.fori_loop(0, 2 * i + 2, functools.partial(step, True), carry)
        else:
            if i:
                carry = step(True, 0, carry)
                carry = lax.fori_loop(1, 2 * i, functools.partial(step, False), carry)
            carry = lax.fori_loop(2 * i, 2 * i + 2, functools.partial(step, True), carry)
        dq_ref[rows] = jnp.concatenate(carry, axis=0).T

VM = pl.BlockSpec(memory_space=pltpu.VMEM)

def attention_forward(q, k, v, start):
    rows = q.shape[0]
    f = jax.ShapeDtypeStruct
    return pl.pallas_call(
        attn_fwd, out_shape=(f((rows, 128), jnp.bfloat16), f((128, rows), jnp.float32), f((8, rows), jnp.float32)),
        in_specs=[VM] * 4, out_specs=(VM,) * 3,
        scratch_shapes=[pltpu.VMEM((2, rows, 128), jnp.bfloat16), pltpu.VMEM((128, rows), jnp.bfloat16)],
        compiler_params=pltpu.CompilerParams(vmem_limit_bytes=56 * 2**20), name="attend",
    )(q, k, v, start)

def attention_backward(q, k, v, start, ot, lse, do):
    rows = q.shape[0]
    f = jax.ShapeDtypeStruct
    return pl.pallas_call(
        attn_bwd, out_shape=(f((rows, 128), jnp.float32),) * 3,
        in_specs=[VM] * 7, out_specs=(VM,) * 3,
        scratch_shapes=[pltpu.VMEM((2, rows, 128), jnp.bfloat16)] * 4 + [pltpu.VMEM((128, rows), jnp.bfloat16), pltpu.VMEM((128, rows), jnp.float32)],
        compiler_params=pltpu.CompilerParams(vmem_limit_bytes=56 * 2**20), name="attend_back",
    )(q, k, v, start, ot, lse, do)
def params(cid):
    return pltpu.CompilerParams(collective_id=cid, has_side_effects=True, vmem_limit_bytes=56 * 2**20)

def dma(n):
    return pltpu.SemaphoreType.DMA((n,))

def gather_kernel(axis, x, o, ss, rs, ls):
    pn = Plane(axis)
    greet([pn.left, pn.right, pn.pair])
    cp = pltpu.make_async_copy(x, o.at[pn.block(0, 0)], ls)
    cp.start()
    steps, tail, done = gather_steps(pn, x, o, x.shape[0], ss, rs)
    for f in steps + tail:
        f()
    done()
    cp.wait()

def gather(axis, cid, x):
    return pl.pallas_call(
        functools.partial(gather_kernel, axis), out_shape=jax.ShapeDtypeStruct((8,) + x.shape, x.dtype),
        in_specs=[VM], out_specs=VM, scratch_shapes=[dma(18), dma(18), pltpu.SemaphoreType.DMA],
        compiler_params=params(cid), name="gather_" + axis)(x)

def gather_both_kernel(axis, x, o, ss, rs, ls, ts, tr):
    pn = Plane(axis)
    greet([pn.left, pn.right, pn.pair, pn.twin])
    index = lambda j: 2 * j + pn.c
    mine = index(pn.block(0, 0))
    cp = pltpu.make_async_copy(x, o.at[mine], ls)
    cp.start()
    cp.wait()
    steps, tail, done = gather_steps(pn, x, o, x.shape[0], ss, rs, index)
    order = [(0, 0), (0, 1), (-1, 1), (1, 1), (-1, 0), (1, 0), (2, 0), (2, 1)]
    def hand(k):
        j = index(pn.block(*order[k]))
        remote(o.at[j], o.at[j], ts, tr, k, pn.twin).start()
    steps[0]()
    hand(0)
    for f in steps[1:]:
        f()
    ready = {0: [1], 1: [2], 2: [3], 3: [4], 4: [5], 6: [6], 8: [7]}
    for i, f in enumerate(tail):
        f()
        for k in ready.get(i, []):
            hand(k)
    done()
    for k in range(8):
        j = 2 * pn.block(*order[k]) + 1 - pn.c
        remote(o.at[j], o.at[j], ts, tr, k, pn.twin).wait()

def gather_both(axis, cid, x):
    return pl.pallas_call(
        functools.partial(gather_both_kernel, axis), out_shape=jax.ShapeDtypeStruct((16,) + x.shape, x.dtype),
        in_specs=[VM], out_specs=VM, scratch_shapes=[dma(18), dma(18), pltpu.SemaphoreType.DMA, dma(8), dma(8)],
        compiler_params=params(cid), name="gather_both_" + axis)(x)

def scatter_kernel(axis, x, o, buf, land, ss, rs, ls):
    pn = Plane(axis)
    cp = pltpu.make_async_copy(x, buf, ls)
    cp.start()
    greet([pn.left, pn.right, pn.pair])
    cp.wait()
    steps, done = sum_steps(pn, buf, land, x.shape[1], ss, rs, o)
    for f in steps:
        f()
    done()

def scatter(axis, cid, x):
    _, rows, cols = x.shape
    return pl.pallas_call(
        functools.partial(scatter_kernel, axis), out_shape=jax.ShapeDtypeStruct((rows, cols), jnp.float32),
        in_specs=[ANY], out_specs=VM,
        scratch_shapes=[pltpu.VMEM(x.shape, x.dtype), pltpu.VMEM((7 * rows, cols), x.dtype), dma(17), dma(17), pltpu.SemaphoreType.DMA],
        compiler_params=params(cid), name="scatter_" + axis)(x)

def scatter_both_kernel(axis, x, o, buf, tland, land, ss, rs, ls, ts, tr):
    pn = Plane(axis)
    rows = x.shape[1]
    cp = pltpu.make_async_copy(x, buf, ls)
    cp.start()
    greet([pn.left, pn.right, pn.pair, pn.twin])
    cp.wait()
    order = [(2, 0), (2, 1), (-1, 1), (1, 1), (-1, 0), (1, 0), (0, 1), (0, 0)]
    for k in range(8):
        j = pn.block(*order[k])
        remote(buf.at[2 * j + 1 - pn.c], tland.at[k], ts, tr, k, pn.twin).start()
    for k in range(8):
        j = 2 * pn.block(*order[k]) + pn.c
        remote(tland.at[k], tland.at[k], ts, tr, k, pn.twin).wait_recv()
        def body(i, _):
            r = pl.ds(pl.multiple_of(i * 16, 16), 16)
            buf[j, r] = (buf[j, r].astype(jnp.float32) + tland[k, r].astype(jnp.float32)).astype(buf.dtype)
            return 0
        lax.fori_loop(0, rows // 16, body, 0)
    steps, done = sum_steps(pn, buf, land, rows, ss, rs, o, lambda j: 2 * j + pn.c)
    for f in steps:
        f()
    done()
    for k in range(8):
        remote(tland.at[k], tland.at[k], ts, tr, k, pn.twin).wait_send()

def scatter_both(axis, cid, x):
    _, rows, cols = x.shape
    return pl.pallas_call(
        functools.partial(scatter_both_kernel, axis), out_shape=jax.ShapeDtypeStruct((rows, cols), jnp.float32),
        in_specs=[ANY], out_specs=VM,
        scratch_shapes=[pltpu.VMEM(x.shape, x.dtype), pltpu.VMEM((8, rows, cols), x.dtype), pltpu.VMEM((7 * rows, cols), x.dtype),
                        dma(17), dma(17), pltpu.SemaphoreType.DMA, dma(8), dma(8)],
        compiler_params=params(cid), name="scatter_both_" + axis)(x)

def swap_kernel(axis, n, x, o, ss, rs, ls):
    me = lax.axis_index(axis)
    peers = [lax.rem(me + d, n) for d in range(1, n)]
    bar = pltpu.get_barrier_semaphore()
    for p in peers:
        pl.semaphore_signal(bar, inc=1, device_id={axis: p}, device_id_type=MESH)
    cp = pltpu.make_async_copy(x.at[me], o.at[me], ls)
    cp.start()
    pl.semaphore_wait(bar, n - 1)
    def copy(d):
        return remote(x.at[lax.rem(me + d, n)], o.at[me], ss, rs, d - 1, {axis: lax.rem(me + d, n)})
    for d in range(1, n):
        copy(d).start()
    for d in range(1, n):
        j = lax.rem(me - d + n, n)
        remote(x.at[j], o.at[j], ss, rs, d - 1, {axis: j}).wait()
    cp.wait()

def swap(axis, n, cid, x):
    return pl.pallas_call(
        functools.partial(swap_kernel, axis, n), out_shape=jax.ShapeDtypeStruct(x.shape, x.dtype),
        in_specs=[VM], out_specs=VM, scratch_shapes=[dma(n - 1), dma(n - 1), pltpu.SemaphoreType.DMA],
        compiler_params=params(cid), name="swap_" + axis)(x)

def fetch_kernel(x, o, ss, rs, ls):
    s, w = lax.axis_index("seq"), lax.axis_index("wt")
    bar = pltpu.get_barrier_semaphore()
    for d in range(1, 8):
        pl.semaphore_signal(bar, inc=1, device_id={"wt": lax.rem(w + d, 8)}, device_id_type=MESH)
    pl.semaphore_wait(bar, 7)
    for p in range(3):
        g = 16 * p + s
        @pl.when(w == g // 6)
        def _():
            src = x.at[lax.rem(g, 6)]
            cp = pltpu.make_async_copy(src, o.at[p], ls)
            cp.start()
            for d in range(1, 8):
                remote(src, o.at[p], ss.at[p], rs, p, {"wt": lax.rem(w + d, 8)}).start() if False else pltpu.make_async_remote_copy(src_ref=src, dst_ref=o.at[p], send_sem=ss.at[p, d - 1], recv_sem=rs.at[p], device_id={"wt": lax.rem(w + d, 8)}, device_id_type=MESH).start()
            cp.wait()
    for p in range(3):
        g = 16 * p + s
        @pl.when(w == g // 6)
        def _():
            for d in range(1, 8):
                pltpu.make_async_remote_copy(src_ref=o.at[p], dst_ref=o.at[p], send_sem=ss.at[p, d - 1], recv_sem=rs.at[p], device_id={"wt": lax.rem(w + d, 8)}, device_id_type=MESH).wait_send()
        @pl.when(w != g // 6)
        def _():
            pltpu.make_async_remote_copy(src_ref=o.at[p], dst_ref=o.at[p], send_sem=ss.at[p, 0], recv_sem=rs.at[p], device_id={"wt": lax.rem(w + 1, 8)}, device_id_type=MESH).wait_recv()

def fetch(cid, x):
    return pl.pallas_call(
        fetch_kernel, out_shape=jax.ShapeDtypeStruct((3,) + x.shape[1:], x.dtype),
        in_specs=[VM], out_specs=VM, scratch_shapes=[pltpu.SemaphoreType.DMA((3, 7)), dma(3), pltpu.SemaphoreType.DMA],
        compiler_params=params(cid), name="fetch_heads")(x)

def place_kernel(x, o, ss, rs, ls):
    s, w = lax.axis_index("seq"), lax.axis_index("wt")
    bar = pltpu.get_barrier_semaphore()
    def source(b):
        g = 6 * w + b
        return lax.rem(g, 16), s // 2
    def target(i, p):
        g = 16 * p + s
        return 2 * w + i, g // 6, lax.rem(g, 6)
    own = jnp.int32(0)
    for b in range(6):
        ts, tw = source(b)
        same = (ts == s) & (tw == w)
        own += same.astype(jnp.int32)
        @pl.when(jnp.logical_not(same))
        def _():
            pl.semaphore_signal(bar, inc=1, device_id={"seq": ts, "wt": tw}, device_id_type=MESH)
    pl.semaphore_wait(bar, 6 - own)
    def copy(i, p):
        ts, tw, slot = target(i, p)
        return pltpu.make_async_remote_copy(src_ref=x.at[i, p], dst_ref=o.at[slot], send_sem=ss.at[i, p], recv_sem=rs.at[slot], device_id={"seq": ts, "wt": tw}, device_id_type=MESH)
    def local(i, p):
        return pltpu.make_async_copy(x.at[i, p], o.at[target(i, p)[2]], ls.at[i, p])
    for i in range(2):
        for p in range(3):
            ts, tw, _ = target(i, p)
            same = (ts == s) & (tw == w)
            @pl.when(same)
            def _():
                local(i, p).start()
            @pl.when(jnp.logical_not(same))
            def _():
                copy(i, p).start()
    for i in range(2):
        for p in range(3):
            ts, tw, _ = target(i, p)
            same = (ts == s) & (tw == w)
            @pl.when(same)
            def _():
                local(i, p).wait()
            @pl.when(jnp.logical_not(same))
            def _():
                copy(i, p).wait_send()
    for b in range(6):
        ts, tw = source(b)
        @pl.when(jnp.logical_not((ts == s) & (tw == w)))
        def _():
            pltpu.make_async_remote_copy(src_ref=o.at[b], dst_ref=o.at[b], send_sem=ss.at[0, 0], recv_sem=rs.at[b], device_id={"seq": ts, "wt": tw}, device_id_type=MESH).wait_recv()

def place(cid, x):
    return pl.pallas_call(
        place_kernel, out_shape=jax.ShapeDtypeStruct((6, 128, 128), x.dtype),
        in_specs=[VM], out_specs=VM, scratch_shapes=[pltpu.SemaphoreType.DMA((2, 3)), dma(6), pltpu.SemaphoreType.DMA((2, 3))],
        compiler_params=params(cid), name="place_qkv")(x)

def small_kernel(x, o, land, mid, land2, ss, rs, ss2, rs2):
    s, w = lax.axis_index("seq"), lax.axis_index("wt")
    bar = pltpu.get_barrier_semaphore()
    for d in range(1, 8):
        pl.semaphore_signal(bar, inc=1, device_id={"wt": lax.rem(w + d, 8)}, device_id_type=MESH)
    for d in range(1, 16):
        pl.semaphore_signal(bar, inc=1, device_id={"seq": lax.rem(s + d, 16)}, device_id_type=MESH)
    pl.semaphore_wait(bar, 22)
    for d in range(1, 8):
        remote(x.at[lax.rem(w + d, 8)], land.at[d - 1], ss, rs, d - 1, {"wt": lax.rem(w + d, 8)}).start()
    for d in range(1, 8):
        remote(x.at[0], land.at[d - 1], ss, rs, d - 1, {"wt": lax.rem(w + d, 8)}).wait()
    mid[:, 0] = x[w] + jnp.sum(land[...], axis=0)
    for d in range(1, 16):
        remote(mid.at[lax.rem(s + d, 16)], land2.at[d - 1], ss2, rs2, d - 1, {"seq": lax.rem(s + d, 16)}).start()
    for d in range(1, 16):
        remote(mid.at[0], land2.at[d - 1], ss2, rs2, d - 1, {"seq": lax.rem(s + d, 16)}).wait()
    o[...] = mid[s] + jnp.sum(land2[...], axis=0)

def small_sum(cid, x):
    f = jnp.float32
    return pl.pallas_call(
        small_kernel, out_shape=jax.ShapeDtypeStruct((1, 128), f),
        in_specs=[VM], out_specs=VM,
        scratch_shapes=[pltpu.VMEM((7, 16, 128), f), pltpu.VMEM((16, 1, 128), f), pltpu.VMEM((15, 1, 128), f), dma(7), dma(7), dma(15), dma(15)],
        compiler_params=params(cid), name="small_sum")(x)


norm_eps = 1e-05
theta_base = 10000.0
ROT = 16
HEAD_DIM = 64


def layer_norm_parts(values, gain, shift):
    average = jnp.mean(values, axis=-1, keepdims=True)
    centred = values - average
    spread = jnp.mean(centred * centred, axis=-1, keepdims=True)
    inverse = lax.rsqrt(spread + norm_eps)
    scaled = centred * inverse
    return (scaled * gain + shift, scaled, inverse)


def layer_norm_back(upward, scaled, inverse, gain):
    weighted = upward * gain
    first_mean = jnp.mean(weighted, axis=-1, keepdims=True)
    second_mean = jnp.mean(weighted * scaled, axis=-1, keepdims=True)
    return inverse * (weighted - first_mean - scaled * second_mean)


def rotary_tables(segment_row):
    rows = segment_row.shape[0]
    ends = [jnp.sum((segment_row < i).astype(jnp.int32)) for i in (1, 2)]
    start = jnp.where(segment_row == 0, 0, jnp.where(segment_row == 1, ends[0], ends[1]))
    offsets = (jnp.arange(rows, dtype=jnp.int32) - start).astype(jnp.float32)
    inv_freq = jnp.exp(jnp.arange(ROT // 2, dtype=jnp.float32) * (-2.0 * math.log(theta_base) / ROT))
    angles = offsets[:, None] * inv_freq[None, :]
    c, s = jnp.cos(angles), jnp.sin(angles)
    one, nil = jnp.ones((rows, 48), jnp.float32), jnp.zeros((rows, 56), jnp.float32)
    z8 = jnp.zeros((rows, 8), jnp.float32)
    keep = jnp.concatenate([c, c, one] * 2, axis=1)
    ahead = jnp.concatenate([-s, nil] * 2, axis=1)
    behind = jnp.concatenate([z8, s, nil[:, :48]] * 2, axis=1)
    return start, keep, ahead, behind


def rotate(v, keep, ahead, behind):
    return v * keep + jnp.roll(v, -8, axis=1) * ahead + jnp.roll(v, 8, axis=1) * behind


def contract_first(left, right):
    return lax.dot_general(left, right, (((0,), (0,)), ((), ())), preferred_element_type=jnp.float32)


def contract_last(left, right):
    return lax.dot_general(left, right, (((1,), (1,)), ((), ())), preferred_element_type=jnp.float32)


def per_device(layer_in, segment_ids, norm_one_gain, norm_one_shift, qkv_weight, qkv_bias, out_weight, norm_two_gain,
               norm_two_shift, gate_up_weight, down_weight, layer_grad):
    f32, bf16 = jnp.float32, jnp.bfloat16
    s, w = lax.axis_index("seq"), lax.axis_index("wt")
    tok, width = layer_in.shape[1:]
    rows = segment_ids.shape[1]
    hidden = down_weight.shape[0]
    scale = 1.0 / math.sqrt(HEAD_DIM)
    inputs = layer_in.reshape(tok, width).astype(f32)
    upstream = layer_grad.reshape(tok, width)
    start, keep, ahead, behind = rotary_tables(segment_ids.reshape(rows))
    start = start.reshape(1, rows)
    normed_one, scaled_one, inverse_one = layer_norm_parts(inputs, norm_one_gain, norm_one_shift)
    row_normed = gather_both("seq", 0, normed_one.astype(bf16)).reshape(rows, width)
    head_weight = fetch(1, qkv_weight.reshape(width, 6, 128).transpose(1, 0, 2))
    head_weight = head_weight.transpose(1, 0, 2).reshape(width, 384)
    bias = lax.dynamic_index_in_dim(qkv_bias.reshape(3, 16, 128), s, 1, keepdims=False).reshape(384)
    proj = jnp.dot(row_normed, head_weight, preferred_element_type=f32) + bias
    q = (rotate(proj[:, :128], keep, ahead, behind) * scale).astype(bf16)
    k = rotate(proj[:, 128:256], keep, ahead, behind).astype(bf16)
    v = proj[:, 256:].astype(bf16)
    o, ot, lse = attention_forward(q, k, v, start)
    attended = swap("seq", 16, 2, o.reshape(16, tok, 128)).transpose(1, 0, 2).reshape(tok, width)
    half = lax.dynamic_slice_in_dim(out_weight, (s % 2) * (width // 2), width // 2, 0)
    out_all = gather_both("wt", 3, half).reshape(8, 2, width // 2, 256)
    branch = jnp.einsum("tck,wckn->twn", attended.reshape(tok, 2, width // 2), out_all, preferred_element_type=f32).reshape(tok, width)
    middle = inputs + branch
    normed_two, scaled_two, inverse_two = layer_norm_parts(middle, norm_two_gain, norm_two_shift)
    all_two = gather("wt", 4, normed_two.astype(bf16)).reshape(8 * tok, width)
    all_up = gather("wt", 5, upstream).reshape(8 * tok, width)
    weight_gu = gate_up_weight.reshape(width, 2 * hidden)
    gu = jnp.dot(all_two, weight_gu, preferred_element_type=f32)
    g, u = gu[:, :hidden], gu[:, hidden:]
    sigma = jax.nn.sigmoid(g)
    act = (g * sigma * u).astype(bf16)
    ffn_part = jnp.dot(act, down_weight, preferred_element_type=f32).astype(bf16)
    dact = contract_last(all_up, down_weight)
    dg = (dact * u * sigma * (1.0 + g * (1.0 - sigma))).astype(bf16)
    du = (dact * g * sigma).astype(bf16)
    dgu = jnp.concatenate([dg, du], axis=1)
    dh2_part = contract_last(dgu, weight_gu).astype(bf16)
    dh2 = scatter("wt", 6, dh2_part.reshape(8, tok, width))
    ffn_out = scatter("wt", 7, ffn_part.reshape(8, tok, width))
    layer_out = (middle + ffn_out).astype(bf16).reshape(1, tok, width)
    gain_two = jnp.sum(dh2 * scaled_two, axis=0)
    shift_two = jnp.sum(dh2, axis=0)
    middle_grad = upstream.astype(f32) + layer_norm_back(dh2, scaled_two, inverse_two, norm_two_gain)
    da = middle_grad.astype(bf16)
    dout = jnp.einsum("twn,wckn->tck", da.reshape(tok, 8, 256), out_all, preferred_element_type=f32).astype(bf16)
    do = swap("seq", 16, 8, dout.reshape(tok, 16, 128).transpose(1, 0, 2)).reshape(rows, 128)
    dq, dk, dv = attention_backward(q, k, v, start, ot, lse, do)
    low = lambda t: t.astype(bf16).astype(f32)
    dproj = jnp.concatenate([rotate(low(dq) * scale, keep, -ahead, -behind), rotate(low(dk), keep, -ahead, -behind), dv], axis=1).astype(bf16)
    dh1_part = contract_last(dproj, head_weight).astype(bf16)
    dh1 = scatter_both("seq", 9, dh1_part.reshape(16, tok, width))
    gain_one = jnp.sum(dh1 * scaled_one, axis=0)
    shift_one = jnp.sum(dh1, axis=0)
    dx = middle_grad + layer_norm_back(dh1, scaled_one, inverse_one, norm_one_gain)
    input_grad = dx.astype(bf16).reshape(1, tok, width)
    qkv_part = contract_first(row_normed, dproj).astype(bf16)
    qkv_rows = scatter("wt", 10, qkv_part.reshape(8, 256, 384)).astype(bf16)
    qkv_grad = place(11, qkv_rows.reshape(2, 128, 3, 128).transpose(0, 2, 1, 3))
    qkv_grad = qkv_grad.transpose(1, 0, 2).reshape(128, 768).astype(f32)
    all_att = gather("wt", 12, attended).reshape(8 * tok, width)
    da_cols = swap("wt", 8, 13, da.reshape(tok, 8, 256).transpose(1, 0, 2)).reshape(8 * tok, 256)
    out_part = contract_first(all_att, da_cols).astype(bf16)
    gate_part = contract_first(all_two, dgu).astype(bf16)
    down_part = contract_first(all_up, act).astype(bf16)
    joined = jnp.concatenate([gate_part, down_part, out_part], axis=1).reshape(16, 128, 3 * hidden + 256)
    joined = scatter_both("seq", 14, joined)
    gate_grad = joined[:, :2 * hidden].reshape(128, 2, hidden)
    down_grad = joined[:, 2 * hidden:3 * hidden].T
    out_grad = joined[:, 3 * hidden:]
    bias_grad = lax.dynamic_update_slice(jnp.zeros((3, 16, 128), f32), jnp.sum(dproj.astype(f32), axis=0).reshape(3, 1, 128), (0, s, 0))
    blocks = [t.reshape(16, 8, -1) for t in (gain_one, shift_one, bias_grad, gain_two, shift_two, jnp.zeros((16 * 8 * 16,), f32))]
    small = small_sum(15, jnp.concatenate(blocks, axis=2).transpose(1, 0, 2))[0]
    return (layer_out, input_grad, small[0:16], small[16:32], qkv_grad, small[32:80], out_grad, small[80:96], small[96:112], gate_grad, down_grad)


def solution(mesh):
    both = P(("seq", "wt"))
    return jax.shard_map(
        per_device, mesh=mesh,
        in_specs=(P("wt", "seq", None), P("wt", None), P(), P(), P(None, "wt"), P(), P(None, "wt"), P(), P(), P(None, None, "wt"), P("wt", None), P("wt", "seq", None)),
        out_specs=(P("wt", "seq", None), P("wt", "seq", None), both, both, P("seq", "wt"), both, P("seq", "wt"), both, both, P("seq", None, "wt"), P("wt", "seq")),
        check_vma=False)
```

```python
import functools, math
import jax, jax.numpy as jnp
from jax import lax
from jax.experimental import pallas as pl
from jax.experimental.pallas import tpu as pltpu
from jax.sharding import PartitionSpec as P

MESH = pl.DeviceIdType.MESH

def coords():
    s = lax.axis_index("seq")
    w = lax.axis_index("wt")
    return s // 8, lax.rem(s // 2, 4), lax.rem(s, 2), w // 2, lax.rem(w, 2)

def at(yh, z, c, x, yl):
    return {"seq": yh * 8 + z * 2 + c, "wt": x * 2 + yl}

class Plane:
    def __init__(self, axis):
        self.axis = axis
        yh, z, c, x, yl = coords()
        self.c = c
        if axis == "wt":
            self.a, self.b = x, yl
            move = lambda da, db: at(yh, z, c, lax.rem(x + da + 4, 4), lax.rem(yl + db, 2))
        else:
            self.a, self.b = z, yh
            move = lambda da, db: at(lax.rem(yh + db, 2), lax.rem(z + da + 4, 4), c, x, yl)
        self.left, self.right, self.pair = move(-1, 0), move(1, 0), move(0, 1)
        self.twin = at(yh, z, 1 - c, x, yl)

    def block(self, da, db):
        a, b = lax.rem(self.a + da + 4, 4), lax.rem(self.b + db, 2)
        return a * 2 + b if self.axis == "wt" else b * 4 + a

def remote(src, dst, ssem, rsem, k, target):
    return pltpu.make_async_remote_copy(src_ref=src, dst_ref=dst, send_sem=ssem.at[k], recv_sem=rsem.at[k], device_id=target, device_id_type=MESH)

def greet(targets):
    bar = pltpu.get_barrier_semaphore()
    for t in targets:
        pl.semaphore_signal(bar, inc=1, device_id=t, device_id_type=MESH)
    pl.semaphore_wait(bar, len(targets))

GATHER_MSGS = 18
def gather_steps(pn, own, buf, rows, ssem, rsem, index=lambda j: j):
    h, q = rows // 2, rows // 4
    P_, Q_ = (0, h), (h, h)
    P0, P1, Q0, Q1 = (0, q), (q, q), (h, q), (h + q, q)
    L, Rt, Y = pn.left, pn.right, pn.pair
    table = {
        0: (Y, (0, 0), P_, (0, 1)),
        1: (Rt, (0, 0), Q_, (-1, 0)),
        2: (L, (0, 0), Q_, (1, 0)),
        3: (Rt, (0, 0), P_, (-1, 0)),
        4: (L, (0, 0), P_, (1, 0)),
        5: (Y, (0, 0), Q_, (0, 1)),
        6: (Rt, (-1, 0), Q0, (2, 0)),
        7: (Y, (-1, 0), Q_, (-1, 1)),
        8: (L, (1, 0), Q1, (2, 0)),
        9: (Y, (1, 0), Q_, (1, 1)),
        10: (Rt, (0, 1), P_, (-1, 1)),
        11: (L, (0, 1), P_, (1, 1)),
        12: (Rt, (-1, 0), P0, (2, 0)),
        13: (L, (1, 0), P1, (2, 0)),
        14: (Y, (2, 0), Q0, (2, 1)),
        15: (Y, (2, 0), Q1, (2, 1)),
        16: (Rt, (-1, 1), P0, (2, 1)),
        17: (L, (1, 1), P1, (2, 1)),
    }
    def part(d, r):
        return buf.at[index(pn.block(*d)), pl.ds(*r)]
    def send(k):
        t, d, r, _ = table[k]
        src = own.at[pl.ds(*r)] if d == (0, 0) else part(d, r)
        remote(src, part(d, r), ssem, rsem, k, t).start()
    def got(k):
        t, _, r, d = table[k]
        remote(part(d, r), part(d, r), ssem, rsem, k, t).wait_recv()
    def sent(k):
        t, d, r, _ = table[k]
        remote(part(d, r), part(d, r), ssem, rsem, k, t).wait_send()
    def first():
        for k in (0, 1, 2, 3, 4, 5): send(k)
    def after(k, *next_):
        def f():
            got(k)
            for n in next_: send(n)
        return f
    steps = [first, after(1, 6, 7), after(2, 8, 9), after(0, 10, 11), after(3, 12), after(4, 13),
             after(6, 14), after(8, 15), after(10, 16), after(11, 17)]
    tail = [after(5), after(7), after(9), after(12), after(13), after(14), after(15), after(16), after(17)]
    def done():
        for k in range(18): sent(k)
    return steps, tail, done

SUM_MSGS = 17
def sum_steps(pn, buf, land, rows, ssem, rsem, out, index=lambda j: j, add=None):
    h, q = rows // 2, rows // 4
    P_, Q_ = (0, h), (h, h)
    P0, P1, Q0, Q1 = (0, q), (q, q), (h, q), (h + q, q)
    L, Rt, Y = pn.left, pn.right, pn.pair
    table = {}
    off = 0
    def msg(k, t, d, r, r_to):
        nonlocal off
        table[k] = (t, d, r, off, r_to)
        off += r[1]
    msg(0, L, (-2, 0), P0, (-1, 0)); msg(1, Rt, (2, 0), P1, (1, 0))
    msg(2, L, (-2, 1), P0, (-1, 1)); msg(3, Rt, (2, 1), P1, (1, 1))
    msg(4, Y, (2, 1), Q_, (2, 0)); msg(5, Y, (-1, 1), Q_, (-1, 0)); msg(6, Y, (1, 1), Q_, (1, 0)); msg(7, Y, (0, 1), Q_, (0, 0))
    msg(8, L, (-1, 1), P_, (0, 1)); msg(9, Rt, (1, 1), P_, (0, 1))
    msg(10, L, (-1, 0), P_, (0, 0)); msg(11, Rt, (1, 0), P_, (0, 0))
    msg(12, L, (-2, 0), Q0, (-1, 0)); msg(13, Rt, (2, 0), Q1, (1, 0))
    msg(14, L, (-1, 0), Q_, (0, 0)); msg(15, Rt, (1, 0), Q_, (0, 0))
    msg(16, Y, (0, 1), P_, (0, 0))
    assert off <= 7 * rows, off
    def part(d, r):
        return buf.at[index(pn.block(*d)), pl.ds(*r)]
    def landing(k):
        _, _, r, o, _ = table[k]
        return land.at[pl.ds(o, r[1])]
    def send(k):
        t, d, r, _, _ = table[k]
        remote(part(d, r), landing(k), ssem, rsem, k, t).start()
    def got(k):
        remote(landing(k), landing(k), ssem, rsem, k, table[k][0]).wait_recv()
    def sent(k):
        remote(landing(k), landing(k), ssem, rsem, k, table[k][0]).wait_send()
    def accumulate(d, r, ks, to=None):
        j = index(pn.block(*d))
        step = 16
        def body(i, _):
            at_ = pl.multiple_of(r[0] + i * step, step)
            v = buf[j, pl.ds(at_, step)].astype(jnp.float32)
            for k in ks:
                v = v + land[pl.ds(pl.multiple_of(table[k][3] + i * step, step), step)].astype(jnp.float32)
            if to is None:
                buf[j, pl.ds(at_, step)] = v.astype(buf.dtype)
            else:
                to[pl.ds(at_, step)] = v.astype(to.dtype)
            return 0
        lax.fori_loop(0, r[1] // step, body, 0)
    def s0():
        for k in range(8): send(k)
    def s1():
        got(2); accumulate((-1, 1), P0, [2]); send(8)
        got(3); accumulate((1, 1), P1, [3]); send(9)
    def s2():
        got(0); accumulate((-1, 0), P0, [0]); send(10)
        got(1); accumulate((1, 0), P1, [1]); send(11)
    def s3():
        got(4); accumulate((2, 0), Q_, [4]); send(12); send(13)
    def s4():
        got(5); accumulate((-1, 0), Q_, [5]); got(12); accumulate((-1, 0), Q0, [12]); send(14)
        got(6); accumulate((1, 0), Q_, [6]); got(13); accumulate((1, 0), Q1, [13]); send(15)
    def s5():
        got(8); got(9); accumulate((0, 1), P_, [8, 9]); send(16)
    def s6():
        got(7); got(14); got(15); accumulate((0, 0), Q_, [7, 14, 15], out)
        got(10); got(11); got(16); accumulate((0, 0), P_, [10, 11, 16], out)
    def done():
        for k in range(17): sent(k)
    return [s0, s1, s2, s3, s4, s5, s6], done
ANY = pl.BlockSpec(memory_space=pl.ANY)
QB, KB = 512, 256
MASKED = -1e30
NT = (((1,), (1,)), ((), ()))

def halves(ref, kept):
    lane = lax.broadcasted_iota(jnp.int32, (1, 128), 1)
    low = (lane < 64).astype(jnp.float32)
    v = ref[...].astype(jnp.float32)
    kept[0] = (v * low).astype(jnp.bfloat16)
    kept[1] = (v * (1.0 - low)).astype(jnp.bfloat16)

def allowed(i, j, start):
    key = j * KB + lax.broadcasted_iota(jnp.int32, (KB, QB), 0)
    query = i * QB + lax.broadcasted_iota(jnp.int32, (KB, QB), 1)
    return (key <= query) & (key >= start)

def attn_fwd(q_ref, k_ref, v_ref, start_ref, o_ref, ot_ref, lse_ref, kept, vt):
    halves(k_ref, kept)
    vt[...] = v_ref[...].astype(jnp.float32).T.astype(jnp.bfloat16)
    n = q_ref.shape[0] // QB
    for i in range(n):
        q = q_ref[QB * i:QB * (i + 1)]
        start = start_ref[:, QB * i:QB * (i + 1)]
        def step(masked, j, carry):
            r = pl.ds(pl.multiple_of(j * KB, KB), KB)
            out = []
            for h in range(2):
                m, l, acc = carry[h]
                s = lax.dot_general(kept[h, r], q, NT, preferred_element_type=jnp.float32)
                if masked:
                    s = jnp.where(allowed(i, j, start), s, MASKED)
                top = jnp.maximum(m, jnp.max(s, axis=0, keepdims=True))
                p = jnp.exp(s - top)
                fade = jnp.exp(m - top)
                l = l * fade + jnp.sum(p, axis=0, keepdims=True)
                acc = acc * fade + jnp.dot(vt[64 * h:64 * h + 64, r], p.astype(jnp.bfloat16), preferred_element_type=jnp.float32)
                out.append((top, l, acc))
            return tuple(out)
        one = (jnp.full((1, QB), MASKED, jnp.float32), jnp.zeros((1, QB), jnp.float32), jnp.zeros((64, QB), jnp.float32))
        carry = (one, one)
        if i == n - 1:
            carry = lax.fori_loop(0, 2 * i + 2, functools.partial(step, True), carry)
        else:
            if i:
                carry = step(True, 0, carry)
                carry = lax.fori_loop(1, 2 * i, functools.partial(step, False), carry)
            carry = lax.fori_loop(2 * i, 2 * i + 2, functools.partial(step, True), carry)
        cols = pl.ds(QB * i, QB)
        for h in range(2):
            m, l, acc = carry[h]
            ot_ref[64 * h:64 * h + 64, cols] = acc / l
            lse_ref[h:h + 1, cols] = m + jnp.log(l)
        o_ref[QB * i:QB * (i + 1)] = ot_ref[:, cols].T.astype(jnp.bfloat16)

def attn_bwd(q_ref, k_ref, v_ref, start_ref, ot_ref, lse_ref, do_ref, dq_ref, dk_ref, dv_ref, keptk, keptv, keptq, keptd, kt, dot_):
    halves(k_ref, keptk)
    halves(v_ref, keptv)
    halves(q_ref, keptq)
    halves(do_ref, keptd)
    kt[...] = k_ref[...].astype(jnp.float32).T.astype(jnp.bfloat16)
    dot_[...] = do_ref[...].astype(jnp.float32).T
    dk_ref[...] = jnp.zeros_like(dk_ref)
    dv_ref[...] = jnp.zeros_like(dv_ref)
    n = q_ref.shape[0] // QB
    for i in range(n):
        rows = pl.ds(QB * i, QB)
        q = q_ref[rows]
        do = do_ref[rows]
        start = start_ref[:, rows]
        both = ot_ref[:, rows] * dot_[:, rows]
        inner = [jnp.sum(both[64 * h:64 * h + 64], axis=0, keepdims=True) for h in range(2)]
        lse = [lse_ref[h:h + 1, rows] for h in range(2)]
        def step(masked, j, carry):
            r = pl.ds(pl.multiple_of(j * KB, KB), KB)
            out, ps, ds = [], [], []
            for h in range(2):
                s = lax.dot_general(keptk[h, r], q, NT, preferred_element_type=jnp.float32)
                if masked:
                    s = jnp.where(allowed(i, j, start), s, MASKED)
                p = jnp.exp(s - lse[h])
                dp = lax.dot_general(keptv[h, r], do, NT, preferred_element_type=jnp.float32)
                g = (p * (dp - inner[h])).astype(jnp.bfloat16)
                out.append(carry[h] + jnp.dot(kt[64 * h:64 * h + 64, r], g, preferred_element_type=jnp.float32))
                ps.append(p.astype(jnp.bfloat16))
                ds.append(g)
            dv_ref[r] += sum(jnp.dot(ps[h], keptd[h, rows], preferred_element_type=jnp.float32) for h in range(2))
            dk_ref[r] += sum(jnp.dot(ds[h], keptq[h, rows], preferred_element_type=jnp.float32) for h in range(2))
            return tuple(out)
        carry = (jnp.zeros((64, QB), jnp.float32),) * 2
        if i == n - 1:
            carry = lax.fori_loop(0, 2 * i + 2, functools.partial(step, True), carry)
        else:
            if i:
                carry = step(True, 0, carry)
                carry = lax.fori_loop(1, 2 * i, functools.partial(step, False), carry)
            carry = lax.fori_loop(2 * i, 2 * i + 2, functools.partial(step, True), carry)
        dq_ref[rows] = jnp.concatenate(carry, axis=0).T

VM = pl.BlockSpec(memory_space=pltpu.VMEM)

def attention_forward(q, k, v, start):
    rows = q.shape[0]
    f = jax.ShapeDtypeStruct
    return pl.pallas_call(
        attn_fwd, out_shape=(f((rows, 128), jnp.bfloat16), f((128, rows), jnp.float32), f((8, rows), jnp.float32)),
        in_specs=[VM] * 4, out_specs=(VM,) * 3,
        scratch_shapes=[pltpu.VMEM((2, rows, 128), jnp.bfloat16), pltpu.VMEM((128, rows), jnp.bfloat16)],
        compiler_params=pltpu.CompilerParams(vmem_limit_bytes=56 * 2**20), name="attend",
    )(q, k, v, start)

def attention_backward(q, k, v, start, ot, lse, do):
    rows = q.shape[0]
    f = jax.ShapeDtypeStruct
    return pl.pallas_call(
        attn_bwd, out_shape=(f((rows, 128), jnp.float32),) * 3,
        in_specs=[VM] * 7, out_specs=(VM,) * 3,
        scratch_shapes=[pltpu.VMEM((2, rows, 128), jnp.bfloat16)] * 4 + [pltpu.VMEM((128, rows), jnp.bfloat16), pltpu.VMEM((128, rows), jnp.float32)],
        compiler_params=pltpu.CompilerParams(vmem_limit_bytes=56 * 2**20), name="attend_back",
    )(q, k, v, start, ot, lse, do)
ORDER = [(0, 0), (0, 1), (-1, 1), (1, 1), (-1, 0), (1, 0), (2, 0), (2, 1)]

class Gather:
    def __init__(self, pn, own, buf, rows, ss, rs, twin=None):
        self.pn, self.buf, self.twin = pn, buf, twin
        self.index = (lambda j: 2 * j + pn.c) if twin else (lambda j: j)
        steps, tail, done = gather_steps(pn, own, buf, rows, ss, rs, self.index)
        self.done = done
        ready = {0: [1], 1: [2], 2: [3], 3: [4], 4: [5], 6: [6], 8: [7]}
        def follow(i, f):
            def g():
                f()
                for k in ready.get(i, []):
                    self.hand(k)
            return g
        def first():
            steps[0]()
            self.hand(0)
        self.steps = [first] + steps[1:] + [follow(i, f) for i, f in enumerate(tail)]

    def handed(self, k, mine):
        c = self.pn.c if mine else 1 - self.pn.c
        j = self.buf.at[2 * self.pn.block(*ORDER[k]) + c]
        return remote(j, j, self.twin[0], self.twin[1], k, self.pn.twin)

    def hand(self, k):
        if self.twin:
            self.handed(k, True).start()

    def wait_twin(self, k):
        self.handed(k, False).wait_recv()

    def finish(self, waited=()):
        self.done()
        if self.twin:
            for k in range(8):
                self.handed(k, True).wait_send()
                if k not in waited:
                    self.wait_twin(k)

def fetch_steps(pn, weight, hw, ss, rs, ls):
    s = lax.axis_index("seq")
    rows = hw.shape[0]
    h, q = rows // 2, rows // 4
    W = {"P": (0, h), "Q": (h, h), "P0": (0, q), "P1": (q, q), "Q0": (h, q), "Q1": (h + q, q)}
    kinds = ["P", "P0", "P1", "Q", "Q0", "Q1"]
    both = []
    for p in range(3):
        g = 16 * p + s
        src = g // 6
        da = lax.rem(pn.a - src // 2 + 4, 4)
        b0 = pn.b == lax.rem(src, 2)
        both.append((p, lax.rem(g, 6), da, b0))
    def part(p, kind):
        return hw.at[pl.ds(*W[kind]), pl.ds(128 * p, 128)]
    def send(p, kind, slot, target):
        pltpu.make_async_remote_copy(src_ref=part(p, kind), dst_ref=part(p, kind), send_sem=ss.at[6 * p + slot],
                                     recv_sem=rs.at[6 * p + kinds.index(kind)], device_id=target, device_id_type=MESH).start()
    def wait(p, kind, slot=None):
        cp = pltpu.make_async_remote_copy(src_ref=part(p, kind), dst_ref=part(p, kind), send_sem=ss.at[6 * p + (slot or 0)],
                                          recv_sem=rs.at[6 * p + kinds.index(kind)], device_id=pn.right, device_id_type=MESH)
        cp.wait_recv() if slot is None else cp.wait_send()
    no = jnp.logical_not
    def local(p, b):
        return pltpu.make_async_copy(weight.at[:, pl.ds(pl.multiple_of(128 * b, 128), 128)], hw.at[:, pl.ds(128 * p, 128)], ls.at[p])
    def begin():
        for p, b, da, b0 in both:
            @pl.when(b0 & (da == 0))
            def _():
                local(p, b).start()
    def st0():
        for p, b, da, b0 in both:
            @pl.when(b0 & (da == 0))
            def _():
                local(p, b).wait()
                send(p, "Q", 0, pn.right); send(p, "Q", 1, pn.left); send(p, "P", 5, pn.pair)
                send(p, "P", 3, pn.right); send(p, "P", 4, pn.left); send(p, "Q", 2, pn.pair)
    def st1():
        for p, b, da, b0 in both:
            @pl.when(b0 & (da == 1))
            def _():
                wait(p, "Q"); send(p, "Q0", 0, pn.right); send(p, "Q", 2, pn.pair)
            @pl.when(b0 & (da == 3))
            def _():
                wait(p, "Q"); send(p, "Q1", 1, pn.left); send(p, "Q", 2, pn.pair)
            @pl.when(no(b0) & (da == 0))
            def _():
                wait(p, "P"); send(p, "P", 3, pn.right); send(p, "P", 4, pn.left)
    def st2():
        for p, b, da, b0 in both:
            @pl.when(da == 1)
            def _():
                wait(p, "P"); send(p, "P0", 3, pn.right)
            @pl.when(da == 3)
            def _():
                wait(p, "P"); send(p, "P1", 4, pn.left)
    def st3():
        for p, b, da, b0 in both:
            @pl.when(b0 & (da == 2))
            def _():
                wait(p, "Q0"); wait(p, "Q1"); send(p, "Q", 2, pn.pair)
    def st4():
        for p, b, da, b0 in both:
            @pl.when(da == 2)
            def _():
                wait(p, "P0"); wait(p, "P1")
            @pl.when(no(b0))
            def _():
                wait(p, "Q")
    def done():
        for p, b, da, b0 in both:
            @pl.when(b0)
            def _():
                wait(p, "Q", 2)
            @pl.when(b0 & (da == 0))
            def _():
                wait(p, "Q", 0); wait(p, "Q", 1); wait(p, "P", 5)
            @pl.when(da == 0)
            def _():
                wait(p, "P", 3); wait(p, "P", 4)
            @pl.when(b0 & (da == 1))
            def _():
                wait(p, "Q0", 0)
            @pl.when(b0 & (da == 3))
            def _():
                wait(p, "Q1", 1)
            @pl.when(da == 1)
            def _():
                wait(p, "P0", 3)
            @pl.when(da == 3)
            def _():
                wait(p, "P1", 4)
    return begin, [st0, st1, st2, st3, st4], done

def turn(v, keep, ahead, behind):
    return v * keep + pltpu.roll(v, 120, 1) * ahead + pltpu.roll(v, 8, 1) * behind

def norm_rows(x, gain, shift):
    average = jnp.mean(x, axis=-1, keepdims=True)
    centred = x - average
    inverse = lax.rsqrt(jnp.mean(centred * centred, axis=-1, keepdims=True) + norm_eps)
    return centred * inverse * gain + shift

def rotary_tables_to(cs, tables):
    rows = cs.shape[1]
    c, s = cs[0:8, :], cs[8:16, :]
    one, nil, z8 = jnp.ones((48, rows), jnp.float32), jnp.zeros((48, rows), jnp.float32), jnp.zeros((8, rows), jnp.float32)
    tables[0][...] = jnp.concatenate([c, c, one] * 2, axis=0).T
    tables[1][...] = jnp.concatenate([-s, z8, nil] * 2, axis=0).T
    tables[2][...] = jnp.concatenate([z8, s, nil] * 2, axis=0).T

def front_kernel(x, gain, shift, weight, bias, cs, start_ref, dy, ow,
                 rn, hw, q_ref, k_ref, v_ref, ot_ref, lse_ref, att, out_all, dy_all,
                 own, kept, vt, t0, t1, t2, ob, ox,
                 ssA, rsA, tsA, trA, ssB, rsB, lsB, ssC, rsC, ssD, rsD, tsD, trD, ssO, rsO, ssT, rsT, lsO, ls):
    sp, wp = Plane("seq"), Plane("wt")
    tok = x.shape[0]
    c, m = sp.c, sp.block(0, 0)
    A = Gather(sp, own, rn, tok, ssA, rsA, (tsA, trA))
    begin, fetch, fetch_done = fetch_steps(wp, weight, hw, ssB, rsB, lsB)
    C = Gather(wp, dy, dy_all, tok, ssC, rsC)
    D = Gather(wp, ow, out_all, ow.shape[0], ssD, rsD, (tsD, trD))
    begin()
    chips = [at(j // 4, j % 4, c, wp.a, wp.b) for j in range(8)]
    bar = pltpu.get_barrier_semaphore()
    for j in range(8):
        @pl.when(m != j)
        def _():
            pl.semaphore_signal(bar, inc=1, device_id=chips[j], device_id_type=MESH)
    for t in (sp.twin, wp.left, wp.right, wp.pair):
        pl.semaphore_signal(bar, inc=1, device_id=t, device_id_type=MESH)
    def ln(i, _):
        r = pl.ds(pl.multiple_of(i * 16, 16), 16)
        own[r] = norm_rows(x[r].astype(jnp.float32), gain[...], shift[...]).astype(jnp.bfloat16)
        return 0
    lax.fori_loop(0, tok // 16, ln, 0)
    copies = [pltpu.make_async_copy(own, rn.at[2 * m + c], ls.at[0]),
              pltpu.make_async_copy(dy, dy_all.at[wp.block(0, 0)], ls.at[1]),
              pltpu.make_async_copy(ow, out_all.at[2 * wp.block(0, 0) + c], ls.at[2])]
    for cp in copies:
        cp.start()
    copies[0].wait()
    pl.semaphore_wait(bar, 11)
    A.steps[0]()
    fetch[0]()
    rotary_tables_to(cs, (t0, t1, t2))
    copies[1].wait()
    copies[2].wait()
    a, b, cc, d = iter(A.steps[1:]), iter(fetch[1:]), iter(C.steps), iter(D.steps)
    def pump(*its):
        for it in its:
            f = next(it, None)
            if f is not None:
                f()
    pump(a, a, b, a, a, a, b, a, a, b, b, a, a, cc)
    def project(k):
        A.wait_twin(k)
        j = sp.block(*ORDER[k])
        rows = pl.ds(pl.multiple_of(j * 256, 256), 256)
        h = rn[pl.ds(2 * j, 2)].reshape(256, rn.shape[2])
        y = jnp.dot(h, hw[...], preferred_element_type=jnp.float32) + bias[...]
        tabs = (t0[rows], t1[rows], t2[rows])
        q_ref[rows] = (turn(y[:, :128], *tabs) * 0.125).astype(jnp.bfloat16)
        k_ref[rows] = turn(y[:, 128:256], *tabs).astype(jnp.bfloat16)
        v_ref[rows] = y[:, 256:].astype(jnp.bfloat16)
    project(0); pump(a); project(1); pump(a); pump(cc); project(2); pump(a); project(3)
    pump(a); project(4); pump(a, cc); project(5); pump(a, a); pump(cc); project(6); pump(a, a); project(7)
    halves(k_ref, kept)
    pump(cc, cc)
    vt[...] = v_ref[...].astype(jnp.float32).T.astype(jnp.bfloat16)
    def to_twin(j):
        return pltpu.make_async_remote_copy(src_ref=ox.at[j], dst_ref=ob.at[j, :, pl.ds(pl.multiple_of(128 * c, 128), 128)],
                                            send_sem=ssT.at[j], recv_sem=rsT.at[j], device_id=sp.twin, device_id_type=MESH)
    def from_twin(j):
        there = ob.at[j, :, pl.ds(pl.multiple_of(128 * (1 - c), 128), 128)]
        return pltpu.make_async_remote_copy(src_ref=there, dst_ref=there, send_sem=ssT.at[j], recv_sem=rsT.at[j], device_id=sp.twin, device_id_type=MESH)
    def cols(j):
        return att.at[:, pl.ds(pl.multiple_of(256 * j, 256), 256)]
    def to_chip(j):
        return pltpu.make_async_remote_copy(src_ref=ob.at[j], dst_ref=cols(m), send_sem=ssO.at[j], recv_sem=rsO.at[m], device_id=chips[j], device_id_type=MESH)
    def ship(i):
        for j in (2 * i, 2 * i + 1):
            from_twin(j).wait_recv()
            @pl.when(m == j)
            def _():
                pltpu.make_async_copy(ob.at[j], cols(j), lsO).start()
            @pl.when(m != j)
            def _():
                to_chip(j).start()
    n = q_ref.shape[0] // QB
    for i in range(n):
        q = q_ref[QB * i:QB * (i + 1)]
        start = start_ref[:, QB * i:QB * (i + 1)]
        step = functools.partial(attend_step, kept, vt, q, start, i)
        one = (jnp.full((1, QB), MASKED, jnp.float32), jnp.zeros((1, QB), jnp.float32), jnp.zeros((64, QB), jnp.float32))
        carry = (one, one)
        if i == n - 1:
            for j in range(0, 2 * i + 2, 2):
                carry = lax.fori_loop(j, j + 2, functools.partial(step, True), carry)
                pump(cc, d)
        else:
            if i:
                carry = step(True, 0, carry)
                carry = lax.fori_loop(1, 2 * i, functools.partial(step, False), carry)
                pump(cc, d) if i == 1 else pump(cc, cc, d)
            carry = lax.fori_loop(2 * i, 2 * i + 2, functools.partial(step, True), carry)
            pump(cc, cc)
        where = pl.ds(QB * i, QB)
        for h in range(2):
            top, l, acc = carry[h]
            ot_ref[64 * h:64 * h + 64, where] = acc / l
            lse_ref[h:h + 1, where] = top + jnp.log(l)
        if i:
            ship(i - 1)
        o = ot_ref[:, where].T.astype(jnp.bfloat16)
        for j in (0, 1):
            mine = pl.ds(pl.multiple_of(128 * c, 128), 128)
            first, second = o[256 * j:256 * j + 128], o[256 * j + 128:256 * j + 256]
            @pl.when(c == 0)
            def _():
                ob[2 * i + j, :, 0:128] = first
                ox[2 * i + j] = second
            @pl.when(c == 1)
            def _():
                ob[2 * i + j, :, 128:256] = second
                ox[2 * i + j] = first
            to_twin(2 * i + j).start()
    ship(n - 1)
    for f in cc:
        f()
    for f in d:
        f()
    for j in range(8):
        to_twin(j).wait_send()
        @pl.when(m == j)
        def _():
            pltpu.make_async_copy(ob.at[j], cols(j), lsO).wait()
        @pl.when(m != j)
        def _():
            to_chip(j).wait_send()
            pltpu.make_async_remote_copy(src_ref=cols(j), dst_ref=cols(j), send_sem=ssO.at[j], recv_sem=rsO.at[j], device_id=chips[j], device_id_type=MESH).wait_recv()
    A.finish(range(8))
    fetch_done()
    C.finish()
    D.finish()

def attend_step(kept, vt, q, start, i, masked, j, carry):
    r = pl.ds(pl.multiple_of(j * KB, KB), KB)
    out = []
    for h in range(2):
        m, l, acc = carry[h]
        s = lax.dot_general(kept[h, r], q, NT, preferred_element_type=jnp.float32)
        if masked:
            s = jnp.where(allowed(i, j, start), s, MASKED)
        top = jnp.maximum(m, jnp.max(s, axis=0, keepdims=True))
        p = jnp.exp(s - top)
        fade = jnp.exp(m - top)
        l = l * fade + jnp.sum(p, axis=0, keepdims=True)
        acc = acc * fade + jnp.dot(vt[64 * h:64 * h + 64, r], p.astype(jnp.bfloat16), preferred_element_type=jnp.float32)
        out.append((top, l, acc))
    return tuple(out)

def front(cid, x, gain, shift, weight, bias, cs, start, dy, ow):
    tok, width = x.shape
    rows = start.shape[1]
    f, b16, f32 = jax.ShapeDtypeStruct, jnp.bfloat16, jnp.float32
    vm = pltpu.VMEM
    return pl.pallas_call(
        front_kernel,
        out_shape=(f((16, tok, width), b16), f((width, 384), b16), f((rows, 128), b16), f((rows, 128), b16), f((rows, 128), b16),
                   f((128, rows), f32), f((8, rows), f32), f((tok, width), b16), f((16,) + ow.shape, b16), f((8, tok, width), b16)),
        in_specs=[VM, VM, VM, ANY, VM, VM, VM, VM, VM], out_specs=(VM,) * 10,
        scratch_shapes=[vm((tok, width), b16), vm((2, rows, 128), b16), vm((128, rows), b16)] + [vm((rows, 128), f32)] * 3
        + [vm((8, 128, 256), b16), vm((8, 128, 128), b16)]
        + [dma(n) for n in (18, 18, 8, 8, 18, 18, 3, 18, 18, 18, 18, 8, 8, 8, 8, 8, 8)] + [pltpu.SemaphoreType.DMA, dma(3)],
        compiler_params=params(cid), name="front",
    )(x, gain, shift, weight, bias, cs, start, dy, ow)
def params(cid):
    return pltpu.CompilerParams(collective_id=cid, has_side_effects=True, vmem_limit_bytes=56 * 2**20)

def dma(n):
    return pltpu.SemaphoreType.DMA((n,))

def gather_kernel(axis, x, o, ss, rs, ls):
    pn = Plane(axis)
    greet([pn.left, pn.right, pn.pair])
    cp = pltpu.make_async_copy(x, o.at[pn.block(0, 0)], ls)
    cp.start()
    steps, tail, done = gather_steps(pn, x, o, x.shape[0], ss, rs)
    for f in steps + tail:
        f()
    done()
    cp.wait()

def gather(axis, cid, x):
    return pl.pallas_call(
        functools.partial(gather_kernel, axis), out_shape=jax.ShapeDtypeStruct((8,) + x.shape, x.dtype),
        in_specs=[VM], out_specs=VM, scratch_shapes=[dma(18), dma(18), pltpu.SemaphoreType.DMA],
        compiler_params=params(cid), name="gather_" + axis)(x)

def gather_both_kernel(axis, x, o, ss, rs, ls, ts, tr):
    pn = Plane(axis)
    greet([pn.left, pn.right, pn.pair, pn.twin])
    index = lambda j: 2 * j + pn.c
    mine = index(pn.block(0, 0))
    cp = pltpu.make_async_copy(x, o.at[mine], ls)
    cp.start()
    cp.wait()
    steps, tail, done = gather_steps(pn, x, o, x.shape[0], ss, rs, index)
    order = [(0, 0), (0, 1), (-1, 1), (1, 1), (-1, 0), (1, 0), (2, 0), (2, 1)]
    def hand(k):
        j = index(pn.block(*order[k]))
        remote(o.at[j], o.at[j], ts, tr, k, pn.twin).start()
    steps[0]()
    hand(0)
    for f in steps[1:]:
        f()
    ready = {0: [1], 1: [2], 2: [3], 3: [4], 4: [5], 6: [6], 8: [7]}
    for i, f in enumerate(tail):
        f()
        for k in ready.get(i, []):
            hand(k)
    done()
    for k in range(8):
        j = 2 * pn.block(*order[k]) + 1 - pn.c
        remote(o.at[j], o.at[j], ts, tr, k, pn.twin).wait()

def gather_both(axis, cid, x):
    return pl.pallas_call(
        functools.partial(gather_both_kernel, axis), out_shape=jax.ShapeDtypeStruct((16,) + x.shape, x.dtype),
        in_specs=[VM], out_specs=VM, scratch_shapes=[dma(18), dma(18), pltpu.SemaphoreType.DMA, dma(8), dma(8)],
        compiler_params=params(cid), name="gather_both_" + axis)(x)

def scatter_kernel(axis, x, o, buf, land, ss, rs, ls):
    pn = Plane(axis)
    cp = pltpu.make_async_copy(x, buf, ls)
    cp.start()
    greet([pn.left, pn.right, pn.pair])
    cp.wait()
    steps, done = sum_steps(pn, buf, land, x.shape[1], ss, rs, o)
    for f in steps:
        f()
    done()

def scatter(axis, cid, x):
    _, rows, cols = x.shape
    return pl.pallas_call(
        functools.partial(scatter_kernel, axis), out_shape=jax.ShapeDtypeStruct((rows, cols), jnp.float32),
        in_specs=[ANY], out_specs=VM,
        scratch_shapes=[pltpu.VMEM(x.shape, x.dtype), pltpu.VMEM((7 * rows, cols), x.dtype), dma(17), dma(17), pltpu.SemaphoreType.DMA],
        compiler_params=params(cid), name="scatter_" + axis)(x)

def scatter_both_kernel(axis, x, o, buf, tland, land, ss, rs, ls, ts, tr):
    pn = Plane(axis)
    rows = x.shape[1]
    cp = pltpu.make_async_copy(x, buf, ls)
    cp.start()
    greet([pn.left, pn.right, pn.pair, pn.twin])
    cp.wait()
    order = [(2, 0), (2, 1), (-1, 1), (1, 1), (-1, 0), (1, 0), (0, 1), (0, 0)]
    for k in range(8):
        j = pn.block(*order[k])
        remote(buf.at[2 * j + 1 - pn.c], tland.at[k], ts, tr, k, pn.twin).start()
    for k in range(8):
        j = 2 * pn.block(*order[k]) + pn.c
        remote(tland.at[k], tland.at[k], ts, tr, k, pn.twin).wait_recv()
        def body(i, _):
            r = pl.ds(pl.multiple_of(i * 16, 16), 16)
            buf[j, r] = (buf[j, r].astype(jnp.float32) + tland[k, r].astype(jnp.float32)).astype(buf.dtype)
            return 0
        lax.fori_loop(0, rows // 16, body, 0)
    steps, done = sum_steps(pn, buf, land, rows, ss, rs, o, lambda j: 2 * j + pn.c)
    for f in steps:
        f()
    done()
    for k in range(8):
        remote(tland.at[k], tland.at[k], ts, tr, k, pn.twin).wait_send()

def scatter_both(axis, cid, x):
    _, rows, cols = x.shape
    return pl.pallas_call(
        functools.partial(scatter_both_kernel, axis), out_shape=jax.ShapeDtypeStruct((rows, cols), jnp.float32),
        in_specs=[ANY], out_specs=VM,
        scratch_shapes=[pltpu.VMEM(x.shape, x.dtype), pltpu.VMEM((8, rows, cols), x.dtype), pltpu.VMEM((7 * rows, cols), x.dtype),
                        dma(17), dma(17), pltpu.SemaphoreType.DMA, dma(8), dma(8)],
        compiler_params=params(cid), name="scatter_both_" + axis)(x)

def swap_kernel(axis, n, x, o, ss, rs, ls):
    me = lax.axis_index(axis)
    peers = [lax.rem(me + d, n) for d in range(1, n)]
    bar = pltpu.get_barrier_semaphore()
    for p in peers:
        pl.semaphore_signal(bar, inc=1, device_id={axis: p}, device_id_type=MESH)
    cp = pltpu.make_async_copy(x.at[me], o.at[me], ls)
    cp.start()
    pl.semaphore_wait(bar, n - 1)
    def copy(d):
        return remote(x.at[lax.rem(me + d, n)], o.at[me], ss, rs, d - 1, {axis: lax.rem(me + d, n)})
    for d in range(1, n):
        copy(d).start()
    for d in range(1, n):
        j = lax.rem(me - d + n, n)
        remote(x.at[j], o.at[j], ss, rs, d - 1, {axis: j}).wait()
    cp.wait()

def swap(axis, n, cid, x):
    return pl.pallas_call(
        functools.partial(swap_kernel, axis, n), out_shape=jax.ShapeDtypeStruct(x.shape, x.dtype),
        in_specs=[VM], out_specs=VM, scratch_shapes=[dma(n - 1), dma(n - 1), pltpu.SemaphoreType.DMA],
        compiler_params=params(cid), name="swap_" + axis)(x)

def fetch_kernel(x, o, ss, rs, ls):
    s, w = lax.axis_index("seq"), lax.axis_index("wt")
    bar = pltpu.get_barrier_semaphore()
    for d in range(1, 8):
        pl.semaphore_signal(bar, inc=1, device_id={"wt": lax.rem(w + d, 8)}, device_id_type=MESH)
    pl.semaphore_wait(bar, 7)
    for p in range(3):
        g = 16 * p + s
        @pl.when(w == g // 6)
        def _():
            src = x.at[lax.rem(g, 6)]
            cp = pltpu.make_async_copy(src, o.at[p], ls)
            cp.start()
            for d in range(1, 8):
                remote(src, o.at[p], ss.at[p], rs, p, {"wt": lax.rem(w + d, 8)}).start() if False else pltpu.make_async_remote_copy(src_ref=src, dst_ref=o.at[p], send_sem=ss.at[p, d - 1], recv_sem=rs.at[p], device_id={"wt": lax.rem(w + d, 8)}, device_id_type=MESH).start()
            cp.wait()
    for p in range(3):
        g = 16 * p + s
        @pl.when(w == g // 6)
        def _():
            for d in range(1, 8):
                pltpu.make_async_remote_copy(src_ref=o.at[p], dst_ref=o.at[p], send_sem=ss.at[p, d - 1], recv_sem=rs.at[p], device_id={"wt": lax.rem(w + d, 8)}, device_id_type=MESH).wait_send()
        @pl.when(w != g // 6)
        def _():
            pltpu.make_async_remote_copy(src_ref=o.at[p], dst_ref=o.at[p], send_sem=ss.at[p, 0], recv_sem=rs.at[p], device_id={"wt": lax.rem(w + 1, 8)}, device_id_type=MESH).wait_recv()

def fetch(cid, x):
    return pl.pallas_call(
        fetch_kernel, out_shape=jax.ShapeDtypeStruct((3,) + x.shape[1:], x.dtype),
        in_specs=[VM], out_specs=VM, scratch_shapes=[pltpu.SemaphoreType.DMA((3, 7)), dma(3), pltpu.SemaphoreType.DMA],
        compiler_params=params(cid), name="fetch_heads")(x)

def place_kernel(x, o, ss, rs, ls):
    s, w = lax.axis_index("seq"), lax.axis_index("wt")
    bar = pltpu.get_barrier_semaphore()
    def source(b):
        g = 6 * w + b
        return lax.rem(g, 16), s // 2
    def target(i, p):
        g = 16 * p + s
        return 2 * w + i, g // 6, lax.rem(g, 6)
    own = jnp.int32(0)
    for b in range(6):
        ts, tw = source(b)
        same = (ts == s) & (tw == w)
        own += same.astype(jnp.int32)
        @pl.when(jnp.logical_not(same))
        def _():
            pl.semaphore_signal(bar, inc=1, device_id={"seq": ts, "wt": tw}, device_id_type=MESH)
    pl.semaphore_wait(bar, 6 - own)
    def copy(i, p):
        ts, tw, slot = target(i, p)
        return pltpu.make_async_remote_copy(src_ref=x.at[i, p], dst_ref=o.at[slot], send_sem=ss.at[i, p], recv_sem=rs.at[slot], device_id={"seq": ts, "wt": tw}, device_id_type=MESH)
    def local(i, p):
        return pltpu.make_async_copy(x.at[i, p], o.at[target(i, p)[2]], ls.at[i, p])
    for i in range(2):
        for p in range(3):
            ts, tw, _ = target(i, p)
            same = (ts == s) & (tw == w)
            @pl.when(same)
            def _():
                local(i, p).start()
            @pl.when(jnp.logical_not(same))
            def _():
                copy(i, p).start()
    for i in range(2):
        for p in range(3):
            ts, tw, _ = target(i, p)
            same = (ts == s) & (tw == w)
            @pl.when(same)
            def _():
                local(i, p).wait()
            @pl.when(jnp.logical_not(same))
            def _():
                copy(i, p).wait_send()
    for b in range(6):
        ts, tw = source(b)
        @pl.when(jnp.logical_not((ts == s) & (tw == w)))
        def _():
            pltpu.make_async_remote_copy(src_ref=o.at[b], dst_ref=o.at[b], send_sem=ss.at[0, 0], recv_sem=rs.at[b], device_id={"seq": ts, "wt": tw}, device_id_type=MESH).wait_recv()

def place(cid, x):
    return pl.pallas_call(
        place_kernel, out_shape=jax.ShapeDtypeStruct((6, 128, 128), x.dtype),
        in_specs=[VM], out_specs=VM, scratch_shapes=[pltpu.SemaphoreType.DMA((2, 3)), dma(6), pltpu.SemaphoreType.DMA((2, 3))],
        compiler_params=params(cid), name="place_qkv")(x)

def small_kernel(x, o, land, mid, land2, ss, rs, ss2, rs2):
    s, w = lax.axis_index("seq"), lax.axis_index("wt")
    bar = pltpu.get_barrier_semaphore()
    for d in range(1, 8):
        pl.semaphore_signal(bar, inc=1, device_id={"wt": lax.rem(w + d, 8)}, device_id_type=MESH)
    for d in range(1, 16):
        pl.semaphore_signal(bar, inc=1, device_id={"seq": lax.rem(s + d, 16)}, device_id_type=MESH)
    pl.semaphore_wait(bar, 22)
    for d in range(1, 8):
        remote(x.at[lax.rem(w + d, 8)], land.at[d - 1], ss, rs, d - 1, {"wt": lax.rem(w + d, 8)}).start()
    for d in range(1, 8):
        remote(x.at[0], land.at[d - 1], ss, rs, d - 1, {"wt": lax.rem(w + d, 8)}).wait()
    mid[:, 0] = x[w] + jnp.sum(land[...], axis=0)
    for d in range(1, 16):
        remote(mid.at[lax.rem(s + d, 16)], land2.at[d - 1], ss2, rs2, d - 1, {"seq": lax.rem(s + d, 16)}).start()
    for d in range(1, 16):
        remote(mid.at[0], land2.at[d - 1], ss2, rs2, d - 1, {"seq": lax.rem(s + d, 16)}).wait()
    o[...] = mid[s] + jnp.sum(land2[...], axis=0)

def small_sum(cid, x):
    f = jnp.float32
    return pl.pallas_call(
        small_kernel, out_shape=jax.ShapeDtypeStruct((1, 128), f),
        in_specs=[VM], out_specs=VM,
        scratch_shapes=[pltpu.VMEM((7, 16, 128), f), pltpu.VMEM((16, 1, 128), f), pltpu.VMEM((15, 1, 128), f), dma(7), dma(7), dma(15), dma(15)],
        compiler_params=params(cid), name="small_sum")(x)


norm_eps = 1e-05
theta_base = 10000.0
ROT = 16
HEAD_DIM = 64


def layer_norm_parts(values, gain, shift):
    average = jnp.mean(values, axis=-1, keepdims=True)
    centred = values - average
    spread = jnp.mean(centred * centred, axis=-1, keepdims=True)
    inverse = lax.rsqrt(spread + norm_eps)
    scaled = centred * inverse
    return (scaled * gain + shift, scaled, inverse)


def layer_norm_back(upward, scaled, inverse, gain):
    weighted = upward * gain
    first_mean = jnp.mean(weighted, axis=-1, keepdims=True)
    second_mean = jnp.mean(weighted * scaled, axis=-1, keepdims=True)
    return inverse * (weighted - first_mean - scaled * second_mean)


def rotary_angles(segment_row):
    rows = segment_row.shape[0]
    ends = [jnp.sum((segment_row < i).astype(jnp.int32)) for i in (1, 2)]
    start = jnp.where(segment_row == 0, 0, jnp.where(segment_row == 1, ends[0], ends[1]))
    offsets = (jnp.arange(rows, dtype=jnp.int32) - start).astype(jnp.float32)
    inv_freq = jnp.exp(jnp.arange(ROT // 2, dtype=jnp.float32) * (-2.0 * math.log(theta_base) / ROT))
    angles = inv_freq[:, None] * offsets[None, :]
    return start.reshape(1, rows), jnp.concatenate([jnp.cos(angles), jnp.sin(angles)], axis=0)


def wide_tables(cs):
    c, s = cs[0:8], cs[8:16]
    one, nil, z8 = jnp.ones((48, c.shape[1]), jnp.float32), jnp.zeros((48, c.shape[1]), jnp.float32), jnp.zeros((8, c.shape[1]), jnp.float32)
    return [jnp.concatenate(p * 2, axis=0).T for p in ([c, c, one], [-s, z8, nil], [z8, s, nil])]


def rotate(v, keep, ahead, behind):
    return v * keep + jnp.roll(v, -8, axis=1) * ahead + jnp.roll(v, 8, axis=1) * behind


def contract_first(left, right):
    return lax.dot_general(left, right, (((0,), (0,)), ((), ())), preferred_element_type=jnp.float32)


def contract_last(left, right):
    return lax.dot_general(left, right, (((1,), (1,)), ((), ())), preferred_element_type=jnp.float32)


def per_device(layer_in, segment_ids, norm_one_gain, norm_one_shift, qkv_weight, qkv_bias, out_weight, norm_two_gain,
               norm_two_shift, gate_up_weight, down_weight, layer_grad):
    f32, bf16 = jnp.float32, jnp.bfloat16
    s, w = lax.axis_index("seq"), lax.axis_index("wt")
    tok, width = layer_in.shape[1:]
    rows = segment_ids.shape[1]
    hidden = down_weight.shape[0]
    scale = 1.0 / math.sqrt(HEAD_DIM)
    inputs = layer_in.reshape(tok, width).astype(f32)
    upstream = layer_grad.reshape(tok, width)
    start, cs = rotary_angles(segment_ids.reshape(rows))
    keep, ahead, behind = wide_tables(cs)
    _, scaled_one, inverse_one = layer_norm_parts(inputs, norm_one_gain, norm_one_shift)
    bias = lax.dynamic_index_in_dim(qkv_bias.reshape(3, 16, 128), s, 1, keepdims=False).reshape(1, 384)
    half = lax.dynamic_slice_in_dim(out_weight, (s % 2) * (width // 2), width // 2, 0)
    row_normed, head_weight, q, k, v, ot, lse, attended, out_all, all_up = front(
        0, layer_in.reshape(tok, width), norm_one_gain.reshape(1, width), norm_one_shift.reshape(1, width), qkv_weight, bias, cs, start, upstream, half)
    row_normed = row_normed.reshape(rows, width)
    out_all = out_all.reshape(8, 2, width // 2, 256)
    all_up = all_up.reshape(8 * tok, width)
    branch = jnp.einsum("tck,wckn->twn", attended.reshape(tok, 2, width // 2), out_all, preferred_element_type=f32).reshape(tok, width)
    middle = inputs + branch
    normed_two, scaled_two, inverse_two = layer_norm_parts(middle, norm_two_gain, norm_two_shift)
    all_two = gather("wt", 4, normed_two.astype(bf16)).reshape(8 * tok, width)
    weight_gu = gate_up_weight.reshape(width, 2 * hidden)
    gu = jnp.dot(all_two, weight_gu, preferred_element_type=f32)
    g, u = gu[:, :hidden], gu[:, hidden:]
    sigma = jax.nn.sigmoid(g)
    act = (g * sigma * u).astype(bf16)
    ffn_part = jnp.dot(act, down_weight, preferred_element_type=f32).astype(bf16)
    dact = contract_last(all_up, down_weight)
    dg = (dact * u * sigma * (1.0 + g * (1.0 - sigma))).astype(bf16)
    du = (dact * g * sigma).astype(bf16)
    dgu = jnp.concatenate([dg, du], axis=1)
    dh2_part = contract_last(dgu, weight_gu).astype(bf16)
    dh2 = scatter("wt", 6, dh2_part.reshape(8, tok, width))
    ffn_out = scatter("wt", 7, ffn_part.reshape(8, tok, width))
    layer_out = (middle + ffn_out).astype(bf16).reshape(1, tok, width)
    gain_two = jnp.sum(dh2 * scaled_two, axis=0)
    shift_two = jnp.sum(dh2, axis=0)
    middle_grad = upstream.astype(f32) + layer_norm_back(dh2, scaled_two, inverse_two, norm_two_gain)
    da = middle_grad.astype(bf16)
    dout = jnp.einsum("twn,wckn->tck", da.reshape(tok, 8, 256), out_all, preferred_element_type=f32).astype(bf16)
    do = swap("seq", 16, 8, dout.reshape(tok, 16, 128).transpose(1, 0, 2)).reshape(rows, 128)
    dq, dk, dv = attention_backward(q, k, v, start, ot, lse, do)
    low = lambda t: t.astype(bf16).astype(f32)
    dproj = jnp.concatenate([rotate(low(dq) * scale, keep, -ahead, -behind), rotate(low(dk), keep, -ahead, -behind), dv], axis=1).astype(bf16)
    dh1_part = contract_last(dproj, head_weight).astype(bf16)
    dh1 = scatter_both("seq", 9, dh1_part.reshape(16, tok, width))
    gain_one = jnp.sum(dh1 * scaled_one, axis=0)
    shift_one = jnp.sum(dh1, axis=0)
    dx = middle_grad + layer_norm_back(dh1, scaled_one, inverse_one, norm_one_gain)
    input_grad = dx.astype(bf16).reshape(1, tok, width)
    qkv_part = contract_first(row_normed, dproj).astype(bf16)
    qkv_rows = scatter("wt", 10, qkv_part.reshape(8, 256, 384)).astype(bf16)
    qkv_grad = place(11, qkv_rows.reshape(2, 128, 3, 128).transpose(0, 2, 1, 3))
    qkv_grad = qkv_grad.transpose(1, 0, 2).reshape(128, 768).astype(f32)
    all_att = gather("wt", 12, attended).reshape(8 * tok, width)
    da_cols = swap("wt", 8, 13, da.reshape(tok, 8, 256).transpose(1, 0, 2)).reshape(8 * tok, 256)
    out_part = contract_first(all_att, da_cols).astype(bf16)
    gate_part = contract_first(all_two, dgu).astype(bf16)
    down_part = contract_first(all_up, act).astype(bf16)
    joined = jnp.concatenate([gate_part, down_part, out_part], axis=1).reshape(16, 128, 3 * hidden + 256)
    joined = scatter_both("seq", 14, joined)
    gate_grad = joined[:, :2 * hidden].reshape(128, 2, hidden)
    down_grad = joined[:, 2 * hidden:3 * hidden].T
    out_grad = joined[:, 3 * hidden:]
    bias_grad = lax.dynamic_update_slice(jnp.zeros((3, 16, 128), f32), jnp.sum(dproj.astype(f32), axis=0).reshape(3, 1, 128), (0, s, 0))
    blocks = [t.reshape(16, 8, -1) for t in (gain_one, shift_one, bias_grad, gain_two, shift_two, jnp.zeros((16 * 8 * 16,), f32))]
    small = small_sum(15, jnp.concatenate(blocks, axis=2).transpose(1, 0, 2))[0]
    return (layer_out, input_grad, small[0:16], small[16:32], qkv_grad, small[32:80], out_grad, small[80:96], small[96:112], gate_grad, down_grad)


def solution(mesh):
    both = P(("seq", "wt"))
    return jax.shard_map(
        per_device, mesh=mesh,
        in_specs=(P("wt", "seq", None), P("wt", None), P(), P(), P(None, "wt"), P(), P(None, "wt"), P(), P(), P(None, None, "wt"), P("wt", None), P("wt", "seq", None)),
        out_specs=(P("wt", "seq", None), P("wt", "seq", None), both, both, P("seq", "wt"), both, P("seq", "wt"), both, both, P("seq", None, "wt"), P("wt", "seq")),
        check_vma=False)
```

```python
import functools, math
import jax, jax.numpy as jnp
from jax import lax
from jax.experimental import pallas as pl
from jax.experimental.pallas import tpu as pltpu
from jax.sharding import PartitionSpec as P

MESH = pl.DeviceIdType.MESH

def coords():
    s = lax.axis_index("seq")
    w = lax.axis_index("wt")
    return s // 8, lax.rem(s // 2, 4), lax.rem(s, 2), w // 2, lax.rem(w, 2)

def at(yh, z, c, x, yl):
    return {"seq": yh * 8 + z * 2 + c, "wt": x * 2 + yl}

class Plane:
    def __init__(self, axis):
        self.axis = axis
        yh, z, c, x, yl = coords()
        self.c = c
        if axis == "wt":
            self.a, self.b = x, yl
            move = lambda da, db: at(yh, z, c, lax.rem(x + da + 4, 4), lax.rem(yl + db, 2))
        else:
            self.a, self.b = z, yh
            move = lambda da, db: at(lax.rem(yh + db, 2), lax.rem(z + da + 4, 4), c, x, yl)
        self.left, self.right, self.pair = move(-1, 0), move(1, 0), move(0, 1)
        self.twin = at(yh, z, 1 - c, x, yl)

    def block(self, da, db):
        a, b = lax.rem(self.a + da + 4, 4), lax.rem(self.b + db, 2)
        return a * 2 + b if self.axis == "wt" else b * 4 + a

def cuts(rows, split):
    p = split or rows // 2
    q = rows - p
    return (0, p), (p, q), (0, p // 2), (p // 2, p // 2), (p, q // 2), (p + q // 2, q // 2)

def remote(src, dst, ssem, rsem, k, target):
    return pltpu.make_async_remote_copy(src_ref=src, dst_ref=dst, send_sem=ssem.at[k], recv_sem=rsem.at[k], device_id=target, device_id_type=MESH)

def greet(targets):
    bar = pltpu.get_barrier_semaphore()
    for t in targets:
        pl.semaphore_signal(bar, inc=1, device_id=t, device_id_type=MESH)
    pl.semaphore_wait(bar, len(targets))

def pace(rows, cols):
    return max(n for n in range(16, rows + 1, 16) if rows % n == 0 and n * cols <= 65536)

def gather_steps(pn, own, buf, rows, ssem, rsem, index=lambda j: j, split=None):
    P_, Q_, P0, P1, Q0, Q1 = cuts(rows, split)
    L, Rt, Y = pn.left, pn.right, pn.pair
    table = {
        0: (Y, (0, 0), P_, (0, 1)),
        1: (Rt, (0, 0), Q_, (-1, 0)),
        2: (L, (0, 0), Q_, (1, 0)),
        3: (Rt, (0, 0), P_, (-1, 0)),
        4: (L, (0, 0), P_, (1, 0)),
        5: (Y, (0, 0), Q_, (0, 1)),
        6: (Rt, (-1, 0), Q0, (2, 0)),
        7: (Y, (-1, 0), Q_, (-1, 1)),
        8: (L, (1, 0), Q1, (2, 0)),
        9: (Y, (1, 0), Q_, (1, 1)),
        10: (Rt, (0, 1), P_, (-1, 1)),
        11: (L, (0, 1), P_, (1, 1)),
        12: (Rt, (-1, 0), P0, (2, 0)),
        13: (L, (1, 0), P1, (2, 0)),
        14: (Y, (2, 0), Q0, (2, 1)),
        15: (Y, (2, 0), Q1, (2, 1)),
        16: (Rt, (-1, 1), P0, (2, 1)),
        17: (L, (1, 1), P1, (2, 1)),
    }
    def part(d, r):
        return buf.at[index(pn.block(*d)), pl.ds(*r)]
    def send(k):
        t, d, r, _ = table[k]
        if not r[1]:
            return
        src = own.at[pl.ds(*r)] if d == (0, 0) else part(d, r)
        remote(src, part(d, r), ssem, rsem, k, t).start()
    def got(k):
        t, _, r, d = table[k]
        if not r[1]:
            return
        remote(part(d, r), part(d, r), ssem, rsem, k, t).wait_recv()
    def sent(k):
        t, d, r, _ = table[k]
        if not r[1]:
            return
        remote(part(d, r), part(d, r), ssem, rsem, k, t).wait_send()
    def first():
        for k in (0, 1, 2, 3, 4, 5): send(k)
    def after(k, *next_):
        def f():
            got(k)
            for n in next_: send(n)
        return f
    steps = [first, after(1, 6, 7), after(2, 8, 9), after(0, 10, 11), after(3, 12), after(4, 13),
             after(6, 14), after(8, 15), after(10, 16), after(11, 17)]
    tail = [after(5), after(7), after(9), after(12), after(13), after(14), after(15), after(16), after(17)]
    def done():
        for k in range(18): sent(k)
    return steps, tail, done

def sum_steps(pn, buf, land, rows, ssem, rsem, out, index=lambda j: j, split=None):
    P_, Q_, P0, P1, Q0, Q1 = cuts(rows, split)
    L, Rt, Y = pn.left, pn.right, pn.pair
    table = {}
    off = 0
    def msg(k, t, d, r, r_to):
        nonlocal off
        table[k] = (t, d, r, off, r_to)
        off += r[1]
    msg(0, L, (-2, 0), P0, (-1, 0)); msg(1, Rt, (2, 0), P1, (1, 0))
    msg(2, L, (-2, 1), P0, (-1, 1)); msg(3, Rt, (2, 1), P1, (1, 1))
    msg(4, Y, (2, 1), Q_, (2, 0)); msg(5, Y, (-1, 1), Q_, (-1, 0)); msg(6, Y, (1, 1), Q_, (1, 0)); msg(7, Y, (0, 1), Q_, (0, 0))
    msg(8, L, (-1, 1), P_, (0, 1)); msg(9, Rt, (1, 1), P_, (0, 1))
    msg(10, L, (-1, 0), P_, (0, 0)); msg(11, Rt, (1, 0), P_, (0, 0))
    msg(12, L, (-2, 0), Q0, (-1, 0)); msg(13, Rt, (2, 0), Q1, (1, 0))
    msg(14, L, (-1, 0), Q_, (0, 0)); msg(15, Rt, (1, 0), Q_, (0, 0))
    msg(16, Y, (0, 1), P_, (0, 0))
    assert off <= land.shape[0]
    def part(d, r):
        return buf.at[index(pn.block(*d)), pl.ds(*r)]
    def landing(k):
        _, _, r, o, _ = table[k]
        return land.at[pl.ds(o, r[1])]
    def send(k):
        t, d, r, _, _ = table[k]
        if not r[1]:
            return
        remote(part(d, r), landing(k), ssem, rsem, k, t).start()
    def got(k):
        if not table[k][2][1]:
            return
        remote(landing(k), landing(k), ssem, rsem, k, table[k][0]).wait_recv()
    def sent(k):
        if not table[k][2][1]:
            return
        remote(landing(k), landing(k), ssem, rsem, k, table[k][0]).wait_send()
    def accumulate(d, r, ks, to=None):
        if not r[1]:
            return
        j = index(pn.block(*d))
        step = pace(r[1], buf.shape[2])
        def body(i, _):
            at_ = pl.multiple_of(r[0] + i * step, step)
            v = buf[j, pl.ds(at_, step)].astype(jnp.float32)
            for k in ks:
                v = v + land[pl.ds(pl.multiple_of(table[k][3] + i * step, step), step)].astype(jnp.float32)
            if to is None:
                buf[j, pl.ds(at_, step)] = v.astype(buf.dtype)
            else:
                to[pl.ds(at_, step)] = v.astype(to.dtype)
            return 0
        lax.fori_loop(0, r[1] // step, body, 0)
    def s0():
        for k in range(8): send(k)
    def s1():
        got(2); accumulate((-1, 1), P0, [2]); send(8)
        got(3); accumulate((1, 1), P1, [3]); send(9)
    def s2():
        got(0); accumulate((-1, 0), P0, [0]); send(10)
        got(1); accumulate((1, 0), P1, [1]); send(11)
    def s3():
        got(4); accumulate((2, 0), Q_, [4]); send(12); send(13)
    def s4():
        got(5); accumulate((-1, 0), Q_, [5]); got(12); accumulate((-1, 0), Q0, [12]); send(14)
        got(6); accumulate((1, 0), Q_, [6]); got(13); accumulate((1, 0), Q1, [13]); send(15)
    def s5():
        got(8); got(9); accumulate((0, 1), P_, [8, 9]); send(16)
    def s6():
        got(7); got(14); got(15); accumulate((0, 0), Q_, [7, 14, 15], out)
        got(10); got(11); got(16); accumulate((0, 0), P_, [10, 11, 16], out)
    def done():
        for k in range(17): sent(k)
    return [s0, s1, s2, s3, s4, s5, s6], done
ANY = pl.BlockSpec(memory_space=pl.ANY)
QB, KB = 512, 256
MASKED = -1e30
NT = (((1,), (1,)), ((), ()))

def halves(ref, kept):
    lane = lax.broadcasted_iota(jnp.int32, (1, 128), 1)
    low = (lane < 64).astype(jnp.float32)
    v = ref[...].astype(jnp.float32)
    kept[0] = (v * low).astype(jnp.bfloat16)
    kept[1] = (v * (1.0 - low)).astype(jnp.bfloat16)

def allowed(i, j, start):
    key = j * KB + lax.broadcasted_iota(jnp.int32, (KB, QB), 0)
    query = i * QB + lax.broadcasted_iota(jnp.int32, (KB, QB), 1)
    return (key <= query) & (key >= start)

def attn_fwd(q_ref, k_ref, v_ref, start_ref, o_ref, ot_ref, lse_ref, kept, vt):
    halves(k_ref, kept)
    vt[...] = v_ref[...].astype(jnp.float32).T.astype(jnp.bfloat16)
    n = q_ref.shape[0] // QB
    for i in range(n):
        q = q_ref[QB * i:QB * (i + 1)]
        start = start_ref[:, QB * i:QB * (i + 1)]
        def step(masked, j, carry):
            r = pl.ds(pl.multiple_of(j * KB, KB), KB)
            out = []
            for h in range(2):
                m, l, acc = carry[h]
                s = lax.dot_general(kept[h, r], q, NT, preferred_element_type=jnp.float32)
                if masked:
                    s = jnp.where(allowed(i, j, start), s, MASKED)
                top = jnp.maximum(m, jnp.max(s, axis=0, keepdims=True))
                p = jnp.exp(s - top)
                fade = jnp.exp(m - top)
                l = l * fade + jnp.sum(p, axis=0, keepdims=True)
                acc = acc * fade + jnp.dot(vt[64 * h:64 * h + 64, r], p.astype(jnp.bfloat16), preferred_element_type=jnp.float32)
                out.append((top, l, acc))
            return tuple(out)
        one = (jnp.full((1, QB), MASKED, jnp.float32), jnp.zeros((1, QB), jnp.float32), jnp.zeros((64, QB), jnp.float32))
        carry = (one, one)
        if i == n - 1:
            carry = lax.fori_loop(0, 2 * i + 2, functools.partial(step, True), carry)
        else:
            if i:
                carry = step(True, 0, carry)
                carry = lax.fori_loop(1, 2 * i, functools.partial(step, False), carry)
            carry = lax.fori_loop(2 * i, 2 * i + 2, functools.partial(step, True), carry)
        cols = pl.ds(QB * i, QB)
        for h in range(2):
            m, l, acc = carry[h]
            ot_ref[64 * h:64 * h + 64, cols] = acc / l
            lse_ref[h:h + 1, cols] = m + jnp.log(l)
        o_ref[QB * i:QB * (i + 1)] = ot_ref[:, cols].T.astype(jnp.bfloat16)

def attn_bwd(q_ref, k_ref, v_ref, start_ref, ot_ref, lse_ref, do_ref, dq_ref, dk_ref, dv_ref, keptk, keptv, keptq, keptd, kt, dot_):
    halves(k_ref, keptk)
    halves(v_ref, keptv)
    halves(q_ref, keptq)
    halves(do_ref, keptd)
    kt[...] = k_ref[...].astype(jnp.float32).T.astype(jnp.bfloat16)
    dot_[...] = do_ref[...].astype(jnp.float32).T
    dk_ref[...] = jnp.zeros_like(dk_ref)
    dv_ref[...] = jnp.zeros_like(dv_ref)
    n = q_ref.shape[0] // QB
    for i in range(n):
        rows = pl.ds(QB * i, QB)
        q = q_ref[rows]
        do = do_ref[rows]
        start = start_ref[:, rows]
        both = ot_ref[:, rows] * dot_[:, rows]
        inner = [jnp.sum(both[64 * h:64 * h + 64], axis=0, keepdims=True) for h in range(2)]
        lse = [lse_ref[h:h + 1, rows] for h in range(2)]
        def step(masked, j, carry):
            r = pl.ds(pl.multiple_of(j * KB, KB), KB)
            out, ps, ds = [], [], []
            for h in range(2):
                s = lax.dot_general(keptk[h, r], q, NT, preferred_element_type=jnp.float32)
                if masked:
                    s = jnp.where(allowed(i, j, start), s, MASKED)
                p = jnp.exp(s - lse[h])
                dp = lax.dot_general(keptv[h, r], do, NT, preferred_element_type=jnp.float32)
                g = (p * (dp - inner[h])).astype(jnp.bfloat16)
                out.append(carry[h] + jnp.dot(kt[64 * h:64 * h + 64, r], g, preferred_element_type=jnp.float32))
                ps.append(p.astype(jnp.bfloat16))
                ds.append(g)
            dv_ref[r] += sum(jnp.dot(ps[h], keptd[h, rows], preferred_element_type=jnp.float32) for h in range(2))
            dk_ref[r] += sum(jnp.dot(ds[h], keptq[h, rows], preferred_element_type=jnp.float32) for h in range(2))
            return tuple(out)
        carry = (jnp.zeros((64, QB), jnp.float32),) * 2
        if i == n - 1:
            carry = lax.fori_loop(0, 2 * i + 2, functools.partial(step, True), carry)
        else:
            if i:
                carry = step(True, 0, carry)
                carry = lax.fori_loop(1, 2 * i, functools.partial(step, False), carry)
            carry = lax.fori_loop(2 * i, 2 * i + 2, functools.partial(step, True), carry)
        dq_ref[rows] = jnp.concatenate(carry, axis=0).T

VM = pl.BlockSpec(memory_space=pltpu.VMEM)

def attention_forward(q, k, v, start):
    rows = q.shape[0]
    f = jax.ShapeDtypeStruct
    return pl.pallas_call(
        attn_fwd, out_shape=(f((rows, 128), jnp.bfloat16), f((128, rows), jnp.float32), f((8, rows), jnp.float32)),
        in_specs=[VM] * 4, out_specs=(VM,) * 3,
        scratch_shapes=[pltpu.VMEM((2, rows, 128), jnp.bfloat16), pltpu.VMEM((128, rows), jnp.bfloat16)],
        compiler_params=pltpu.CompilerParams(vmem_limit_bytes=56 * 2**20), name="attend",
    )(q, k, v, start)

def attention_backward(q, k, v, start, ot, lse, do):
    rows = q.shape[0]
    f = jax.ShapeDtypeStruct
    return pl.pallas_call(
        attn_bwd, out_shape=(f((rows, 128), jnp.float32),) * 3,
        in_specs=[VM] * 7, out_specs=(VM,) * 3,
        scratch_shapes=[pltpu.VMEM((2, rows, 128), jnp.bfloat16)] * 4 + [pltpu.VMEM((128, rows), jnp.bfloat16), pltpu.VMEM((128, rows), jnp.float32)],
        compiler_params=pltpu.CompilerParams(vmem_limit_bytes=56 * 2**20), name="attend_back",
    )(q, k, v, start, ot, lse, do)
SPLIT_A, SPLIT_C, SPLIT_D = 128, 96, 768
ORDER = [(0, 0), (0, 1), (-1, 1), (1, 1), (-1, 0), (1, 0), (2, 0), (2, 1)]

class Gather:
    def __init__(self, pn, own, buf, rows, ss, rs, twin=None, split=None):
        self.pn, self.buf, self.twin = pn, buf, twin
        self.index = (lambda j: 2 * j + pn.c) if twin else (lambda j: j)
        steps, tail, done = gather_steps(pn, own, buf, rows, ss, rs, self.index, split)
        self.done = done
        ready = {0: [1], 1: [2], 2: [3], 3: [4], 4: [5], 6: [6], 8: [7]}
        def follow(i, f):
            def g():
                f()
                for k in ready.get(i, []):
                    self.hand(k)
            return g
        def first():
            steps[0]()
            self.hand(0)
        self.steps = [first] + steps[1:] + [follow(i, f) for i, f in enumerate(tail)]

    def handed(self, k, mine):
        c = self.pn.c if mine else 1 - self.pn.c
        j = self.buf.at[2 * self.pn.block(*ORDER[k]) + c]
        return remote(j, j, self.twin[0], self.twin[1], k, self.pn.twin)

    def hand(self, k):
        if self.twin:
            self.handed(k, True).start()

    def wait_twin(self, k):
        self.handed(k, False).wait_recv()

    def finish(self, waited=()):
        self.done()
        if self.twin:
            for k in range(8):
                self.handed(k, True).wait_send()
                if k not in waited:
                    self.wait_twin(k)

def fetch_steps(pn, weight, hw, ss, rs, ls):
    s = lax.axis_index("seq")
    rows = hw.shape[0]
    h, q = rows // 2, rows // 4
    W = {"P": (0, h), "Q": (h, h), "P0": (0, q), "P1": (q, q), "Q0": (h, q), "Q1": (h + q, q)}
    kinds = ["P", "P0", "P1", "Q", "Q0", "Q1"]
    both = []
    for p in range(3):
        g = 16 * p + s
        src = g // 6
        da = lax.rem(pn.a - src // 2 + 4, 4)
        b0 = pn.b == lax.rem(src, 2)
        both.append((p, lax.rem(g, 6), da, b0))
    def part(p, kind):
        return hw.at[pl.ds(*W[kind]), pl.ds(128 * p, 128)]
    def send(p, kind, slot, target):
        pltpu.make_async_remote_copy(src_ref=part(p, kind), dst_ref=part(p, kind), send_sem=ss.at[6 * p + slot],
                                     recv_sem=rs.at[6 * p + kinds.index(kind)], device_id=target, device_id_type=MESH).start()
    def wait(p, kind, slot=None):
        cp = pltpu.make_async_remote_copy(src_ref=part(p, kind), dst_ref=part(p, kind), send_sem=ss.at[6 * p + (slot or 0)],
                                          recv_sem=rs.at[6 * p + kinds.index(kind)], device_id=pn.right, device_id_type=MESH)
        cp.wait_recv() if slot is None else cp.wait_send()
    no = jnp.logical_not
    def local(p, b):
        return pltpu.make_async_copy(weight.at[:, pl.ds(pl.multiple_of(128 * b, 128), 128)], hw.at[:, pl.ds(128 * p, 128)], ls.at[p])
    def begin():
        for p, b, da, b0 in both:
            @pl.when(b0 & (da == 0))
            def _():
                local(p, b).start()
    def st0():
        for p, b, da, b0 in both:
            @pl.when(b0 & (da == 0))
            def _():
                local(p, b).wait()
                send(p, "Q", 0, pn.right); send(p, "Q", 1, pn.left); send(p, "P", 5, pn.pair)
                send(p, "P", 3, pn.right); send(p, "P", 4, pn.left); send(p, "Q", 2, pn.pair)
    def st1():
        for p, b, da, b0 in both:
            @pl.when(b0 & (da == 1))
            def _():
                wait(p, "Q"); send(p, "Q0", 0, pn.right); send(p, "Q", 2, pn.pair)
            @pl.when(b0 & (da == 3))
            def _():
                wait(p, "Q"); send(p, "Q1", 1, pn.left); send(p, "Q", 2, pn.pair)
            @pl.when(no(b0) & (da == 0))
            def _():
                wait(p, "P"); send(p, "P", 3, pn.right); send(p, "P", 4, pn.left)
    def st2():
        for p, b, da, b0 in both:
            @pl.when(da == 1)
            def _():
                wait(p, "P"); send(p, "P0", 3, pn.right)
            @pl.when(da == 3)
            def _():
                wait(p, "P"); send(p, "P1", 4, pn.left)
    def st3():
        for p, b, da, b0 in both:
            @pl.when(b0 & (da == 2))
            def _():
                wait(p, "Q0"); wait(p, "Q1"); send(p, "Q", 2, pn.pair)
    def st4():
        for p, b, da, b0 in both:
            @pl.when(da == 2)
            def _():
                wait(p, "P0"); wait(p, "P1")
            @pl.when(no(b0))
            def _():
                wait(p, "Q")
    def done():
        for p, b, da, b0 in both:
            @pl.when(b0)
            def _():
                wait(p, "Q", 2)
            @pl.when(b0 & (da == 0))
            def _():
                wait(p, "Q", 0); wait(p, "Q", 1); wait(p, "P", 5)
            @pl.when(da == 0)
            def _():
                wait(p, "P", 3); wait(p, "P", 4)
            @pl.when(b0 & (da == 1))
            def _():
                wait(p, "Q0", 0)
            @pl.when(b0 & (da == 3))
            def _():
                wait(p, "Q1", 1)
            @pl.when(da == 1)
            def _():
                wait(p, "P0", 3)
            @pl.when(da == 3)
            def _():
                wait(p, "P1", 4)
    return begin, [st0, st1, st2, st3, st4], done

def turn(v, keep, ahead, behind):
    return v * keep + pltpu.roll(v, 120, 1) * ahead + pltpu.roll(v, 8, 1) * behind

def norm_rows(x, gain, shift):
    average = jnp.mean(x, axis=-1, keepdims=True)
    centred = x - average
    inverse = lax.rsqrt(jnp.mean(centred * centred, axis=-1, keepdims=True) + norm_eps)
    return centred * inverse * gain + shift

def rotary_tables_to(cs, tables):
    rows = cs.shape[1]
    c, s = cs[0:8, :], cs[8:16, :]
    one, nil, z8 = jnp.ones((48, rows), jnp.float32), jnp.zeros((48, rows), jnp.float32), jnp.zeros((8, rows), jnp.float32)
    tables[0][...] = jnp.concatenate([c, c, one] * 2, axis=0).T
    tables[1][...] = jnp.concatenate([-s, z8, nil] * 2, axis=0).T
    tables[2][...] = jnp.concatenate([z8, s, nil] * 2, axis=0).T

def pump(*its):
    for it in its:
        f = next(it, None)
        if f is not None:
            f()

def front_kernel(x, gain, shift, weight, bias, cs, start_ref, dy, ow,
                 rn, hw, q_ref, k_ref, v_ref, ot_ref, lse_ref, att, out_all, dy_all,
                 own, kept, vt, t0, t1, t2, ob, ox,
                 ssA, rsA, tsA, trA, ssB, rsB, lsB, ssC, rsC, ssD, rsD, tsD, trD, ssO, rsO, ssT, rsT, lsO, ls):
    sp, wp = Plane("seq"), Plane("wt")
    tok = x.shape[0]
    c, m = sp.c, sp.block(0, 0)
    A = Gather(sp, own, rn, tok, ssA, rsA, (tsA, trA), SPLIT_A)
    begin, fetch, fetch_done = fetch_steps(wp, weight, hw, ssB, rsB, lsB)
    C = Gather(wp, dy, dy_all, tok, ssC, rsC, None, SPLIT_C)
    D = Gather(wp, ow, out_all, ow.shape[0], ssD, rsD, (tsD, trD), SPLIT_D)
    begin()
    chips = [at(j // 4, j % 4, c, wp.a, wp.b) for j in range(8)]
    bar = pltpu.get_barrier_semaphore()
    for j in range(8):
        @pl.when(m != j)
        def _():
            pl.semaphore_signal(bar, inc=1, device_id=chips[j], device_id_type=MESH)
    for t in (sp.twin, wp.left, wp.right, wp.pair):
        pl.semaphore_signal(bar, inc=1, device_id=t, device_id_type=MESH)
    def ln(i, _):
        r = pl.ds(pl.multiple_of(i * 16, 16), 16)
        own[r] = norm_rows(x[r].astype(jnp.float32), gain[...], shift[...]).astype(jnp.bfloat16)
        return 0
    lax.fori_loop(0, tok // 16, ln, 0)
    copies = [pltpu.make_async_copy(own, rn.at[2 * m + c], ls.at[0]),
              pltpu.make_async_copy(dy, dy_all.at[wp.block(0, 0)], ls.at[1]),
              pltpu.make_async_copy(ow, out_all.at[2 * wp.block(0, 0) + c], ls.at[2])]
    for cp in copies:
        cp.start()
    copies[0].wait()
    pl.semaphore_wait(bar, 11)
    A.steps[0]()
    fetch[0]()
    rotary_tables_to(cs, (t0, t1, t2))
    copies[1].wait()
    copies[2].wait()
    a, b, cc, d = iter(A.steps[1:]), iter(fetch[1:]), iter(C.steps), iter(D.steps)
    pump(a, a, b, a, a, a, b, a, a, b, b, a, a, cc)
    def project(k):
        A.wait_twin(k)
        j = sp.block(*ORDER[k])
        rows = pl.ds(pl.multiple_of(j * 256, 256), 256)
        h = rn[pl.ds(2 * j, 2)].reshape(256, rn.shape[2])
        y = jnp.dot(h, hw[...], preferred_element_type=jnp.float32) + bias[...]
        tabs = (t0[rows], t1[rows], t2[rows])
        q_ref[rows] = (turn(y[:, :128], *tabs) * 0.125).astype(jnp.bfloat16)
        k_ref[rows] = turn(y[:, 128:256], *tabs).astype(jnp.bfloat16)
        v_ref[rows] = y[:, 256:].astype(jnp.bfloat16)
    project(0); pump(a); project(1); pump(a); pump(cc); project(2); pump(a); project(3)
    pump(a); project(4); pump(a, cc); project(5); pump(a, a); pump(cc); project(6); pump(a, a); project(7)
    halves(k_ref, kept)
    pump(cc, cc)
    vt[...] = v_ref[...].astype(jnp.float32).T.astype(jnp.bfloat16)
    def to_twin(j):
        return pltpu.make_async_remote_copy(src_ref=ox.at[j], dst_ref=ob.at[j, :, pl.ds(pl.multiple_of(128 * c, 128), 128)],
                                            send_sem=ssT.at[j], recv_sem=rsT.at[j], device_id=sp.twin, device_id_type=MESH)
    def from_twin(j):
        there = ob.at[j, :, pl.ds(pl.multiple_of(128 * (1 - c), 128), 128)]
        return pltpu.make_async_remote_copy(src_ref=there, dst_ref=there, send_sem=ssT.at[j], recv_sem=rsT.at[j], device_id=sp.twin, device_id_type=MESH)
    def cols(j):
        return att.at[:, pl.ds(pl.multiple_of(256 * j, 256), 256)]
    def to_chip(j):
        return pltpu.make_async_remote_copy(src_ref=ob.at[j], dst_ref=cols(m), send_sem=ssO.at[j], recv_sem=rsO.at[m], device_id=chips[j], device_id_type=MESH)
    def ship(i):
        for j in (2 * i, 2 * i + 1):
            from_twin(j).wait_recv()
            @pl.when(m == j)
            def _():
                pltpu.make_async_copy(ob.at[j], cols(j), lsO).start()
            @pl.when(m != j)
            def _():
                to_chip(j).start()
    n = q_ref.shape[0] // QB
    for i in range(n):
        q = q_ref[QB * i:QB * (i + 1)]
        start = start_ref[:, QB * i:QB * (i + 1)]
        step = functools.partial(attend_step, kept, vt, q, start, i)
        one = (jnp.full((1, QB), MASKED, jnp.float32), jnp.zeros((1, QB), jnp.float32), jnp.zeros((64, QB), jnp.float32))
        carry = (one, one)
        if i == n - 1:
            for j in range(0, 2 * i + 2, 2):
                carry = lax.fori_loop(j, j + 2, functools.partial(step, True), carry)
                pump(cc, d)
        else:
            if i:
                carry = step(True, 0, carry)
                carry = lax.fori_loop(1, 2 * i, functools.partial(step, False), carry)
                pump(cc, d) if i == 1 else pump(cc, cc, d)
            carry = lax.fori_loop(2 * i, 2 * i + 2, functools.partial(step, True), carry)
            pump(cc, cc)
        where = pl.ds(QB * i, QB)
        for h in range(2):
            top, l, acc = carry[h]
            ot_ref[64 * h:64 * h + 64, where] = acc / l
            lse_ref[h:h + 1, where] = top + jnp.log(l)
        if i:
            ship(i - 1)
        o = ot_ref[:, where].T.astype(jnp.bfloat16)
        for j in (0, 1):
            mine = pl.ds(pl.multiple_of(128 * c, 128), 128)
            first, second = o[256 * j:256 * j + 128], o[256 * j + 128:256 * j + 256]
            @pl.when(c == 0)
            def _():
                ob[2 * i + j, :, 0:128] = first
                ox[2 * i + j] = second
            @pl.when(c == 1)
            def _():
                ob[2 * i + j, :, 128:256] = second
                ox[2 * i + j] = first
            to_twin(2 * i + j).start()
    ship(n - 1)
    for f in cc:
        f()
    for f in d:
        f()
    for j in range(8):
        to_twin(j).wait_send()
        @pl.when(m == j)
        def _():
            pltpu.make_async_copy(ob.at[j], cols(j), lsO).wait()
        @pl.when(m != j)
        def _():
            to_chip(j).wait_send()
            pltpu.make_async_remote_copy(src_ref=cols(j), dst_ref=cols(j), send_sem=ssO.at[j], recv_sem=rsO.at[j], device_id=chips[j], device_id_type=MESH).wait_recv()
    A.finish(range(8))
    fetch_done()
    C.finish()
    D.finish()

def attend_step(kept, vt, q, start, i, masked, j, carry):
    r = pl.ds(pl.multiple_of(j * KB, KB), KB)
    out = []
    for h in range(2):
        m, l, acc = carry[h]
        s = lax.dot_general(kept[h, r], q, NT, preferred_element_type=jnp.float32)
        if masked:
            s = jnp.where(allowed(i, j, start), s, MASKED)
        top = jnp.maximum(m, jnp.max(s, axis=0, keepdims=True))
        p = jnp.exp(s - top)
        fade = jnp.exp(m - top)
        l = l * fade + jnp.sum(p, axis=0, keepdims=True)
        acc = acc * fade + jnp.dot(vt[64 * h:64 * h + 64, r], p.astype(jnp.bfloat16), preferred_element_type=jnp.float32)
        out.append((top, l, acc))
    return tuple(out)

def front(cid, x, gain, shift, weight, bias, cs, start, dy, ow):
    tok, width = x.shape
    rows = start.shape[1]
    f, b16, f32 = jax.ShapeDtypeStruct, jnp.bfloat16, jnp.float32
    vm = pltpu.VMEM
    return pl.pallas_call(
        front_kernel,
        out_shape=(f((16, tok, width), b16), f((width, 384), b16), f((rows, 128), b16), f((rows, 128), b16), f((rows, 128), b16),
                   f((128, rows), f32), f((8, rows), f32), f((tok, width), b16), f((16,) + ow.shape, b16), f((8, tok, width), b16)),
        in_specs=[VM, VM, VM, ANY, VM, VM, VM, VM, VM], out_specs=(VM,) * 10,
        scratch_shapes=[vm((tok, width), b16), vm((2, rows, 128), b16), vm((128, rows), b16)] + [vm((rows, 128), f32)] * 3
        + [vm((8, 128, 256), b16), vm((8, 128, 128), b16)]
        + [dma(n) for n in (18, 18, 8, 8, 18, 18, 3, 18, 18, 18, 18, 8, 8, 8, 8, 8, 8)] + [pltpu.SemaphoreType.DMA, dma(3)],
        compiler_params=params(cid), name="front",
    )(x, gain, shift, weight, bias, cs, start, dy, ow)
TN = (((0,), (0,)), ((), ()))

def middle_kernel(att, x, out_all, gain, shift, dy_all, wgu, wd,
                  mid, dh2, ffp, joined,
                  own, h2, wbuf, dga, tr, dh2p, land, ssG, rsG, ssS, rsS, lsw, ls):
    wp = Plane("wt")
    tok, width = mid.shape
    hidden = wd.shape[0]
    for t in (wp.left, wp.right, wp.pair):
        pl.semaphore_signal(pltpu.get_barrier_semaphore(), inc=1, device_id=t, device_id_type=MESH)
    def load(w, slot):
        return pltpu.make_async_copy(out_all.at[pl.ds(2 * w, 2)], wbuf.at[slot], lsw.at[slot])
    load(0, 0).start()
    def project(w):
        slot = w % 2
        load(w, slot).wait()
        if w < 7:
            load(w + 1, 1 - slot).start()
        cols = pl.ds(256 * w, 256)
        y = jnp.dot(att[:, :width // 2], wbuf[slot, 0], preferred_element_type=jnp.float32)
        y += jnp.dot(att[:, width // 2:], wbuf[slot, 1], preferred_element_type=jnp.float32)
        mid[:, cols] = x[:, cols].astype(jnp.float32) + y
    for w in range(8):
        project(w)
    def ln(i, _):
        r = pl.ds(pl.multiple_of(i * 16, 16), 16)
        own[r] = norm_rows(mid[r], gain[...], shift[...]).astype(jnp.bfloat16)
        return 0
    lax.fori_loop(0, tok // 16, ln, 0)
    cp = pltpu.make_async_copy(own, h2.at[wp.block(0, 0)], ls)
    cp.start()
    pl.semaphore_wait(pltpu.get_barrier_semaphore(), 3)
    G = Gather(wp, own, h2, tok, ssG, rsG)
    part = hidden // 2
    def chunk_up(da):
        a = lax.rem(wp.a + da + 4, 4)
        cols = pl.ds(pl.multiple_of(256 * a, 256), 256)
        hc = h2[pl.ds(2 * a, 2)].reshape(2 * tok, width)
        dc = dy_all[pl.ds(2 * a, 2)].reshape(2 * tok, width)
        def tile(i, _):
            r = pl.ds(pl.multiple_of(i * part, 16), part)
            r2 = pl.ds(pl.multiple_of(hidden + i * part, 16), part)
            r3 = pl.ds(pl.multiple_of(2 * hidden + i * part, 16), part)
            g = lax.dot_general(wgu[r], hc, NT, preferred_element_type=jnp.float32)
            u = lax.dot_general(wgu[r2], hc, NT, preferred_element_type=jnp.float32)
            e = lax.dot_general(wd[r], dc, NT, preferred_element_type=jnp.float32)
            sigma = 1.0 / (1.0 + jnp.exp(-g))
            gs = g * sigma
            dga[r, cols] = (e * u * sigma * (1.0 + g * (1.0 - sigma))).astype(jnp.bfloat16)
            dga[r2, cols] = (e * gs).astype(jnp.bfloat16)
            dga[r3, cols] = (gs * u).astype(jnp.bfloat16)
            return 0
        lax.fori_loop(0, 2, tile, 0)
    def chunk_down(da):
        a = lax.rem(wp.a + da + 4, 4)
        cols = pl.ds(pl.multiple_of(256 * a, 256), 256)
        def flip(i, _):
            r = pl.ds(pl.multiple_of(i * 128, 128), 128)
            tr[:, r] = dga[r, cols].astype(jnp.float32).T.astype(jnp.bfloat16)
            return 0
        lax.fori_loop(0, 3 * hidden // 128, flip, 0)
        last = 3 * hidden // 128 * 128
        tr[:, last:] = dga[last:, cols].astype(jnp.float32).T.astype(jnp.bfloat16)
        def tile(i, _):
            n = pl.ds(pl.multiple_of(i * 512, 512), 512)
            y = jnp.dot(tr[:, :2 * hidden], wgu[:, n], preferred_element_type=jnp.float32)
            dh2p[pl.ds(2 * a, 2), :, n] = y.astype(jnp.bfloat16).reshape(2, tok, 512)
            y = jnp.dot(tr[:, 2 * hidden:], wd[:, n], preferred_element_type=jnp.float32)
            ffp[pl.ds(2 * a, 2), :, n] = y.astype(jnp.bfloat16).reshape(2, tok, 512)
            return 0
        lax.fori_loop(0, width // 512, tile, 0)
    S = G.steps
    S[0]()
    cp.wait()
    for f in S[1:6]:
        f()
    S[10]()
    chunk_up(0)
    S[6](); S[7]()
    chunk_down(0)
    S[8](); S[9](); S[11](); S[12]()
    chunk_up(-1)
    chunk_down(-1)
    chunk_up(1)
    chunk_down(1)
    for f in S[13:]:
        f()
    chunk_up(2)
    chunk_down(2)
    G.finish()
    R, done = sum_steps(wp, dh2p, land, tok, ssS, rsS, dh2)
    def weights(lo, hi):
        def one(j, _):
            f = pl.ds(pl.multiple_of(256 * j, 256), 256)
            for k, other in ((0, h2), (1, h2), (2, dy_all)):
                r = pl.ds(hidden * k, hidden)
                y = jnp.dot(dga[r], other[:, :, f].reshape(8 * tok, 256), preferred_element_type=jnp.float32).astype(jnp.bfloat16)
                joined[2 * j, r] = y[:, :128]
                joined[2 * j + 1, r] = y[:, 128:]
            return 0
        lax.fori_loop(lo, hi, one, 0)
    R[0]()
    weights(0, 2); R[1](); R[2](); weights(2, 3); R[3](); weights(3, 4); R[4](); weights(4, 6); R[5](); weights(6, 8); R[6]()
    done()

def middle_part(cid, att, x, out_all, gain, shift, dy_all, wgu, wd):
    tok, width = x.shape
    hidden = wd.shape[0]
    f, b16, f32, vm = jax.ShapeDtypeStruct, jnp.bfloat16, jnp.float32, pltpu.VMEM
    return pl.pallas_call(
        middle_kernel,
        out_shape=(f((tok, width), f32), f((tok, width), f32), f((8, tok, width), b16), f((16, 3 * hidden, 128), b16)),
        in_specs=[VM, VM, ANY, VM, VM, VM, VM, VM], out_specs=(VM,) * 4,
        scratch_shapes=[vm((tok, width), b16), vm((8, tok, width), b16), vm((2, 2) + out_all.shape[1:], b16), vm((3 * hidden, 8 * tok), b16),
                        vm((2 * tok, 3 * hidden), b16), vm((8, tok, width), b16), vm((7 * tok, width), b16)]
        + [dma(n) for n in (18, 18, 17, 17, 2)] + [pltpu.SemaphoreType.DMA],
        compiler_params=params(cid), name="middle",
    )(att, x, out_all, gain, shift, dy_all, wgu, wd)
def params(cid):
    return pltpu.CompilerParams(collective_id=cid, has_side_effects=True, vmem_limit_bytes=56 * 2**20)

def dma(n):
    return pltpu.SemaphoreType.DMA((n,))

def gather_kernel(axis, x, o, ss, rs, ls):
    pn = Plane(axis)
    greet([pn.left, pn.right, pn.pair])
    cp = pltpu.make_async_copy(x, o.at[pn.block(0, 0)], ls)
    cp.start()
    steps, tail, done = gather_steps(pn, x, o, x.shape[0], ss, rs)
    for f in steps + tail:
        f()
    done()
    cp.wait()

def gather(axis, cid, x):
    return pl.pallas_call(
        functools.partial(gather_kernel, axis), out_shape=jax.ShapeDtypeStruct((8,) + x.shape, x.dtype),
        in_specs=[VM], out_specs=VM, scratch_shapes=[dma(18), dma(18), pltpu.SemaphoreType.DMA],
        compiler_params=params(cid), name="gather_" + axis)(x)

def gather_both_kernel(axis, x, o, ss, rs, ls, ts, tr):
    pn = Plane(axis)
    greet([pn.left, pn.right, pn.pair, pn.twin])
    index = lambda j: 2 * j + pn.c
    mine = index(pn.block(0, 0))
    cp = pltpu.make_async_copy(x, o.at[mine], ls)
    cp.start()
    cp.wait()
    steps, tail, done = gather_steps(pn, x, o, x.shape[0], ss, rs, index)
    order = [(0, 0), (0, 1), (-1, 1), (1, 1), (-1, 0), (1, 0), (2, 0), (2, 1)]
    def hand(k):
        j = index(pn.block(*order[k]))
        remote(o.at[j], o.at[j], ts, tr, k, pn.twin).start()
    steps[0]()
    hand(0)
    for f in steps[1:]:
        f()
    ready = {0: [1], 1: [2], 2: [3], 3: [4], 4: [5], 6: [6], 8: [7]}
    for i, f in enumerate(tail):
        f()
        for k in ready.get(i, []):
            hand(k)
    done()
    for k in range(8):
        j = 2 * pn.block(*order[k]) + 1 - pn.c
        remote(o.at[j], o.at[j], ts, tr, k, pn.twin).wait()

def gather_both(axis, cid, x):
    return pl.pallas_call(
        functools.partial(gather_both_kernel, axis), out_shape=jax.ShapeDtypeStruct((16,) + x.shape, x.dtype),
        in_specs=[VM], out_specs=VM, scratch_shapes=[dma(18), dma(18), pltpu.SemaphoreType.DMA, dma(8), dma(8)],
        compiler_params=params(cid), name="gather_both_" + axis)(x)

def scatter_kernel(axis, x, o, buf, land, ss, rs, ls):
    pn = Plane(axis)
    cp = pltpu.make_async_copy(x, buf, ls)
    cp.start()
    greet([pn.left, pn.right, pn.pair])
    cp.wait()
    steps, done = sum_steps(pn, buf, land, x.shape[1], ss, rs, o)
    for f in steps:
        f()
    done()

def scatter(axis, cid, x):
    _, rows, cols = x.shape
    return pl.pallas_call(
        functools.partial(scatter_kernel, axis), out_shape=jax.ShapeDtypeStruct((rows, cols), jnp.float32),
        in_specs=[ANY], out_specs=VM,
        scratch_shapes=[pltpu.VMEM(x.shape, x.dtype), pltpu.VMEM((7 * rows, cols), x.dtype), dma(17), dma(17), pltpu.SemaphoreType.DMA],
        compiler_params=params(cid), name="scatter_" + axis)(x)

def scatter_both_kernel(axis, x, o, buf, tland, land, ss, rs, ls, ts, tr):
    pn = Plane(axis)
    rows = x.shape[1]
    cp = pltpu.make_async_copy(x, buf, ls)
    cp.start()
    greet([pn.left, pn.right, pn.pair, pn.twin])
    cp.wait()
    order = [(2, 0), (2, 1), (-1, 1), (1, 1), (-1, 0), (1, 0), (0, 1), (0, 0)]
    for k in range(8):
        j = pn.block(*order[k])
        remote(buf.at[2 * j + 1 - pn.c], tland.at[k], ts, tr, k, pn.twin).start()
    for k in range(8):
        j = 2 * pn.block(*order[k]) + pn.c
        remote(tland.at[k], tland.at[k], ts, tr, k, pn.twin).wait_recv()
        step = pace(rows, x.shape[2])
        def body(i, _):
            r = pl.ds(pl.multiple_of(i * step, 16), step)
            buf[j, r] = (buf[j, r].astype(jnp.float32) + tland[k, r].astype(jnp.float32)).astype(buf.dtype)
            return 0
        lax.fori_loop(0, rows // step, body, 0)
    steps, done = sum_steps(pn, buf, land, rows, ss, rs, o, lambda j: 2 * j + pn.c)
    for f in steps:
        f()
    done()
    for k in range(8):
        remote(tland.at[k], tland.at[k], ts, tr, k, pn.twin).wait_send()

def scatter_both(axis, cid, x):
    _, rows, cols = x.shape
    return pl.pallas_call(
        functools.partial(scatter_both_kernel, axis), out_shape=jax.ShapeDtypeStruct((rows, cols), jnp.float32),
        in_specs=[ANY], out_specs=VM,
        scratch_shapes=[pltpu.VMEM(x.shape, x.dtype), pltpu.VMEM((8, rows, cols), x.dtype), pltpu.VMEM((7 * rows, cols), x.dtype),
                        dma(17), dma(17), pltpu.SemaphoreType.DMA, dma(8), dma(8)],
        compiler_params=params(cid), name="scatter_both_" + axis)(x)

def swap_kernel(axis, n, x, o, ss, rs, ls):
    me = lax.axis_index(axis)
    peers = [lax.rem(me + d, n) for d in range(1, n)]
    bar = pltpu.get_barrier_semaphore()
    for p in peers:
        pl.semaphore_signal(bar, inc=1, device_id={axis: p}, device_id_type=MESH)
    cp = pltpu.make_async_copy(x.at[me], o.at[me], ls)
    cp.start()
    pl.semaphore_wait(bar, n - 1)
    def copy(d):
        return remote(x.at[lax.rem(me + d, n)], o.at[me], ss, rs, d - 1, {axis: lax.rem(me + d, n)})
    for d in range(1, n):
        copy(d).start()
    for d in range(1, n):
        j = lax.rem(me - d + n, n)
        remote(x.at[j], o.at[j], ss, rs, d - 1, {axis: j}).wait()
    cp.wait()

def swap(axis, n, cid, x):
    return pl.pallas_call(
        functools.partial(swap_kernel, axis, n), out_shape=jax.ShapeDtypeStruct(x.shape, x.dtype),
        in_specs=[VM], out_specs=VM, scratch_shapes=[dma(n - 1), dma(n - 1), pltpu.SemaphoreType.DMA],
        compiler_params=params(cid), name="swap_" + axis)(x)

def fetch_kernel(x, o, ss, rs, ls):
    s, w = lax.axis_index("seq"), lax.axis_index("wt")
    bar = pltpu.get_barrier_semaphore()
    for d in range(1, 8):
        pl.semaphore_signal(bar, inc=1, device_id={"wt": lax.rem(w + d, 8)}, device_id_type=MESH)
    pl.semaphore_wait(bar, 7)
    for p in range(3):
        g = 16 * p + s
        @pl.when(w == g // 6)
        def _():
            src = x.at[lax.rem(g, 6)]
            cp = pltpu.make_async_copy(src, o.at[p], ls)
            cp.start()
            for d in range(1, 8):
                remote(src, o.at[p], ss.at[p], rs, p, {"wt": lax.rem(w + d, 8)}).start() if False else pltpu.make_async_remote_copy(src_ref=src, dst_ref=o.at[p], send_sem=ss.at[p, d - 1], recv_sem=rs.at[p], device_id={"wt": lax.rem(w + d, 8)}, device_id_type=MESH).start()
            cp.wait()
    for p in range(3):
        g = 16 * p + s
        @pl.when(w == g // 6)
        def _():
            for d in range(1, 8):
                pltpu.make_async_remote_copy(src_ref=o.at[p], dst_ref=o.at[p], send_sem=ss.at[p, d - 1], recv_sem=rs.at[p], device_id={"wt": lax.rem(w + d, 8)}, device_id_type=MESH).wait_send()
        @pl.when(w != g // 6)
        def _():
            pltpu.make_async_remote_copy(src_ref=o.at[p], dst_ref=o.at[p], send_sem=ss.at[p, 0], recv_sem=rs.at[p], device_id={"wt": lax.rem(w + 1, 8)}, device_id_type=MESH).wait_recv()

def fetch(cid, x):
    return pl.pallas_call(
        fetch_kernel, out_shape=jax.ShapeDtypeStruct((3,) + x.shape[1:], x.dtype),
        in_specs=[VM], out_specs=VM, scratch_shapes=[pltpu.SemaphoreType.DMA((3, 7)), dma(3), pltpu.SemaphoreType.DMA],
        compiler_params=params(cid), name="fetch_heads")(x)

def place_kernel(x, o, ss, rs, ls):
    s, w = lax.axis_index("seq"), lax.axis_index("wt")
    bar = pltpu.get_barrier_semaphore()
    def source(b):
        g = 6 * w + b
        return lax.rem(g, 16), s // 2
    def target(i, p):
        g = 16 * p + s
        return 2 * w + i, g // 6, lax.rem(g, 6)
    own = jnp.int32(0)
    for b in range(6):
        ts, tw = source(b)
        same = (ts == s) & (tw == w)
        own += same.astype(jnp.int32)
        @pl.when(jnp.logical_not(same))
        def _():
            pl.semaphore_signal(bar, inc=1, device_id={"seq": ts, "wt": tw}, device_id_type=MESH)
    pl.semaphore_wait(bar, 6 - own)
    def copy(i, p):
        ts, tw, slot = target(i, p)
        return pltpu.make_async_remote_copy(src_ref=x.at[i, p], dst_ref=o.at[slot], send_sem=ss.at[i, p], recv_sem=rs.at[slot], device_id={"seq": ts, "wt": tw}, device_id_type=MESH)
    def local(i, p):
        return pltpu.make_async_copy(x.at[i, p], o.at[target(i, p)[2]], ls.at[i, p])
    for i in range(2):
        for p in range(3):
            ts, tw, _ = target(i, p)
            same = (ts == s) & (tw == w)
            @pl.when(same)
            def _():
                local(i, p).start()
            @pl.when(jnp.logical_not(same))
            def _():
                copy(i, p).start()
    for i in range(2):
        for p in range(3):
            ts, tw, _ = target(i, p)
            same = (ts == s) & (tw == w)
            @pl.when(same)
            def _():
                local(i, p).wait()
            @pl.when(jnp.logical_not(same))
            def _():
                copy(i, p).wait_send()
    for b in range(6):
        ts, tw = source(b)
        @pl.when(jnp.logical_not((ts == s) & (tw == w)))
        def _():
            pltpu.make_async_remote_copy(src_ref=o.at[b], dst_ref=o.at[b], send_sem=ss.at[0, 0], recv_sem=rs.at[b], device_id={"seq": ts, "wt": tw}, device_id_type=MESH).wait_recv()

def place(cid, x):
    return pl.pallas_call(
        place_kernel, out_shape=jax.ShapeDtypeStruct((6, 128, 128), x.dtype),
        in_specs=[VM], out_specs=VM, scratch_shapes=[pltpu.SemaphoreType.DMA((2, 3)), dma(6), pltpu.SemaphoreType.DMA((2, 3))],
        compiler_params=params(cid), name="place_qkv")(x)

def small_kernel(x, o, land, mid, land2, ss, rs, ss2, rs2):
    s, w = lax.axis_index("seq"), lax.axis_index("wt")
    bar = pltpu.get_barrier_semaphore()
    for d in range(1, 8):
        pl.semaphore_signal(bar, inc=1, device_id={"wt": lax.rem(w + d, 8)}, device_id_type=MESH)
    for d in range(1, 16):
        pl.semaphore_signal(bar, inc=1, device_id={"seq": lax.rem(s + d, 16)}, device_id_type=MESH)
    pl.semaphore_wait(bar, 22)
    for d in range(1, 8):
        remote(x.at[lax.rem(w + d, 8)], land.at[d - 1], ss, rs, d - 1, {"wt": lax.rem(w + d, 8)}).start()
    for d in range(1, 8):
        remote(x.at[0], land.at[d - 1], ss, rs, d - 1, {"wt": lax.rem(w + d, 8)}).wait()
    mid[:, 0] = x[w] + jnp.sum(land[...], axis=0)
    for d in range(1, 16):
        remote(mid.at[lax.rem(s + d, 16)], land2.at[d - 1], ss2, rs2, d - 1, {"seq": lax.rem(s + d, 16)}).start()
    for d in range(1, 16):
        remote(mid.at[0], land2.at[d - 1], ss2, rs2, d - 1, {"seq": lax.rem(s + d, 16)}).wait()
    o[...] = mid[s] + jnp.sum(land2[...], axis=0)

def small_sum(cid, x):
    f = jnp.float32
    return pl.pallas_call(
        small_kernel, out_shape=jax.ShapeDtypeStruct((1, 128), f),
        in_specs=[VM], out_specs=VM,
        scratch_shapes=[pltpu.VMEM((7, 16, 128), f), pltpu.VMEM((16, 1, 128), f), pltpu.VMEM((15, 1, 128), f), dma(7), dma(7), dma(15), dma(15)],
        compiler_params=params(cid), name="small_sum")(x)


norm_eps = 1e-05
theta_base = 10000.0
ROT = 16
HEAD_DIM = 64


def layer_norm_parts(values, gain, shift):
    average = jnp.mean(values, axis=-1, keepdims=True)
    centred = values - average
    spread = jnp.mean(centred * centred, axis=-1, keepdims=True)
    inverse = lax.rsqrt(spread + norm_eps)
    scaled = centred * inverse
    return (scaled * gain + shift, scaled, inverse)


def layer_norm_back(upward, scaled, inverse, gain):
    weighted = upward * gain
    first_mean = jnp.mean(weighted, axis=-1, keepdims=True)
    second_mean = jnp.mean(weighted * scaled, axis=-1, keepdims=True)
    return inverse * (weighted - first_mean - scaled * second_mean)


def rotary_angles(segment_row):
    rows = segment_row.shape[0]
    ends = [jnp.sum((segment_row < i).astype(jnp.int32)) for i in (1, 2)]
    start = jnp.where(segment_row == 0, 0, jnp.where(segment_row == 1, ends[0], ends[1]))
    offsets = (jnp.arange(rows, dtype=jnp.int32) - start).astype(jnp.float32)
    inv_freq = jnp.exp(jnp.arange(ROT // 2, dtype=jnp.float32) * (-2.0 * math.log(theta_base) / ROT))
    angles = inv_freq[:, None] * offsets[None, :]
    return start.reshape(1, rows), jnp.concatenate([jnp.cos(angles), jnp.sin(angles)], axis=0)


def wide_tables(cs):
    c, s = cs[0:8], cs[8:16]
    one, nil, z8 = jnp.ones((48, c.shape[1]), jnp.float32), jnp.zeros((48, c.shape[1]), jnp.float32), jnp.zeros((8, c.shape[1]), jnp.float32)
    return [jnp.concatenate(p * 2, axis=0).T for p in ([c, c, one], [-s, z8, nil], [z8, s, nil])]


def rotate(v, keep, ahead, behind):
    return v * keep + jnp.roll(v, -8, axis=1) * ahead + jnp.roll(v, 8, axis=1) * behind


def contract_first(left, right):
    return lax.dot_general(left, right, (((0,), (0,)), ((), ())), preferred_element_type=jnp.float32)


def contract_last(left, right):
    return lax.dot_general(left, right, (((1,), (1,)), ((), ())), preferred_element_type=jnp.float32)


def per_device(layer_in, segment_ids, norm_one_gain, norm_one_shift, qkv_weight, qkv_bias, out_weight, norm_two_gain,
               norm_two_shift, gate_up_weight, down_weight, layer_grad):
    f32, bf16 = jnp.float32, jnp.bfloat16
    s, w = lax.axis_index("seq"), lax.axis_index("wt")
    tok, width = layer_in.shape[1:]
    rows = segment_ids.shape[1]
    hidden = down_weight.shape[0]
    scale = 1.0 / math.sqrt(HEAD_DIM)
    inputs = layer_in.reshape(tok, width).astype(f32)
    upstream = layer_grad.reshape(tok, width)
    start, cs = rotary_angles(segment_ids.reshape(rows))
    keep, ahead, behind = wide_tables(cs)
    _, scaled_one, inverse_one = layer_norm_parts(inputs, norm_one_gain, norm_one_shift)
    bias = lax.dynamic_index_in_dim(qkv_bias.reshape(3, 16, 128), s, 1, keepdims=False).reshape(1, 384)
    half = lax.dynamic_slice_in_dim(out_weight, (s % 2) * (width // 2), width // 2, 0)
    row_normed, head_weight, q, k, v, ot, lse, attended, out_all, all_up = front(
        0, layer_in.reshape(tok, width), norm_one_gain.reshape(1, width), norm_one_shift.reshape(1, width), qkv_weight, bias, cs, start, upstream, half)
    row_normed = row_normed.reshape(rows, width)
    out_all = out_all.reshape(8, 2, width // 2, 256)
    middle, dh2, ffn_part, joined = middle_part(
        4, attended, layer_in.reshape(tok, width), out_all.reshape(16, width // 2, 256), norm_two_gain.reshape(1, width),
        norm_two_shift.reshape(1, width), all_up, gate_up_weight.transpose(1, 2, 0).reshape(2 * hidden, width), down_weight)
    _, scaled_two, inverse_two = layer_norm_parts(middle, norm_two_gain, norm_two_shift)
    ffn_out = scatter("wt", 7, ffn_part)
    layer_out = (middle + ffn_out).astype(bf16).reshape(1, tok, width)
    gain_two = jnp.sum(dh2 * scaled_two, axis=0)
    shift_two = jnp.sum(dh2, axis=0)
    middle_grad = upstream.astype(f32) + layer_norm_back(dh2, scaled_two, inverse_two, norm_two_gain)
    da = middle_grad.astype(bf16)
    dout = jnp.einsum("twn,wckn->tck", da.reshape(tok, 8, 256), out_all, preferred_element_type=f32).astype(bf16)
    do = swap("seq", 16, 8, dout.reshape(tok, 16, 128).transpose(1, 0, 2)).reshape(rows, 128)
    dq, dk, dv = attention_backward(q, k, v, start, ot, lse, do)
    low = lambda t: t.astype(bf16).astype(f32)
    dproj = jnp.concatenate([rotate(low(dq) * scale, keep, -ahead, -behind), rotate(low(dk), keep, -ahead, -behind), dv], axis=1).astype(bf16)
    dh1_part = contract_last(dproj, head_weight).astype(bf16)
    dh1 = scatter_both("seq", 9, dh1_part.reshape(16, tok, width))
    gain_one = jnp.sum(dh1 * scaled_one, axis=0)
    shift_one = jnp.sum(dh1, axis=0)
    dx = middle_grad + layer_norm_back(dh1, scaled_one, inverse_one, norm_one_gain)
    input_grad = dx.astype(bf16).reshape(1, tok, width)
    qkv_part = contract_first(row_normed, dproj).astype(bf16)
    qkv_rows = scatter("wt", 10, qkv_part.reshape(8, 256, 384)).astype(bf16)
    qkv_grad = place(11, qkv_rows.reshape(2, 128, 3, 128).transpose(0, 2, 1, 3))
    qkv_grad = qkv_grad.transpose(1, 0, 2).reshape(128, 768).astype(f32)
    all_att = gather("wt", 12, attended).reshape(8 * tok, width)
    da_cols = swap("wt", 8, 13, da.reshape(tok, 8, 256).transpose(1, 0, 2)).reshape(8 * tok, 256)
    out_part = contract_first(all_att, da_cols).astype(bf16)
    out_grad = scatter_both("seq", 16, out_part.reshape(16, 128, 256))
    joined = scatter_both("seq", 14, joined)
    gate_grad = joined[:2 * hidden].reshape(2, hidden, 128).transpose(2, 0, 1)
    down_grad = joined[2 * hidden:]
    bias_grad = lax.dynamic_update_slice(jnp.zeros((3, 16, 128), f32), jnp.sum(dproj.astype(f32), axis=0).reshape(3, 1, 128), (0, s, 0))
    blocks = [t.reshape(16, 8, -1) for t in (gain_one, shift_one, bias_grad, gain_two, shift_two, jnp.zeros((16 * 8 * 16,), f32))]
    small = small_sum(15, jnp.concatenate(blocks, axis=2).transpose(1, 0, 2))[0]
    return (layer_out, input_grad, small[0:16], small[16:32], qkv_grad, small[32:80], out_grad, small[80:96], small[96:112], gate_grad, down_grad)


def solution(mesh):
    both = P(("seq", "wt"))
    return jax.shard_map(
        per_device, mesh=mesh,
        in_specs=(P("wt", "seq", None), P("wt", None), P(), P(), P(None, "wt"), P(), P(None, "wt"), P(), P(), P(None, None, "wt"), P("wt", None), P("wt", "seq", None)),
        out_specs=(P("wt", "seq", None), P("wt", "seq", None), both, both, P("seq", "wt"), both, P("seq", "wt"), both, both, P("seq", None, "wt"), P("wt", "seq")),
        check_vma=False)
```

```python
import functools, math
import jax, jax.numpy as jnp
from jax import lax
from jax.experimental import pallas as pl
from jax.experimental.pallas import tpu as pltpu
from jax.sharding import PartitionSpec as P

MESH = pl.DeviceIdType.MESH

def coords():
    s = lax.axis_index("seq")
    w = lax.axis_index("wt")
    return s // 8, lax.rem(s // 2, 4), lax.rem(s, 2), w // 2, lax.rem(w, 2)

def at(yh, z, c, x, yl):
    return {"seq": yh * 8 + z * 2 + c, "wt": x * 2 + yl}

class Plane:
    def __init__(self, axis):
        self.axis = axis
        yh, z, c, x, yl = coords()
        self.c = c
        if axis == "wt":
            self.a, self.b = x, yl
            move = lambda da, db: at(yh, z, c, lax.rem(x + da + 4, 4), lax.rem(yl + db, 2))
        else:
            self.a, self.b = z, yh
            move = lambda da, db: at(lax.rem(yh + db, 2), lax.rem(z + da + 4, 4), c, x, yl)
        self.left, self.right, self.pair = move(-1, 0), move(1, 0), move(0, 1)
        self.twin = at(yh, z, 1 - c, x, yl)

    def block(self, da, db):
        a, b = lax.rem(self.a + da + 4, 4), lax.rem(self.b + db, 2)
        return a * 2 + b if self.axis == "wt" else b * 4 + a

def cuts(rows, split):
    p = split or rows // 2
    q = rows - p
    return (0, p), (p, q), (0, p // 2), (p // 2, p // 2), (p, q // 2), (p + q // 2, q // 2)

def remote(src, dst, ssem, rsem, k, target):
    return pltpu.make_async_remote_copy(src_ref=src, dst_ref=dst, send_sem=ssem.at[k], recv_sem=rsem.at[k], device_id=target, device_id_type=MESH)

def greet(targets):
    bar = pltpu.get_barrier_semaphore()
    for t in targets:
        pl.semaphore_signal(bar, inc=1, device_id=t, device_id_type=MESH)
    pl.semaphore_wait(bar, len(targets))

def repeat(n, body):
    if n == 1:
        body(0, 0)
    else:
        lax.fori_loop(0, n, body, 0)

def pace(rows, cols):
    return max(n for n in range(16, rows + 1, 16) if rows % n == 0 and n * cols <= 300000)

def gather_steps(pn, own, buf, rows, ssem, rsem, index=lambda j: j, split=None):
    P_, Q_, P0, P1, Q0, Q1 = cuts(rows, split)
    L, Rt, Y = pn.left, pn.right, pn.pair
    table = {
        0: (Y, (0, 0), P_, (0, 1)),
        1: (Rt, (0, 0), Q_, (-1, 0)),
        2: (L, (0, 0), Q_, (1, 0)),
        3: (Rt, (0, 0), P_, (-1, 0)),
        4: (L, (0, 0), P_, (1, 0)),
        5: (Y, (0, 0), Q_, (0, 1)),
        6: (Rt, (-1, 0), Q0, (2, 0)),
        7: (Y, (-1, 0), Q_, (-1, 1)),
        8: (L, (1, 0), Q1, (2, 0)),
        9: (Y, (1, 0), Q_, (1, 1)),
        10: (Rt, (0, 1), P_, (-1, 1)),
        11: (L, (0, 1), P_, (1, 1)),
        12: (Rt, (-1, 0), P0, (2, 0)),
        13: (L, (1, 0), P1, (2, 0)),
        14: (Y, (2, 0), Q0, (2, 1)),
        15: (Y, (2, 0), Q1, (2, 1)),
        16: (Rt, (-1, 1), P0, (2, 1)),
        17: (L, (1, 1), P1, (2, 1)),
    }
    def part(d, r):
        return buf.at[index(pn.block(*d)), pl.ds(*r)]
    def send(k):
        t, d, r, _ = table[k]
        if not r[1]:
            return
        src = own.at[pl.ds(*r)] if d == (0, 0) else part(d, r)
        remote(src, part(d, r), ssem, rsem, k, t).start()
    def got(k):
        t, _, r, d = table[k]
        if not r[1]:
            return
        remote(part(d, r), part(d, r), ssem, rsem, k, t).wait_recv()
    def sent(k):
        t, d, r, _ = table[k]
        if not r[1]:
            return
        remote(part(d, r), part(d, r), ssem, rsem, k, t).wait_send()
    def first():
        for k in (0, 1, 2, 3, 4, 5): send(k)
    def after(k, *next_):
        def f():
            got(k)
            for n in next_: send(n)
        return f
    steps = [first, after(1, 6, 7), after(2, 8, 9), after(0, 10, 11), after(3, 12), after(4, 13),
             after(6, 14), after(8, 15), after(10, 16), after(11, 17)]
    tail = [after(5), after(7), after(9), after(12), after(13), after(14), after(15), after(16), after(17)]
    def done():
        for k in range(18): sent(k)
    return steps, tail, done

def sum_steps(pn, buf, land, rows, ssem, rsem, out, index=lambda j: j, split=None):
    P_, Q_, P0, P1, Q0, Q1 = cuts(rows, split)
    L, Rt, Y = pn.left, pn.right, pn.pair
    table = {}
    off = 0
    def msg(k, t, d, r, r_to):
        nonlocal off
        table[k] = (t, d, r, off, r_to)
        off += r[1]
    msg(0, L, (-2, 0), P0, (-1, 0)); msg(1, Rt, (2, 0), P1, (1, 0))
    msg(2, L, (-2, 1), P0, (-1, 1)); msg(3, Rt, (2, 1), P1, (1, 1))
    msg(4, Y, (2, 1), Q_, (2, 0)); msg(5, Y, (-1, 1), Q_, (-1, 0)); msg(6, Y, (1, 1), Q_, (1, 0)); msg(7, Y, (0, 1), Q_, (0, 0))
    msg(8, L, (-1, 1), P_, (0, 1)); msg(9, Rt, (1, 1), P_, (0, 1))
    msg(10, L, (-1, 0), P_, (0, 0)); msg(11, Rt, (1, 0), P_, (0, 0))
    msg(12, L, (-2, 0), Q0, (-1, 0)); msg(13, Rt, (2, 0), Q1, (1, 0))
    msg(14, L, (-1, 0), Q_, (0, 0)); msg(15, Rt, (1, 0), Q_, (0, 0))
    msg(16, Y, (0, 1), P_, (0, 0))
    assert off <= land.shape[0]
    def part(d, r):
        return buf.at[index(pn.block(*d)), pl.ds(*r)]
    def landing(k):
        _, _, r, o, _ = table[k]
        return land.at[pl.ds(o, r[1])]
    def send(k):
        t, d, r, _, _ = table[k]
        if not r[1]:
            return
        remote(part(d, r), landing(k), ssem, rsem, k, t).start()
    def got(k):
        if not table[k][2][1]:
            return
        remote(landing(k), landing(k), ssem, rsem, k, table[k][0]).wait_recv()
    def sent(k):
        if not table[k][2][1]:
            return
        remote(landing(k), landing(k), ssem, rsem, k, table[k][0]).wait_send()
    def accumulate(d, r, ks, to=None):
        if not r[1]:
            return
        j = index(pn.block(*d))
        step = pace(r[1], buf.shape[2])
        def body(i, _):
            at_ = pl.multiple_of(r[0] + i * step, 16)
            v = buf[j, pl.ds(at_, step)].astype(jnp.float32)
            for k in ks:
                v = v + land[pl.ds(pl.multiple_of(table[k][3] + i * step, 16), step)].astype(jnp.float32)
            if to is None:
                buf[j, pl.ds(at_, step)] = v.astype(buf.dtype)
            else:
                to[pl.ds(at_, step)] = v.astype(to.dtype)
            return 0
        repeat(r[1] // step, body)
    def s0():
        for k in range(8): send(k)
    def s1():
        got(2); accumulate((-1, 1), P0, [2]); send(8)
        got(3); accumulate((1, 1), P1, [3]); send(9)
    def s2():
        got(0); accumulate((-1, 0), P0, [0]); send(10)
        got(1); accumulate((1, 0), P1, [1]); send(11)
    def s3():
        got(4); accumulate((2, 0), Q_, [4]); send(12); send(13)
    def s4():
        got(5); accumulate((-1, 0), Q_, [5]); got(12); accumulate((-1, 0), Q0, [12]); send(14)
        got(6); accumulate((1, 0), Q_, [6]); got(13); accumulate((1, 0), Q1, [13]); send(15)
    def s5():
        got(8); got(9); accumulate((0, 1), P_, [8, 9]); send(16)
    def s6():
        got(7); got(14); got(15); accumulate((0, 0), Q_, [7, 14, 15], out)
        got(10); got(11); got(16); accumulate((0, 0), P_, [10, 11, 16], out)
    def done():
        for k in range(17): sent(k)
    return [s0, s1, s2, s3, s4, s5, s6], done
ANY = pl.BlockSpec(memory_space=pl.ANY)
QB, KB = 512, 512
MASKED = -1e30
NT = (((1,), (1,)), ((), ()))

def halves(ref, kept):
    lane = lax.broadcasted_iota(jnp.int32, (1, 128), 1)
    low = (lane < 64).astype(jnp.float32)
    v = ref[...].astype(jnp.float32)
    kept[0] = (v * low).astype(jnp.bfloat16)
    kept[1] = (v * (1.0 - low)).astype(jnp.bfloat16)

def allowed(i, j, start):
    key = j * KB + lax.broadcasted_iota(jnp.int32, (KB, QB), 0)
    query = i * QB + lax.broadcasted_iota(jnp.int32, (KB, QB), 1)
    return (key <= query) & (key >= start)

VM = pl.BlockSpec(memory_space=pltpu.VMEM)

SPLIT_A, SPLIT_C, SPLIT_D = 128, 96, 768
ORDER = [(0, 0), (0, 1), (-1, 1), (1, 1), (-1, 0), (1, 0), (2, 0), (2, 1)]

class Gather:
    def __init__(self, pn, own, buf, rows, ss, rs, twin=None, split=None):
        self.pn, self.buf, self.twin = pn, buf, twin
        self.index = (lambda j: 2 * j + pn.c) if twin else (lambda j: j)
        steps, tail, done = gather_steps(pn, own, buf, rows, ss, rs, self.index, split)
        self.done = done
        ready = {0: [1], 1: [2], 2: [3], 3: [4], 4: [5], 6: [6], 8: [7]}
        def follow(i, f):
            def g():
                f()
                for k in ready.get(i, []):
                    self.hand(k)
            return g
        def first():
            steps[0]()
            self.hand(0)
        self.steps = [first] + steps[1:] + [follow(i, f) for i, f in enumerate(tail)]

    def handed(self, k, mine):
        c = self.pn.c if mine else 1 - self.pn.c
        j = self.buf.at[2 * self.pn.block(*ORDER[k]) + c]
        return remote(j, j, self.twin[0], self.twin[1], k, self.pn.twin)

    def hand(self, k):
        if self.twin:
            self.handed(k, True).start()

    def wait_twin(self, k):
        self.handed(k, False).wait_recv()

    def finish(self, waited=()):
        self.done()
        if self.twin:
            for k in range(8):
                self.handed(k, True).wait_send()
                if k not in waited:
                    self.wait_twin(k)

def fetch_steps(pn, weight, hw, ss, rs, ls):
    s = lax.axis_index("seq")
    rows = hw.shape[0]
    h, q = rows // 2, rows // 4
    W = {"P": (0, h), "Q": (h, h), "P0": (0, q), "P1": (q, q), "Q0": (h, q), "Q1": (h + q, q)}
    kinds = ["P", "P0", "P1", "Q", "Q0", "Q1"]
    both = []
    for p in range(3):
        g = 16 * p + s
        src = g // 6
        da = lax.rem(pn.a - src // 2 + 4, 4)
        b0 = pn.b == lax.rem(src, 2)
        both.append((p, lax.rem(g, 6), da, b0))
    def part(p, kind):
        return hw.at[pl.ds(*W[kind]), pl.ds(128 * p, 128)]
    def send(p, kind, slot, target):
        pltpu.make_async_remote_copy(src_ref=part(p, kind), dst_ref=part(p, kind), send_sem=ss.at[6 * p + slot],
                                     recv_sem=rs.at[6 * p + kinds.index(kind)], device_id=target, device_id_type=MESH).start()
    def wait(p, kind, slot=None):
        cp = pltpu.make_async_remote_copy(src_ref=part(p, kind), dst_ref=part(p, kind), send_sem=ss.at[6 * p + (slot or 0)],
                                          recv_sem=rs.at[6 * p + kinds.index(kind)], device_id=pn.right, device_id_type=MESH)
        cp.wait_recv() if slot is None else cp.wait_send()
    no = jnp.logical_not
    def local(p, b):
        return pltpu.make_async_copy(weight.at[:, pl.ds(pl.multiple_of(128 * b, 128), 128)], hw.at[:, pl.ds(128 * p, 128)], ls.at[p])
    def begin():
        for p, b, da, b0 in both:
            @pl.when(b0 & (da == 0))
            def _():
                local(p, b).start()
    def st0():
        for p, b, da, b0 in both:
            @pl.when(b0 & (da == 0))
            def _():
                local(p, b).wait()
                send(p, "Q", 0, pn.right); send(p, "Q", 1, pn.left); send(p, "P", 5, pn.pair)
                send(p, "P", 3, pn.right); send(p, "P", 4, pn.left); send(p, "Q", 2, pn.pair)
    def st1():
        for p, b, da, b0 in both:
            @pl.when(b0 & (da == 1))
            def _():
                wait(p, "Q"); send(p, "Q0", 0, pn.right); send(p, "Q", 2, pn.pair)
            @pl.when(b0 & (da == 3))
            def _():
                wait(p, "Q"); send(p, "Q1", 1, pn.left); send(p, "Q", 2, pn.pair)
            @pl.when(no(b0) & (da == 0))
            def _():
                wait(p, "P"); send(p, "P", 3, pn.right); send(p, "P", 4, pn.left)
    def st2():
        for p, b, da, b0 in both:
            @pl.when(da == 1)
            def _():
                wait(p, "P"); send(p, "P0", 3, pn.right)
            @pl.when(da == 3)
            def _():
                wait(p, "P"); send(p, "P1", 4, pn.left)
    def st3():
        for p, b, da, b0 in both:
            @pl.when(b0 & (da == 2))
            def _():
                wait(p, "Q0"); wait(p, "Q1"); send(p, "Q", 2, pn.pair)
    def st4():
        for p, b, da, b0 in both:
            @pl.when(da == 2)
            def _():
                wait(p, "P0"); wait(p, "P1")
            @pl.when(no(b0))
            def _():
                wait(p, "Q")
    def done():
        for p, b, da, b0 in both:
            @pl.when(b0)
            def _():
                wait(p, "Q", 2)
            @pl.when(b0 & (da == 0))
            def _():
                wait(p, "Q", 0); wait(p, "Q", 1); wait(p, "P", 5)
            @pl.when(da == 0)
            def _():
                wait(p, "P", 3); wait(p, "P", 4)
            @pl.when(b0 & (da == 1))
            def _():
                wait(p, "Q0", 0)
            @pl.when(b0 & (da == 3))
            def _():
                wait(p, "Q1", 1)
            @pl.when(da == 1)
            def _():
                wait(p, "P0", 3)
            @pl.when(da == 3)
            def _():
                wait(p, "P1", 4)
    return begin, [st0, st1, st2, st3, st4], done

def turn(v, keep, ahead, behind):
    return v * keep + pltpu.roll(v, 120, 1) * ahead + pltpu.roll(v, 8, 1) * behind

def norm_rows(x, gain, shift):
    average = jnp.mean(x, axis=-1, keepdims=True)
    centred = x - average
    inverse = lax.rsqrt(jnp.mean(centred * centred, axis=-1, keepdims=True) + norm_eps)
    return centred * inverse * gain + shift

def rotary_tables_to(cs, tables):
    rows = cs.shape[1]
    c, s = cs[0:8, :], cs[8:16, :]
    one, nil, z8 = jnp.ones((48, rows), jnp.float32), jnp.zeros((48, rows), jnp.float32), jnp.zeros((8, rows), jnp.float32)
    tables[0][...] = jnp.concatenate([c, c, one] * 2, axis=0).T
    tables[1][...] = jnp.concatenate([-s, z8, nil] * 2, axis=0).T
    tables[2][...] = jnp.concatenate([z8, s, nil] * 2, axis=0).T

def pump(*its):
    for it in its:
        f = next(it, None)
        if f is not None:
            f()

def front_kernel(x, gain, shift, weight, bias, cs, start_ref, dy, ow,
                 rn, hw, q_ref, k_ref, v_ref, ot_ref, lse_ref, att, out_all, dy_all,
                 own, kept, vt, t0, t1, t2, ob, ox,
                 ssA, rsA, tsA, trA, ssB, rsB, lsB, ssC, rsC, ssD, rsD, tsD, trD, ssO, rsO, ssT, rsT, lsO, ls):
    sp, wp = Plane("seq"), Plane("wt")
    tok = x.shape[0]
    c, m = sp.c, sp.block(0, 0)
    A = Gather(sp, own, rn, tok, ssA, rsA, (tsA, trA), SPLIT_A)
    begin, fetch, fetch_done = fetch_steps(wp, weight, hw, ssB, rsB, lsB)
    C = Gather(wp, dy, dy_all, tok, ssC, rsC, None, SPLIT_C)
    D = Gather(wp, ow, out_all, ow.shape[0], ssD, rsD, (tsD, trD), SPLIT_D)
    begin()
    chips = [at(j // 4, j % 4, c, wp.a, wp.b) for j in range(8)]
    bar = pltpu.get_barrier_semaphore()
    for j in range(8):
        @pl.when(m != j)
        def _():
            pl.semaphore_signal(bar, inc=1, device_id=chips[j], device_id_type=MESH)
    for t in (sp.twin, wp.left, wp.right, wp.pair):
        pl.semaphore_signal(bar, inc=1, device_id=t, device_id_type=MESH)
    def ln(i, _):
        r = pl.ds(pl.multiple_of(i * 16, 16), 16)
        own[r] = norm_rows(x[r].astype(jnp.float32), gain[...], shift[...]).astype(jnp.bfloat16)
        return 0
    lax.fori_loop(0, tok // 16, ln, 0)
    copies = [pltpu.make_async_copy(own, rn.at[2 * m + c], ls.at[0]),
              pltpu.make_async_copy(dy, dy_all.at[wp.block(0, 0)], ls.at[1]),
              pltpu.make_async_copy(ow, out_all.at[2 * wp.block(0, 0) + c], ls.at[2])]
    for cp in copies:
        cp.start()
    copies[0].wait()
    pl.semaphore_wait(bar, 11)
    A.steps[0]()
    fetch[0]()
    rotary_tables_to(cs, (t0, t1, t2))
    copies[1].wait()
    copies[2].wait()
    a, b, cc, d = iter(A.steps[1:]), iter(fetch[1:]), iter(C.steps), iter(D.steps)
    pump(a, a, b, a, a, a, b, a, a, b, b, a, a, cc)
    def project(k):
        A.wait_twin(k)
        j = sp.block(*ORDER[k])
        rows = pl.ds(pl.multiple_of(j * 256, 256), 256)
        h = rn[pl.ds(2 * j, 2)].reshape(256, rn.shape[2])
        y = jnp.dot(h, hw[...], preferred_element_type=jnp.float32) + bias[...]
        tabs = (t0[rows], t1[rows], t2[rows])
        q_ref[rows] = (turn(y[:, :128], *tabs) * 0.125).astype(jnp.bfloat16)
        k_ref[rows] = turn(y[:, 128:256], *tabs).astype(jnp.bfloat16)
        v_ref[rows] = y[:, 256:].astype(jnp.bfloat16)
    project(0); pump(a); project(1); pump(a); pump(cc); project(2); pump(a); project(3)
    pump(a); project(4); pump(a, cc); project(5); pump(a, a); pump(cc); project(6); pump(a, a); project(7)
    halves(k_ref, kept)
    pump(cc, cc)
    vt[...] = v_ref[...].astype(jnp.float32).T.astype(jnp.bfloat16)
    def to_twin(j):
        return pltpu.make_async_remote_copy(src_ref=ox.at[j], dst_ref=ob.at[j, :, pl.ds(pl.multiple_of(128 * c, 128), 128)],
                                            send_sem=ssT.at[j], recv_sem=rsT.at[j], device_id=sp.twin, device_id_type=MESH)
    def from_twin(j):
        there = ob.at[j, :, pl.ds(pl.multiple_of(128 * (1 - c), 128), 128)]
        return pltpu.make_async_remote_copy(src_ref=there, dst_ref=there, send_sem=ssT.at[j], recv_sem=rsT.at[j], device_id=sp.twin, device_id_type=MESH)
    def cols(j):
        return att.at[:, pl.ds(pl.multiple_of(256 * j, 256), 256)]
    def to_chip(j):
        return pltpu.make_async_remote_copy(src_ref=ob.at[j], dst_ref=cols(m), send_sem=ssO.at[j], recv_sem=rsO.at[m], device_id=chips[j], device_id_type=MESH)
    def ship(i):
        for j in (2 * i, 2 * i + 1):
            from_twin(j).wait_recv()
            @pl.when(m == j)
            def _():
                pltpu.make_async_copy(ob.at[j], cols(j), lsO).start()
            @pl.when(m != j)
            def _():
                to_chip(j).start()
    n = q_ref.shape[0] // QB
    for i in range(n):
        q = q_ref[QB * i:QB * (i + 1)]
        start = start_ref[:, QB * i:QB * (i + 1)]
        step = functools.partial(attend_step, kept, vt, q, start, i)
        one = (jnp.full((1, QB), MASKED, jnp.float32), jnp.zeros((1, QB), jnp.float32), jnp.zeros((64, QB), jnp.float32))
        carry = (one, one)
        for j in range(i + 1):
            carry = step(j == 0 or j == i or i == n - 1, j, carry)
            pump(cc, cc, d)
        where = pl.ds(QB * i, QB)
        for h in range(2):
            top, l, acc = carry[h]
            ot_ref[64 * h:64 * h + 64, where] = acc / l
            lse_ref[h:h + 1, where] = top + jnp.log(l)
        if i:
            ship(i - 1)
        o = ot_ref[:, where].T.astype(jnp.bfloat16)
        for j in (0, 1):
            mine = pl.ds(pl.multiple_of(128 * c, 128), 128)
            first, second = o[256 * j:256 * j + 128], o[256 * j + 128:256 * j + 256]
            @pl.when(c == 0)
            def _():
                ob[2 * i + j, :, 0:128] = first
                ox[2 * i + j] = second
            @pl.when(c == 1)
            def _():
                ob[2 * i + j, :, 128:256] = second
                ox[2 * i + j] = first
            to_twin(2 * i + j).start()
    ship(n - 1)
    for f in cc:
        f()
    for f in d:
        f()
    for j in range(8):
        to_twin(j).wait_send()
        @pl.when(m == j)
        def _():
            pltpu.make_async_copy(ob.at[j], cols(j), lsO).wait()
        @pl.when(m != j)
        def _():
            to_chip(j).wait_send()
            pltpu.make_async_remote_copy(src_ref=cols(j), dst_ref=cols(j), send_sem=ssO.at[j], recv_sem=rsO.at[j], device_id=chips[j], device_id_type=MESH).wait_recv()
    A.finish(range(8))
    fetch_done()
    C.finish()
    D.finish()

def attend_step(kept, vt, q, start, i, masked, j, carry):
    r = pl.ds(j * KB, KB)
    out = []
    for h in range(2):
        m, l, acc = carry[h]
        s = lax.dot_general(kept[h, r], q, NT, preferred_element_type=jnp.float32)
        if masked:
            s = jnp.where(allowed(i, j, start), s, MASKED)
        top = jnp.maximum(m, jnp.max(s, axis=0, keepdims=True))
        p = jnp.exp(s - top)
        fade = jnp.exp(m - top)
        l = l * fade + jnp.sum(p, axis=0, keepdims=True)
        acc = acc * fade + jnp.dot(vt[64 * h:64 * h + 64, r], p.astype(jnp.bfloat16), preferred_element_type=jnp.float32)
        out.append((top, l, acc))
    return tuple(out)

def front(cid, x, gain, shift, weight, bias, cs, start, dy, ow):
    tok, width = x.shape
    rows = start.shape[1]
    f, b16, f32 = jax.ShapeDtypeStruct, jnp.bfloat16, jnp.float32
    vm = pltpu.VMEM
    return pl.pallas_call(
        front_kernel,
        out_shape=(f((16, tok, width), b16), f((width, 384), b16), f((rows, 128), b16), f((rows, 128), b16), f((rows, 128), b16),
                   f((128, rows), f32), f((8, rows), f32), f((tok, width), b16), f((16,) + ow.shape, b16), f((8, tok, width), b16)),
        in_specs=[VM, VM, VM, ANY, VM, VM, VM, VM, VM], out_specs=(VM,) * 10,
        scratch_shapes=[vm((tok, width), b16), vm((2, rows, 128), b16), vm((128, rows), b16)] + [vm((rows, 128), f32)] * 3
        + [vm((8, 128, 256), b16), vm((8, 128, 128), b16)]
        + [dma(n) for n in (18, 18, 8, 8, 18, 18, 3, 18, 18, 18, 18, 8, 8, 8, 8, 8, 8)] + [pltpu.SemaphoreType.DMA, dma(3)],
        compiler_params=params(cid), name="front",
    )(x, gain, shift, weight, bias, cs, start, dy, ow)
TN = (((0,), (0,)), ((), ()))

def middle_kernel(att, x, out_all, gain, shift, dy_all, wgu, wd,
                  mid, dh2, ffp, joined,
                  own, h2, wbuf, dga, tr, dh2p, land, ssG, rsG, ssS, rsS, lsw, ls):
    wp = Plane("wt")
    tok, width = mid.shape
    hidden = wd.shape[0]
    for t in (wp.left, wp.right, wp.pair):
        pl.semaphore_signal(pltpu.get_barrier_semaphore(), inc=1, device_id=t, device_id_type=MESH)
    def load(w, slot):
        return pltpu.make_async_copy(out_all.at[pl.ds(2 * w, 2)], wbuf.at[slot], lsw.at[slot])
    load(0, 0).start()
    def project(w):
        slot = w % 2
        load(w, slot).wait()
        if w < 7:
            load(w + 1, 1 - slot).start()
        cols = pl.ds(256 * w, 256)
        y = jnp.dot(att[:, :width // 2], wbuf[slot, 0], preferred_element_type=jnp.float32)
        y += jnp.dot(att[:, width // 2:], wbuf[slot, 1], preferred_element_type=jnp.float32)
        mid[:, cols] = x[:, cols].astype(jnp.float32) + y
    for w in range(8):
        project(w)
    def ln(i, _):
        r = pl.ds(pl.multiple_of(i * 16, 16), 16)
        own[r] = norm_rows(mid[r], gain[...], shift[...]).astype(jnp.bfloat16)
        return 0
    lax.fori_loop(0, tok // 16, ln, 0)
    cp = pltpu.make_async_copy(own, h2.at[wp.block(0, 0)], ls)
    cp.start()
    pl.semaphore_wait(pltpu.get_barrier_semaphore(), 3)
    G = Gather(wp, own, h2, tok, ssG, rsG)
    part = hidden // 2
    def chunk_up(da):
        a = lax.rem(wp.a + da + 4, 4)
        cols = pl.ds(pl.multiple_of(256 * a, 256), 256)
        hc = h2[pl.ds(2 * a, 2)].reshape(2 * tok, width)
        dc = dy_all[pl.ds(2 * a, 2)].reshape(2 * tok, width)
        def tile(i, _):
            r = pl.ds(pl.multiple_of(i * part, 16), part)
            r2 = pl.ds(pl.multiple_of(hidden + i * part, 16), part)
            r3 = pl.ds(pl.multiple_of(2 * hidden + i * part, 16), part)
            g = lax.dot_general(wgu[r], hc, NT, preferred_element_type=jnp.float32)
            u = lax.dot_general(wgu[r2], hc, NT, preferred_element_type=jnp.float32)
            e = lax.dot_general(wd[r], dc, NT, preferred_element_type=jnp.float32)
            sigma = 1.0 / (1.0 + jnp.exp(-g))
            gs = g * sigma
            dga[r, cols] = (e * u * sigma * (1.0 + g * (1.0 - sigma))).astype(jnp.bfloat16)
            dga[r2, cols] = (e * gs).astype(jnp.bfloat16)
            dga[r3, cols] = (gs * u).astype(jnp.bfloat16)
            return 0
        lax.fori_loop(0, 2, tile, 0)
    def chunk_down(da):
        a = lax.rem(wp.a + da + 4, 4)
        cols = pl.ds(pl.multiple_of(256 * a, 256), 256)
        def flip(i, _):
            r = pl.ds(pl.multiple_of(i * 128, 128), 128)
            tr[:, r] = dga[r, cols].astype(jnp.float32).T.astype(jnp.bfloat16)
            return 0
        lax.fori_loop(0, 3 * hidden // 128, flip, 0)
        last = 3 * hidden // 128 * 128
        tr[:, last:] = dga[last:, cols].astype(jnp.float32).T.astype(jnp.bfloat16)
        def tile(i, _):
            n = pl.ds(pl.multiple_of(i * 512, 512), 512)
            y = jnp.dot(tr[:, :2 * hidden], wgu[:, n], preferred_element_type=jnp.float32)
            dh2p[pl.ds(2 * a, 2), :, n] = y.astype(jnp.bfloat16).reshape(2, tok, 512)
            y = jnp.dot(tr[:, 2 * hidden:], wd[:, n], preferred_element_type=jnp.float32)
            ffp[pl.ds(2 * a, 2), :, n] = y.astype(jnp.bfloat16).reshape(2, tok, 512)
            return 0
        lax.fori_loop(0, width // 512, tile, 0)
    S = G.steps
    S[0]()
    cp.wait()
    for f in S[1:6]:
        f()
    S[10]()
    chunk_up(0)
    S[6](); S[7]()
    chunk_down(0)
    S[8](); S[9](); S[11](); S[12]()
    chunk_up(-1)
    chunk_down(-1)
    chunk_up(1)
    chunk_down(1)
    for f in S[13:]:
        f()
    chunk_up(2)
    chunk_down(2)
    G.finish()
    R, done = sum_steps(wp, dh2p, land, tok, ssS, rsS, dh2)
    def weights(lo, hi):
        def one(j, _):
            f = pl.ds(pl.multiple_of(256 * j, 256), 256)
            for k, other in ((0, h2), (1, h2), (2, dy_all)):
                r = pl.ds(hidden * k, hidden)
                y = jnp.dot(dga[r], other[:, :, f].reshape(8 * tok, 256), preferred_element_type=jnp.float32).astype(jnp.bfloat16)
                joined[2 * j, r] = y[:, :128]
                joined[2 * j + 1, r] = y[:, 128:]
            return 0
        lax.fori_loop(lo, hi, one, 0)
    R[0]()
    weights(0, 2); R[1](); R[2](); weights(2, 3); R[3](); weights(3, 4); R[4](); weights(4, 6); R[5](); weights(6, 8); R[6]()
    done()

def middle_part(cid, att, x, out_all, gain, shift, dy_all, wgu, wd):
    tok, width = x.shape
    hidden = wd.shape[0]
    f, b16, f32, vm = jax.ShapeDtypeStruct, jnp.bfloat16, jnp.float32, pltpu.VMEM
    return pl.pallas_call(
        middle_kernel,
        out_shape=(f((tok, width), f32), f((tok, width), f32), f((8, tok, width), b16), f((16, 3 * hidden, 128), b16)),
        in_specs=[VM, VM, ANY, VM, VM, VM, VM, VM], out_specs=(VM,) * 4,
        scratch_shapes=[vm((tok, width), b16), vm((8, tok, width), b16), vm((2, 2) + out_all.shape[1:], b16), vm((3 * hidden, 8 * tok), b16),
                        vm((2 * tok, 3 * hidden), b16), vm((8, tok, width), b16), vm((7 * tok, width), b16)]
        + [dma(n) for n in (18, 18, 17, 17, 2)] + [pltpu.SemaphoreType.DMA],
        compiler_params=params(cid), name="middle",
    )(att, x, out_all, gain, shift, dy_all, wgu, wd)
class ScatterBoth:
    def __init__(self, pn, buf, tland, land, ss, rs, ts, tr, out, split=None):
        self.pn, self.tland, self.ts, self.tr = pn, tland, ts, tr
        rows, cols = buf.shape[1:]
        order = [(2, 0), (2, 1), (-1, 1), (1, 1), (-1, 0), (1, 0), (0, 1), (0, 0)]
        def send(k):
            j = pn.block(*order[k])
            remote(buf.at[2 * j + 1 - pn.c], tland.at[k], ts, tr, k, pn.twin).start()
        def add(k):
            self.copy(k).wait_recv()
            j = 2 * pn.block(*order[k]) + pn.c
            step = pace(rows, cols)
            def body(i, _):
                r = pl.ds(pl.multiple_of(i * step, 16), step)
                buf[j, r] = (buf[j, r].astype(jnp.float32) + tland[k, r].astype(jnp.float32)).astype(buf.dtype)
                return 0
            repeat(rows // step, body)
        self.sends = [functools.partial(send, k) for k in range(8)]
        self.adds = [functools.partial(add, k) for k in range(8)]
        self.sums, self.done = sum_steps(pn, buf, land, rows, ss, rs, out, lambda j: 2 * j + pn.c, split)

    def copy(self, k):
        return remote(self.tland.at[k], self.tland.at[k], self.ts, self.tr, k, self.pn.twin)

    def finish(self):
        self.done()
        for k in range(8):
            self.copy(k).wait_send()

SPLIT_F, SPLIT_J = 96, 1568

def back_kernel(dh2, mid, dy, gain, out_all, q_ref, k_ref, v_ref, start_ref, ot_ref, lse_ref, cs, ffp, joined,
                mgrad, da, dproj, bias, sums, layer_out, grads,
                wbuf, dg, inbox, do_ref, keptk, keptv, keptq, keptd, kt, dot_, dq_ref, dk_ref, dv_ref, t0, t1, t2, fbuf, fland, fsum, jbuf, tland, jland,
                ssO, rsO, ssT, rsT, ssF, rsF, ssJ, rsJ, tsJ, trJ, lsw, ls):
    sp, wp = Plane("seq"), Plane("wt")
    tok, width = dh2.shape
    c, m = sp.c, sp.block(0, 0)
    chips = [at(j // 4, j % 4, c, wp.a, wp.b) for j in range(8)]
    bar = pltpu.get_barrier_semaphore()
    for j in range(8):
        @pl.when(m != j)
        def _():
            pl.semaphore_signal(bar, inc=1, device_id=chips[j], device_id_type=MESH)
    for t in (sp.twin, wp.left, wp.right, wp.pair):
        pl.semaphore_signal(bar, inc=1, device_id=t, device_id_type=MESH)
    def load(w, slot):
        return pltpu.make_async_copy(out_all.at[pl.ds(2 * w, 2)], wbuf.at[slot], lsw.at[slot])
    load(0, 0).start()
    here = [pltpu.make_async_copy(ffp, fbuf, ls.at[0]), pltpu.make_async_copy(joined, jbuf, ls.at[1])]
    for cp in here:
        cp.start()
    def ln(i, carry):
        r = pl.ds(pl.multiple_of(i * 32, 32), 32)
        y = mid[r]
        centred = y - jnp.mean(y, axis=-1, keepdims=True)
        inverse = lax.rsqrt(jnp.mean(centred * centred, axis=-1, keepdims=True) + norm_eps)
        scaled = centred * inverse
        up = dh2[r]
        w = up * gain[...]
        back = inverse * (w - jnp.mean(w, axis=-1, keepdims=True) - scaled * jnp.mean(w * scaled, axis=-1, keepdims=True))
        g = dy[r].astype(jnp.float32) + back
        mgrad[r] = g
        da[r] = g.astype(jnp.bfloat16)
        return carry[0] + jnp.sum((up * scaled).reshape(4, 8, width), axis=0), carry[1] + jnp.sum(up.reshape(4, 8, width), axis=0)
    nil = jnp.zeros((8, width), jnp.float32)
    gsum, ssum = lax.fori_loop(0, tok // 32, ln, (nil, nil))
    sums[0:1] = jnp.sum(gsum, axis=0, keepdims=True)
    sums[1:2] = jnp.sum(ssum, axis=0, keepdims=True)
    total = [jnp.zeros((tok, width // 2), jnp.float32)] * 2
    for w in range(8):
        load(w, w % 2).wait()
        if w < 7:
            load(w + 1, 1 - w % 2).start()
        g = da[:, 256 * w:256 * w + 256]
        both = wbuf[w % 2]
        total = [total[h] + lax.dot_general(g, both[h], NT, preferred_element_type=jnp.float32) for h in range(2)]
    dg[...] = jnp.concatenate(total, axis=1).astype(jnp.bfloat16)
    pl.semaphore_wait(bar, 11)
    def to_chip(j):
        return pltpu.make_async_remote_copy(src_ref=dg.at[:, pl.ds(256 * j, 256)], dst_ref=inbox.at[m], send_sem=ssO.at[j], recv_sem=rsO.at[m], device_id=chips[j], device_id_type=MESH)
    for j in range(8):
        @pl.when(m != j)
        def _():
            to_chip(j).start()
    mine = pltpu.make_async_copy(dg.at[:, pl.ds(pl.multiple_of(256 * m, 256), 256)], inbox.at[m], ls.at[2])
    mine.start()
    for cp in here:
        cp.wait()
    F, fdone = sum_steps(wp, fbuf, fland, tok, ssF, rsF, fsum, split=SPLIT_F)
    J = ScatterBoth(sp, jbuf, tland, jland, ssJ, rsJ, tsJ, trJ, grads, SPLIT_J)
    for f in J.sends:
        f()
    F[0]()
    rotary_tables_to(cs, (t0, t1, t2))
    halves(k_ref, keptk)
    halves(v_ref, keptv)
    halves(q_ref, keptq)
    kt[...] = k_ref[...].astype(jnp.float32).T.astype(jnp.bfloat16)
    dk_ref[...] = jnp.zeros_like(dk_ref)
    dv_ref[...] = jnp.zeros_like(dv_ref)
    mine.wait()
    def pass_on(j, own):
        r = do_ref.at[pl.ds(pl.multiple_of(128 * (2 * j + (c if own else 1 - c)), 128), 128)]
        src = inbox.at[j, :, pl.ds(pl.multiple_of(128 * (1 - c), 128), 128)] if own else r
        return pltpu.make_async_remote_copy(src_ref=src, dst_ref=r, send_sem=ssT.at[j], recv_sem=rsT.at[j], device_id=sp.twin, device_id_type=MESH)
    for j in range(8):
        @pl.when(m != j)
        def _():
            pltpu.make_async_remote_copy(src_ref=inbox.at[j], dst_ref=inbox.at[j], send_sem=ssO.at[j], recv_sem=rsO.at[j], device_id=chips[j], device_id_type=MESH).wait_recv()
        pass_on(j, True).start()
        @pl.when(c == 0)
        def _():
            do_ref[256 * j:256 * j + 128] = inbox[j, :, 0:128]
        @pl.when(c == 1)
        def _():
            do_ref[256 * j + 128:256 * j + 256] = inbox[j, :, 128:256]
    for j in range(8):
        pass_on(j, False).wait_recv()
    halves(do_ref, keptd)
    dot_[...] = do_ref[...].astype(jnp.float32).T
    fi, ji = iter(F[1:]), iter(J.adds + J.sums)
    n = q_ref.shape[0] // QB
    for i in range(n):
        rows = pl.ds(QB * i, QB)
        q = q_ref[rows]
        do = do_ref[rows]
        do_h, q_h = keptd[:, rows], keptq[:, rows]
        start = start_ref[:, rows]
        both = ot_ref[:, rows] * dot_[:, rows]
        inner = [jnp.sum(both[64 * h:64 * h + 64], axis=0, keepdims=True) for h in range(2)]
        lse2 = lse_ref[:, rows]
        lse = [lse2[h:h + 1] for h in range(2)]
        def step(masked, j, carry):
            r = pl.ds(j * KB, KB)
            out, ps, ds = [], [], []
            kk, vv, kk_t = keptk[:, r], keptv[:, r], kt[:, r]
            for h in range(2):
                s = lax.dot_general(kk[h], q, NT, preferred_element_type=jnp.float32)
                if masked:
                    s = jnp.where(allowed(i, j, start), s, MASKED)
                p = jnp.exp(s - lse[h])
                dp = lax.dot_general(vv[h], do, NT, preferred_element_type=jnp.float32)
                g = (p * (dp - inner[h])).astype(jnp.bfloat16)
                out.append(carry[h] + jnp.dot(kk_t[64 * h:64 * h + 64], g, preferred_element_type=jnp.float32))
                ps.append(p.astype(jnp.bfloat16))
                ds.append(g)
            dv_ref[r] += sum(jnp.dot(ps[h], do_h[h], preferred_element_type=jnp.float32) for h in range(2))
            dk_ref[r] += sum(jnp.dot(ds[h], q_h[h], preferred_element_type=jnp.float32) for h in range(2))
            return tuple(out)
        carry = (jnp.zeros((64, QB), jnp.float32),) * 2
        for j in range(i + 1):
            carry = step(j == 0 or j == i or i == n - 1, j, carry)
            pump(ji, ji, fi)
        dq_ref[rows] = jnp.concatenate(carry, axis=0).T
    def low(v):
        return v.astype(jnp.bfloat16).astype(jnp.float32)
    def unturn(i, total):
        rows = pl.ds(pl.multiple_of(i * 512, 512), 512)
        keep, ahead, behind = t0[rows], -t1[rows], -t2[rows]
        parts = (turn(low(dq_ref[rows]) * 0.125, keep, ahead, behind), turn(low(dk_ref[rows]), keep, ahead, behind), dv_ref[rows])
        new = []
        for p in range(3):
            y = parts[p].astype(jnp.bfloat16)
            dproj[rows, 128 * p:128 * p + 128] = y
            new.append(total[p] + jnp.sum(y.astype(jnp.float32).reshape(64, 8, 128), axis=0))
        return tuple(new)
    total = lax.fori_loop(0, dq_ref.shape[0] // 512, unturn, (jnp.zeros((8, 128), jnp.float32),) * 3)
    for p in range(3):
        bias[:, 128 * p:128 * p + 128] = jnp.sum(total[p], axis=0, keepdims=True)
    for f in fi:
        f()
    layer_out[...] = (mid[...] + fsum[...]).astype(jnp.bfloat16)
    for f in ji:
        f()
    fdone()
    J.finish()
    for j in range(8):
        @pl.when(m != j)
        def _():
            to_chip(j).wait_send()
        pass_on(j, True).wait_send()

def back_part(cid, dh2, mid, dy, gain, out_all, q, k, v, start, ot, lse, cs, ffp, joined):
    tok, width = dy.shape
    rows = q.shape[0]
    f, b16, f32, vm = jax.ShapeDtypeStruct, jnp.bfloat16, jnp.float32, pltpu.VMEM
    wide = joined.shape[1]
    return pl.pallas_call(
        back_kernel,
        out_shape=(f((tok, width), f32), f((tok, width), b16), f((rows, 384), b16), f((1, 384), f32), f((2, width), f32), f((tok, width), b16), f((wide, 128), f32)),
        in_specs=[VM, VM, VM, VM, ANY, VM, VM, VM, VM, VM, VM, VM, ANY, ANY], out_specs=(VM,) * 7,
        scratch_shapes=[vm((2, 2) + out_all.shape[1:], b16), vm((tok, width), b16), vm((8, tok, 256), b16), vm((rows, 128), b16)]
        + [vm((2, rows, 128), b16)] * 4 + [vm((128, rows), b16), vm((128, rows), f32)] + [vm((rows, 128), f32)] * 6
        + [vm((8, tok, width), b16), vm((7 * tok, width), b16), vm((tok, width), f32)]
        + [vm((16, wide, 128), b16), vm((8, wide, 128), b16), vm((7 * wide, 128), b16)]
        + [dma(n) for n in (8, 8, 8, 8, 17, 17, 17, 17, 8, 8, 2, 3)],
        compiler_params=params(cid), name="back",
    )(dh2, mid, dy, gain, out_all, q, k, v, start, ot, lse, cs, ffp, joined)
def params(cid):
    return pltpu.CompilerParams(collective_id=cid, has_side_effects=True, vmem_limit_bytes=56 * 2**20)

def dma(n):
    return pltpu.SemaphoreType.DMA((n,))

def gather_kernel(axis, x, o, ss, rs, ls):
    pn = Plane(axis)
    greet([pn.left, pn.right, pn.pair])
    cp = pltpu.make_async_copy(x, o.at[pn.block(0, 0)], ls)
    cp.start()
    steps, tail, done = gather_steps(pn, x, o, x.shape[0], ss, rs)
    for f in steps + tail:
        f()
    done()
    cp.wait()

def gather(axis, cid, x):
    return pl.pallas_call(
        functools.partial(gather_kernel, axis), out_shape=jax.ShapeDtypeStruct((8,) + x.shape, x.dtype),
        in_specs=[VM], out_specs=VM, scratch_shapes=[dma(18), dma(18), pltpu.SemaphoreType.DMA],
        compiler_params=params(cid), name="gather_" + axis)(x)

def gather_both_kernel(axis, x, o, ss, rs, ls, ts, tr):
    pn = Plane(axis)
    greet([pn.left, pn.right, pn.pair, pn.twin])
    index = lambda j: 2 * j + pn.c
    mine = index(pn.block(0, 0))
    cp = pltpu.make_async_copy(x, o.at[mine], ls)
    cp.start()
    cp.wait()
    steps, tail, done = gather_steps(pn, x, o, x.shape[0], ss, rs, index)
    order = [(0, 0), (0, 1), (-1, 1), (1, 1), (-1, 0), (1, 0), (2, 0), (2, 1)]
    def hand(k):
        j = index(pn.block(*order[k]))
        remote(o.at[j], o.at[j], ts, tr, k, pn.twin).start()
    steps[0]()
    hand(0)
    for f in steps[1:]:
        f()
    ready = {0: [1], 1: [2], 2: [3], 3: [4], 4: [5], 6: [6], 8: [7]}
    for i, f in enumerate(tail):
        f()
        for k in ready.get(i, []):
            hand(k)
    done()
    for k in range(8):
        j = 2 * pn.block(*order[k]) + 1 - pn.c
        remote(o.at[j], o.at[j], ts, tr, k, pn.twin).wait()

def gather_both(axis, cid, x):
    return pl.pallas_call(
        functools.partial(gather_both_kernel, axis), out_shape=jax.ShapeDtypeStruct((16,) + x.shape, x.dtype),
        in_specs=[VM], out_specs=VM, scratch_shapes=[dma(18), dma(18), pltpu.SemaphoreType.DMA, dma(8), dma(8)],
        compiler_params=params(cid), name="gather_both_" + axis)(x)

def scatter_kernel(axis, x, o, buf, land, ss, rs, ls):
    pn = Plane(axis)
    cp = pltpu.make_async_copy(x, buf, ls)
    cp.start()
    greet([pn.left, pn.right, pn.pair])
    cp.wait()
    steps, done = sum_steps(pn, buf, land, x.shape[1], ss, rs, o)
    for f in steps:
        f()
    done()

def scatter(axis, cid, x):
    _, rows, cols = x.shape
    return pl.pallas_call(
        functools.partial(scatter_kernel, axis), out_shape=jax.ShapeDtypeStruct((rows, cols), jnp.float32),
        in_specs=[ANY], out_specs=VM,
        scratch_shapes=[pltpu.VMEM(x.shape, x.dtype), pltpu.VMEM((7 * rows, cols), x.dtype), dma(17), dma(17), pltpu.SemaphoreType.DMA],
        compiler_params=params(cid), name="scatter_" + axis)(x)

def scatter_both_kernel(axis, x, o, buf, tland, land, ss, rs, ls, ts, tr):
    pn = Plane(axis)
    rows = x.shape[1]
    cp = pltpu.make_async_copy(x, buf, ls)
    cp.start()
    greet([pn.left, pn.right, pn.pair, pn.twin])
    cp.wait()
    order = [(2, 0), (2, 1), (-1, 1), (1, 1), (-1, 0), (1, 0), (0, 1), (0, 0)]
    for k in range(8):
        j = pn.block(*order[k])
        remote(buf.at[2 * j + 1 - pn.c], tland.at[k], ts, tr, k, pn.twin).start()
    for k in range(8):
        j = 2 * pn.block(*order[k]) + pn.c
        remote(tland.at[k], tland.at[k], ts, tr, k, pn.twin).wait_recv()
        step = pace(rows, x.shape[2])
        def body(i, _):
            r = pl.ds(pl.multiple_of(i * step, 16), step)
            buf[j, r] = (buf[j, r].astype(jnp.float32) + tland[k, r].astype(jnp.float32)).astype(buf.dtype)
            return 0
        repeat(rows // step, body)
    steps, done = sum_steps(pn, buf, land, rows, ss, rs, o, lambda j: 2 * j + pn.c)
    for f in steps:
        f()
    done()
    for k in range(8):
        remote(tland.at[k], tland.at[k], ts, tr, k, pn.twin).wait_send()

def scatter_both(axis, cid, x):
    _, rows, cols = x.shape
    return pl.pallas_call(
        functools.partial(scatter_both_kernel, axis), out_shape=jax.ShapeDtypeStruct((rows, cols), jnp.float32),
        in_specs=[ANY], out_specs=VM,
        scratch_shapes=[pltpu.VMEM(x.shape, x.dtype), pltpu.VMEM((8, rows, cols), x.dtype), pltpu.VMEM((7 * rows, cols), x.dtype),
                        dma(17), dma(17), pltpu.SemaphoreType.DMA, dma(8), dma(8)],
        compiler_params=params(cid), name="scatter_both_" + axis)(x)

def swap_kernel(axis, n, x, o, ss, rs, ls):
    me = lax.axis_index(axis)
    peers = [lax.rem(me + d, n) for d in range(1, n)]
    bar = pltpu.get_barrier_semaphore()
    for p in peers:
        pl.semaphore_signal(bar, inc=1, device_id={axis: p}, device_id_type=MESH)
    cp = pltpu.make_async_copy(x.at[me], o.at[me], ls)
    cp.start()
    pl.semaphore_wait(bar, n - 1)
    def copy(d):
        return remote(x.at[lax.rem(me + d, n)], o.at[me], ss, rs, d - 1, {axis: lax.rem(me + d, n)})
    for d in range(1, n):
        copy(d).start()
    for d in range(1, n):
        j = lax.rem(me - d + n, n)
        remote(x.at[j], o.at[j], ss, rs, d - 1, {axis: j}).wait()
    cp.wait()

def swap(axis, n, cid, x):
    return pl.pallas_call(
        functools.partial(swap_kernel, axis, n), out_shape=jax.ShapeDtypeStruct(x.shape, x.dtype),
        in_specs=[VM], out_specs=VM, scratch_shapes=[dma(n - 1), dma(n - 1), pltpu.SemaphoreType.DMA],
        compiler_params=params(cid), name="swap_" + axis)(x)

def fetch_kernel(x, o, ss, rs, ls):
    s, w = lax.axis_index("seq"), lax.axis_index("wt")
    bar = pltpu.get_barrier_semaphore()
    for d in range(1, 8):
        pl.semaphore_signal(bar, inc=1, device_id={"wt": lax.rem(w + d, 8)}, device_id_type=MESH)
    pl.semaphore_wait(bar, 7)
    for p in range(3):
        g = 16 * p + s
        @pl.when(w == g // 6)
        def _():
            src = x.at[lax.rem(g, 6)]
            cp = pltpu.make_async_copy(src, o.at[p], ls)
            cp.start()
            for d in range(1, 8):
                remote(src, o.at[p], ss.at[p], rs, p, {"wt": lax.rem(w + d, 8)}).start() if False else pltpu.make_async_remote_copy(src_ref=src, dst_ref=o.at[p], send_sem=ss.at[p, d - 1], recv_sem=rs.at[p], device_id={"wt": lax.rem(w + d, 8)}, device_id_type=MESH).start()
            cp.wait()
    for p in range(3):
        g = 16 * p + s
        @pl.when(w == g // 6)
        def _():
            for d in range(1, 8):
                pltpu.make_async_remote_copy(src_ref=o.at[p], dst_ref=o.at[p], send_sem=ss.at[p, d - 1], recv_sem=rs.at[p], device_id={"wt": lax.rem(w + d, 8)}, device_id_type=MESH).wait_send()
        @pl.when(w != g // 6)
        def _():
            pltpu.make_async_remote_copy(src_ref=o.at[p], dst_ref=o.at[p], send_sem=ss.at[p, 0], recv_sem=rs.at[p], device_id={"wt": lax.rem(w + 1, 8)}, device_id_type=MESH).wait_recv()

def fetch(cid, x):
    return pl.pallas_call(
        fetch_kernel, out_shape=jax.ShapeDtypeStruct((3,) + x.shape[1:], x.dtype),
        in_specs=[VM], out_specs=VM, scratch_shapes=[pltpu.SemaphoreType.DMA((3, 7)), dma(3), pltpu.SemaphoreType.DMA],
        compiler_params=params(cid), name="fetch_heads")(x)

def place_kernel(x, o, ss, rs, ls):
    s, w = lax.axis_index("seq"), lax.axis_index("wt")
    bar = pltpu.get_barrier_semaphore()
    def source(b):
        g = 6 * w + b
        return lax.rem(g, 16), s // 2
    def target(i, p):
        g = 16 * p + s
        return 2 * w + i, g // 6, lax.rem(g, 6)
    own = jnp.int32(0)
    for b in range(6):
        ts, tw = source(b)
        same = (ts == s) & (tw == w)
        own += same.astype(jnp.int32)
        @pl.when(jnp.logical_not(same))
        def _():
            pl.semaphore_signal(bar, inc=1, device_id={"seq": ts, "wt": tw}, device_id_type=MESH)
    pl.semaphore_wait(bar, 6 - own)
    def copy(i, p):
        ts, tw, slot = target(i, p)
        return pltpu.make_async_remote_copy(src_ref=x.at[i, p], dst_ref=o.at[slot], send_sem=ss.at[i, p], recv_sem=rs.at[slot], device_id={"seq": ts, "wt": tw}, device_id_type=MESH)
    def local(i, p):
        return pltpu.make_async_copy(x.at[i, p], o.at[target(i, p)[2]], ls.at[i, p])
    for i in range(2):
        for p in range(3):
            ts, tw, _ = target(i, p)
            same = (ts == s) & (tw == w)
            @pl.when(same)
            def _():
                local(i, p).start()
            @pl.when(jnp.logical_not(same))
            def _():
                copy(i, p).start()
    for i in range(2):
        for p in range(3):
            ts, tw, _ = target(i, p)
            same = (ts == s) & (tw == w)
            @pl.when(same)
            def _():
                local(i, p).wait()
            @pl.when(jnp.logical_not(same))
            def _():
                copy(i, p).wait_send()
    for b in range(6):
        ts, tw = source(b)
        @pl.when(jnp.logical_not((ts == s) & (tw == w)))
        def _():
            pltpu.make_async_remote_copy(src_ref=o.at[b], dst_ref=o.at[b], send_sem=ss.at[0, 0], recv_sem=rs.at[b], device_id={"seq": ts, "wt": tw}, device_id_type=MESH).wait_recv()

def place(cid, x):
    return pl.pallas_call(
        place_kernel, out_shape=jax.ShapeDtypeStruct((6, 128, 128), x.dtype),
        in_specs=[VM], out_specs=VM, scratch_shapes=[pltpu.SemaphoreType.DMA((2, 3)), dma(6), pltpu.SemaphoreType.DMA((2, 3))],
        compiler_params=params(cid), name="place_qkv")(x)

def small_kernel(x, o, land, mid, land2, ss, rs, ss2, rs2):
    s, w = lax.axis_index("seq"), lax.axis_index("wt")
    bar = pltpu.get_barrier_semaphore()
    for d in range(1, 8):
        pl.semaphore_signal(bar, inc=1, device_id={"wt": lax.rem(w + d, 8)}, device_id_type=MESH)
    for d in range(1, 16):
        pl.semaphore_signal(bar, inc=1, device_id={"seq": lax.rem(s + d, 16)}, device_id_type=MESH)
    pl.semaphore_wait(bar, 22)
    for d in range(1, 8):
        remote(x.at[lax.rem(w + d, 8)], land.at[d - 1], ss, rs, d - 1, {"wt": lax.rem(w + d, 8)}).start()
    for d in range(1, 8):
        remote(x.at[0], land.at[d - 1], ss, rs, d - 1, {"wt": lax.rem(w + d, 8)}).wait()
    mid[:, 0] = x[w] + jnp.sum(land[...], axis=0)
    for d in range(1, 16):
        remote(mid.at[lax.rem(s + d, 16)], land2.at[d - 1], ss2, rs2, d - 1, {"seq": lax.rem(s + d, 16)}).start()
    for d in range(1, 16):
        remote(mid.at[0], land2.at[d - 1], ss2, rs2, d - 1, {"seq": lax.rem(s + d, 16)}).wait()
    o[...] = mid[s] + jnp.sum(land2[...], axis=0)

def small_sum(cid, x):
    f = jnp.float32
    return pl.pallas_call(
        small_kernel, out_shape=jax.ShapeDtypeStruct((1, 128), f),
        in_specs=[VM], out_specs=VM,
        scratch_shapes=[pltpu.VMEM((7, 16, 128), f), pltpu.VMEM((16, 1, 128), f), pltpu.VMEM((15, 1, 128), f), dma(7), dma(7), dma(15), dma(15)],
        compiler_params=params(cid), name="small_sum")(x)


norm_eps = 1e-05
theta_base = 10000.0
ROT = 16
HEAD_DIM = 64


def layer_norm_parts(values, gain, shift):
    average = jnp.mean(values, axis=-1, keepdims=True)
    centred = values - average
    spread = jnp.mean(centred * centred, axis=-1, keepdims=True)
    inverse = lax.rsqrt(spread + norm_eps)
    scaled = centred * inverse
    return (scaled * gain + shift, scaled, inverse)


def layer_norm_back(upward, scaled, inverse, gain):
    weighted = upward * gain
    first_mean = jnp.mean(weighted, axis=-1, keepdims=True)
    second_mean = jnp.mean(weighted * scaled, axis=-1, keepdims=True)
    return inverse * (weighted - first_mean - scaled * second_mean)


def rotary_angles(segment_row):
    rows = segment_row.shape[0]
    ends = [jnp.sum((segment_row < i).astype(jnp.int32)) for i in (1, 2)]
    start = jnp.where(segment_row == 0, 0, jnp.where(segment_row == 1, ends[0], ends[1]))
    offsets = (jnp.arange(rows, dtype=jnp.int32) - start).astype(jnp.float32)
    inv_freq = jnp.exp(jnp.arange(ROT // 2, dtype=jnp.float32) * (-2.0 * math.log(theta_base) / ROT))
    angles = inv_freq[:, None] * offsets[None, :]
    return start.reshape(1, rows), jnp.concatenate([jnp.cos(angles), jnp.sin(angles)], axis=0)


def contract_first(left, right):
    return lax.dot_general(left, right, (((0,), (0,)), ((), ())), preferred_element_type=jnp.float32)


def contract_last(left, right):
    return lax.dot_general(left, right, (((1,), (1,)), ((), ())), preferred_element_type=jnp.float32)


def per_device(layer_in, segment_ids, norm_one_gain, norm_one_shift, qkv_weight, qkv_bias, out_weight, norm_two_gain,
               norm_two_shift, gate_up_weight, down_weight, layer_grad):
    f32, bf16 = jnp.float32, jnp.bfloat16
    s, w = lax.axis_index("seq"), lax.axis_index("wt")
    tok, width = layer_in.shape[1:]
    rows = segment_ids.shape[1]
    hidden = down_weight.shape[0]
    scale = 1.0 / math.sqrt(HEAD_DIM)
    inputs = layer_in.reshape(tok, width).astype(f32)
    upstream = layer_grad.reshape(tok, width)
    start, cs = rotary_angles(segment_ids.reshape(rows))
    _, scaled_one, inverse_one = layer_norm_parts(inputs, norm_one_gain, norm_one_shift)
    bias = lax.dynamic_index_in_dim(qkv_bias.reshape(3, 16, 128), s, 1, keepdims=False).reshape(1, 384)
    half = lax.dynamic_slice_in_dim(out_weight, (s % 2) * (width // 2), width // 2, 0)
    row_normed, head_weight, q, k, v, ot, lse, attended, out_all, all_up = front(
        0, layer_in.reshape(tok, width), norm_one_gain.reshape(1, width), norm_one_shift.reshape(1, width), qkv_weight, bias, cs, start, upstream, half)
    row_normed = row_normed.reshape(rows, width)
    out_all = out_all.reshape(8, 2, width // 2, 256)
    middle, dh2, ffn_part, joined = middle_part(
        4, attended, layer_in.reshape(tok, width), out_all.reshape(16, width // 2, 256), norm_two_gain.reshape(1, width),
        norm_two_shift.reshape(1, width), all_up, gate_up_weight.transpose(1, 2, 0).reshape(2 * hidden, width), down_weight)
    middle_grad, da, dproj, bias_sum, sums_two, layer_out, joined = back_part(
        6, dh2, middle, upstream, norm_two_gain.reshape(1, width), out_all.reshape(16, width // 2, 256), q, k, v, start, ot, lse, cs, ffn_part, joined)
    layer_out = layer_out.reshape(1, tok, width)
    gain_two, shift_two = sums_two[0], sums_two[1]
    dh1_part = contract_last(dproj, head_weight).astype(bf16)
    dh1 = scatter_both("seq", 9, dh1_part.reshape(16, tok, width))
    gain_one = jnp.sum(dh1 * scaled_one, axis=0)
    shift_one = jnp.sum(dh1, axis=0)
    dx = middle_grad + layer_norm_back(dh1, scaled_one, inverse_one, norm_one_gain)
    input_grad = dx.astype(bf16).reshape(1, tok, width)
    qkv_part = contract_first(row_normed, dproj).astype(bf16)
    qkv_rows = scatter("wt", 10, qkv_part.reshape(8, 256, 384)).astype(bf16)
    qkv_grad = place(11, qkv_rows.reshape(2, 128, 3, 128).transpose(0, 2, 1, 3))
    qkv_grad = qkv_grad.transpose(1, 0, 2).reshape(128, 768).astype(f32)
    all_att = gather("wt", 12, attended).reshape(8 * tok, width)
    da_cols = swap("wt", 8, 13, da.reshape(tok, 8, 256).transpose(1, 0, 2)).reshape(8 * tok, 256)
    out_part = contract_first(all_att, da_cols).astype(bf16)
    out_grad = scatter_both("seq", 16, out_part.reshape(16, 128, 256))
    gate_grad = joined[:2 * hidden].reshape(2, hidden, 128).transpose(2, 0, 1)
    down_grad = joined[2 * hidden:]
    bias_grad = lax.dynamic_update_slice(jnp.zeros((3, 16, 128), f32), bias_sum.reshape(3, 1, 128), (0, s, 0))
    blocks = [t.reshape(16, 8, -1) for t in (gain_one, shift_one, bias_grad, gain_two, shift_two, jnp.zeros((16 * 8 * 16,), f32))]
    small = small_sum(15, jnp.concatenate(blocks, axis=2).transpose(1, 0, 2))[0]
    return (layer_out, input_grad, small[0:16], small[16:32], qkv_grad, small[32:80], out_grad, small[80:96], small[96:112], gate_grad, down_grad)


def solution(mesh):
    both = P(("seq", "wt"))
    return jax.shard_map(
        per_device, mesh=mesh,
        in_specs=(P("wt", "seq", None), P("wt", None), P(), P(), P(None, "wt"), P(), P(None, "wt"), P(), P(), P(None, None, "wt"), P("wt", None), P("wt", "seq", None)),
        out_specs=(P("wt", "seq", None), P("wt", "seq", None), both, both, P("seq", "wt"), both, P("seq", "wt"), both, both, P("seq", None, "wt"), P("wt", "seq")),
        check_vma=False)
```

```python
import functools, math
import jax, jax.numpy as jnp
from jax import lax
from jax.experimental import pallas as pl
from jax.experimental.pallas import tpu as pltpu
from jax.sharding import PartitionSpec as P

MESH = pl.DeviceIdType.MESH

def coords():
    s = lax.axis_index("seq")
    w = lax.axis_index("wt")
    return s // 8, lax.rem(s // 2, 4), lax.rem(s, 2), w // 2, lax.rem(w, 2)

def at(yh, z, c, x, yl):
    return {"seq": yh * 8 + z * 2 + c, "wt": x * 2 + yl}

class Plane:
    def __init__(self, axis):
        self.axis = axis
        yh, z, c, x, yl = coords()
        self.c = c
        if axis == "wt":
            self.a, self.b = x, yl
            move = lambda da, db: at(yh, z, c, lax.rem(x + da + 4, 4), lax.rem(yl + db, 2))
        else:
            self.a, self.b = z, yh
            move = lambda da, db: at(lax.rem(yh + db, 2), lax.rem(z + da + 4, 4), c, x, yl)
        self.left, self.right, self.pair = move(-1, 0), move(1, 0), move(0, 1)
        self.twin = at(yh, z, 1 - c, x, yl)

    def block(self, da, db):
        a, b = lax.rem(self.a + da + 4, 4), lax.rem(self.b + db, 2)
        return a * 2 + b if self.axis == "wt" else b * 4 + a

def cuts(rows, split):
    p = split or rows // 2
    q = rows - p
    return (0, p), (p, q), (0, p // 2), (p // 2, p // 2), (p, q // 2), (p + q // 2, q // 2)

def remote(src, dst, ssem, rsem, k, target):
    return pltpu.make_async_remote_copy(src_ref=src, dst_ref=dst, send_sem=ssem.at[k], recv_sem=rsem.at[k], device_id=target, device_id_type=MESH)

def greet(targets):
    bar = pltpu.get_barrier_semaphore()
    for t in targets:
        pl.semaphore_signal(bar, inc=1, device_id=t, device_id_type=MESH)
    pl.semaphore_wait(bar, len(targets))

def repeat(n, body):
    if n == 1:
        body(0, 0)
    else:
        lax.fori_loop(0, n, body, 0)

def pace(rows, cols):
    return max(n for n in range(16, rows + 1, 16) if rows % n == 0 and n * cols <= 300000)

def gather_steps(pn, own, buf, rows, ssem, rsem, index=lambda j: j, split=None):
    P_, Q_, P0, P1, Q0, Q1 = cuts(rows, split)
    L, Rt, Y = pn.left, pn.right, pn.pair
    table = {
        0: (Y, (0, 0), P_, (0, 1)),
        1: (Rt, (0, 0), Q_, (-1, 0)),
        2: (L, (0, 0), Q_, (1, 0)),
        3: (Rt, (0, 0), P_, (-1, 0)),
        4: (L, (0, 0), P_, (1, 0)),
        5: (Y, (0, 0), Q_, (0, 1)),
        6: (Rt, (-1, 0), Q0, (2, 0)),
        7: (Y, (-1, 0), Q_, (-1, 1)),
        8: (L, (1, 0), Q1, (2, 0)),
        9: (Y, (1, 0), Q_, (1, 1)),
        10: (Rt, (0, 1), P_, (-1, 1)),
        11: (L, (0, 1), P_, (1, 1)),
        12: (Rt, (-1, 0), P0, (2, 0)),
        13: (L, (1, 0), P1, (2, 0)),
        14: (Y, (2, 0), Q0, (2, 1)),
        15: (Y, (2, 0), Q1, (2, 1)),
        16: (Rt, (-1, 1), P0, (2, 1)),
        17: (L, (1, 1), P1, (2, 1)),
    }
    def part(d, r):
        return buf.at[index(pn.block(*d)), pl.ds(*r)]
    def send(k):
        t, d, r, _ = table[k]
        if not r[1]:
            return
        src = own.at[pl.ds(*r)] if d == (0, 0) else part(d, r)
        remote(src, part(d, r), ssem, rsem, k, t).start()
    def got(k):
        t, _, r, d = table[k]
        if not r[1]:
            return
        remote(part(d, r), part(d, r), ssem, rsem, k, t).wait_recv()
    def sent(k):
        t, d, r, _ = table[k]
        if not r[1]:
            return
        remote(part(d, r), part(d, r), ssem, rsem, k, t).wait_send()
    def first():
        for k in (0, 1, 2, 3, 4, 5): send(k)
    def after(k, *next_):
        def f():
            got(k)
            for n in next_: send(n)
        return f
    steps = [first, after(1, 6, 7), after(2, 8, 9), after(0, 10, 11), after(3, 12), after(4, 13),
             after(6, 14), after(8, 15), after(10, 16), after(11, 17)]
    tail = [after(5), after(7), after(9), after(12), after(13), after(14), after(15), after(16), after(17)]
    def done():
        for k in range(18): sent(k)
    return steps, tail, done

def sum_steps(pn, buf, land, rows, ssem, rsem, out, index=lambda j: j, split=None):
    P_, Q_, P0, P1, Q0, Q1 = cuts(rows, split)
    L, Rt, Y = pn.left, pn.right, pn.pair
    table = {}
    off = 0
    def msg(k, t, d, r, r_to):
        nonlocal off
        table[k] = (t, d, r, off, r_to)
        off += r[1]
    msg(0, L, (-2, 0), P0, (-1, 0)); msg(1, Rt, (2, 0), P1, (1, 0))
    msg(2, L, (-2, 1), P0, (-1, 1)); msg(3, Rt, (2, 1), P1, (1, 1))
    msg(4, Y, (2, 1), Q_, (2, 0)); msg(5, Y, (-1, 1), Q_, (-1, 0)); msg(6, Y, (1, 1), Q_, (1, 0)); msg(7, Y, (0, 1), Q_, (0, 0))
    msg(8, L, (-1, 1), P_, (0, 1)); msg(9, Rt, (1, 1), P_, (0, 1))
    msg(10, L, (-1, 0), P_, (0, 0)); msg(11, Rt, (1, 0), P_, (0, 0))
    msg(12, L, (-2, 0), Q0, (-1, 0)); msg(13, Rt, (2, 0), Q1, (1, 0))
    msg(14, L, (-1, 0), Q_, (0, 0)); msg(15, Rt, (1, 0), Q_, (0, 0))
    msg(16, Y, (0, 1), P_, (0, 0))
    assert off <= land.shape[0]
    def part(d, r):
        return buf.at[index(pn.block(*d)), pl.ds(*r)]
    def landing(k):
        _, _, r, o, _ = table[k]
        return land.at[pl.ds(o, r[1])]
    def send(k):
        t, d, r, _, _ = table[k]
        if not r[1]:
            return
        remote(part(d, r), landing(k), ssem, rsem, k, t).start()
    def got(k):
        if not table[k][2][1]:
            return
        remote(landing(k), landing(k), ssem, rsem, k, table[k][0]).wait_recv()
    def sent(k):
        if not table[k][2][1]:
            return
        remote(landing(k), landing(k), ssem, rsem, k, table[k][0]).wait_send()
    def accumulate(d, r, ks, to=None):
        if not r[1]:
            return
        j = index(pn.block(*d))
        step = pace(r[1], buf.shape[2])
        def body(i, _):
            at_ = pl.multiple_of(r[0] + i * step, 16)
            v = buf[j, pl.ds(at_, step)].astype(jnp.float32)
            for k in ks:
                v = v + land[pl.ds(pl.multiple_of(table[k][3] + i * step, 16), step)].astype(jnp.float32)
            if to is None:
                buf[j, pl.ds(at_, step)] = v.astype(buf.dtype)
            else:
                to[pl.ds(at_, step)] = v.astype(to.dtype)
            return 0
        repeat(r[1] // step, body)
    def s0():
        for k in range(8): send(k)
    def s1():
        got(2); accumulate((-1, 1), P0, [2]); send(8)
        got(3); accumulate((1, 1), P1, [3]); send(9)
    def s2():
        got(0); accumulate((-1, 0), P0, [0]); send(10)
        got(1); accumulate((1, 0), P1, [1]); send(11)
    def s3():
        got(4); accumulate((2, 0), Q_, [4]); send(12); send(13)
    def s4():
        got(5); accumulate((-1, 0), Q_, [5]); got(12); accumulate((-1, 0), Q0, [12]); send(14)
        got(6); accumulate((1, 0), Q_, [6]); got(13); accumulate((1, 0), Q1, [13]); send(15)
    def s5():
        got(8); got(9); accumulate((0, 1), P_, [8, 9]); send(16)
    def s6():
        got(7); got(14); got(15); accumulate((0, 0), Q_, [7, 14, 15], out)
        got(10); got(11); got(16); accumulate((0, 0), P_, [10, 11, 16], out)
    def done():
        for k in range(17): sent(k)
    return [s0, s1, s2, s3, s4, s5, s6], done
ANY = pl.BlockSpec(memory_space=pl.ANY)
QB, KB = 512, 512
MASKED = -1e30
NT = (((1,), (1,)), ((), ()))

def halves(ref, kept):
    lane = lax.broadcasted_iota(jnp.int32, (1, 128), 1)
    low = (lane < 64).astype(jnp.float32)
    v = ref[...].astype(jnp.float32)
    kept[0] = (v * low).astype(jnp.bfloat16)
    kept[1] = (v * (1.0 - low)).astype(jnp.bfloat16)

def allowed(i, j, start):
    key = j * KB + lax.broadcasted_iota(jnp.int32, (KB, QB), 0)
    query = i * QB + lax.broadcasted_iota(jnp.int32, (KB, QB), 1)
    return (key <= query) & (key >= start)

VM = pl.BlockSpec(memory_space=pltpu.VMEM)

SPLIT_A, SPLIT_C, SPLIT_D = 128, 96, 768
ORDER = [(0, 0), (0, 1), (-1, 1), (1, 1), (-1, 0), (1, 0), (2, 0), (2, 1)]

class Gather:
    def __init__(self, pn, own, buf, rows, ss, rs, twin=None, split=None):
        self.pn, self.buf, self.twin = pn, buf, twin
        self.index = (lambda j: 2 * j + pn.c) if twin else (lambda j: j)
        steps, tail, done = gather_steps(pn, own, buf, rows, ss, rs, self.index, split)
        self.done = done
        ready = {0: [1], 1: [2], 2: [3], 3: [4], 4: [5], 6: [6], 8: [7]}
        def follow(i, f):
            def g():
                f()
                for k in ready.get(i, []):
                    self.hand(k)
            return g
        def first():
            steps[0]()
            self.hand(0)
        self.steps = [first] + steps[1:] + [follow(i, f) for i, f in enumerate(tail)]

    def handed(self, k, mine):
        c = self.pn.c if mine else 1 - self.pn.c
        j = self.buf.at[2 * self.pn.block(*ORDER[k]) + c]
        return remote(j, j, self.twin[0], self.twin[1], k, self.pn.twin)

    def hand(self, k):
        if self.twin:
            self.handed(k, True).start()

    def wait_twin(self, k):
        self.handed(k, False).wait_recv()

    def finish(self, waited=()):
        self.done()
        if self.twin:
            for k in range(8):
                self.handed(k, True).wait_send()
                if k not in waited:
                    self.wait_twin(k)

def fetch_steps(pn, weight, hw, ss, rs, ls):
    s = lax.axis_index("seq")
    rows = hw.shape[0]
    h, q = rows // 2, rows // 4
    W = {"P": (0, h), "Q": (h, h), "P0": (0, q), "P1": (q, q), "Q0": (h, q), "Q1": (h + q, q)}
    kinds = ["P", "P0", "P1", "Q", "Q0", "Q1"]
    both = []
    for p in range(3):
        g = 16 * p + s
        src = g // 6
        da = lax.rem(pn.a - src // 2 + 4, 4)
        b0 = pn.b == lax.rem(src, 2)
        both.append((p, lax.rem(g, 6), da, b0))
    def part(p, kind):
        return hw.at[pl.ds(*W[kind]), pl.ds(128 * p, 128)]
    def send(p, kind, slot, target):
        pltpu.make_async_remote_copy(src_ref=part(p, kind), dst_ref=part(p, kind), send_sem=ss.at[6 * p + slot],
                                     recv_sem=rs.at[6 * p + kinds.index(kind)], device_id=target, device_id_type=MESH).start()
    def wait(p, kind, slot=None):
        cp = pltpu.make_async_remote_copy(src_ref=part(p, kind), dst_ref=part(p, kind), send_sem=ss.at[6 * p + (slot or 0)],
                                          recv_sem=rs.at[6 * p + kinds.index(kind)], device_id=pn.right, device_id_type=MESH)
        cp.wait_recv() if slot is None else cp.wait_send()
    no = jnp.logical_not
    def local(p, b):
        return pltpu.make_async_copy(weight.at[:, pl.ds(pl.multiple_of(128 * b, 128), 128)], hw.at[:, pl.ds(128 * p, 128)], ls.at[p])
    def begin():
        for p, b, da, b0 in both:
            @pl.when(b0 & (da == 0))
            def _():
                local(p, b).start()
    def st0():
        for p, b, da, b0 in both:
            @pl.when(b0 & (da == 0))
            def _():
                local(p, b).wait()
                send(p, "Q", 0, pn.right); send(p, "Q", 1, pn.left); send(p, "P", 5, pn.pair)
                send(p, "P", 3, pn.right); send(p, "P", 4, pn.left); send(p, "Q", 2, pn.pair)
    def st1():
        for p, b, da, b0 in both:
            @pl.when(b0 & (da == 1))
            def _():
                wait(p, "Q"); send(p, "Q0", 0, pn.right); send(p, "Q", 2, pn.pair)
            @pl.when(b0 & (da == 3))
            def _():
                wait(p, "Q"); send(p, "Q1", 1, pn.left); send(p, "Q", 2, pn.pair)
            @pl.when(no(b0) & (da == 0))
            def _():
                wait(p, "P"); send(p, "P", 3, pn.right); send(p, "P", 4, pn.left)
    def st2():
        for p, b, da, b0 in both:
            @pl.when(da == 1)
            def _():
                wait(p, "P"); send(p, "P0", 3, pn.right)
            @pl.when(da == 3)
            def _():
                wait(p, "P"); send(p, "P1", 4, pn.left)
    def st3():
        for p, b, da, b0 in both:
            @pl.when(b0 & (da == 2))
            def _():
                wait(p, "Q0"); wait(p, "Q1"); send(p, "Q", 2, pn.pair)
    def st4():
        for p, b, da, b0 in both:
            @pl.when(da == 2)
            def _():
                wait(p, "P0"); wait(p, "P1")
            @pl.when(no(b0))
            def _():
                wait(p, "Q")
    def done():
        for p, b, da, b0 in both:
            @pl.when(b0)
            def _():
                wait(p, "Q", 2)
            @pl.when(b0 & (da == 0))
            def _():
                wait(p, "Q", 0); wait(p, "Q", 1); wait(p, "P", 5)
            @pl.when(da == 0)
            def _():
                wait(p, "P", 3); wait(p, "P", 4)
            @pl.when(b0 & (da == 1))
            def _():
                wait(p, "Q0", 0)
            @pl.when(b0 & (da == 3))
            def _():
                wait(p, "Q1", 1)
            @pl.when(da == 1)
            def _():
                wait(p, "P0", 3)
            @pl.when(da == 3)
            def _():
                wait(p, "P1", 4)
    return begin, [st0, st1, st2, st3, st4], done

def turn(v, keep, ahead, behind):
    return v * keep + pltpu.roll(v, 120, 1) * ahead + pltpu.roll(v, 8, 1) * behind

def norm_rows(x, gain, shift):
    average = jnp.mean(x, axis=-1, keepdims=True)
    centred = x - average
    inverse = lax.rsqrt(jnp.mean(centred * centred, axis=-1, keepdims=True) + norm_eps)
    return centred * inverse * gain + shift

def rotary_tables_to(cs, tables):
    rows = cs.shape[1]
    c, s = cs[0:8, :], cs[8:16, :]
    one, nil, z8 = jnp.ones((48, rows), jnp.float32), jnp.zeros((48, rows), jnp.float32), jnp.zeros((8, rows), jnp.float32)
    tables[0][...] = jnp.concatenate([c, c, one] * 2, axis=0).T
    tables[1][...] = jnp.concatenate([-s, z8, nil] * 2, axis=0).T
    tables[2][...] = jnp.concatenate([z8, s, nil] * 2, axis=0).T

def pump(*its):
    for it in its:
        f = next(it, None)
        if f is not None:
            f()

def front_kernel(x, gain, shift, weight, bias, cs, start_ref, dy, ow,
                 rn, hw, q_ref, k_ref, v_ref, ot_ref, lse_ref, att, out_all, dy_all,
                 own, kept, vt, t0, t1, t2, ob, ox,
                 ssA, rsA, tsA, trA, ssB, rsB, lsB, ssC, rsC, ssD, rsD, tsD, trD, ssO, rsO, ssT, rsT, lsO, ls):
    sp, wp = Plane("seq"), Plane("wt")
    tok = x.shape[0]
    c, m = sp.c, sp.block(0, 0)
    A = Gather(sp, own, rn, tok, ssA, rsA, (tsA, trA), SPLIT_A)
    begin, fetch, fetch_done = fetch_steps(wp, weight, hw, ssB, rsB, lsB)
    C = Gather(wp, dy, dy_all, tok, ssC, rsC, None, SPLIT_C)
    D = Gather(wp, ow, out_all, ow.shape[0], ssD, rsD, (tsD, trD), SPLIT_D)
    begin()
    chips = [at(j // 4, j % 4, c, wp.a, wp.b) for j in range(8)]
    bar = pltpu.get_barrier_semaphore()
    for j in range(8):
        @pl.when(m != j)
        def _():
            pl.semaphore_signal(bar, inc=1, device_id=chips[j], device_id_type=MESH)
    for t in (sp.twin, wp.left, wp.right, wp.pair):
        pl.semaphore_signal(bar, inc=1, device_id=t, device_id_type=MESH)
    def ln(i, _):
        r = pl.ds(pl.multiple_of(i * 16, 16), 16)
        own[r] = norm_rows(x[r].astype(jnp.float32), gain[...], shift[...]).astype(jnp.bfloat16)
        return 0
    lax.fori_loop(0, tok // 16, ln, 0)
    copies = [pltpu.make_async_copy(own, rn.at[2 * m + c], ls.at[0]),
              pltpu.make_async_copy(dy, dy_all.at[wp.block(0, 0)], ls.at[1]),
              pltpu.make_async_copy(ow, out_all.at[2 * wp.block(0, 0) + c], ls.at[2])]
    for cp in copies:
        cp.start()
    copies[0].wait()
    pl.semaphore_wait(bar, 11)
    A.steps[0]()
    fetch[0]()
    rotary_tables_to(cs, (t0, t1, t2))
    copies[1].wait()
    copies[2].wait()
    a, b, cc, d = iter(A.steps[1:]), iter(fetch[1:]), iter(C.steps), iter(D.steps)
    pump(a, a, b, a, a, a, b, a, a, b, b, a, a, cc)
    def project(k):
        A.wait_twin(k)
        j = sp.block(*ORDER[k])
        rows = pl.ds(pl.multiple_of(j * 256, 256), 256)
        h = rn[pl.ds(2 * j, 2)].reshape(256, rn.shape[2])
        y = jnp.dot(h, hw[...], preferred_element_type=jnp.float32) + bias[...]
        tabs = (t0[rows], t1[rows], t2[rows])
        q_ref[rows] = (turn(y[:, :128], *tabs) * 0.125).astype(jnp.bfloat16)
        k_ref[rows] = turn(y[:, 128:256], *tabs).astype(jnp.bfloat16)
        v_ref[rows] = y[:, 256:].astype(jnp.bfloat16)
    project(0); pump(a); project(1); pump(a); pump(cc); project(2); pump(a); project(3)
    pump(a); project(4); pump(a, cc); project(5); pump(a, a); pump(cc); project(6); pump(a, a); project(7)
    halves(k_ref, kept)
    pump(cc, cc)
    vt[...] = v_ref[...].astype(jnp.float32).T.astype(jnp.bfloat16)
    def to_twin(j):
        return pltpu.make_async_remote_copy(src_ref=ox.at[j], dst_ref=ob.at[j, :, pl.ds(pl.multiple_of(128 * c, 128), 128)],
                                            send_sem=ssT.at[j], recv_sem=rsT.at[j], device_id=sp.twin, device_id_type=MESH)
    def from_twin(j):
        there = ob.at[j, :, pl.ds(pl.multiple_of(128 * (1 - c), 128), 128)]
        return pltpu.make_async_remote_copy(src_ref=there, dst_ref=there, send_sem=ssT.at[j], recv_sem=rsT.at[j], device_id=sp.twin, device_id_type=MESH)
    def cols(j):
        return att.at[:, pl.ds(pl.multiple_of(256 * j, 256), 256)]
    def to_chip(j):
        return pltpu.make_async_remote_copy(src_ref=ob.at[j], dst_ref=cols(m), send_sem=ssO.at[j], recv_sem=rsO.at[m], device_id=chips[j], device_id_type=MESH)
    def ship(i):
        for j in (2 * i, 2 * i + 1):
            from_twin(j).wait_recv()
            @pl.when(m == j)
            def _():
                pltpu.make_async_copy(ob.at[j], cols(j), lsO).start()
            @pl.when(m != j)
            def _():
                to_chip(j).start()
    n = q_ref.shape[0] // QB
    for i in range(n):
        q = q_ref[QB * i:QB * (i + 1)]
        start = start_ref[:, QB * i:QB * (i + 1)]
        step = functools.partial(attend_step, kept, vt, q, start, i)
        one = (jnp.full((1, QB), MASKED, jnp.float32), jnp.zeros((1, QB), jnp.float32), jnp.zeros((64, QB), jnp.float32))
        carry = (one, one)
        for j in range(i + 1):
            carry = step(j == 0 or j == i or i == n - 1, j, carry)
            pump(cc, cc, d)
        where = pl.ds(QB * i, QB)
        for h in range(2):
            top, l, acc = carry[h]
            ot_ref[64 * h:64 * h + 64, where] = acc / l
            lse_ref[h:h + 1, where] = top + jnp.log(l)
        if i:
            ship(i - 1)
        o = ot_ref[:, where].T.astype(jnp.bfloat16)
        for j in (0, 1):
            mine = pl.ds(pl.multiple_of(128 * c, 128), 128)
            first, second = o[256 * j:256 * j + 128], o[256 * j + 128:256 * j + 256]
            @pl.when(c == 0)
            def _():
                ob[2 * i + j, :, 0:128] = first
                ox[2 * i + j] = second
            @pl.when(c == 1)
            def _():
                ob[2 * i + j, :, 128:256] = second
                ox[2 * i + j] = first
            to_twin(2 * i + j).start()
    ship(n - 1)
    for f in cc:
        f()
    for f in d:
        f()
    for j in range(8):
        to_twin(j).wait_send()
        @pl.when(m == j)
        def _():
            pltpu.make_async_copy(ob.at[j], cols(j), lsO).wait()
        @pl.when(m != j)
        def _():
            to_chip(j).wait_send()
            pltpu.make_async_remote_copy(src_ref=cols(j), dst_ref=cols(j), send_sem=ssO.at[j], recv_sem=rsO.at[j], device_id=chips[j], device_id_type=MESH).wait_recv()
    A.finish(range(8))
    fetch_done()
    C.finish()
    D.finish()

def attend_step(kept, vt, q, start, i, masked, j, carry):
    r = pl.ds(j * KB, KB)
    out = []
    for h in range(2):
        m, l, acc = carry[h]
        s = lax.dot_general(kept[h, r], q, NT, preferred_element_type=jnp.float32)
        if masked:
            s = jnp.where(allowed(i, j, start), s, MASKED)
        top = jnp.maximum(m, jnp.max(s, axis=0, keepdims=True))
        p = jnp.exp(s - top)
        fade = jnp.exp(m - top)
        l = l * fade + jnp.sum(p, axis=0, keepdims=True)
        acc = acc * fade + jnp.dot(vt[64 * h:64 * h + 64, r], p.astype(jnp.bfloat16), preferred_element_type=jnp.float32)
        out.append((top, l, acc))
    return tuple(out)

def front(cid, x, gain, shift, weight, bias, cs, start, dy, ow):
    tok, width = x.shape
    rows = start.shape[1]
    f, b16, f32 = jax.ShapeDtypeStruct, jnp.bfloat16, jnp.float32
    vm = pltpu.VMEM
    return pl.pallas_call(
        front_kernel,
        out_shape=(f((16, tok, width), b16), f((width, 384), b16), f((rows, 128), b16), f((rows, 128), b16), f((rows, 128), b16),
                   f((128, rows), f32), f((8, rows), f32), f((tok, width), b16), f((16,) + ow.shape, b16), f((8, tok, width), b16)),
        in_specs=[VM, VM, VM, ANY, VM, VM, VM, VM, VM], out_specs=(VM,) * 10,
        scratch_shapes=[vm((tok, width), b16), vm((2, rows, 128), b16), vm((128, rows), b16)] + [vm((rows, 128), f32)] * 3
        + [vm((8, 128, 256), b16), vm((8, 128, 128), b16)]
        + [dma(n) for n in (18, 18, 8, 8, 18, 18, 3, 18, 18, 18, 18, 8, 8, 8, 8, 8, 8)] + [pltpu.SemaphoreType.DMA, dma(3)],
        compiler_params=params(cid), name="front",
    )(x, gain, shift, weight, bias, cs, start, dy, ow)
TN = (((0,), (0,)), ((), ()))

def middle_kernel(att, x, out_all, gain, shift, dy_all, wgu, wd,
                  mid, dh2, ffp, joined,
                  own, h2, wbuf, dga, tr, dh2p, land, ssG, rsG, ssS, rsS, lsw, ls):
    wp = Plane("wt")
    tok, width = mid.shape
    hidden = wd.shape[0]
    for t in (wp.left, wp.right, wp.pair):
        pl.semaphore_signal(pltpu.get_barrier_semaphore(), inc=1, device_id=t, device_id_type=MESH)
    def load(w, slot):
        return pltpu.make_async_copy(out_all.at[pl.ds(2 * w, 2)], wbuf.at[slot], lsw.at[slot])
    load(0, 0).start()
    def project(w):
        slot = w % 2
        load(w, slot).wait()
        if w < 7:
            load(w + 1, 1 - slot).start()
        cols = pl.ds(256 * w, 256)
        y = jnp.dot(att[:, :width // 2], wbuf[slot, 0], preferred_element_type=jnp.float32)
        y += jnp.dot(att[:, width // 2:], wbuf[slot, 1], preferred_element_type=jnp.float32)
        mid[:, cols] = x[:, cols].astype(jnp.float32) + y
    for w in range(8):
        project(w)
    def ln(i, _):
        r = pl.ds(pl.multiple_of(i * 16, 16), 16)
        own[r] = norm_rows(mid[r], gain[...], shift[...]).astype(jnp.bfloat16)
        return 0
    lax.fori_loop(0, tok // 16, ln, 0)
    cp = pltpu.make_async_copy(own, h2.at[wp.block(0, 0)], ls)
    cp.start()
    pl.semaphore_wait(pltpu.get_barrier_semaphore(), 3)
    G = Gather(wp, own, h2, tok, ssG, rsG)
    part = hidden // 2
    def chunk_up(da):
        a = lax.rem(wp.a + da + 4, 4)
        cols = pl.ds(pl.multiple_of(256 * a, 256), 256)
        hc = h2[pl.ds(2 * a, 2)].reshape(2 * tok, width)
        dc = dy_all[pl.ds(2 * a, 2)].reshape(2 * tok, width)
        def tile(i, _):
            r = pl.ds(pl.multiple_of(i * part, 16), part)
            r2 = pl.ds(pl.multiple_of(hidden + i * part, 16), part)
            r3 = pl.ds(pl.multiple_of(2 * hidden + i * part, 16), part)
            g = lax.dot_general(wgu[r], hc, NT, preferred_element_type=jnp.float32)
            u = lax.dot_general(wgu[r2], hc, NT, preferred_element_type=jnp.float32)
            e = lax.dot_general(wd[r], dc, NT, preferred_element_type=jnp.float32)
            sigma = 1.0 / (1.0 + jnp.exp(-g))
            gs = g * sigma
            dga[r, cols] = (e * u * sigma * (1.0 + g * (1.0 - sigma))).astype(jnp.bfloat16)
            dga[r2, cols] = (e * gs).astype(jnp.bfloat16)
            dga[r3, cols] = (gs * u).astype(jnp.bfloat16)
            return 0
        lax.fori_loop(0, 2, tile, 0)
    def chunk_down(da):
        a = lax.rem(wp.a + da + 4, 4)
        cols = pl.ds(pl.multiple_of(256 * a, 256), 256)
        def flip(i, _):
            r = pl.ds(pl.multiple_of(i * 128, 128), 128)
            tr[:, r] = dga[r, cols].astype(jnp.float32).T.astype(jnp.bfloat16)
            return 0
        lax.fori_loop(0, 3 * hidden // 128, flip, 0)
        last = 3 * hidden // 128 * 128
        tr[:, last:] = dga[last:, cols].astype(jnp.float32).T.astype(jnp.bfloat16)
        def tile(i, _):
            n = pl.ds(pl.multiple_of(i * 512, 512), 512)
            y = jnp.dot(tr[:, :2 * hidden], wgu[:, n], preferred_element_type=jnp.float32)
            dh2p[pl.ds(2 * a, 2), :, n] = y.astype(jnp.bfloat16).reshape(2, tok, 512)
            y = jnp.dot(tr[:, 2 * hidden:], wd[:, n], preferred_element_type=jnp.float32)
            ffp[pl.ds(2 * a, 2), :, n] = y.astype(jnp.bfloat16).reshape(2, tok, 512)
            return 0
        lax.fori_loop(0, width // 512, tile, 0)
    S = G.steps
    S[0]()
    cp.wait()
    for f in S[1:6]:
        f()
    S[10]()
    chunk_up(0)
    S[6](); S[7]()
    chunk_down(0)
    S[8](); S[9](); S[11](); S[12]()
    chunk_up(-1)
    chunk_down(-1)
    chunk_up(1)
    chunk_down(1)
    for f in S[13:]:
        f()
    chunk_up(2)
    chunk_down(2)
    G.finish()
    R, done = sum_steps(wp, dh2p, land, tok, ssS, rsS, dh2)
    def weights(lo, hi):
        def one(j, _):
            f = pl.ds(pl.multiple_of(256 * j, 256), 256)
            for k, other in ((0, h2), (1, h2), (2, dy_all)):
                r = pl.ds(hidden * k, hidden)
                y = jnp.dot(dga[r], other[:, :, f].reshape(8 * tok, 256), preferred_element_type=jnp.float32).astype(jnp.bfloat16)
                joined[2 * j, r] = y[:, :128]
                joined[2 * j + 1, r] = y[:, 128:]
            return 0
        lax.fori_loop(lo, hi, one, 0)
    R[0]()
    weights(0, 2); R[1](); R[2](); weights(2, 3); R[3](); weights(3, 4); R[4](); weights(4, 6); R[5](); weights(6, 8); R[6]()
    done()

def middle_part(cid, att, x, out_all, gain, shift, dy_all, wgu, wd):
    tok, width = x.shape
    hidden = wd.shape[0]
    f, b16, f32, vm = jax.ShapeDtypeStruct, jnp.bfloat16, jnp.float32, pltpu.VMEM
    return pl.pallas_call(
        middle_kernel,
        out_shape=(f((tok, width), f32), f((tok, width), f32), f((8, tok, width), b16), f((16, 3 * hidden, 128), b16)),
        in_specs=[VM, VM, ANY, VM, VM, VM, VM, VM], out_specs=(VM,) * 4,
        scratch_shapes=[vm((tok, width), b16), vm((8, tok, width), b16), vm((2, 2) + out_all.shape[1:], b16), vm((3 * hidden, 8 * tok), b16),
                        vm((2 * tok, 3 * hidden), b16), vm((8, tok, width), b16), vm((7 * tok, width), b16)]
        + [dma(n) for n in (18, 18, 17, 17, 2)] + [pltpu.SemaphoreType.DMA],
        compiler_params=params(cid), name="middle",
    )(att, x, out_all, gain, shift, dy_all, wgu, wd)
class ScatterBoth:
    def __init__(self, pn, buf, tland, land, ss, rs, ts, tr, out, split=None):
        self.pn, self.tland, self.ts, self.tr = pn, tland, ts, tr
        rows, cols = buf.shape[1:]
        order = [(2, 0), (2, 1), (-1, 1), (1, 1), (-1, 0), (1, 0), (0, 1), (0, 0)]
        def send(k):
            j = pn.block(*order[k])
            remote(buf.at[2 * j + 1 - pn.c], tland.at[k], ts, tr, k, pn.twin).start()
        def add(k):
            self.copy(k).wait_recv()
            j = 2 * pn.block(*order[k]) + pn.c
            step = pace(rows, cols)
            def body(i, _):
                r = pl.ds(pl.multiple_of(i * step, 16), step)
                buf[j, r] = (buf[j, r].astype(jnp.float32) + tland[k, r].astype(jnp.float32)).astype(buf.dtype)
                return 0
            repeat(rows // step, body)
        self.sends = [functools.partial(send, k) for k in range(8)]
        self.adds = [functools.partial(add, k) for k in range(8)]
        self.sums, self.done = sum_steps(pn, buf, land, rows, ss, rs, out, lambda j: 2 * j + pn.c, split)

    def copy(self, k):
        return remote(self.tland.at[k], self.tland.at[k], self.ts, self.tr, k, self.pn.twin)

    def finish(self):
        self.done()
        for k in range(8):
            self.copy(k).wait_send()

SPLIT_F, SPLIT_J = 96, 1568

def back_kernel(dh2, mid, dy, gain, out_all, q_ref, k_ref, v_ref, start_ref, ot_ref, lse_ref, cs, ffp, joined,
                mgrad, da, dproj, bias, sums, layer_out, grads,
                wbuf, dg, inbox, do_ref, keptk, keptv, keptq, keptd, kt, dot_, dq_ref, dk_ref, dv_ref, t0, t1, t2, fbuf, fland, fsum, jbuf, tland, jland,
                ssO, rsO, ssT, rsT, ssF, rsF, ssJ, rsJ, tsJ, trJ, lsw, ls):
    sp, wp = Plane("seq"), Plane("wt")
    tok, width = dh2.shape
    c, m = sp.c, sp.block(0, 0)
    chips = [at(j // 4, j % 4, c, wp.a, wp.b) for j in range(8)]
    bar = pltpu.get_barrier_semaphore()
    for j in range(8):
        @pl.when(m != j)
        def _():
            pl.semaphore_signal(bar, inc=1, device_id=chips[j], device_id_type=MESH)
    for t in (sp.twin, wp.left, wp.right, wp.pair):
        pl.semaphore_signal(bar, inc=1, device_id=t, device_id_type=MESH)
    def load(w, slot):
        return pltpu.make_async_copy(out_all.at[pl.ds(2 * w, 2)], wbuf.at[slot], lsw.at[slot])
    load(0, 0).start()
    here = [pltpu.make_async_copy(ffp, fbuf, ls.at[0]), pltpu.make_async_copy(joined, jbuf, ls.at[1])]
    for cp in here:
        cp.start()
    def ln(i, carry):
        r = pl.ds(pl.multiple_of(i * 32, 32), 32)
        y = mid[r]
        centred = y - jnp.mean(y, axis=-1, keepdims=True)
        inverse = lax.rsqrt(jnp.mean(centred * centred, axis=-1, keepdims=True) + norm_eps)
        scaled = centred * inverse
        up = dh2[r]
        w = up * gain[...]
        back = inverse * (w - jnp.mean(w, axis=-1, keepdims=True) - scaled * jnp.mean(w * scaled, axis=-1, keepdims=True))
        g = dy[r].astype(jnp.float32) + back
        mgrad[r] = g
        da[r] = g.astype(jnp.bfloat16)
        return carry[0] + jnp.sum((up * scaled).reshape(4, 8, width), axis=0), carry[1] + jnp.sum(up.reshape(4, 8, width), axis=0)
    nil = jnp.zeros((8, width), jnp.float32)
    gsum, ssum = lax.fori_loop(0, tok // 32, ln, (nil, nil))
    sums[0:1] = jnp.sum(gsum, axis=0, keepdims=True)
    sums[1:2] = jnp.sum(ssum, axis=0, keepdims=True)
    total = [jnp.zeros((tok, width // 2), jnp.float32)] * 2
    for w in range(8):
        load(w, w % 2).wait()
        if w < 7:
            load(w + 1, 1 - w % 2).start()
        g = da[:, 256 * w:256 * w + 256]
        both = wbuf[w % 2]
        total = [total[h] + lax.dot_general(g, both[h], NT, preferred_element_type=jnp.float32) for h in range(2)]
    dg[...] = jnp.concatenate(total, axis=1).astype(jnp.bfloat16)
    pl.semaphore_wait(bar, 11)
    def to_chip(j):
        return pltpu.make_async_remote_copy(src_ref=dg.at[:, pl.ds(256 * j, 256)], dst_ref=inbox.at[m], send_sem=ssO.at[j], recv_sem=rsO.at[m], device_id=chips[j], device_id_type=MESH)
    for j in range(8):
        @pl.when(m != j)
        def _():
            to_chip(j).start()
    mine = pltpu.make_async_copy(dg.at[:, pl.ds(pl.multiple_of(256 * m, 256), 256)], inbox.at[m], ls.at[2])
    mine.start()
    for cp in here:
        cp.wait()
    F, fdone = sum_steps(wp, fbuf, fland, tok, ssF, rsF, fsum, split=SPLIT_F)
    J = ScatterBoth(sp, jbuf, tland, jland, ssJ, rsJ, tsJ, trJ, grads, SPLIT_J)
    for f in J.sends:
        f()
    F[0]()
    rotary_tables_to(cs, (t0, t1, t2))
    halves(k_ref, keptk)
    halves(v_ref, keptv)
    halves(q_ref, keptq)
    kt[...] = k_ref[...].astype(jnp.float32).T.astype(jnp.bfloat16)
    dk_ref[...] = jnp.zeros_like(dk_ref)
    dv_ref[...] = jnp.zeros_like(dv_ref)
    mine.wait()
    def pass_on(j, own):
        r = do_ref.at[pl.ds(pl.multiple_of(128 * (2 * j + (c if own else 1 - c)), 128), 128)]
        src = inbox.at[j, :, pl.ds(pl.multiple_of(128 * (1 - c), 128), 128)] if own else r
        return pltpu.make_async_remote_copy(src_ref=src, dst_ref=r, send_sem=ssT.at[j], recv_sem=rsT.at[j], device_id=sp.twin, device_id_type=MESH)
    for j in range(8):
        @pl.when(m != j)
        def _():
            pltpu.make_async_remote_copy(src_ref=inbox.at[j], dst_ref=inbox.at[j], send_sem=ssO.at[j], recv_sem=rsO.at[j], device_id=chips[j], device_id_type=MESH).wait_recv()
        pass_on(j, True).start()
        @pl.when(c == 0)
        def _():
            do_ref[256 * j:256 * j + 128] = inbox[j, :, 0:128]
        @pl.when(c == 1)
        def _():
            do_ref[256 * j + 128:256 * j + 256] = inbox[j, :, 128:256]
    for j in range(8):
        pass_on(j, False).wait_recv()
    halves(do_ref, keptd)
    dot_[...] = do_ref[...].astype(jnp.float32).T
    fi, ji = iter(F[1:]), iter(J.adds + J.sums)
    n = q_ref.shape[0] // QB
    for i in range(n):
        rows = pl.ds(QB * i, QB)
        q = q_ref[rows]
        do = do_ref[rows]
        do_h, q_h = keptd[:, rows], keptq[:, rows]
        start = start_ref[:, rows]
        both = ot_ref[:, rows] * dot_[:, rows]
        inner = [jnp.sum(both[64 * h:64 * h + 64], axis=0, keepdims=True) for h in range(2)]
        lse2 = lse_ref[:, rows]
        lse = [lse2[h:h + 1] for h in range(2)]
        def step(masked, j, carry):
            r = pl.ds(j * KB, KB)
            out, ps, ds = [], [], []
            kk, vv, kk_t = keptk[:, r], keptv[:, r], kt[:, r]
            for h in range(2):
                s = lax.dot_general(kk[h], q, NT, preferred_element_type=jnp.float32)
                if masked:
                    s = jnp.where(allowed(i, j, start), s, MASKED)
                p = jnp.exp(s - lse[h])
                dp = lax.dot_general(vv[h], do, NT, preferred_element_type=jnp.float32)
                g = (p * (dp - inner[h])).astype(jnp.bfloat16)
                out.append(carry[h] + jnp.dot(kk_t[64 * h:64 * h + 64], g, preferred_element_type=jnp.float32))
                ps.append(p.astype(jnp.bfloat16))
                ds.append(g)
            dv_ref[r] += sum(jnp.dot(ps[h], do_h[h], preferred_element_type=jnp.float32) for h in range(2))
            dk_ref[r] += sum(jnp.dot(ds[h], q_h[h], preferred_element_type=jnp.float32) for h in range(2))
            return tuple(out)
        carry = (jnp.zeros((64, QB), jnp.float32),) * 2
        for j in range(i + 1):
            carry = step(j == 0 or j == i or i == n - 1, j, carry)
            pump(ji, ji, fi)
        dq_ref[rows] = jnp.concatenate(carry, axis=0).T
    def low(v):
        return v.astype(jnp.bfloat16).astype(jnp.float32)
    def unturn(i, total):
        rows = pl.ds(pl.multiple_of(i * 512, 512), 512)
        keep, ahead, behind = t0[rows], -t1[rows], -t2[rows]
        parts = (turn(low(dq_ref[rows]) * 0.125, keep, ahead, behind), turn(low(dk_ref[rows]), keep, ahead, behind), dv_ref[rows])
        new = []
        for p in range(3):
            y = parts[p].astype(jnp.bfloat16)
            dproj[rows, 128 * p:128 * p + 128] = y
            new.append(total[p] + jnp.sum(y.astype(jnp.float32).reshape(64, 8, 128), axis=0))
        return tuple(new)
    total = lax.fori_loop(0, dq_ref.shape[0] // 512, unturn, (jnp.zeros((8, 128), jnp.float32),) * 3)
    for p in range(3):
        bias[:, 128 * p:128 * p + 128] = jnp.sum(total[p], axis=0, keepdims=True)
    for f in fi:
        f()
    layer_out[...] = (mid[...] + fsum[...]).astype(jnp.bfloat16)
    for f in ji:
        f()
    fdone()
    J.finish()
    for j in range(8):
        @pl.when(m != j)
        def _():
            to_chip(j).wait_send()
        pass_on(j, True).wait_send()

def back_part(cid, dh2, mid, dy, gain, out_all, q, k, v, start, ot, lse, cs, ffp, joined):
    tok, width = dy.shape
    rows = q.shape[0]
    f, b16, f32, vm = jax.ShapeDtypeStruct, jnp.bfloat16, jnp.float32, pltpu.VMEM
    wide = joined.shape[1]
    return pl.pallas_call(
        back_kernel,
        out_shape=(f((tok, width), f32), f((tok, width), b16), f((rows, 384), b16), f((1, 384), f32), f((2, width), f32), f((tok, width), b16), f((wide, 128), f32)),
        in_specs=[VM, VM, VM, VM, ANY, VM, VM, VM, VM, VM, VM, VM, ANY, ANY], out_specs=(VM,) * 7,
        scratch_shapes=[vm((2, 2) + out_all.shape[1:], b16), vm((tok, width), b16), vm((8, tok, 256), b16), vm((rows, 128), b16)]
        + [vm((2, rows, 128), b16)] * 4 + [vm((128, rows), b16), vm((128, rows), f32)] + [vm((rows, 128), f32)] * 6
        + [vm((8, tok, width), b16), vm((7 * tok, width), b16), vm((tok, width), f32)]
        + [vm((16, wide, 128), b16), vm((8, wide, 128), b16), vm((7 * wide, 128), b16)]
        + [dma(n) for n in (8, 8, 8, 8, 17, 17, 17, 17, 8, 8, 2, 3)],
        compiler_params=params(cid), name="back",
    )(dh2, mid, dy, gain, out_all, q, k, v, start, ot, lse, cs, ffp, joined)
SPLIT_Z, SPLIT_O, SPLIT_Q, SPLIT_T = 96, 96, 288, 192

def last_kernel(dproj, hw, rn, att, da, mgrad, x, gain, bias, sums2,
                input_grad, out_grad, qkv_grad, small,
                dpt, dh1p, dtland, dland, dsum, o_all, dac, dact, qp, qland, qr, qs, qin, op, otland, oland, sm, smt, smc, smw, smx,
                ssZ, rsZ, tsZ, trZ, ssO, rsO, ssS, rsS, ssQ, rsQ, ssP, rsP, lsP, ssT, rsT, tsT, trT, ssM, rsM, ssW, rsW, ssX, rsX, ls):
    sp, wp = Plane("seq"), Plane("wt")
    tok, width = x.shape
    s, w = lax.axis_index("seq"), lax.axis_index("wt")
    c, m = sp.c, sp.block(0, 0)
    no = jnp.logical_not
    chips = [at(j // 4, j % 4, c, wp.a, wp.b) for j in range(8)]
    bar = pltpu.get_barrier_semaphore()
    for j in range(8):
        @pl.when(m != j)
        def _():
            pl.semaphore_signal(bar, inc=1, device_id=chips[j], device_id_type=MESH)
    pl.semaphore_signal(bar, inc=1, device_id=sp.twin, device_id_type=MESH)
    for d in range(1, 8):
        pl.semaphore_signal(bar, inc=1, device_id={"wt": lax.rem(w + d, 8)}, device_id_type=MESH)
    def source(b):
        return lax.rem(6 * w + b, 16), s // 2
    def target(i, p):
        g = 16 * p + s
        return 2 * w + i, g // 6, lax.rem(g, 6)
    own = jnp.int32(0)
    for b in range(6):
        ts, tw = source(b)
        same = (ts == s) & (tw == w)
        own += same.astype(jnp.int32)
        @pl.when(no(same))
        def _():
            pl.semaphore_signal(bar, inc=1, device_id={"seq": ts, "wt": tw}, device_id_type=MESH)
    dpt[...] = dproj[...].astype(jnp.float32).T.astype(jnp.bfloat16)
    mine = [pltpu.make_async_copy(att, o_all.at[wp.block(0, 0)], ls.at[0]),
            pltpu.make_async_copy(da.at[:, pl.ds(pl.multiple_of(256 * w, 256), 256)], dac.at[w], ls.at[1])]
    for cp in mine:
        cp.start()
    pl.semaphore_wait(bar, 21 - own)
    O = Gather(wp, att, o_all, tok, ssO, rsO, None, SPLIT_O)
    O.steps[0]()
    def column(d, j):
        return pltpu.make_async_remote_copy(src_ref=da.at[:, pl.ds(pl.multiple_of(256 * j, 256), 256)], dst_ref=dac.at[w], send_sem=ssS.at[d - 1], recv_sem=rsS.at[d - 1],
                                            device_id={"wt": j}, device_id_type=MESH)
    for d in range(1, 8):
        column(d, lax.rem(w + d, 8)).start()
    Z = ScatterBoth(sp, dh1p, dtland, dland, ssZ, rsZ, tsZ, trZ, dsum, SPLIT_Z)
    order = [(2, 0), (2, 1), (-1, 1), (1, 1), (-1, 0), (1, 0), (0, 1), (0, 0)]
    for k in range(8):
        j = sp.block(*order[k])
        y = lax.dot_general(dproj[pl.ds(pl.multiple_of(256 * j, 256), 256)], hw[...], NT, preferred_element_type=jnp.float32)
        dh1p[pl.ds(2 * j, 2)] = y.astype(jnp.bfloat16).reshape(2, tok, width)
        Z.sends[k]()
        if k:
            Z.adds[k - 1]()
    Z.adds[7]()
    z, o = iter(Z.sums), iter(O.steps[1:])
    pump(z, o, o, o, o)
    def qkv(j):
        y = jnp.dot(dpt[...], rn[:, :, 256 * j:256 * j + 256].reshape(16 * tok, 256), preferred_element_type=jnp.float32)
        qp[j] = y.astype(jnp.bfloat16)
    qkv(0); qkv(1); pump(o, z); qkv(2); qkv(3); pump(o, z); qkv(4); qkv(5); pump(o, o); qkv(6); qkv(7)
    Q, qdone = sum_steps(wp, qp, qland, qp.shape[1], ssQ, rsQ, qr, split=SPLIT_Q)
    q = iter(Q)
    pump(q, z, o, o, o, q, z, o, q, o, o, q, z, o, o, q, o, q, o, o, o)
    for f in o:
        f()
    for cp in mine:
        cp.wait()
    for d in range(1, 8):
        j = lax.rem(w - d + 8, 8)
        pltpu.make_async_remote_copy(src_ref=dac.at[j], dst_ref=dac.at[j], send_sem=ssS.at[d - 1], recv_sem=rsS.at[d - 1], device_id={"wt": j}, device_id_type=MESH).wait_recv()
    dact[...] = dac[...].reshape(8 * tok, 256).astype(jnp.float32).T.astype(jnp.bfloat16)
    T = ScatterBoth(sp, op, otland, oland, ssT, rsT, tsT, trT, out_grad, SPLIT_T)
    for j in range(8):
        y = jnp.dot(dact[...], o_all[:, :, 256 * j:256 * j + 256].reshape(8 * tok, 256), preferred_element_type=jnp.float32).astype(jnp.bfloat16)
        op[2 * j] = y[:, :128]
        op[2 * j + 1] = y[:, 128:]
    for f in T.sends:
        f()
    pump(q, z)
    for f in T.adds:
        f()
    t = iter(T.sums)
    pump(t, z)
    for f in q:
        f()
    for i in range(2):
        for p in range(3):
            qs[i, p] = qr[128 * p:128 * p + 128, 128 * i:128 * i + 128].astype(jnp.bfloat16)
    def place(i, p, which):
        ts, tw, slot = target(i, p)
        same = (ts == s) & (tw == w)
        @pl.when(same)
        def _():
            cp = pltpu.make_async_copy(qs.at[i, p], qin.at[slot], lsP.at[i, p])
            cp.start() if which == "start" else cp.wait()
        @pl.when(no(same))
        def _():
            cp = pltpu.make_async_remote_copy(src_ref=qs.at[i, p], dst_ref=qin.at[slot], send_sem=ssP.at[i, p], recv_sem=rsP.at[slot], device_id={"seq": ts, "wt": tw}, device_id_type=MESH)
            cp.start() if which == "start" else cp.wait_send()
    for i in range(2):
        for p in range(3):
            place(i, p, "start")
    for f in z:
        f()
    def ln(i, carry):
        r = pl.ds(pl.multiple_of(i * 32, 32), 32)
        y = x[r].astype(jnp.float32)
        centred = y - jnp.mean(y, axis=-1, keepdims=True)
        inverse = lax.rsqrt(jnp.mean(centred * centred, axis=-1, keepdims=True) + norm_eps)
        scaled = centred * inverse
        up = dsum[r]
        wgt = up * gain[...]
        back = inverse * (wgt - jnp.mean(wgt, axis=-1, keepdims=True) - scaled * jnp.mean(wgt * scaled, axis=-1, keepdims=True))
        input_grad[r] = (mgrad[r] + back).astype(jnp.bfloat16)
        return carry[0] + jnp.sum((up * scaled).reshape(4, 8, width), axis=0), carry[1] + jnp.sum(up.reshape(4, 8, width), axis=0)
    nil = jnp.zeros((8, width), jnp.float32)
    gsum, ssum = lax.fori_loop(0, tok // 32, ln, (nil, nil))
    four = jnp.concatenate([jnp.sum(gsum, axis=0, keepdims=True), jnp.sum(ssum, axis=0, keepdims=True), sums2[...], jnp.zeros((4, width), jnp.float32)], axis=0)
    for j in range(16):
        sm[j % 2, j // 2] = four[:, 128 * j:128 * j + 128]
    for p in range(3):
        g = 16 * p + s
        sm[lax.rem(g // 3, 2), g // 6, pl.ds(4 + lax.rem(g, 3), 1)] = bias[:, 128 * p:128 * p + 128]
    def twin_small():
        return remote(sm.at[1 - c], smt, ssM, rsM, 0, sp.twin)
    twin_small().start()
    pump(t, t)
    twin_small().wait_recv()
    smc[...] = sm[c] + smt[...]
    def chip_small(j):
        return pltpu.make_async_remote_copy(src_ref=smc.at[j], dst_ref=smw.at[m], send_sem=ssW.at[j], recv_sem=rsW.at[m], device_id=chips[j], device_id_type=MESH)
    smw[m] = smc[m]
    for j in range(8):
        @pl.when(m != j)
        def _():
            chip_small(j).start()
    pump(t, t)
    for j in range(8):
        @pl.when(m != j)
        def _():
            pltpu.make_async_remote_copy(src_ref=smw.at[j], dst_ref=smw.at[j], send_sem=ssW.at[j], recv_sem=rsW.at[j], device_id=chips[j], device_id_type=MESH).wait_recv()
    smx[0] = jnp.sum(smw[...], axis=0)
    def row_small(d):
        return remote(smx.at[0], smx.at[d], ssX, rsX, d - 1, {"wt": lax.rem(w + d, 8)})
    for d in range(1, 8):
        row_small(d).start()
    for f in t:
        f()
    for b in range(6):
        ts, tw = source(b)
        @pl.when(no((ts == s) & (tw == w)))
        def _():
            pltpu.make_async_remote_copy(src_ref=qin.at[b], dst_ref=qin.at[b], send_sem=ssP.at[0, 0], recv_sem=rsP.at[b], device_id={"seq": ts, "wt": tw}, device_id_type=MESH).wait_recv()
    for i in range(2):
        for p in range(3):
            place(i, p, "wait")
    for b in range(6):
        qkv_grad[:, 128 * b:128 * b + 128] = qin[b].astype(jnp.float32).T
    for d in range(1, 8):
        row_small(d).wait()
    small[...] = jnp.sum(smx[...], axis=0)
    O.finish()
    qdone()
    Z.finish()
    T.finish()
    twin_small().wait_send()
    for j in range(8):
        @pl.when(m != j)
        def _():
            chip_small(j).wait_send()
    for d in range(1, 8):
        column(d, lax.rem(w + d, 8)).wait_send()

def last_part(cid, dproj, hw, rn, att, da, mgrad, x, gain, bias, sums2):
    tok, width = x.shape
    f, b16, f32, vm = jax.ShapeDtypeStruct, jnp.bfloat16, jnp.float32, pltpu.VMEM
    return pl.pallas_call(
        last_kernel,
        out_shape=(f((tok, width), b16), f((256, 128), f32), f((128, 768), f32), f((8, 128), f32)),
        in_specs=[VM] * 10, out_specs=(VM,) * 4,
        scratch_shapes=[vm((384, 16 * tok), b16), vm((16, tok, width), b16), vm((8, tok, width), b16), vm((7 * tok, width), b16), vm((tok, width), f32),
                        vm((8, tok, width), b16), vm((8, tok, 256), b16), vm((256, 8 * tok), b16), vm((8, 384, 256), b16), vm((7 * 384, 256), b16), vm((384, 256), f32),
                        vm((2, 3, 128, 128), b16), vm((6, 128, 128), b16), vm((16, 256, 128), b16), vm((8, 256, 128), b16), vm((7 * 256, 128), b16),
                        vm((2, 8, 8, 128), f32), vm((8, 8, 128), f32), vm((8, 8, 128), f32), vm((8, 8, 128), f32), vm((8, 8, 128), f32)]
        + [dma(n) for n in (17, 17, 8, 8, 18, 18, 7, 7, 17, 17)] + [pltpu.SemaphoreType.DMA((2, 3)), dma(6), pltpu.SemaphoreType.DMA((2, 3))]
        + [dma(n) for n in (17, 17, 8, 8, 1, 1, 8, 8, 7, 7, 2)],
        compiler_params=params(cid), name="last",
    )(dproj, hw, rn, att, da, mgrad, x, gain, bias, sums2)
def params(cid):
    return pltpu.CompilerParams(collective_id=cid, has_side_effects=True, vmem_limit_bytes=56 * 2**20)

def dma(n):
    return pltpu.SemaphoreType.DMA((n,))

norm_eps = 1e-05
theta_base = 10000.0
ROT = 16
HEAD_DIM = 64


def rotary_angles(segment_row):
    rows = segment_row.shape[0]
    ends = [jnp.sum((segment_row < i).astype(jnp.int32)) for i in (1, 2)]
    start = jnp.where(segment_row == 0, 0, jnp.where(segment_row == 1, ends[0], ends[1]))
    offsets = (jnp.arange(rows, dtype=jnp.int32) - start).astype(jnp.float32)
    inv_freq = jnp.exp(jnp.arange(ROT // 2, dtype=jnp.float32) * (-2.0 * math.log(theta_base) / ROT))
    angles = inv_freq[:, None] * offsets[None, :]
    return start.reshape(1, rows), jnp.concatenate([jnp.cos(angles), jnp.sin(angles)], axis=0)


def per_device(layer_in, segment_ids, norm_one_gain, norm_one_shift, qkv_weight, qkv_bias, out_weight, norm_two_gain,
               norm_two_shift, gate_up_weight, down_weight, layer_grad):
    f32, bf16 = jnp.float32, jnp.bfloat16
    s, w = lax.axis_index("seq"), lax.axis_index("wt")
    tok, width = layer_in.shape[1:]
    rows = segment_ids.shape[1]
    hidden = down_weight.shape[0]
    upstream = layer_grad.reshape(tok, width)
    start, cs = rotary_angles(segment_ids.reshape(rows))
    bias = lax.dynamic_index_in_dim(qkv_bias.reshape(3, 16, 128), s, 1, keepdims=False).reshape(1, 384)
    half = lax.dynamic_slice_in_dim(out_weight, (s % 2) * (width // 2), width // 2, 0)
    row_normed, head_weight, q, k, v, ot, lse, attended, out_all, all_up = front(
        0, layer_in.reshape(tok, width), norm_one_gain.reshape(1, width), norm_one_shift.reshape(1, width), qkv_weight, bias, cs, start, upstream, half)
    out_all = out_all.reshape(8, 2, width // 2, 256)
    middle, dh2, ffn_part, joined = middle_part(
        4, attended, layer_in.reshape(tok, width), out_all.reshape(16, width // 2, 256), norm_two_gain.reshape(1, width),
        norm_two_shift.reshape(1, width), all_up, gate_up_weight.transpose(1, 2, 0).reshape(2 * hidden, width), down_weight)
    middle_grad, da, dproj, bias_sum, sums_two, layer_out, joined = back_part(
        6, dh2, middle, upstream, norm_two_gain.reshape(1, width), out_all.reshape(16, width // 2, 256), q, k, v, start, ot, lse, cs, ffn_part, joined)
    layer_out = layer_out.reshape(1, tok, width)
    input_grad, out_grad, qkv_grad, small = last_part(
        9, dproj, head_weight, row_normed, attended, da, middle_grad, layer_in.reshape(tok, width), norm_one_gain.reshape(1, width), bias_sum, sums_two)
    gate_grad = joined[:2 * hidden].reshape(2, hidden, 128).transpose(2, 0, 1)
    down_grad = joined[2 * hidden:]
    norms = lax.dynamic_slice_in_dim(small[:4], 16 * w, 16, 1)
    bias_grad = lax.dynamic_slice_in_dim(small[4:7].reshape(384), 48 * w, 48, 0)
    return (layer_out, input_grad.reshape(1, tok, width), norms[0], norms[1], qkv_grad, bias_grad, out_grad.T, norms[2], norms[3], gate_grad, down_grad)


def solution(mesh):
    both = P(("seq", "wt"))
    return jax.shard_map(
        per_device, mesh=mesh,
        in_specs=(P("wt", "seq", None), P("wt", None), P(), P(), P(None, "wt"), P(), P(None, "wt"), P(), P(), P(None, None, "wt"), P("wt", None), P("wt", "seq", None)),
        out_specs=(P("wt", "seq", None), P("wt", "seq", None), both, both, P("seq", "wt"), both, P("seq", "wt"), both, both, P("seq", None, "wt"), P("wt", "seq")),
        check_vma=False)
```

```python
import functools, math
import jax, jax.numpy as jnp
from jax import lax
from jax.experimental import pallas as pl
from jax.experimental.pallas import tpu as pltpu
from jax.sharding import PartitionSpec as P

MESH = pl.DeviceIdType.MESH

def coords():
    s = lax.axis_index("seq")
    w = lax.axis_index("wt")
    return s // 8, lax.rem(s // 2, 4), lax.rem(s, 2), w // 2, lax.rem(w, 2)

def at(yh, z, c, x, yl):
    return {"seq": yh * 8 + z * 2 + c, "wt": x * 2 + yl}

class Plane:
    def __init__(self, axis):
        self.axis = axis
        yh, z, c, x, yl = coords()
        self.c = c
        if axis == "wt":
            self.a, self.b = x, yl
            move = lambda da, db: at(yh, z, c, lax.rem(x + da + 4, 4), lax.rem(yl + db, 2))
        else:
            self.a, self.b = z, yh
            move = lambda da, db: at(lax.rem(yh + db, 2), lax.rem(z + da + 4, 4), c, x, yl)
        self.left, self.right, self.pair = move(-1, 0), move(1, 0), move(0, 1)
        self.twin = at(yh, z, 1 - c, x, yl)

    def block(self, da, db):
        a, b = lax.rem(self.a + da + 4, 4), lax.rem(self.b + db, 2)
        return a * 2 + b if self.axis == "wt" else b * 4 + a

def cuts(rows, split):
    p = split or rows // 2
    q = rows - p
    return (0, p), (p, q), (0, p // 2), (p // 2, p // 2), (p, q // 2), (p + q // 2, q // 2)

def remote(src, dst, ssem, rsem, k, target):
    return pltpu.make_async_remote_copy(src_ref=src, dst_ref=dst, send_sem=ssem.at[k], recv_sem=rsem.at[k], device_id=target, device_id_type=MESH)

def greet(targets):
    bar = pltpu.get_barrier_semaphore()
    for t in targets:
        pl.semaphore_signal(bar, inc=1, device_id=t, device_id_type=MESH)
    pl.semaphore_wait(bar, len(targets))

def repeat(n, body):
    if n == 1:
        body(0, 0)
    else:
        lax.fori_loop(0, n, body, 0)

def pace(rows, cols):
    return max(n for n in range(16, rows + 1, 16) if rows % n == 0 and n * cols <= 300000)

def gather_steps(pn, own, buf, rows, ssem, rsem, index=lambda j: j, split=None):
    P_, Q_, P0, P1, Q0, Q1 = cuts(rows, split)
    L, Rt, Y = pn.left, pn.right, pn.pair
    table = {
        0: (Y, (0, 0), P_, (0, 1)),
        1: (Rt, (0, 0), Q_, (-1, 0)),
        2: (L, (0, 0), Q_, (1, 0)),
        3: (Rt, (0, 0), P_, (-1, 0)),
        4: (L, (0, 0), P_, (1, 0)),
        5: (Y, (0, 0), Q_, (0, 1)),
        6: (Rt, (-1, 0), Q0, (2, 0)),
        7: (Y, (-1, 0), Q_, (-1, 1)),
        8: (L, (1, 0), Q1, (2, 0)),
        9: (Y, (1, 0), Q_, (1, 1)),
        10: (Rt, (0, 1), P_, (-1, 1)),
        11: (L, (0, 1), P_, (1, 1)),
        12: (Rt, (-1, 0), P0, (2, 0)),
        13: (L, (1, 0), P1, (2, 0)),
        14: (Y, (2, 0), Q0, (2, 1)),
        15: (Y, (2, 0), Q1, (2, 1)),
        16: (Rt, (-1, 1), P0, (2, 1)),
        17: (L, (1, 1), P1, (2, 1)),
    }
    def part(d, r):
        return buf.at[index(pn.block(*d)), pl.ds(*r)]
    def send(k):
        t, d, r, _ = table[k]
        if not r[1]:
            return
        src = own.at[pl.ds(*r)] if d == (0, 0) else part(d, r)
        remote(src, part(d, r), ssem, rsem, k, t).start()
    def got(k):
        t, _, r, d = table[k]
        if not r[1]:
            return
        remote(part(d, r), part(d, r), ssem, rsem, k, t).wait_recv()
    def sent(k):
        t, d, r, _ = table[k]
        if not r[1]:
            return
        remote(part(d, r), part(d, r), ssem, rsem, k, t).wait_send()
    def first():
        for k in (0, 1, 2, 3, 4, 5): send(k)
    def after(k, *next_):
        def f():
            got(k)
            for n in next_: send(n)
        return f
    steps = [first, after(1, 6, 7), after(2, 8, 9), after(0, 10, 11), after(3, 12), after(4, 13),
             after(6, 14), after(8, 15), after(10, 16), after(11, 17)]
    tail = [after(5), after(7), after(9), after(12), after(13), after(14), after(15), after(16), after(17)]
    def done():
        for k in range(18): sent(k)
    return steps, tail, done

def sum_steps(pn, buf, land, rows, ssem, rsem, out, index=lambda j: j, split=None):
    P_, Q_, P0, P1, Q0, Q1 = cuts(rows, split)
    L, Rt, Y = pn.left, pn.right, pn.pair
    table = {}
    off = 0
    def msg(k, t, d, r, r_to):
        nonlocal off
        table[k] = (t, d, r, off, r_to)
        off += r[1]
    msg(0, L, (-2, 0), P0, (-1, 0)); msg(1, Rt, (2, 0), P1, (1, 0))
    msg(2, L, (-2, 1), P0, (-1, 1)); msg(3, Rt, (2, 1), P1, (1, 1))
    msg(4, Y, (2, 1), Q_, (2, 0)); msg(5, Y, (-1, 1), Q_, (-1, 0)); msg(6, Y, (1, 1), Q_, (1, 0)); msg(7, Y, (0, 1), Q_, (0, 0))
    msg(8, L, (-1, 1), P_, (0, 1)); msg(9, Rt, (1, 1), P_, (0, 1))
    msg(10, L, (-1, 0), P_, (0, 0)); msg(11, Rt, (1, 0), P_, (0, 0))
    msg(12, L, (-2, 0), Q0, (-1, 0)); msg(13, Rt, (2, 0), Q1, (1, 0))
    msg(14, L, (-1, 0), Q_, (0, 0)); msg(15, Rt, (1, 0), Q_, (0, 0))
    msg(16, Y, (0, 1), P_, (0, 0))
    assert off <= land.shape[0]
    def part(d, r):
        return buf.at[index(pn.block(*d)), pl.ds(*r)]
    def landing(k):
        _, _, r, o, _ = table[k]
        return land.at[pl.ds(o, r[1])]
    def send(k):
        t, d, r, _, _ = table[k]
        if not r[1]:
            return
        remote(part(d, r), landing(k), ssem, rsem, k, t).start()
    def got(k):
        if not table[k][2][1]:
            return
        remote(landing(k), landing(k), ssem, rsem, k, table[k][0]).wait_recv()
    def sent(k):
        if not table[k][2][1]:
            return
        remote(landing(k), landing(k), ssem, rsem, k, table[k][0]).wait_send()
    def accumulate(d, r, ks, to=None):
        if not r[1]:
            return
        j = index(pn.block(*d))
        step = pace(r[1], buf.shape[2])
        def body(i, _):
            at_ = pl.multiple_of(r[0] + i * step, 16)
            v = buf[j, pl.ds(at_, step)].astype(jnp.float32)
            for k in ks:
                v = v + land[pl.ds(pl.multiple_of(table[k][3] + i * step, 16), step)].astype(jnp.float32)
            if to is None:
                buf[j, pl.ds(at_, step)] = v.astype(buf.dtype)
            else:
                to[pl.ds(at_, step)] = v.astype(to.dtype)
            return 0
        repeat(r[1] // step, body)
    def s0():
        for k in range(8): send(k)
    def s1():
        got(2); accumulate((-1, 1), P0, [2]); send(8)
        got(3); accumulate((1, 1), P1, [3]); send(9)
    def s2():
        got(0); accumulate((-1, 0), P0, [0]); send(10)
        got(1); accumulate((1, 0), P1, [1]); send(11)
    def s3():
        got(4); accumulate((2, 0), Q_, [4]); send(12); send(13)
    def s4():
        got(5); accumulate((-1, 0), Q_, [5]); got(12); accumulate((-1, 0), Q0, [12]); send(14)
        got(6); accumulate((1, 0), Q_, [6]); got(13); accumulate((1, 0), Q1, [13]); send(15)
    def s5():
        got(8); got(9); accumulate((0, 1), P_, [8, 9]); send(16)
    def s6():
        got(7); got(14); got(15); accumulate((0, 0), Q_, [7, 14, 15], out)
        got(10); got(11); got(16); accumulate((0, 0), P_, [10, 11, 16], out)
    def done():
        for k in range(17): sent(k)
    return [s0, s1, s2, s3, s4, s5, s6], done
ANY = pl.BlockSpec(memory_space=pl.ANY)
QB, KB = 512, 512
MASKED = -1e30
NT = (((1,), (1,)), ((), ()))

def halves(ref, kept):
    lane = lax.broadcasted_iota(jnp.int32, (1, 128), 1)
    low = (lane < 64).astype(jnp.float32)
    v = ref[...].astype(jnp.float32)
    kept[0] = (v * low).astype(jnp.bfloat16)
    kept[1] = (v * (1.0 - low)).astype(jnp.bfloat16)

def allowed(i, j, start):
    key = j * KB + lax.broadcasted_iota(jnp.int32, (KB, QB), 0)
    query = i * QB + lax.broadcasted_iota(jnp.int32, (KB, QB), 1)
    return (key <= query) & (key >= start)

VM = pl.BlockSpec(memory_space=pltpu.VMEM)

SPLIT_A, SPLIT_C, SPLIT_D = 128, 96, 96
ORDER = [(0, 0), (0, 1), (-1, 1), (1, 1), (-1, 0), (1, 0), (2, 0), (2, 1)]

class Gather:
    def __init__(self, pn, own, buf, rows, ss, rs, twin=None, split=None):
        self.pn, self.buf, self.twin = pn, buf, twin
        self.index = (lambda j: 2 * j + pn.c) if twin else (lambda j: j)
        steps, tail, done = gather_steps(pn, own, buf, rows, ss, rs, self.index, split)
        self.done = done
        ready = {0: [1], 1: [2], 2: [3], 3: [4], 4: [5], 6: [6], 8: [7]}
        def follow(i, f):
            def g():
                f()
                for k in ready.get(i, []):
                    self.hand(k)
            return g
        def first():
            steps[0]()
            self.hand(0)
        self.steps = [first] + steps[1:] + [follow(i, f) for i, f in enumerate(tail)]

    def handed(self, k, mine):
        c = self.pn.c if mine else 1 - self.pn.c
        j = self.buf.at[2 * self.pn.block(*ORDER[k]) + c]
        return remote(j, j, self.twin[0], self.twin[1], k, self.pn.twin)

    def hand(self, k):
        if self.twin:
            self.handed(k, True).start()

    def wait_twin(self, k):
        self.handed(k, False).wait_recv()

    def finish(self, waited=()):
        self.done()
        if self.twin:
            for k in range(8):
                self.handed(k, True).wait_send()
                if k not in waited:
                    self.wait_twin(k)

def fetch_steps(pn, weight, hw, ss, rs, ls):
    s = lax.axis_index("seq")
    rows = hw.shape[0]
    h, q = rows // 2, rows // 4
    W = {"P": (0, h), "Q": (h, h), "P0": (0, q), "P1": (q, q), "Q0": (h, q), "Q1": (h + q, q)}
    kinds = ["P", "P0", "P1", "Q", "Q0", "Q1"]
    both = []
    for p in range(3):
        g = 16 * p + s
        src = g // 6
        da = lax.rem(pn.a - src // 2 + 4, 4)
        b0 = pn.b == lax.rem(src, 2)
        both.append((p, lax.rem(g, 6), da, b0))
    def part(p, kind):
        return hw.at[pl.ds(*W[kind]), pl.ds(128 * p, 128)]
    def send(p, kind, slot, target):
        pltpu.make_async_remote_copy(src_ref=part(p, kind), dst_ref=part(p, kind), send_sem=ss.at[6 * p + slot],
                                     recv_sem=rs.at[6 * p + kinds.index(kind)], device_id=target, device_id_type=MESH).start()
    def wait(p, kind, slot=None):
        cp = pltpu.make_async_remote_copy(src_ref=part(p, kind), dst_ref=part(p, kind), send_sem=ss.at[6 * p + (slot or 0)],
                                          recv_sem=rs.at[6 * p + kinds.index(kind)], device_id=pn.right, device_id_type=MESH)
        cp.wait_recv() if slot is None else cp.wait_send()
    no = jnp.logical_not
    def local(p, b):
        return pltpu.make_async_copy(weight.at[:, pl.ds(pl.multiple_of(128 * b, 128), 128)], hw.at[:, pl.ds(128 * p, 128)], ls.at[p])
    def begin():
        for p, b, da, b0 in both:
            @pl.when(b0 & (da == 0))
            def _():
                local(p, b).start()
    def st0():
        for p, b, da, b0 in both:
            @pl.when(b0 & (da == 0))
            def _():
                local(p, b).wait()
                send(p, "Q", 0, pn.right); send(p, "Q", 1, pn.left); send(p, "P", 5, pn.pair)
                send(p, "P", 3, pn.right); send(p, "P", 4, pn.left); send(p, "Q", 2, pn.pair)
    def st1():
        for p, b, da, b0 in both:
            @pl.when(b0 & (da == 1))
            def _():
                wait(p, "Q"); send(p, "Q0", 0, pn.right); send(p, "Q", 2, pn.pair)
            @pl.when(b0 & (da == 3))
            def _():
                wait(p, "Q"); send(p, "Q1", 1, pn.left); send(p, "Q", 2, pn.pair)
            @pl.when(no(b0) & (da == 0))
            def _():
                wait(p, "P"); send(p, "P", 3, pn.right); send(p, "P", 4, pn.left)
    def st2():
        for p, b, da, b0 in both:
            @pl.when(da == 1)
            def _():
                wait(p, "P"); send(p, "P0", 3, pn.right)
            @pl.when(da == 3)
            def _():
                wait(p, "P"); send(p, "P1", 4, pn.left)
    def st3():
        for p, b, da, b0 in both:
            @pl.when(b0 & (da == 2))
            def _():
                wait(p, "Q0"); wait(p, "Q1"); send(p, "Q", 2, pn.pair)
    def st4():
        for p, b, da, b0 in both:
            @pl.when(da == 2)
            def _():
                wait(p, "P0"); wait(p, "P1")
            @pl.when(no(b0))
            def _():
                wait(p, "Q")
    def done():
        for p, b, da, b0 in both:
            @pl.when(b0)
            def _():
                wait(p, "Q", 2)
            @pl.when(b0 & (da == 0))
            def _():
                wait(p, "Q", 0); wait(p, "Q", 1); wait(p, "P", 5)
            @pl.when(da == 0)
            def _():
                wait(p, "P", 3); wait(p, "P", 4)
            @pl.when(b0 & (da == 1))
            def _():
                wait(p, "Q0", 0)
            @pl.when(b0 & (da == 3))
            def _():
                wait(p, "Q1", 1)
            @pl.when(da == 1)
            def _():
                wait(p, "P0", 3)
            @pl.when(da == 3)
            def _():
                wait(p, "P1", 4)
    return begin, [st0, st1, st2, st3, st4], done

def turn(v, keep, ahead, behind):
    return v * keep + pltpu.roll(v, 120, 1) * ahead + pltpu.roll(v, 8, 1) * behind

def norm_rows(x, gain, shift):
    average = jnp.mean(x, axis=-1, keepdims=True)
    centred = x - average
    inverse = lax.rsqrt(jnp.mean(centred * centred, axis=-1, keepdims=True) + norm_eps)
    return centred * inverse * gain + shift

def rotary_tables_to(cs, tables):
    rows = cs.shape[1]
    c, s = cs[0:8, :], cs[8:16, :]
    one, nil, z8 = jnp.ones((48, rows), jnp.float32), jnp.zeros((48, rows), jnp.float32), jnp.zeros((8, rows), jnp.float32)
    tables[0][...] = jnp.concatenate([c, c, one] * 2, axis=0).T
    tables[1][...] = jnp.concatenate([-s, z8, nil] * 2, axis=0).T
    tables[2][...] = jnp.concatenate([z8, s, nil] * 2, axis=0).T

def pump(*its):
    for it in its:
        f = next(it, None)
        if f is not None:
            f()

def front_kernel(x, gain, shift, weight, bias, cs, start_ref, dy, ow,
                 rn, hw, q_ref, k_ref, v_ref, ot_ref, lse_ref, att, out_all, dy_all,
                 own, owr, kept, vt, t0, t1, t2, ob, ox,
                 ssA, rsA, tsA, trA, ssB, rsB, lsB, ssC, rsC, ssD, rsD, tsD, trD, ssR, rsR, ssO, rsO, ssT, rsT, lsO, ls):
    sp, wp = Plane("seq"), Plane("wt")
    tok = x.shape[0]
    c, m = sp.c, sp.block(0, 0)
    A = Gather(sp, own, rn, tok, ssA, rsA, (tsA, trA), SPLIT_A)
    begin, fetch, fetch_done = fetch_steps(wp, weight, hw, ssB, rsB, lsB)
    C = Gather(wp, dy, dy_all, tok, ssC, rsC, None, SPLIT_C)
    D = Gather(sp, owr, out_all, tok, ssD, rsD, (tsD, trD), SPLIT_D)
    begin()
    chips = [at(j // 4, j % 4, c, wp.a, wp.b) for j in range(8)]
    bar = pltpu.get_barrier_semaphore()
    for j in range(8):
        @pl.when(m != j)
        def _():
            pl.semaphore_signal(bar, inc=1, device_id=chips[j], device_id_type=MESH)
    pl.semaphore_signal(bar, inc=1, device_id=sp.twin, device_id_type=MESH)
    me = lax.axis_index("wt")
    for d in range(1, 8):
        pl.semaphore_signal(bar, inc=1, device_id={"wt": lax.rem(me + d, 8)}, device_id_type=MESH)
    def ln(i, _):
        r = pl.ds(pl.multiple_of(i * 16, 16), 16)
        own[r] = norm_rows(x[r].astype(jnp.float32), gain[...], shift[...]).astype(jnp.bfloat16)
        return 0
    lax.fori_loop(0, tok // 16, ln, 0)
    strip = ow.at[pl.ds(pl.multiple_of(128 * (2 * m + c), 128), 128)]
    copies = [pltpu.make_async_copy(own, rn.at[2 * m + c], ls.at[0]),
              pltpu.make_async_copy(dy, dy_all.at[wp.block(0, 0)], ls.at[1]),
              pltpu.make_async_copy(strip, owr.at[:, pl.ds(pl.multiple_of(256 * me, 256), 256)], ls.at[2])]
    for cp in copies:
        cp.start()
    copies[0].wait()
    pl.semaphore_wait(bar, 15)
    A.steps[0]()
    fetch[0]()
    def strips(d, j):
        return pltpu.make_async_remote_copy(src_ref=strip, dst_ref=owr.at[:, pl.ds(pl.multiple_of(256 * me, 256), 256)], send_sem=ssR.at[d - 1], recv_sem=rsR.at[d - 1],
                                            device_id={"wt": j}, device_id_type=MESH)
    for d in range(1, 8):
        strips(d, lax.rem(me + d, 8)).start()
    rotary_tables_to(cs, (t0, t1, t2))
    copies[1].wait()
    def rows_first():
        copies[2].wait()
        for e in range(1, 8):
            j = lax.rem(me - e + 8, 8)
            there = owr.at[:, pl.ds(pl.multiple_of(256 * j, 256), 256)]
            pltpu.make_async_remote_copy(src_ref=there, dst_ref=there, send_sem=ssR.at[e - 1], recv_sem=rsR.at[e - 1], device_id={"wt": j}, device_id_type=MESH).wait_recv()
        whole = pltpu.make_async_copy(owr, out_all.at[2 * m + c], ls.at[2])
        whole.start()
        whole.wait()
        D.steps[0]()
    a, b, cc, d = iter(A.steps[1:]), iter(fetch[1:]), iter(C.steps), iter([rows_first] + D.steps[1:])
    pump(a, a, b, a, a, a, cc, b, a, a, a, a, d, b, b)
    def project(k):
        A.wait_twin(k)
        j = sp.block(*ORDER[k])
        rows = pl.ds(pl.multiple_of(j * 256, 256), 256)
        h = rn[pl.ds(2 * j, 2)].reshape(256, rn.shape[2])
        y = jnp.dot(h, hw[...], preferred_element_type=jnp.float32) + bias[...]
        tabs = (t0[rows], t1[rows], t2[rows])
        q_ref[rows] = (turn(y[:, :128], *tabs) * 0.125).astype(jnp.bfloat16)
        k_ref[rows] = turn(y[:, 128:256], *tabs).astype(jnp.bfloat16)
        v_ref[rows] = y[:, 256:].astype(jnp.bfloat16)
    project(0); pump(a, cc); project(1); pump(a, cc); project(2); pump(a, cc, cc); project(3)
    pump(a, d); project(4); pump(a, cc, d); project(5); pump(a, a, cc); project(6); pump(a, a, d); project(7)
    halves(k_ref, kept)
    pump(cc)
    vt[...] = v_ref[...].astype(jnp.float32).T.astype(jnp.bfloat16)
    def to_twin(j):
        return pltpu.make_async_remote_copy(src_ref=ox.at[j], dst_ref=ob.at[j, :, pl.ds(pl.multiple_of(128 * c, 128), 128)],
                                            send_sem=ssT.at[j], recv_sem=rsT.at[j], device_id=sp.twin, device_id_type=MESH)
    def from_twin(j):
        there = ob.at[j, :, pl.ds(pl.multiple_of(128 * (1 - c), 128), 128)]
        return pltpu.make_async_remote_copy(src_ref=there, dst_ref=there, send_sem=ssT.at[j], recv_sem=rsT.at[j], device_id=sp.twin, device_id_type=MESH)
    def cols(j):
        return att.at[:, pl.ds(pl.multiple_of(256 * j, 256), 256)]
    def to_chip(j):
        return pltpu.make_async_remote_copy(src_ref=ob.at[j], dst_ref=cols(m), send_sem=ssO.at[j], recv_sem=rsO.at[m], device_id=chips[j], device_id_type=MESH)
    def ship(i):
        for j in (2 * i, 2 * i + 1):
            from_twin(j).wait_recv()
            @pl.when(m == j)
            def _():
                pltpu.make_async_copy(ob.at[j], cols(j), lsO).start()
            @pl.when(m != j)
            def _():
                to_chip(j).start()
    n = q_ref.shape[0] // QB
    for i in range(n):
        q = q_ref[QB * i:QB * (i + 1)]
        start = start_ref[:, QB * i:QB * (i + 1)]
        step = functools.partial(attend_step, kept, vt, q, start, i)
        one = (jnp.full((1, QB), MASKED, jnp.float32), jnp.zeros((1, QB), jnp.float32), jnp.zeros((64, QB), jnp.float32))
        carry = (one, one)
        for j in range(i + 1):
            carry = step(j == 0 or j == i or i == n - 1, j, carry)
            pump(cc, d)
        where = pl.ds(QB * i, QB)
        for h in range(2):
            top, l, acc = carry[h]
            ot_ref[64 * h:64 * h + 64, where] = acc / l
            lse_ref[h:h + 1, where] = top + jnp.log(l)
        if i:
            ship(i - 1)
        o = ot_ref[:, where].T.astype(jnp.bfloat16)
        for j in (0, 1):
            mine = pl.ds(pl.multiple_of(128 * c, 128), 128)
            first, second = o[256 * j:256 * j + 128], o[256 * j + 128:256 * j + 256]
            @pl.when(c == 0)
            def _():
                ob[2 * i + j, :, 0:128] = first
                ox[2 * i + j] = second
            @pl.when(c == 1)
            def _():
                ob[2 * i + j, :, 128:256] = second
                ox[2 * i + j] = first
            to_twin(2 * i + j).start()
    ship(n - 1)
    for f in cc:
        f()
    for f in d:
        f()
    for j in range(8):
        to_twin(j).wait_send()
        @pl.when(m == j)
        def _():
            pltpu.make_async_copy(ob.at[j], cols(j), lsO).wait()
        @pl.when(m != j)
        def _():
            to_chip(j).wait_send()
            pltpu.make_async_remote_copy(src_ref=cols(j), dst_ref=cols(j), send_sem=ssO.at[j], recv_sem=rsO.at[j], device_id=chips[j], device_id_type=MESH).wait_recv()
    A.finish(range(8))
    fetch_done()
    C.finish()
    D.finish()
    for e in range(1, 8):
        strips(e, lax.rem(me + e, 8)).wait_send()

def attend_step(kept, vt, q, start, i, masked, j, carry):
    r = pl.ds(j * KB, KB)
    out = []
    for h in range(2):
        m, l, acc = carry[h]
        s = lax.dot_general(kept[h, r], q, NT, preferred_element_type=jnp.float32)
        if masked:
            s = jnp.where(allowed(i, j, start), s, MASKED)
        top = jnp.maximum(m, jnp.max(s, axis=0, keepdims=True))
        p = jnp.exp(s - top)
        fade = jnp.exp(m - top)
        l = l * fade + jnp.sum(p, axis=0, keepdims=True)
        acc = acc * fade + jnp.dot(vt[64 * h:64 * h + 64, r], p.astype(jnp.bfloat16), preferred_element_type=jnp.float32)
        out.append((top, l, acc))
    return tuple(out)

def front(cid, x, gain, shift, weight, bias, cs, start, dy, ow):
    tok, width = x.shape
    rows = start.shape[1]
    f, b16, f32 = jax.ShapeDtypeStruct, jnp.bfloat16, jnp.float32
    vm = pltpu.VMEM
    return pl.pallas_call(
        front_kernel,
        out_shape=(f((16, tok, width), b16), f((width, 384), b16), f((rows, 128), b16), f((rows, 128), b16), f((rows, 128), b16),
                   f((128, rows), f32), f((8, rows), f32), f((tok, width), b16), f((16, tok, width), b16), f((8, tok, width), b16)),
        in_specs=[VM, VM, VM, ANY, VM, VM, VM, VM, ANY], out_specs=(VM,) * 10,
        scratch_shapes=[vm((tok, width), b16), vm((tok, width), b16), vm((2, rows, 128), b16), vm((128, rows), b16)] + [vm((rows, 128), f32)] * 3
        + [vm((8, 128, 256), b16), vm((8, 128, 128), b16)]
        + [dma(n) for n in (18, 18, 8, 8, 18, 18, 3, 18, 18, 18, 18, 8, 8, 7, 7, 8, 8, 8, 8)] + [pltpu.SemaphoreType.DMA, dma(3)],
        compiler_params=params(cid), name="front",
    )(x, gain, shift, weight, bias, cs, start, dy, ow)
TN = (((0,), (0,)), ((), ()))

def middle_kernel(att, x, out_all, gain, shift, dy_all, wgu, wd,
                  mid, dh2, ffp, joined,
                  own, h2, wbuf, dga, tr, dh2p, land, jsend, tland, ssG, rsG, ssS, rsS, ssT, rsT, lsw, ls):
    wp = Plane("wt")
    tok, width = mid.shape
    hidden = wd.shape[0]
    there = Plane("seq").twin
    for t in (wp.left, wp.right, wp.pair, there):
        pl.semaphore_signal(pltpu.get_barrier_semaphore(), inc=1, device_id=t, device_id_type=MESH)
    def load(w, slot):
        return pltpu.make_async_copy(out_all.at[:, pl.ds(256 * w, 256)], wbuf.at[slot], lsw.at[slot])
    load(0, 0).start()
    for w in range(8):
        load(w, w % 2).wait()
        if w < 7:
            load(w + 1, 1 - w % 2).start()
        cols = pl.ds(256 * w, 256)
        mid[:, cols] = x[:, cols].astype(jnp.float32) + jnp.dot(att[...], wbuf[w % 2], preferred_element_type=jnp.float32)
    def ln(i, _):
        r = pl.ds(pl.multiple_of(i * 16, 16), 16)
        own[r] = norm_rows(mid[r], gain[...], shift[...]).astype(jnp.bfloat16)
        return 0
    lax.fori_loop(0, tok // 16, ln, 0)
    cp = pltpu.make_async_copy(own, h2.at[wp.block(0, 0)], ls)
    cp.start()
    pl.semaphore_wait(pltpu.get_barrier_semaphore(), 4)
    G = Gather(wp, own, h2, tok, ssG, rsG)
    part = hidden // 2
    def chunk_up(da):
        a = lax.rem(wp.a + da + 4, 4)
        cols = pl.ds(pl.multiple_of(256 * a, 256), 256)
        hc = h2[pl.ds(2 * a, 2)].reshape(2 * tok, width)
        dc = dy_all[pl.ds(2 * a, 2)].reshape(2 * tok, width)
        for i in range(2):
            r = pl.ds(i * part, part)
            r2 = pl.ds(hidden + i * part, part)
            r3 = pl.ds(2 * hidden + i * part, part)
            g = lax.dot_general(wgu[r], hc, NT, preferred_element_type=jnp.float32)
            u = lax.dot_general(wgu[r2], hc, NT, preferred_element_type=jnp.float32)
            e = lax.dot_general(wd[r], dc, NT, preferred_element_type=jnp.float32)
            sigma = 1.0 / (1.0 + jnp.exp(-g))
            gs = g * sigma
            dga[r, cols] = (e * u * sigma * (1.0 + g * (1.0 - sigma))).astype(jnp.bfloat16)
            dga[r2, cols] = (e * gs).astype(jnp.bfloat16)
            dga[r3, cols] = (gs * u).astype(jnp.bfloat16)
    def chunk_down(da):
        a = lax.rem(wp.a + da + 4, 4)
        cols = pl.ds(pl.multiple_of(256 * a, 256), 256)
        tr[...] = dga[:, cols].astype(jnp.float32).T.astype(jnp.bfloat16)
        for i in range(width // 512):
            n = pl.ds(i * 512, 512)
            y = jnp.dot(tr[:, :2 * hidden], wgu[:, n], preferred_element_type=jnp.float32).astype(jnp.bfloat16)
            dh2p[2 * a, :, n] = y[:tok]
            dh2p[2 * a + 1, :, n] = y[tok:]
            y = jnp.dot(tr[:, 2 * hidden:], wd[:, n], preferred_element_type=jnp.float32).astype(jnp.bfloat16)
            ffp[2 * a, :, n] = y[:tok]
            ffp[2 * a + 1, :, n] = y[tok:]
    S = G.steps
    S[0]()
    cp.wait()
    for f in S[1:6]:
        f()
    S[10]()
    chunk_up(0)
    S[6](); S[7]()
    chunk_down(0)
    S[8](); S[9](); S[11](); S[12]()
    chunk_up(-1)
    chunk_down(-1)
    chunk_up(1)
    chunk_down(1)
    for f in S[13:]:
        f()
    chunk_up(2)
    chunk_down(2)
    G.finish()
    R, done = sum_steps(wp, dh2p, land, tok, ssS, rsS, dh2)
    def twin(j):
        return pltpu.make_async_remote_copy(src_ref=jsend.at[j], dst_ref=tland.at[j], send_sem=ssT.at[j], recv_sem=rsT.at[j], device_id=there, device_id_type=MESH)
    def weights(i):
        f = pl.ds(512 * i, 512)
        hc, dc = h2[:, :, f].reshape(8 * tok, 512), dy_all[:, :, f].reshape(8 * tok, 512)
        for k in range(3):
            r = pl.ds(hidden * k, hidden)
            y = jnp.dot(dga[r], dc if k == 2 else hc, preferred_element_type=jnp.float32).astype(jnp.bfloat16)
            for j in range(2):
                low, high = y[:, 256 * j:256 * j + 128], y[:, 256 * j + 128:256 * j + 256]
                @pl.when(wp.c == 0)
                def _():
                    joined[2 * i + j, r] = low
                    jsend[2 * i + j, r] = high
                @pl.when(wp.c == 1)
                def _():
                    joined[2 * i + j, r] = high
                    jsend[2 * i + j, r] = low
        twin(2 * i).start()
        twin(2 * i + 1).start()
    def add(j):
        twin(j).wait_recv()
        joined[j] = (joined[j].astype(jnp.float32) + tland[j].astype(jnp.float32)).astype(jnp.bfloat16)
    R[0]()
    weights(0); R[1](); R[2]()
    weights(1); R[3]()
    add(0); add(1); R[4]()
    weights(2); R[5]()
    weights(3)
    for j in range(2, 6):
        add(j)
    R[6]()
    add(6); add(7)
    done()
    for j in range(8):
        twin(j).wait_send()

def middle_part(cid, att, x, out_all, gain, shift, dy_all, wgu, wd):
    tok, width = x.shape
    hidden = wd.shape[0]
    f, b16, f32, vm = jax.ShapeDtypeStruct, jnp.bfloat16, jnp.float32, pltpu.VMEM
    return pl.pallas_call(
        middle_kernel,
        out_shape=(f((tok, width), f32), f((tok, width), f32), f((8, tok, width), b16), f((8, 3 * hidden, 128), b16)),
        in_specs=[VM, VM, ANY, VM, VM, VM, VM, VM], out_specs=(VM,) * 4,
        scratch_shapes=[vm((tok, width), b16), vm((8, tok, width), b16), vm((2, width, 256), b16), vm((3 * hidden, 8 * tok), b16),
                        vm((2 * tok, 3 * hidden), b16), vm((8, tok, width), b16), vm((7 * tok, width), b16),
                        vm((8, 3 * hidden, 128), b16), vm((8, 3 * hidden, 128), b16)]
        + [dma(n) for n in (18, 18, 17, 17, 8, 8, 2)] + [pltpu.SemaphoreType.DMA],
        compiler_params=params(cid), name="middle",
    )(att, x, out_all, gain, shift, dy_all, wgu, wd)
class ScatterBoth:
    def __init__(self, pn, buf, tland, land, ss, rs, ts, tr, out, split=None):
        self.pn, self.tland, self.ts, self.tr = pn, tland, ts, tr
        rows, cols = buf.shape[1:]
        order = [(2, 0), (2, 1), (-1, 1), (1, 1), (-1, 0), (1, 0), (0, 1), (0, 0)]
        def send(k):
            j = pn.block(*order[k])
            remote(buf.at[2 * j + 1 - pn.c], tland.at[k], ts, tr, k, pn.twin).start()
        def add(k):
            self.copy(k).wait_recv()
            j = 2 * pn.block(*order[k]) + pn.c
            step = pace(rows, cols)
            def body(i, _):
                r = pl.ds(pl.multiple_of(i * step, 16), step)
                buf[j, r] = (buf[j, r].astype(jnp.float32) + tland[k, r].astype(jnp.float32)).astype(buf.dtype)
                return 0
            repeat(rows // step, body)
        self.sends = [functools.partial(send, k) for k in range(8)]
        self.adds = [functools.partial(add, k) for k in range(8)]
        self.sums, self.done = sum_steps(pn, buf, land, rows, ss, rs, out, lambda j: 2 * j + pn.c, split)

    def copy(self, k):
        return remote(self.tland.at[k], self.tland.at[k], self.ts, self.tr, k, self.pn.twin)

    def finish(self):
        self.done()
        for k in range(8):
            self.copy(k).wait_send()

SPLIT_F, SPLIT_J = 96, 1568

def back_kernel(dh2, mid, dy, gain, out_all, q_ref, k_ref, v_ref, start_ref, ot_ref, lse_ref, cs, ffp, joined,
                mgrad, da, dproj, bias, sums, layer_out, grads,
                wbuf, dg, inbox, do_ref, keptk, keptv, keptq, keptd, kt, dot_, dq_ref, dk_ref, dv_ref, t0, t1, t2, fbuf, fland, fsum, jbuf, jland,
                ssO, rsO, ssT, rsT, ssF, rsF, ssJ, rsJ, lsw, ls):
    sp, wp = Plane("seq"), Plane("wt")
    tok, width = dh2.shape
    c, m = sp.c, sp.block(0, 0)
    chips = [at(j // 4, j % 4, c, wp.a, wp.b) for j in range(8)]
    bar = pltpu.get_barrier_semaphore()
    for j in range(8):
        @pl.when(m != j)
        def _():
            pl.semaphore_signal(bar, inc=1, device_id=chips[j], device_id_type=MESH)
    pl.semaphore_signal(bar, inc=1, device_id=sp.twin, device_id_type=MESH)
    for t in (wp.left, wp.right, wp.pair):
        pl.semaphore_signal(bar, inc=1, device_id=t, device_id_type=MESH)
    def load(w, slot):
        return pltpu.make_async_copy(out_all.at[pl.ds(256 * w, 256)], wbuf.at[slot], lsw.at[slot])
    load(0, 0).start()
    here = [pltpu.make_async_copy(ffp, fbuf, ls.at[0]), pltpu.make_async_copy(joined, jbuf, ls.at[1])]
    for cp in here:
        cp.start()
    def ln(i, carry):
        r = pl.ds(pl.multiple_of(i * 32, 32), 32)
        y = mid[r]
        centred = y - jnp.mean(y, axis=-1, keepdims=True)
        inverse = lax.rsqrt(jnp.mean(centred * centred, axis=-1, keepdims=True) + norm_eps)
        scaled = centred * inverse
        up = dh2[r]
        w = up * gain[...]
        back = inverse * (w - jnp.mean(w, axis=-1, keepdims=True) - scaled * jnp.mean(w * scaled, axis=-1, keepdims=True))
        g = dy[r].astype(jnp.float32) + back
        mgrad[r] = g
        da[r] = g.astype(jnp.bfloat16)
        return carry[0] + jnp.sum((up * scaled).reshape(4, 8, width), axis=0), carry[1] + jnp.sum(up.reshape(4, 8, width), axis=0)
    nil = jnp.zeros((8, width), jnp.float32)
    gsum, ssum = lax.fori_loop(0, tok // 32, ln, (nil, nil))
    sums[0:1] = jnp.sum(gsum, axis=0, keepdims=True)
    sums[1:2] = jnp.sum(ssum, axis=0, keepdims=True)
    for w in range(8):
        load(w, w % 2).wait()
        if w < 7:
            load(w + 1, 1 - w % 2).start()
        dg[:, 256 * w:256 * w + 256] = lax.dot_general(da[...], wbuf[w % 2], NT, preferred_element_type=jnp.float32).astype(jnp.bfloat16)
    pl.semaphore_wait(bar, 11)
    def to_chip(j):
        return pltpu.make_async_remote_copy(src_ref=dg.at[:, pl.ds(256 * j, 256)], dst_ref=inbox.at[m], send_sem=ssO.at[j], recv_sem=rsO.at[m], device_id=chips[j], device_id_type=MESH)
    for j in range(8):
        @pl.when(m != j)
        def _():
            to_chip(j).start()
    mine = pltpu.make_async_copy(dg.at[:, pl.ds(pl.multiple_of(256 * m, 256), 256)], inbox.at[m], ls.at[2])
    mine.start()
    for cp in here:
        cp.wait()
    F, fdone = sum_steps(wp, fbuf, fland, tok, ssF, rsF, fsum, split=SPLIT_F)
    J, jdone = sum_steps(sp, jbuf, jland, joined.shape[1], ssJ, rsJ, grads, split=SPLIT_J)
    F[0]()
    rotary_tables_to(cs, (t0, t1, t2))
    halves(k_ref, keptk)
    halves(v_ref, keptv)
    halves(q_ref, keptq)
    kt[...] = k_ref[...].astype(jnp.float32).T.astype(jnp.bfloat16)
    dk_ref[...] = jnp.zeros_like(dk_ref)
    dv_ref[...] = jnp.zeros_like(dv_ref)
    mine.wait()
    def pass_on(j, own):
        r = do_ref.at[pl.ds(pl.multiple_of(128 * (2 * j + (c if own else 1 - c)), 128), 128)]
        src = inbox.at[j, :, pl.ds(pl.multiple_of(128 * (1 - c), 128), 128)] if own else r
        return pltpu.make_async_remote_copy(src_ref=src, dst_ref=r, send_sem=ssT.at[j], recv_sem=rsT.at[j], device_id=sp.twin, device_id_type=MESH)
    for j in range(8):
        @pl.when(m != j)
        def _():
            pltpu.make_async_remote_copy(src_ref=inbox.at[j], dst_ref=inbox.at[j], send_sem=ssO.at[j], recv_sem=rsO.at[j], device_id=chips[j], device_id_type=MESH).wait_recv()
        pass_on(j, True).start()
        @pl.when(c == 0)
        def _():
            do_ref[256 * j:256 * j + 128] = inbox[j, :, 0:128]
        @pl.when(c == 1)
        def _():
            do_ref[256 * j + 128:256 * j + 256] = inbox[j, :, 128:256]
    for j in range(8):
        pass_on(j, False).wait_recv()
    halves(do_ref, keptd)
    dot_[...] = do_ref[...].astype(jnp.float32).T
    fi, ji = iter(F[1:]), iter(J[1:])
    J[0]()
    turns = iter([(), (), (fi,), (fi,), (ji,), (fi, ji), (fi,), (ji,), (fi, ji), (ji,)])
    n = q_ref.shape[0] // QB
    for i in range(n):
        rows = pl.ds(QB * i, QB)
        q = q_ref[rows]
        do = do_ref[rows]
        do_h, q_h = keptd[:, rows], keptq[:, rows]
        start = start_ref[:, rows]
        both = ot_ref[:, rows] * dot_[:, rows]
        inner = [jnp.sum(both[64 * h:64 * h + 64], axis=0, keepdims=True) for h in range(2)]
        lse2 = lse_ref[:, rows]
        lse = [lse2[h:h + 1] for h in range(2)]
        def step(masked, j, carry):
            r = pl.ds(j * KB, KB)
            out, ps, ds = [], [], []
            kk, vv, kk_t = keptk[:, r], keptv[:, r], kt[:, r]
            for h in range(2):
                s = lax.dot_general(kk[h], q, NT, preferred_element_type=jnp.float32)
                if masked:
                    s = jnp.where(allowed(i, j, start), s, MASKED)
                p = jnp.exp(s - lse[h])
                dp = lax.dot_general(vv[h], do, NT, preferred_element_type=jnp.float32)
                g = (p * (dp - inner[h])).astype(jnp.bfloat16)
                out.append(carry[h] + jnp.dot(kk_t[64 * h:64 * h + 64], g, preferred_element_type=jnp.float32))
                ps.append(p.astype(jnp.bfloat16))
                ds.append(g)
            dv_ref[r] += sum(jnp.dot(ps[h], do_h[h], preferred_element_type=jnp.float32) for h in range(2))
            dk_ref[r] += sum(jnp.dot(ds[h], q_h[h], preferred_element_type=jnp.float32) for h in range(2))
            return tuple(out)
        carry = (jnp.zeros((64, QB), jnp.float32),) * 2
        for j in range(i + 1):
            carry = step(j == 0 or j == i or i == n - 1, j, carry)
            pump(*next(turns))
        dq_ref[rows] = jnp.concatenate(carry, axis=0).T
    def low(v):
        return v.astype(jnp.bfloat16).astype(jnp.float32)
    def unturn(i, total):
        rows = pl.ds(pl.multiple_of(i * 512, 512), 512)
        keep, ahead, behind = t0[rows], -t1[rows], -t2[rows]
        parts = (turn(low(dq_ref[rows]) * 0.125, keep, ahead, behind), turn(low(dk_ref[rows]), keep, ahead, behind), dv_ref[rows])
        new = []
        for p in range(3):
            y = parts[p].astype(jnp.bfloat16)
            dproj[rows, 128 * p:128 * p + 128] = y
            new.append(total[p] + jnp.sum(y.astype(jnp.float32).reshape(64, 8, 128), axis=0))
        return tuple(new)
    total = lax.fori_loop(0, dq_ref.shape[0] // 512, unturn, (jnp.zeros((8, 128), jnp.float32),) * 3)
    for p in range(3):
        bias[:, 128 * p:128 * p + 128] = jnp.sum(total[p], axis=0, keepdims=True)
    for f in ji:
        f()
    for f in fi:
        f()
    layer_out[...] = (mid[...] + fsum[...]).astype(jnp.bfloat16)
    fdone()
    jdone()
    for j in range(8):
        @pl.when(m != j)
        def _():
            to_chip(j).wait_send()
        pass_on(j, True).wait_send()

def back_part(cid, dh2, mid, dy, gain, out_all, q, k, v, start, ot, lse, cs, ffp, joined):
    tok, width = dy.shape
    rows = q.shape[0]
    f, b16, f32, vm = jax.ShapeDtypeStruct, jnp.bfloat16, jnp.float32, pltpu.VMEM
    wide = joined.shape[1]
    return pl.pallas_call(
        back_kernel,
        out_shape=(f((tok, width), f32), f((tok, width), b16), f((rows, 384), b16), f((1, 384), f32), f((2, width), f32), f((tok, width), b16), f((wide, 128), f32)),
        in_specs=[VM, VM, VM, VM, ANY, VM, VM, VM, VM, VM, VM, VM, ANY, ANY], out_specs=(VM,) * 7,
        scratch_shapes=[vm((2, 256, width), b16), vm((tok, width), b16), vm((8, tok, 256), b16), vm((rows, 128), b16)]
        + [vm((2, rows, 128), b16)] * 4 + [vm((128, rows), b16), vm((128, rows), f32)] + [vm((rows, 128), f32)] * 6
        + [vm((8, tok, width), b16), vm((7 * tok, width), b16), vm((tok, width), f32)]
        + [vm((8, wide, 128), b16), vm((7 * wide, 128), b16)]
        + [dma(n) for n in (8, 8, 8, 8, 17, 17, 17, 17, 2, 3)],
        compiler_params=params(cid), name="back",
    )(dh2, mid, dy, gain, out_all, q, k, v, start, ot, lse, cs, ffp, joined)
SPLIT_Z, SPLIT_O, SPLIT_Q, SPLIT_T = 96, 96, 288, 192

def last_kernel(dproj, hw, rn, att, da, mgrad, x, gain, bias, sums2,
                input_grad, out_grad, qkv_grad, small,
                dpt, dh1p, dtland, dland, dsum, o_all, dac, dact, qp, qland, qr, qs, qin, op, otland, oland, sm, smt, smc, smw, smx,
                ssZ, rsZ, tsZ, trZ, ssO, rsO, ssS, rsS, ssQ, rsQ, ssP, rsP, lsP, ssT, rsT, tsT, trT, ssM, rsM, ssW, rsW, ssX, rsX, ls):
    sp, wp = Plane("seq"), Plane("wt")
    tok, width = x.shape
    s, w = lax.axis_index("seq"), lax.axis_index("wt")
    c, m = sp.c, sp.block(0, 0)
    no = jnp.logical_not
    chips = [at(j // 4, j % 4, c, wp.a, wp.b) for j in range(8)]
    bar = pltpu.get_barrier_semaphore()
    for j in range(8):
        @pl.when(m != j)
        def _():
            pl.semaphore_signal(bar, inc=1, device_id=chips[j], device_id_type=MESH)
    pl.semaphore_signal(bar, inc=1, device_id=sp.twin, device_id_type=MESH)
    for d in range(1, 8):
        pl.semaphore_signal(bar, inc=1, device_id={"wt": lax.rem(w + d, 8)}, device_id_type=MESH)
    def source(b):
        return lax.rem(6 * w + b, 16), s // 2
    def target(i, p):
        g = 16 * p + s
        return 2 * w + i, g // 6, lax.rem(g, 6)
    own = jnp.int32(0)
    for b in range(6):
        ts, tw = source(b)
        same = (ts == s) & (tw == w)
        own += same.astype(jnp.int32)
        @pl.when(no(same))
        def _():
            pl.semaphore_signal(bar, inc=1, device_id={"seq": ts, "wt": tw}, device_id_type=MESH)
    dpt[...] = dproj[...].astype(jnp.float32).T.astype(jnp.bfloat16)
    mine = [pltpu.make_async_copy(att, o_all.at[wp.block(0, 0)], ls.at[0]),
            pltpu.make_async_copy(da.at[:, pl.ds(pl.multiple_of(256 * w, 256), 256)], dac.at[w], ls.at[1])]
    for cp in mine:
        cp.start()
    pl.semaphore_wait(bar, 21 - own)
    O = Gather(wp, att, o_all, tok, ssO, rsO, None, SPLIT_O)
    O.steps[0]()
    def column(d, j):
        return pltpu.make_async_remote_copy(src_ref=da.at[:, pl.ds(pl.multiple_of(256 * j, 256), 256)], dst_ref=dac.at[w], send_sem=ssS.at[d - 1], recv_sem=rsS.at[d - 1],
                                            device_id={"wt": j}, device_id_type=MESH)
    for d in range(1, 8):
        column(d, lax.rem(w + d, 8)).start()
    Z = ScatterBoth(sp, dh1p, dtland, dland, ssZ, rsZ, tsZ, trZ, dsum, SPLIT_Z)
    order = [(2, 0), (2, 1), (-1, 1), (1, 1), (-1, 0), (1, 0), (0, 1), (0, 0)]
    for k in range(8):
        j = sp.block(*order[k])
        y = lax.dot_general(dproj[pl.ds(pl.multiple_of(256 * j, 256), 256)], hw[...], NT, preferred_element_type=jnp.float32)
        dh1p[pl.ds(2 * j, 2)] = y.astype(jnp.bfloat16).reshape(2, tok, width)
        Z.sends[k]()
        if k:
            Z.adds[k - 1]()
    Z.adds[7]()
    Z.sums[0]()
    z, o = iter(Z.sums[1:]), iter(O.steps[1:])
    pump(o, o, o, o)
    def qkv(j):
        y = jnp.dot(dpt[...], rn[:, :, 512 * j:512 * j + 512].reshape(16 * tok, 512), preferred_element_type=jnp.float32).astype(jnp.bfloat16)
        qp[2 * j] = y[:, :256]
        qp[2 * j + 1] = y[:, 256:]
    qkv(0); pump(o, o); qkv(1); pump(z); qkv(2); pump(z, o, o); qkv(3)
    Q, qdone = sum_steps(wp, qp, qland, qp.shape[1], ssQ, rsQ, qr, split=SPLIT_Q)
    q = iter(Q)
    pump(q, z, o, o)
    for f in o:
        f()
    for cp in mine:
        cp.wait()
    for d in range(1, 8):
        j = lax.rem(w - d + 8, 8)
        pltpu.make_async_remote_copy(src_ref=dac.at[j], dst_ref=dac.at[j], send_sem=ssS.at[d - 1], recv_sem=rsS.at[d - 1], device_id={"wt": j}, device_id_type=MESH).wait_recv()
    dact[...] = dac[...].reshape(8 * tok, 256).astype(jnp.float32).T.astype(jnp.bfloat16)
    T = ScatterBoth(sp, op, otland, oland, ssT, rsT, tsT, trT, out_grad, SPLIT_T)
    for j in range(4):
        y = jnp.dot(dact[...], o_all[:, :, 512 * j:512 * j + 512].reshape(8 * tok, 512), preferred_element_type=jnp.float32).astype(jnp.bfloat16)
        for i in range(4):
            op[4 * j + i] = y[:, 128 * i:128 * i + 128]
    for f in T.sends:
        f()
    pump(z, q, q)
    for f in T.adds:
        f()
    t = iter(T.sums)
    pump(t, z, q, q, t)
    for f in q:
        f()
    for i in range(2):
        for p in range(3):
            qs[i, p] = qr[128 * p:128 * p + 128, 128 * i:128 * i + 128].astype(jnp.bfloat16)
    def place(i, p, which):
        ts, tw, slot = target(i, p)
        same = (ts == s) & (tw == w)
        @pl.when(same)
        def _():
            cp = pltpu.make_async_copy(qs.at[i, p], qin.at[slot], lsP.at[i, p])
            cp.start() if which == "start" else cp.wait()
        @pl.when(no(same))
        def _():
            cp = pltpu.make_async_remote_copy(src_ref=qs.at[i, p], dst_ref=qin.at[slot], send_sem=ssP.at[i, p], recv_sem=rsP.at[slot], device_id={"seq": ts, "wt": tw}, device_id_type=MESH)
            cp.start() if which == "start" else cp.wait_send()
    for i in range(2):
        for p in range(3):
            place(i, p, "start")
    for f in z:
        f()
    def ln(i, carry):
        r = pl.ds(pl.multiple_of(i * 32, 32), 32)
        y = x[r].astype(jnp.float32)
        centred = y - jnp.mean(y, axis=-1, keepdims=True)
        inverse = lax.rsqrt(jnp.mean(centred * centred, axis=-1, keepdims=True) + norm_eps)
        scaled = centred * inverse
        up = dsum[r]
        wgt = up * gain[...]
        back = inverse * (wgt - jnp.mean(wgt, axis=-1, keepdims=True) - scaled * jnp.mean(wgt * scaled, axis=-1, keepdims=True))
        input_grad[r] = (mgrad[r] + back).astype(jnp.bfloat16)
        return carry[0] + jnp.sum((up * scaled).reshape(4, 8, width), axis=0), carry[1] + jnp.sum(up.reshape(4, 8, width), axis=0)
    nil = jnp.zeros((8, width), jnp.float32)
    gsum, ssum = lax.fori_loop(0, tok // 32, ln, (nil, nil))
    four = jnp.concatenate([jnp.sum(gsum, axis=0, keepdims=True), jnp.sum(ssum, axis=0, keepdims=True), sums2[...], jnp.zeros((4, width), jnp.float32)], axis=0)
    for j in range(16):
        sm[j % 2, j // 2] = four[:, 128 * j:128 * j + 128]
    for p in range(3):
        g = 16 * p + s
        sm[lax.rem(g // 3, 2), g // 6, pl.ds(4 + lax.rem(g, 3), 1)] = bias[:, 128 * p:128 * p + 128]
    def twin_small():
        return remote(sm.at[1 - c], smt, ssM, rsM, 0, sp.twin)
    twin_small().start()
    pump(t, t)
    twin_small().wait_recv()
    smc[...] = sm[c] + smt[...]
    def chip_small(j):
        return pltpu.make_async_remote_copy(src_ref=smc.at[j], dst_ref=smw.at[m], send_sem=ssW.at[j], recv_sem=rsW.at[m], device_id=chips[j], device_id_type=MESH)
    smw[m] = smc[m]
    for j in range(8):
        @pl.when(m != j)
        def _():
            chip_small(j).start()
    pump(t, t)
    for j in range(8):
        @pl.when(m != j)
        def _():
            pltpu.make_async_remote_copy(src_ref=smw.at[j], dst_ref=smw.at[j], send_sem=ssW.at[j], recv_sem=rsW.at[j], device_id=chips[j], device_id_type=MESH).wait_recv()
    smx[0] = jnp.sum(smw[...], axis=0)
    def row_small(d):
        return remote(smx.at[0], smx.at[d], ssX, rsX, d - 1, {"wt": lax.rem(w + d, 8)})
    for d in range(1, 8):
        row_small(d).start()
    for f in t:
        f()
    for b in range(6):
        ts, tw = source(b)
        @pl.when(no((ts == s) & (tw == w)))
        def _():
            pltpu.make_async_remote_copy(src_ref=qin.at[b], dst_ref=qin.at[b], send_sem=ssP.at[0, 0], recv_sem=rsP.at[b], device_id={"seq": ts, "wt": tw}, device_id_type=MESH).wait_recv()
    for i in range(2):
        for p in range(3):
            place(i, p, "wait")
    for b in range(6):
        qkv_grad[:, 128 * b:128 * b + 128] = qin[b].astype(jnp.float32).T
    for d in range(1, 8):
        row_small(d).wait()
    small[...] = jnp.sum(smx[...], axis=0)
    O.finish()
    qdone()
    Z.finish()
    T.finish()
    twin_small().wait_send()
    for j in range(8):
        @pl.when(m != j)
        def _():
            chip_small(j).wait_send()
    for d in range(1, 8):
        column(d, lax.rem(w + d, 8)).wait_send()

def last_part(cid, dproj, hw, rn, att, da, mgrad, x, gain, bias, sums2):
    tok, width = x.shape
    f, b16, f32, vm = jax.ShapeDtypeStruct, jnp.bfloat16, jnp.float32, pltpu.VMEM
    return pl.pallas_call(
        last_kernel,
        out_shape=(f((tok, width), b16), f((256, 128), f32), f((128, 768), f32), f((8, 128), f32)),
        in_specs=[VM] * 10, out_specs=(VM,) * 4,
        scratch_shapes=[vm((384, 16 * tok), b16), vm((16, tok, width), b16), vm((8, tok, width), b16), vm((7 * tok, width), b16), vm((tok, width), f32),
                        vm((8, tok, width), b16), vm((8, tok, 256), b16), vm((256, 8 * tok), b16), vm((8, 384, 256), b16), vm((7 * 384, 256), b16), vm((384, 256), f32),
                        vm((2, 3, 128, 128), b16), vm((6, 128, 128), b16), vm((16, 256, 128), b16), vm((8, 256, 128), b16), vm((7 * 256, 128), b16),
                        vm((2, 8, 8, 128), f32), vm((8, 8, 128), f32), vm((8, 8, 128), f32), vm((8, 8, 128), f32), vm((8, 8, 128), f32)]
        + [dma(n) for n in (17, 17, 8, 8, 18, 18, 7, 7, 17, 17)] + [pltpu.SemaphoreType.DMA((2, 3)), dma(6), pltpu.SemaphoreType.DMA((2, 3))]
        + [dma(n) for n in (17, 17, 8, 8, 1, 1, 8, 8, 7, 7, 2)],
        compiler_params=params(cid), name="last",
    )(dproj, hw, rn, att, da, mgrad, x, gain, bias, sums2)
def params(cid):
    return pltpu.CompilerParams(collective_id=cid, has_side_effects=True, vmem_limit_bytes=56 * 2**20)

def dma(n):
    return pltpu.SemaphoreType.DMA((n,))

norm_eps = 1e-05
theta_base = 10000.0
ROT = 16
HEAD_DIM = 64


def rotary_angles(segment_row):
    rows = segment_row.shape[0]
    ends = [jnp.sum((segment_row < i).astype(jnp.int32)) for i in (1, 2)]
    start = jnp.where(segment_row == 0, 0, jnp.where(segment_row == 1, ends[0], ends[1]))
    offsets = (jnp.arange(rows, dtype=jnp.int32) - start).astype(jnp.float32)
    inv_freq = jnp.exp(jnp.arange(ROT // 2, dtype=jnp.float32) * (-2.0 * math.log(theta_base) / ROT))
    angles = inv_freq[:, None] * offsets[None, :]
    return start.reshape(1, rows), jnp.concatenate([jnp.cos(angles), jnp.sin(angles)], axis=0)


def per_device(layer_in, segment_ids, norm_one_gain, norm_one_shift, qkv_weight, qkv_bias, out_weight, norm_two_gain,
               norm_two_shift, gate_up_weight, down_weight, layer_grad):
    f32, bf16 = jnp.float32, jnp.bfloat16
    s, w = lax.axis_index("seq"), lax.axis_index("wt")
    tok, width = layer_in.shape[1:]
    rows = segment_ids.shape[1]
    hidden = down_weight.shape[0]
    upstream = layer_grad.reshape(tok, width)
    start, cs = rotary_angles(segment_ids.reshape(rows))
    bias = lax.dynamic_index_in_dim(qkv_bias.reshape(3, 16, 128), s, 1, keepdims=False).reshape(1, 384)
    row_normed, head_weight, q, k, v, ot, lse, attended, out_all, all_up = front(
        0, layer_in.reshape(tok, width), norm_one_gain.reshape(1, width), norm_one_shift.reshape(1, width), qkv_weight, bias, cs, start, upstream, out_weight)
    out_all = out_all.reshape(width, width)
    middle, dh2, ffn_part, joined = middle_part(
        4, attended, layer_in.reshape(tok, width), out_all, norm_two_gain.reshape(1, width),
        norm_two_shift.reshape(1, width), all_up, gate_up_weight.transpose(1, 2, 0).reshape(2 * hidden, width), down_weight)
    middle_grad, da, dproj, bias_sum, sums_two, layer_out, joined = back_part(
        6, dh2, middle, upstream, norm_two_gain.reshape(1, width), out_all, q, k, v, start, ot, lse, cs, ffn_part, joined)
    layer_out = layer_out.reshape(1, tok, width)
    input_grad, out_grad, qkv_grad, small = last_part(
        9, dproj, head_weight, row_normed, attended, da, middle_grad, layer_in.reshape(tok, width), norm_one_gain.reshape(1, width), bias_sum, sums_two)
    gate_grad = joined[:2 * hidden].reshape(2, hidden, 128).transpose(2, 0, 1)
    down_grad = joined[2 * hidden:]
    norms = lax.dynamic_slice_in_dim(small[:4], 16 * w, 16, 1)
    bias_grad = lax.dynamic_slice_in_dim(small[4:7].reshape(384), 48 * w, 48, 0)
    return (layer_out, input_grad.reshape(1, tok, width), norms[0], norms[1], qkv_grad, bias_grad, out_grad.T, norms[2], norms[3], gate_grad, down_grad)


def solution(mesh):
    both = P(("seq", "wt"))
    return jax.shard_map(
        per_device, mesh=mesh,
        in_specs=(P("wt", "seq", None), P("wt", None), P(), P(), P(None, "wt"), P(), P(None, "wt"), P(), P(), P(None, None, "wt"), P("wt", None), P("wt", "seq", None)),
        out_specs=(P("wt", "seq", None), P("wt", "seq", None), both, both, P("seq", "wt"), both, P("seq", "wt"), both, both, P("seq", None, "wt"), P("wt", "seq")),
        check_vma=False)
```

```python
import functools, math
import jax, jax.numpy as jnp
from jax import lax
from jax.experimental import pallas as pl
from jax.experimental.pallas import tpu as pltpu
from jax.sharding import PartitionSpec as P

MESH = pl.DeviceIdType.MESH

def coords():
    s = lax.axis_index("seq")
    w = lax.axis_index("wt")
    return s // 8, lax.rem(s // 2, 4), lax.rem(s, 2), w // 2, lax.rem(w, 2)

def at(yh, z, c, x, yl):
    return {"seq": yh * 8 + z * 2 + c, "wt": x * 2 + yl}

class Plane:
    def __init__(self, axis):
        self.axis = axis
        yh, z, c, x, yl = coords()
        self.c = c
        if axis == "wt":
            self.a, self.b = x, yl
            move = lambda da, db: at(yh, z, c, lax.rem(x + da + 4, 4), lax.rem(yl + db, 2))
        else:
            self.a, self.b = z, yh
            move = lambda da, db: at(lax.rem(yh + db, 2), lax.rem(z + da + 4, 4), c, x, yl)
        self.left, self.right, self.pair = move(-1, 0), move(1, 0), move(0, 1)
        self.twin = at(yh, z, 1 - c, x, yl)

    def block(self, da, db):
        a, b = lax.rem(self.a + da + 4, 4), lax.rem(self.b + db, 2)
        return a * 2 + b if self.axis == "wt" else b * 4 + a

def cuts(rows, split):
    p = split or rows // 2
    q = rows - p
    return (0, p), (p, q), (0, p // 2), (p // 2, p // 2), (p, q // 2), (p + q // 2, q // 2)

def remote(src, dst, ssem, rsem, k, target):
    return pltpu.make_async_remote_copy(src_ref=src, dst_ref=dst, send_sem=ssem.at[k], recv_sem=rsem.at[k], device_id=target, device_id_type=MESH)

def greet(targets):
    bar = pltpu.get_barrier_semaphore()
    for t in targets:
        pl.semaphore_signal(bar, inc=1, device_id=t, device_id_type=MESH)
    pl.semaphore_wait(bar, len(targets))

def repeat(n, body):
    if n == 1:
        body(0, 0)
    else:
        lax.fori_loop(0, n, body, 0)

def pace(rows, cols):
    return max(n for n in range(16, rows + 1, 16) if rows % n == 0 and n * cols <= 300000)

def gather_steps(pn, own, buf, rows, ssem, rsem, index=lambda j: j, split=None):
    P_, Q_, P0, P1, Q0, Q1 = cuts(rows, split)
    L, Rt, Y = pn.left, pn.right, pn.pair
    table = {
        0: (Y, (0, 0), P_, (0, 1)),
        1: (Rt, (0, 0), Q_, (-1, 0)),
        2: (L, (0, 0), Q_, (1, 0)),
        3: (Rt, (0, 0), P_, (-1, 0)),
        4: (L, (0, 0), P_, (1, 0)),
        5: (Y, (0, 0), Q_, (0, 1)),
        6: (Rt, (-1, 0), Q0, (2, 0)),
        7: (Y, (-1, 0), Q_, (-1, 1)),
        8: (L, (1, 0), Q1, (2, 0)),
        9: (Y, (1, 0), Q_, (1, 1)),
        10: (Rt, (0, 1), P_, (-1, 1)),
        11: (L, (0, 1), P_, (1, 1)),
        12: (Rt, (-1, 0), P0, (2, 0)),
        13: (L, (1, 0), P1, (2, 0)),
        14: (Y, (2, 0), Q0, (2, 1)),
        15: (Y, (2, 0), Q1, (2, 1)),
        16: (Rt, (-1, 1), P0, (2, 1)),
        17: (L, (1, 1), P1, (2, 1)),
    }
    def part(d, r):
        return buf.at[index(pn.block(*d)), pl.ds(*r)]
    def send(k):
        t, d, r, _ = table[k]
        if not r[1]:
            return
        src = own.at[pl.ds(*r)] if d == (0, 0) else part(d, r)
        remote(src, part(d, r), ssem, rsem, k, t).start()
    def got(k):
        t, _, r, d = table[k]
        if not r[1]:
            return
        remote(part(d, r), part(d, r), ssem, rsem, k, t).wait_recv()
    def sent(k):
        t, d, r, _ = table[k]
        if not r[1]:
            return
        remote(part(d, r), part(d, r), ssem, rsem, k, t).wait_send()
    def first():
        for k in (0, 1, 2, 3, 4, 5): send(k)
    def after(k, *next_):
        def f():
            got(k)
            for n in next_: send(n)
        return f
    steps = [first, after(1, 6, 7), after(2, 8, 9), after(0, 10, 11), after(3, 12), after(4, 13),
             after(6, 14), after(8, 15), after(10, 16), after(11, 17)]
    tail = [after(5), after(7), after(9), after(12), after(13), after(14), after(15), after(16), after(17)]
    def done():
        for k in range(18): sent(k)
    return steps, tail, done

def sum_steps(pn, buf, land, rows, ssem, rsem, out, index=lambda j: j, split=None):
    P_, Q_, P0, P1, Q0, Q1 = cuts(rows, split)
    L, Rt, Y = pn.left, pn.right, pn.pair
    table = {}
    off = 0
    def msg(k, t, d, r, r_to):
        nonlocal off
        table[k] = (t, d, r, off, r_to)
        off += r[1]
    msg(0, L, (-2, 0), P0, (-1, 0)); msg(1, Rt, (2, 0), P1, (1, 0))
    msg(2, L, (-2, 1), P0, (-1, 1)); msg(3, Rt, (2, 1), P1, (1, 1))
    msg(4, Y, (2, 1), Q_, (2, 0)); msg(5, Y, (-1, 1), Q_, (-1, 0)); msg(6, Y, (1, 1), Q_, (1, 0)); msg(7, Y, (0, 1), Q_, (0, 0))
    msg(8, L, (-1, 1), P_, (0, 1)); msg(9, Rt, (1, 1), P_, (0, 1))
    msg(10, L, (-1, 0), P_, (0, 0)); msg(11, Rt, (1, 0), P_, (0, 0))
    msg(12, L, (-2, 0), Q0, (-1, 0)); msg(13, Rt, (2, 0), Q1, (1, 0))
    msg(14, L, (-1, 0), Q_, (0, 0)); msg(15, Rt, (1, 0), Q_, (0, 0))
    msg(16, Y, (0, 1), P_, (0, 0))
    assert off <= land.shape[0]
    def part(d, r):
        return buf.at[index(pn.block(*d)), pl.ds(*r)]
    def landing(k):
        _, _, r, o, _ = table[k]
        return land.at[pl.ds(o, r[1])]
    def send(k):
        t, d, r, _, _ = table[k]
        if not r[1]:
            return
        remote(part(d, r), landing(k), ssem, rsem, k, t).start()
    def got(k):
        if not table[k][2][1]:
            return
        remote(landing(k), landing(k), ssem, rsem, k, table[k][0]).wait_recv()
    def sent(k):
        if not table[k][2][1]:
            return
        remote(landing(k), landing(k), ssem, rsem, k, table[k][0]).wait_send()
    def accumulate(d, r, ks, to=None):
        if not r[1]:
            return
        j = index(pn.block(*d))
        step = pace(r[1], buf.shape[2])
        def body(i, _):
            at_ = pl.multiple_of(r[0] + i * step, 16)
            v = buf[j, pl.ds(at_, step)].astype(jnp.float32)
            for k in ks:
                v = v + land[pl.ds(pl.multiple_of(table[k][3] + i * step, 16), step)].astype(jnp.float32)
            if to is None:
                buf[j, pl.ds(at_, step)] = v.astype(buf.dtype)
            else:
                to[pl.ds(at_, step)] = v.astype(to.dtype)
            return 0
        repeat(r[1] // step, body)
    def s0():
        for k in range(8): send(k)
    def s1():
        got(2); accumulate((-1, 1), P0, [2]); send(8)
        got(3); accumulate((1, 1), P1, [3]); send(9)
    def s2():
        got(0); accumulate((-1, 0), P0, [0]); send(10)
        got(1); accumulate((1, 0), P1, [1]); send(11)
    def s3():
        got(4); accumulate((2, 0), Q_, [4]); send(12); send(13)
    def s4():
        got(5); accumulate((-1, 0), Q_, [5]); got(12); accumulate((-1, 0), Q0, [12]); send(14)
        got(6); accumulate((1, 0), Q_, [6]); got(13); accumulate((1, 0), Q1, [13]); send(15)
    def s5():
        got(8); got(9); accumulate((0, 1), P_, [8, 9]); send(16)
    def s6():
        got(7); got(14); got(15); accumulate((0, 0), Q_, [7, 14, 15], out)
        got(10); got(11); got(16); accumulate((0, 0), P_, [10, 11, 16], out)
    def done():
        for k in range(17): sent(k)
    return [s0, s1, s2, s3, s4, s5, s6], done
ANY = pl.BlockSpec(memory_space=pl.ANY)
QB, KB = 512, 512
MASKED = -1e30
NT = (((1,), (1,)), ((), ()))

def halves(ref, kept):
    lane = lax.broadcasted_iota(jnp.int32, (1, 128), 1)
    low = (lane < 64).astype(jnp.float32)
    v = ref[...].astype(jnp.float32)
    kept[0] = (v * low).astype(jnp.bfloat16)
    kept[1] = (v * (1.0 - low)).astype(jnp.bfloat16)

def allowed(i, j, start):
    key = j * KB + lax.broadcasted_iota(jnp.int32, (KB, QB), 0)
    query = i * QB + lax.broadcasted_iota(jnp.int32, (KB, QB), 1)
    return (key <= query) & (key >= start)

VM = pl.BlockSpec(memory_space=pltpu.VMEM)

SPLIT_A, SPLIT_C, SPLIT_D = 128, 96, 96
ORDER = [(0, 0), (0, 1), (-1, 1), (1, 1), (-1, 0), (1, 0), (2, 0), (2, 1)]

class Gather:
    def __init__(self, pn, own, buf, rows, ss, rs, twin=None, split=None):
        self.pn, self.buf, self.twin = pn, buf, twin
        self.index = (lambda j: 2 * j + pn.c) if twin else (lambda j: j)
        steps, tail, done = gather_steps(pn, own, buf, rows, ss, rs, self.index, split)
        self.done = done
        ready = {0: [1], 1: [2], 2: [3], 3: [4], 4: [5], 6: [6], 8: [7]}
        def follow(i, f):
            def g():
                f()
                for k in ready.get(i, []):
                    self.hand(k)
            return g
        def first():
            steps[0]()
            self.hand(0)
        self.steps = [first] + steps[1:] + [follow(i, f) for i, f in enumerate(tail)]

    def handed(self, k, mine):
        c = self.pn.c if mine else 1 - self.pn.c
        j = self.buf.at[2 * self.pn.block(*ORDER[k]) + c]
        return remote(j, j, self.twin[0], self.twin[1], k, self.pn.twin)

    def hand(self, k):
        if self.twin:
            self.handed(k, True).start()

    def wait_twin(self, k):
        self.handed(k, False).wait_recv()

    def finish(self, waited=()):
        self.done()
        if self.twin:
            for k in range(8):
                self.handed(k, True).wait_send()
                if k not in waited:
                    self.wait_twin(k)

def fetch_steps(pn, weight, hw, ss, rs, ls):
    s = lax.axis_index("seq")
    rows = hw.shape[0]
    h, q = rows // 2, rows // 4
    W = {"P": (0, h), "Q": (h, h), "P0": (0, q), "P1": (q, q), "Q0": (h, q), "Q1": (h + q, q)}
    kinds = ["P", "P0", "P1", "Q", "Q0", "Q1"]
    both = []
    for p in range(3):
        g = 16 * p + s
        src = g // 6
        da = lax.rem(pn.a - src // 2 + 4, 4)
        b0 = pn.b == lax.rem(src, 2)
        both.append((p, lax.rem(g, 6), da, b0))
    def part(p, kind):
        return hw.at[pl.ds(*W[kind]), pl.ds(128 * p, 128)]
    def send(p, kind, slot, target):
        pltpu.make_async_remote_copy(src_ref=part(p, kind), dst_ref=part(p, kind), send_sem=ss.at[6 * p + slot],
                                     recv_sem=rs.at[6 * p + kinds.index(kind)], device_id=target, device_id_type=MESH).start()
    def wait(p, kind, slot=None):
        cp = pltpu.make_async_remote_copy(src_ref=part(p, kind), dst_ref=part(p, kind), send_sem=ss.at[6 * p + (slot or 0)],
                                          recv_sem=rs.at[6 * p + kinds.index(kind)], device_id=pn.right, device_id_type=MESH)
        cp.wait_recv() if slot is None else cp.wait_send()
    no = jnp.logical_not
    def local(p, b):
        return pltpu.make_async_copy(weight.at[:, pl.ds(pl.multiple_of(128 * b, 128), 128)], hw.at[:, pl.ds(128 * p, 128)], ls.at[p])
    def begin():
        for p, b, da, b0 in both:
            @pl.when(b0 & (da == 0))
            def _():
                local(p, b).start()
    def st0():
        for p, b, da, b0 in both:
            @pl.when(b0 & (da == 0))
            def _():
                local(p, b).wait()
                send(p, "Q", 0, pn.right); send(p, "Q", 1, pn.left); send(p, "P", 5, pn.pair)
                send(p, "P", 3, pn.right); send(p, "P", 4, pn.left); send(p, "Q", 2, pn.pair)
    def st1():
        for p, b, da, b0 in both:
            @pl.when(b0 & (da == 1))
            def _():
                wait(p, "Q"); send(p, "Q0", 0, pn.right); send(p, "Q", 2, pn.pair)
            @pl.when(b0 & (da == 3))
            def _():
                wait(p, "Q"); send(p, "Q1", 1, pn.left); send(p, "Q", 2, pn.pair)
            @pl.when(no(b0) & (da == 0))
            def _():
                wait(p, "P"); send(p, "P", 3, pn.right); send(p, "P", 4, pn.left)
    def st2():
        for p, b, da, b0 in both:
            @pl.when(da == 1)
            def _():
                wait(p, "P"); send(p, "P0", 3, pn.right)
            @pl.when(da == 3)
            def _():
                wait(p, "P"); send(p, "P1", 4, pn.left)
    def st3():
        for p, b, da, b0 in both:
            @pl.when(b0 & (da == 2))
            def _():
                wait(p, "Q0"); wait(p, "Q1"); send(p, "Q", 2, pn.pair)
    def st4():
        for p, b, da, b0 in both:
            @pl.when(da == 2)
            def _():
                wait(p, "P0"); wait(p, "P1")
            @pl.when(no(b0))
            def _():
                wait(p, "Q")
    def done():
        for p, b, da, b0 in both:
            @pl.when(b0)
            def _():
                wait(p, "Q", 2)
            @pl.when(b0 & (da == 0))
            def _():
                wait(p, "Q", 0); wait(p, "Q", 1); wait(p, "P", 5)
            @pl.when(da == 0)
            def _():
                wait(p, "P", 3); wait(p, "P", 4)
            @pl.when(b0 & (da == 1))
            def _():
                wait(p, "Q0", 0)
            @pl.when(b0 & (da == 3))
            def _():
                wait(p, "Q1", 1)
            @pl.when(da == 1)
            def _():
                wait(p, "P0", 3)
            @pl.when(da == 3)
            def _():
                wait(p, "P1", 4)
    return begin, [st0, st1, st2, st3, st4], done

def turn(v, keep, ahead, behind):
    return v * keep + pltpu.roll(v, 120, 1) * ahead + pltpu.roll(v, 8, 1) * behind

def norm_rows(x, gain, shift):
    average = jnp.mean(x, axis=-1, keepdims=True)
    centred = x - average
    inverse = lax.rsqrt(jnp.mean(centred * centred, axis=-1, keepdims=True) + norm_eps)
    return centred * inverse * gain + shift

def rotary_tables_to(cs, tables):
    rows = cs.shape[1]
    c, s = cs[0:8, :], cs[8:16, :]
    one, nil, z8 = jnp.ones((48, rows), jnp.float32), jnp.zeros((48, rows), jnp.float32), jnp.zeros((8, rows), jnp.float32)
    tables[0][...] = jnp.concatenate([c, c, one] * 2, axis=0).T
    tables[1][...] = jnp.concatenate([-s, z8, nil] * 2, axis=0).T
    tables[2][...] = jnp.concatenate([z8, s, nil] * 2, axis=0).T

def pump(*its):
    for it in its:
        f = next(it, None)
        if f is not None:
            f()

def front_kernel(x, gain, shift, weight, bias, cs, start_ref, dy, ow,
                 rn_out, hw, q_ref, k_ref, v_ref, ot_ref, lse_ref, att, out_all, dy_out,
                 rn, dy_all, own, owr, kept, vt, t0, t1, t2, ob, ox,
                 ssA, rsA, tsA, trA, ssB, rsB, lsB, ssC, rsC, ssD, rsD, tsD, trD, ssR, rsR, ssO, rsO, ssT, rsT, lsO, ls):
    sp, wp = Plane("seq"), Plane("wt")
    tok = x.shape[0]
    c, m = sp.c, sp.block(0, 0)
    A = Gather(sp, own, rn, tok, ssA, rsA, (tsA, trA), SPLIT_A)
    begin, fetch, fetch_done = fetch_steps(wp, weight, hw, ssB, rsB, lsB)
    C = Gather(wp, dy, dy_all, tok, ssC, rsC, None, SPLIT_C)
    D = Gather(sp, owr, out_all, tok, ssD, rsD, (tsD, trD), SPLIT_D)
    begin()
    chips = [at(j // 4, j % 4, c, wp.a, wp.b) for j in range(8)]
    bar = pltpu.get_barrier_semaphore()
    for j in range(8):
        @pl.when(m != j)
        def _():
            pl.semaphore_signal(bar, inc=1, device_id=chips[j], device_id_type=MESH)
    pl.semaphore_signal(bar, inc=1, device_id=sp.twin, device_id_type=MESH)
    me = lax.axis_index("wt")
    for d in range(1, 8):
        pl.semaphore_signal(bar, inc=1, device_id={"wt": lax.rem(me + d, 8)}, device_id_type=MESH)
    def ln(i, _):
        r = pl.ds(pl.multiple_of(i * 16, 16), 16)
        own[r] = norm_rows(x[r].astype(jnp.float32), gain[...], shift[...]).astype(jnp.bfloat16)
        return 0
    lax.fori_loop(0, tok // 16, ln, 0)
    strip = ow.at[pl.ds(pl.multiple_of(128 * (2 * m + c), 128), 128)]
    copies = [pltpu.make_async_copy(own, rn.at[2 * m + c], ls.at[0]),
              pltpu.make_async_copy(dy, dy_all.at[wp.block(0, 0)], ls.at[1]),
              pltpu.make_async_copy(strip, owr.at[:, pl.ds(pl.multiple_of(256 * me, 256), 256)], ls.at[2])]
    for cp in copies:
        cp.start()
    copies[0].wait()
    pl.semaphore_wait(bar, 15)
    A.steps[0]()
    fetch[0]()
    def strips(d, j):
        return pltpu.make_async_remote_copy(src_ref=strip, dst_ref=owr.at[:, pl.ds(pl.multiple_of(256 * me, 256), 256)], send_sem=ssR.at[d - 1], recv_sem=rsR.at[d - 1],
                                            device_id={"wt": j}, device_id_type=MESH)
    for d in range(1, 8):
        strips(d, lax.rem(me + d, 8)).start()
    rotary_tables_to(cs, (t0, t1, t2))
    copies[1].wait()
    def rows_first():
        copies[2].wait()
        for e in range(1, 8):
            j = lax.rem(me - e + 8, 8)
            there = owr.at[:, pl.ds(pl.multiple_of(256 * j, 256), 256)]
            pltpu.make_async_remote_copy(src_ref=there, dst_ref=there, send_sem=ssR.at[e - 1], recv_sem=rsR.at[e - 1], device_id={"wt": j}, device_id_type=MESH).wait_recv()
        whole = pltpu.make_async_copy(owr, out_all.at[2 * m + c], ls.at[2])
        whole.start()
        whole.wait()
        D.steps[0]()
    a, b, cc, d = iter(A.steps[1:]), iter(fetch[1:]), iter(C.steps), iter([rows_first] + D.steps[1:])
    pump(a, a, b, a, a, a, cc, b, a, a, a, a, d, b, b)
    head_bias = jnp.concatenate([bias[pl.ds(16 * p + lax.axis_index("seq"), 1)] for p in range(3)], axis=1)
    def project(k):
        A.wait_twin(k)
        j = sp.block(*ORDER[k])
        rows = pl.ds(pl.multiple_of(j * 256, 256), 256)
        h = rn[pl.ds(2 * j, 2)].reshape(256, rn.shape[2])
        y = jnp.dot(h, hw[...], preferred_element_type=jnp.float32) + head_bias
        tabs = (t0[rows], t1[rows], t2[rows])
        q_ref[rows] = (turn(y[:, :128], *tabs) * 0.125).astype(jnp.bfloat16)
        k_ref[rows] = turn(y[:, 128:256], *tabs).astype(jnp.bfloat16)
        v_ref[rows] = y[:, 256:].astype(jnp.bfloat16)
    project(0); pump(a, cc); project(1); pump(a, cc); project(2); pump(a, cc, cc); project(3)
    pump(a, d); project(4); pump(a, cc, d); project(5); pump(a, a, cc); project(6); pump(a, a, d); project(7)
    leave = [pltpu.make_async_copy(rn, rn_out, ls.at[0]), pltpu.make_async_copy(dy_all, dy_out, ls.at[1])]
    leave[0].start()
    halves(k_ref, kept)
    pump(cc)
    vt[...] = v_ref[...].astype(jnp.float32).T.astype(jnp.bfloat16)
    def to_twin(j):
        return pltpu.make_async_remote_copy(src_ref=ox.at[j], dst_ref=ob.at[j, :, pl.ds(pl.multiple_of(128 * c, 128), 128)],
                                            send_sem=ssT.at[j], recv_sem=rsT.at[j], device_id=sp.twin, device_id_type=MESH)
    def from_twin(j):
        there = ob.at[j, :, pl.ds(pl.multiple_of(128 * (1 - c), 128), 128)]
        return pltpu.make_async_remote_copy(src_ref=there, dst_ref=there, send_sem=ssT.at[j], recv_sem=rsT.at[j], device_id=sp.twin, device_id_type=MESH)
    def cols(j):
        return att.at[:, pl.ds(pl.multiple_of(256 * j, 256), 256)]
    def to_chip(j):
        return pltpu.make_async_remote_copy(src_ref=ob.at[j], dst_ref=cols(m), send_sem=ssO.at[j], recv_sem=rsO.at[m], device_id=chips[j], device_id_type=MESH)
    def ship(i):
        for j in (2 * i, 2 * i + 1):
            from_twin(j).wait_recv()
            @pl.when(m == j)
            def _():
                pltpu.make_async_copy(ob.at[j], cols(j), lsO).start()
            @pl.when(m != j)
            def _():
                to_chip(j).start()
    n = q_ref.shape[0] // QB
    for i in range(n):
        q = q_ref[QB * i:QB * (i + 1)]
        start = start_ref[:, QB * i:QB * (i + 1)]
        step = functools.partial(attend_step, kept, vt, q, start, i)
        one = (jnp.full((1, QB), MASKED, jnp.float32), jnp.zeros((1, QB), jnp.float32), jnp.zeros((64, QB), jnp.float32))
        carry = (one, one)
        for j in range(i + 1):
            carry = step(j == 0 or j == i or i == n - 1, j, carry)
            pump(cc, d)
        where = pl.ds(QB * i, QB)
        for h in range(2):
            top, l, acc = carry[h]
            ot_ref[64 * h:64 * h + 64, where] = acc / l
            lse_ref[h:h + 1, where] = top + jnp.log(l)
        if i:
            ship(i - 1)
        o = ot_ref[:, where].T.astype(jnp.bfloat16)
        for j in (0, 1):
            mine = pl.ds(pl.multiple_of(128 * c, 128), 128)
            first, second = o[256 * j:256 * j + 128], o[256 * j + 128:256 * j + 256]
            @pl.when(c == 0)
            def _():
                ob[2 * i + j, :, 0:128] = first
                ox[2 * i + j] = second
            @pl.when(c == 1)
            def _():
                ob[2 * i + j, :, 128:256] = second
                ox[2 * i + j] = first
            to_twin(2 * i + j).start()
    ship(n - 1)
    for f in cc:
        f()
    leave[1].start()
    for f in d:
        f()
    for j in range(8):
        to_twin(j).wait_send()
        @pl.when(m == j)
        def _():
            pltpu.make_async_copy(ob.at[j], cols(j), lsO).wait()
        @pl.when(m != j)
        def _():
            to_chip(j).wait_send()
            pltpu.make_async_remote_copy(src_ref=cols(j), dst_ref=cols(j), send_sem=ssO.at[j], recv_sem=rsO.at[j], device_id=chips[j], device_id_type=MESH).wait_recv()
    for cp in leave:
        cp.wait()
    A.finish(range(8))
    fetch_done()
    C.finish()
    D.finish()
    for e in range(1, 8):
        strips(e, lax.rem(me + e, 8)).wait_send()

def attend_step(kept, vt, q, start, i, masked, j, carry):
    r = pl.ds(j * KB, KB)
    out = []
    for h in range(2):
        m, l, acc = carry[h]
        s = lax.dot_general(kept[h, r], q, NT, preferred_element_type=jnp.float32)
        if masked:
            s = jnp.where(allowed(i, j, start), s, MASKED)
        top = jnp.maximum(m, jnp.max(s, axis=0, keepdims=True))
        p = jnp.exp(s - top)
        fade = jnp.exp(m - top)
        l = l * fade + jnp.sum(p, axis=0, keepdims=True)
        acc = acc * fade + jnp.dot(vt[64 * h:64 * h + 64, r], p.astype(jnp.bfloat16), preferred_element_type=jnp.float32)
        out.append((top, l, acc))
    return tuple(out)

def front(cid, x, gain, shift, weight, bias, cs, start, dy, ow):
    tok, width = x.shape
    rows = start.shape[1]
    f, b16, f32 = jax.ShapeDtypeStruct, jnp.bfloat16, jnp.float32
    vm = pltpu.VMEM
    return pl.pallas_call(
        front_kernel,
        out_shape=(f((16, tok, width), b16), f((width, 384), b16), f((rows, 128), b16), f((rows, 128), b16), f((rows, 128), b16),
                   f((128, rows), f32), f((8, rows), f32), f((tok, width), b16), f((16, tok, width), b16), f((8, tok, width), b16)),
        in_specs=[VM, VM, VM, ANY, VM, VM, VM, VM, ANY], out_specs=(ANY,) + (VM,) * 8 + (ANY,),
        scratch_shapes=[vm((16, tok, width), b16), vm((8, tok, width), b16), vm((tok, width), b16), vm((tok, width), b16), vm((2, rows, 128), b16), vm((128, rows), b16)] + [vm((rows, 128), f32)] * 3
        + [vm((8, 128, 256), b16), vm((8, 128, 128), b16)]
        + [dma(n) for n in (18, 18, 8, 8, 18, 18, 3, 18, 18, 18, 18, 8, 8, 7, 7, 8, 8, 8, 8)] + [pltpu.SemaphoreType.DMA, dma(3)],
        compiler_params=params(cid), name="front",
    )(x, gain, shift, weight, bias, cs, start, dy, ow)
TN = (((0,), (0,)), ((), ()))

def middle_kernel(att, x, out_all, gain, shift, dy_in, wgu_in, wd_in,
                  mid, dh2, ffp, joined,
                  dy_all, wgu, wd, own, h2, wbuf, dga, tr, dh2p, land, jsend, tland, ssG, rsG, ssS, rsS, ssT, rsT, lsw, ls, lsi):
    wp = Plane("wt")
    tok, width = mid.shape
    hidden = wd_in.shape[0]
    come = [pltpu.make_async_copy(a, b, lsi.at[i]) for i, (a, b) in enumerate(((wgu_in, wgu), (wd_in, wd), (dy_in, dy_all)))]
    there = Plane("seq").twin
    for t in (wp.left, wp.right, wp.pair, there):
        pl.semaphore_signal(pltpu.get_barrier_semaphore(), inc=1, device_id=t, device_id_type=MESH)
    def load(w, slot):
        return pltpu.make_async_copy(out_all.at[:, pl.ds(256 * w, 256)], wbuf.at[slot], lsw.at[slot])
    load(0, 0).start()
    for cp in come:
        cp.start()
    for w in range(8):
        load(w, w % 2).wait()
        if w < 7:
            load(w + 1, 1 - w % 2).start()
        cols = pl.ds(256 * w, 256)
        mid[:, cols] = x[:, cols].astype(jnp.float32) + jnp.dot(att[...], wbuf[w % 2], preferred_element_type=jnp.float32)
    def ln(i, _):
        r = pl.ds(pl.multiple_of(i * 16, 16), 16)
        own[r] = norm_rows(mid[r], gain[...], shift[...]).astype(jnp.bfloat16)
        return 0
    lax.fori_loop(0, tok // 16, ln, 0)
    cp = pltpu.make_async_copy(own, h2.at[wp.block(0, 0)], ls)
    cp.start()
    pl.semaphore_wait(pltpu.get_barrier_semaphore(), 4)
    G = Gather(wp, own, h2, tok, ssG, rsG)
    part = hidden // 2
    def chunk_up(da):
        a = lax.rem(wp.a + da + 4, 4)
        cols = pl.ds(pl.multiple_of(256 * a, 256), 256)
        hc = h2[pl.ds(2 * a, 2)].reshape(2 * tok, width)
        dc = dy_all[pl.ds(2 * a, 2)].reshape(2 * tok, width)
        for i in range(2):
            r = pl.ds(i * part, part)
            r2 = pl.ds(hidden + i * part, part)
            r3 = pl.ds(2 * hidden + i * part, part)
            g = lax.dot_general(wgu[r], hc, NT, preferred_element_type=jnp.float32)
            u = lax.dot_general(wgu[r2], hc, NT, preferred_element_type=jnp.float32)
            e = lax.dot_general(wd[r], dc, NT, preferred_element_type=jnp.float32)
            sigma = 1.0 / (1.0 + jnp.exp(-g))
            gs = g * sigma
            dga[r, cols] = (e * u * sigma * (1.0 + g * (1.0 - sigma))).astype(jnp.bfloat16)
            dga[r2, cols] = (e * gs).astype(jnp.bfloat16)
            dga[r3, cols] = (gs * u).astype(jnp.bfloat16)
    def chunk_down(da):
        a = lax.rem(wp.a + da + 4, 4)
        cols = pl.ds(pl.multiple_of(256 * a, 256), 256)
        tr[...] = dga[:, cols].astype(jnp.float32).T.astype(jnp.bfloat16)
        for i in range(width // 512):
            n = pl.ds(i * 512, 512)
            y = jnp.dot(tr[:, :2 * hidden], wgu[:, n], preferred_element_type=jnp.float32).astype(jnp.bfloat16)
            dh2p[2 * a, :, n] = y[:tok]
            dh2p[2 * a + 1, :, n] = y[tok:]
            y = jnp.dot(tr[:, 2 * hidden:], wd[:, n], preferred_element_type=jnp.float32).astype(jnp.bfloat16)
            ffp[2 * a, :, n] = y[:tok]
            ffp[2 * a + 1, :, n] = y[tok:]
    S = G.steps
    S[0]()
    cp.wait()
    for f in S[1:6]:
        f()
    S[10]()
    for f in come:
        f.wait()
    chunk_up(0)
    S[6](); S[7]()
    chunk_down(0)
    S[8](); S[9](); S[11](); S[12]()
    chunk_up(-1)
    chunk_down(-1)
    chunk_up(1)
    chunk_down(1)
    for f in S[13:]:
        f()
    chunk_up(2)
    chunk_down(2)
    G.finish()
    R, done = sum_steps(wp, dh2p, land, tok, ssS, rsS, dh2)
    def twin(j):
        return pltpu.make_async_remote_copy(src_ref=jsend.at[j], dst_ref=tland.at[j], send_sem=ssT.at[j], recv_sem=rsT.at[j], device_id=there, device_id_type=MESH)
    def weights(i):
        f = pl.ds(512 * i, 512)
        hc, dc = h2[:, :, f].reshape(8 * tok, 512), dy_all[:, :, f].reshape(8 * tok, 512)
        for k in range(3):
            r = pl.ds(hidden * k, hidden)
            y = jnp.dot(dga[r], dc if k == 2 else hc, preferred_element_type=jnp.float32).astype(jnp.bfloat16)
            for j in range(2):
                low, high = y[:, 256 * j:256 * j + 128], y[:, 256 * j + 128:256 * j + 256]
                @pl.when(wp.c == 0)
                def _():
                    joined[2 * i + j, r] = low
                    jsend[2 * i + j, r] = high
                @pl.when(wp.c == 1)
                def _():
                    joined[2 * i + j, r] = high
                    jsend[2 * i + j, r] = low
        twin(2 * i).start()
        twin(2 * i + 1).start()
    def add(j):
        twin(j).wait_recv()
        joined[j] = (joined[j].astype(jnp.float32) + tland[j].astype(jnp.float32)).astype(jnp.bfloat16)
    R[0]()
    weights(0); R[1](); R[2]()
    weights(1); R[3]()
    add(0); add(1); R[4]()
    weights(2); R[5]()
    weights(3)
    for j in range(2, 6):
        add(j)
    R[6]()
    add(6); add(7)
    done()
    for j in range(8):
        twin(j).wait_send()

def middle_part(cid, att, x, out_all, gain, shift, dy_all, wgu, wd):
    tok, width = x.shape
    hidden = wd.shape[0]
    f, b16, f32, vm = jax.ShapeDtypeStruct, jnp.bfloat16, jnp.float32, pltpu.VMEM
    return pl.pallas_call(
        middle_kernel,
        out_shape=(f((tok, width), f32), f((tok, width), f32), f((8, tok, width), b16), f((8, 3 * hidden, 128), b16)),
        in_specs=[VM, VM, ANY, VM, VM, ANY, ANY, ANY], out_specs=(VM,) * 4,
        scratch_shapes=[vm(dy_all.shape, b16), vm(wgu.shape, b16), vm(wd.shape, b16), vm((tok, width), b16), vm((8, tok, width), b16), vm((2, width, 256), b16), vm((3 * hidden, 8 * tok), b16),
                        vm((2 * tok, 3 * hidden), b16), vm((8, tok, width), b16), vm((7 * tok, width), b16),
                        vm((8, 3 * hidden, 128), b16), vm((8, 3 * hidden, 128), b16)]
        + [dma(n) for n in (18, 18, 17, 17, 8, 8, 2)] + [pltpu.SemaphoreType.DMA, dma(3)],
        compiler_params=params(cid), name="middle",
    )(att, x, out_all, gain, shift, dy_all, wgu, wd)
class ScatterBoth:
    def __init__(self, pn, buf, tland, land, ss, rs, ts, tr, out, split=None):
        self.pn, self.tland, self.ts, self.tr = pn, tland, ts, tr
        rows, cols = buf.shape[1:]
        order = [(2, 0), (2, 1), (-1, 1), (1, 1), (-1, 0), (1, 0), (0, 1), (0, 0)]
        def send(k):
            j = pn.block(*order[k])
            remote(buf.at[2 * j + 1 - pn.c], tland.at[k], ts, tr, k, pn.twin).start()
        def add(k):
            self.copy(k).wait_recv()
            j = 2 * pn.block(*order[k]) + pn.c
            step = pace(rows, cols)
            def body(i, _):
                r = pl.ds(pl.multiple_of(i * step, 16), step)
                buf[j, r] = (buf[j, r].astype(jnp.float32) + tland[k, r].astype(jnp.float32)).astype(buf.dtype)
                return 0
            repeat(rows // step, body)
        self.sends = [functools.partial(send, k) for k in range(8)]
        self.adds = [functools.partial(add, k) for k in range(8)]
        self.sums, self.done = sum_steps(pn, buf, land, rows, ss, rs, out, lambda j: 2 * j + pn.c, split)

    def copy(self, k):
        return remote(self.tland.at[k], self.tland.at[k], self.ts, self.tr, k, self.pn.twin)

    def finish(self):
        self.done()
        for k in range(8):
            self.copy(k).wait_send()

SPLIT_F, SPLIT_J = 128, 1568

def back_kernel(dh2, mid, dy, gain, out_all, q_ref, k_ref, v_ref, start_ref, ot_ref, lse_ref, cs, ffp, joined,
                mgrad, da, dproj, bias, sums, layer_out, gate_grad, down_grad,
                grads, wbuf, dg, inbox, do_ref, keptk, keptv, keptq, keptd, kt, dot_, dq_ref, dk_ref, dv_ref, t0, t1, t2, fbuf, fland, fsum, jbuf, jland,
                ssO, rsO, ssT, rsT, ssF, rsF, ssJ, rsJ, lsw, ls):
    sp, wp = Plane("seq"), Plane("wt")
    tok, width = dh2.shape
    c, m = sp.c, sp.block(0, 0)
    chips = [at(j // 4, j % 4, c, wp.a, wp.b) for j in range(8)]
    bar = pltpu.get_barrier_semaphore()
    for j in range(8):
        @pl.when(m != j)
        def _():
            pl.semaphore_signal(bar, inc=1, device_id=chips[j], device_id_type=MESH)
    pl.semaphore_signal(bar, inc=1, device_id=sp.twin, device_id_type=MESH)
    for t in (wp.left, wp.right, wp.pair):
        pl.semaphore_signal(bar, inc=1, device_id=t, device_id_type=MESH)
    def load(w, slot):
        return pltpu.make_async_copy(out_all.at[pl.ds(256 * w, 256)], wbuf.at[slot], lsw.at[slot])
    load(0, 0).start()
    here = [pltpu.make_async_copy(ffp, fbuf, ls.at[0]), pltpu.make_async_copy(joined, jbuf, ls.at[1])]
    for cp in here:
        cp.start()
    def ln(i, carry):
        r = pl.ds(pl.multiple_of(i * 32, 32), 32)
        y = mid[r]
        centred = y - jnp.mean(y, axis=-1, keepdims=True)
        inverse = lax.rsqrt(jnp.mean(centred * centred, axis=-1, keepdims=True) + norm_eps)
        scaled = centred * inverse
        up = dh2[r]
        w = up * gain[...]
        back = inverse * (w - jnp.mean(w, axis=-1, keepdims=True) - scaled * jnp.mean(w * scaled, axis=-1, keepdims=True))
        g = dy[r].astype(jnp.float32) + back
        mgrad[r] = g
        da[r] = g.astype(jnp.bfloat16)
        return carry[0] + jnp.sum((up * scaled).reshape(4, 8, width), axis=0), carry[1] + jnp.sum(up.reshape(4, 8, width), axis=0)
    nil = jnp.zeros((8, width), jnp.float32)
    gsum, ssum = lax.fori_loop(0, tok // 32, ln, (nil, nil))
    sums[0:1] = jnp.sum(gsum, axis=0, keepdims=True)
    sums[1:2] = jnp.sum(ssum, axis=0, keepdims=True)
    for w in range(8):
        load(w, w % 2).wait()
        if w < 7:
            load(w + 1, 1 - w % 2).start()
        dg[:, 256 * w:256 * w + 256] = lax.dot_general(da[...], wbuf[w % 2], NT, preferred_element_type=jnp.float32).astype(jnp.bfloat16)
    pl.semaphore_wait(bar, 11)
    def to_chip(j):
        return pltpu.make_async_remote_copy(src_ref=dg.at[:, pl.ds(256 * j, 256)], dst_ref=inbox.at[m], send_sem=ssO.at[j], recv_sem=rsO.at[m], device_id=chips[j], device_id_type=MESH)
    for j in range(8):
        @pl.when(m != j)
        def _():
            to_chip(j).start()
    mine = pltpu.make_async_copy(dg.at[:, pl.ds(pl.multiple_of(256 * m, 256), 256)], inbox.at[m], ls.at[2])
    mine.start()
    for cp in here:
        cp.wait()
    F, fdone = sum_steps(wp, fbuf, fland, tok, ssF, rsF, fsum, split=SPLIT_F)
    J, jdone = sum_steps(sp, jbuf, jland, joined.shape[1], ssJ, rsJ, grads, split=SPLIT_J)
    F[0]()
    rotary_tables_to(cs, (t0, t1, t2))
    halves(k_ref, keptk)
    halves(v_ref, keptv)
    halves(q_ref, keptq)
    kt[...] = k_ref[...].astype(jnp.float32).T.astype(jnp.bfloat16)
    dk_ref[...] = jnp.zeros_like(dk_ref)
    dv_ref[...] = jnp.zeros_like(dv_ref)
    mine.wait()
    def pass_on(j, own):
        r = do_ref.at[pl.ds(pl.multiple_of(128 * (2 * j + (c if own else 1 - c)), 128), 128)]
        src = inbox.at[j, :, pl.ds(pl.multiple_of(128 * (1 - c), 128), 128)] if own else r
        return pltpu.make_async_remote_copy(src_ref=src, dst_ref=r, send_sem=ssT.at[j], recv_sem=rsT.at[j], device_id=sp.twin, device_id_type=MESH)
    for j in range(8):
        @pl.when(m != j)
        def _():
            pltpu.make_async_remote_copy(src_ref=inbox.at[j], dst_ref=inbox.at[j], send_sem=ssO.at[j], recv_sem=rsO.at[j], device_id=chips[j], device_id_type=MESH).wait_recv()
        pass_on(j, True).start()
        @pl.when(c == 0)
        def _():
            do_ref[256 * j:256 * j + 128] = inbox[j, :, 0:128]
        @pl.when(c == 1)
        def _():
            do_ref[256 * j + 128:256 * j + 256] = inbox[j, :, 128:256]
    for j in range(8):
        pass_on(j, False).wait_recv()
    halves(do_ref, keptd)
    dot_[...] = do_ref[...].astype(jnp.float32).T
    fi, ji = iter(F[1:]), iter(J[1:])
    J[0]()
    turns = iter([(), (), (fi,), (fi,), (ji,), (fi, ji), (fi,), (ji,), (fi, ji), (ji,)])
    n = q_ref.shape[0] // QB
    for i in range(n):
        rows = pl.ds(QB * i, QB)
        q = q_ref[rows]
        do = do_ref[rows]
        do_h, q_h = keptd[:, rows], keptq[:, rows]
        start = start_ref[:, rows]
        both = ot_ref[:, rows] * dot_[:, rows]
        inner = [jnp.sum(both[64 * h:64 * h + 64], axis=0, keepdims=True) for h in range(2)]
        lse2 = lse_ref[:, rows]
        lse = [lse2[h:h + 1] for h in range(2)]
        def step(masked, j, carry):
            r = pl.ds(j * KB, KB)
            out, ps, ds = [], [], []
            kk, vv, kk_t = keptk[:, r], keptv[:, r], kt[:, r]
            for h in range(2):
                s = lax.dot_general(kk[h], q, NT, preferred_element_type=jnp.float32)
                if masked:
                    s = jnp.where(allowed(i, j, start), s, MASKED)
                p = jnp.exp(s - lse[h])
                dp = lax.dot_general(vv[h], do, NT, preferred_element_type=jnp.float32)
                g = (p * (dp - inner[h])).astype(jnp.bfloat16)
                out.append(carry[h] + jnp.dot(kk_t[64 * h:64 * h + 64], g, preferred_element_type=jnp.float32))
                ps.append(p.astype(jnp.bfloat16))
                ds.append(g)
            dv_ref[r] += sum(jnp.dot(ps[h], do_h[h], preferred_element_type=jnp.float32) for h in range(2))
            dk_ref[r] += sum(jnp.dot(ds[h], q_h[h], preferred_element_type=jnp.float32) for h in range(2))
            return tuple(out)
        carry = (jnp.zeros((64, QB), jnp.float32),) * 2
        for j in range(i + 1):
            carry = step(j == 0 or j == i or i == n - 1, j, carry)
            pump(*next(turns))
        dq_ref[rows] = jnp.concatenate(carry, axis=0).T
    def low(v):
        return v.astype(jnp.bfloat16).astype(jnp.float32)
    def unturn(i, total):
        rows = pl.ds(pl.multiple_of(i * 512, 512), 512)
        keep, ahead, behind = t0[rows], -t1[rows], -t2[rows]
        parts = (turn(low(dq_ref[rows]) * 0.125, keep, ahead, behind), turn(low(dk_ref[rows]), keep, ahead, behind), dv_ref[rows])
        new = []
        for p in range(3):
            y = parts[p].astype(jnp.bfloat16)
            dproj[rows, 128 * p:128 * p + 128] = y
            new.append(total[p] + jnp.sum(y.astype(jnp.float32).reshape(64, 8, 128), axis=0))
        return tuple(new)
    total = lax.fori_loop(0, dq_ref.shape[0] // 512, unturn, (jnp.zeros((8, 128), jnp.float32),) * 3)
    for p in range(3):
        bias[:, 128 * p:128 * p + 128] = jnp.sum(total[p], axis=0, keepdims=True)
    for f in ji:
        f()
    for f in fi:
        f()
    layer_out[...] = (mid[...] + fsum[...]).astype(jnp.bfloat16)
    cut = gate_grad.shape[0]
    gate_grad[...] = grads[0:cut]
    down_grad[...] = grads[cut:]
    fdone()
    jdone()
    for j in range(8):
        @pl.when(m != j)
        def _():
            to_chip(j).wait_send()
        pass_on(j, True).wait_send()

def back_part(cid, dh2, mid, dy, gain, out_all, q, k, v, start, ot, lse, cs, ffp, joined):
    tok, width = dy.shape
    rows = q.shape[0]
    f, b16, f32, vm = jax.ShapeDtypeStruct, jnp.bfloat16, jnp.float32, pltpu.VMEM
    wide = joined.shape[1]
    return pl.pallas_call(
        back_kernel,
        out_shape=(f((tok, width), f32), f((tok, width), b16), f((rows, 384), b16), f((1, 384), f32), f((2, width), f32), f((tok, width), b16), f((wide // 3 * 2, 128), f32), f((wide // 3, 128), f32)),
        in_specs=[VM, VM, VM, VM, ANY, VM, VM, VM, VM, VM, VM, VM, ANY, ANY], out_specs=(VM,) * 8,
        scratch_shapes=[vm((wide, 128), f32), vm((2, 256, width), b16), vm((tok, width), b16), vm((8, tok, 256), b16), vm((rows, 128), b16)]
        + [vm((2, rows, 128), b16)] * 4 + [vm((128, rows), b16), vm((128, rows), f32)] + [vm((rows, 128), f32)] * 6
        + [vm((8, tok, width), b16), vm((7 * tok, width), b16), vm((tok, width), f32)]
        + [vm((8, wide, 128), b16), vm((7 * wide, 128), b16)]
        + [dma(n) for n in (8, 8, 8, 8, 17, 17, 17, 17, 2, 3)],
        compiler_params=params(cid), name="back",
    )(dh2, mid, dy, gain, out_all, q, k, v, start, ot, lse, cs, ffp, joined)
SPLIT_Z, SPLIT_O, SPLIT_Q, SPLIT_T = 96, 96, 288, 192

def last_kernel(dproj, hw, rn_in, att, da, mgrad, x, gain, bias, sums2,
                input_grad, out_grad, qkv_grad, small,
                rn, dpt, dh1p, dtland, dland, dsum, o_all, dac, dact, qp, qland, qr, qs, qin, op, otland, oland, sm, smt, smc, smw, smx, out_sum,
                ssZ, rsZ, tsZ, trZ, ssO, rsO, ssS, rsS, ssQ, rsQ, ssP, rsP, lsP, ssT, rsT, tsT, trT, ssM, rsM, ssW, rsW, ssX, rsX, ls):
    sp, wp = Plane("seq"), Plane("wt")
    tok, width = x.shape
    s, w = lax.axis_index("seq"), lax.axis_index("wt")
    c, m = sp.c, sp.block(0, 0)
    no = jnp.logical_not
    chips = [at(j // 4, j % 4, c, wp.a, wp.b) for j in range(8)]
    bar = pltpu.get_barrier_semaphore()
    for j in range(8):
        @pl.when(m != j)
        def _():
            pl.semaphore_signal(bar, inc=1, device_id=chips[j], device_id_type=MESH)
    pl.semaphore_signal(bar, inc=1, device_id=sp.twin, device_id_type=MESH)
    for d in range(1, 8):
        pl.semaphore_signal(bar, inc=1, device_id={"wt": lax.rem(w + d, 8)}, device_id_type=MESH)
    def source(b):
        return lax.rem(6 * w + b, 16), s // 2
    def target(i, p):
        g = 16 * p + s
        return 2 * w + i, g // 6, lax.rem(g, 6)
    own = jnp.int32(0)
    for b in range(6):
        ts, tw = source(b)
        same = (ts == s) & (tw == w)
        own += same.astype(jnp.int32)
        @pl.when(no(same))
        def _():
            pl.semaphore_signal(bar, inc=1, device_id={"seq": ts, "wt": tw}, device_id_type=MESH)
    dpt[...] = dproj[...].astype(jnp.float32).T.astype(jnp.bfloat16)
    mine = [pltpu.make_async_copy(att, o_all.at[wp.block(0, 0)], ls.at[0]),
            pltpu.make_async_copy(da.at[:, pl.ds(pl.multiple_of(256 * w, 256), 256)], dac.at[w], ls.at[1])]
    rows_in = pltpu.make_async_copy(rn_in, rn, ls.at[2])
    rows_in.start()
    for cp in mine:
        cp.start()
    pl.semaphore_wait(bar, 21 - own)
    O = Gather(wp, att, o_all, tok, ssO, rsO, None, SPLIT_O)
    O.steps[0]()
    def column(d, j):
        return pltpu.make_async_remote_copy(src_ref=da.at[:, pl.ds(pl.multiple_of(256 * j, 256), 256)], dst_ref=dac.at[w], send_sem=ssS.at[d - 1], recv_sem=rsS.at[d - 1],
                                            device_id={"wt": j}, device_id_type=MESH)
    for d in range(1, 8):
        column(d, lax.rem(w + d, 8)).start()
    Z = ScatterBoth(sp, dh1p, dtland, dland, ssZ, rsZ, tsZ, trZ, dsum, SPLIT_Z)
    order = [(2, 0), (2, 1), (-1, 1), (1, 1), (-1, 0), (1, 0), (0, 1), (0, 0)]
    for k in range(8):
        j = sp.block(*order[k])
        y = lax.dot_general(dproj[pl.ds(pl.multiple_of(256 * j, 256), 256)], hw[...], NT, preferred_element_type=jnp.float32)
        dh1p[pl.ds(2 * j, 2)] = y.astype(jnp.bfloat16).reshape(2, tok, width)
        Z.sends[k]()
        if k:
            Z.adds[k - 1]()
    Z.adds[7]()
    Z.sums[0]()
    z, o = iter(Z.sums[1:]), iter(O.steps[1:])
    pump(o, o, o, o)
    def qkv(j):
        y = jnp.dot(dpt[...], rn[:, :, 512 * j:512 * j + 512].reshape(16 * tok, 512), preferred_element_type=jnp.float32).astype(jnp.bfloat16)
        qp[2 * j] = y[:, :256]
        qp[2 * j + 1] = y[:, 256:]
    rows_in.wait()
    qkv(0); pump(o, o); qkv(1); pump(z); qkv(2); pump(z, o, o); qkv(3)
    Q, qdone = sum_steps(wp, qp, qland, qp.shape[1], ssQ, rsQ, qr, split=SPLIT_Q)
    q = iter(Q)
    pump(q, z, o, o)
    for f in o:
        f()
    for cp in mine:
        cp.wait()
    for d in range(1, 8):
        j = lax.rem(w - d + 8, 8)
        pltpu.make_async_remote_copy(src_ref=dac.at[j], dst_ref=dac.at[j], send_sem=ssS.at[d - 1], recv_sem=rsS.at[d - 1], device_id={"wt": j}, device_id_type=MESH).wait_recv()
    dact[...] = dac[...].reshape(8 * tok, 256).astype(jnp.float32).T.astype(jnp.bfloat16)
    T = ScatterBoth(sp, op, otland, oland, ssT, rsT, tsT, trT, out_sum, SPLIT_T)
    for j in range(4):
        y = jnp.dot(dact[...], o_all[:, :, 512 * j:512 * j + 512].reshape(8 * tok, 512), preferred_element_type=jnp.float32).astype(jnp.bfloat16)
        for i in range(4):
            op[4 * j + i] = y[:, 128 * i:128 * i + 128]
    for f in T.sends:
        f()
    pump(z, q, q)
    for f in T.adds:
        f()
    t = iter(T.sums)
    pump(t, z, q, q, t)
    for f in q:
        f()
    for i in range(2):
        for p in range(3):
            qs[i, p] = qr[128 * p:128 * p + 128, 128 * i:128 * i + 128].astype(jnp.bfloat16)
    def place(i, p, which):
        ts, tw, slot = target(i, p)
        same = (ts == s) & (tw == w)
        @pl.when(same)
        def _():
            cp = pltpu.make_async_copy(qs.at[i, p], qin.at[slot], lsP.at[i, p])
            cp.start() if which == "start" else cp.wait()
        @pl.when(no(same))
        def _():
            cp = pltpu.make_async_remote_copy(src_ref=qs.at[i, p], dst_ref=qin.at[slot], send_sem=ssP.at[i, p], recv_sem=rsP.at[slot], device_id={"seq": ts, "wt": tw}, device_id_type=MESH)
            cp.start() if which == "start" else cp.wait_send()
    for i in range(2):
        for p in range(3):
            place(i, p, "start")
    for f in z:
        f()
    def ln(i, carry):
        r = pl.ds(pl.multiple_of(i * 32, 32), 32)
        y = x[r].astype(jnp.float32)
        centred = y - jnp.mean(y, axis=-1, keepdims=True)
        inverse = lax.rsqrt(jnp.mean(centred * centred, axis=-1, keepdims=True) + norm_eps)
        scaled = centred * inverse
        up = dsum[r]
        wgt = up * gain[...]
        back = inverse * (wgt - jnp.mean(wgt, axis=-1, keepdims=True) - scaled * jnp.mean(wgt * scaled, axis=-1, keepdims=True))
        input_grad[r] = (mgrad[r] + back).astype(jnp.bfloat16)
        return carry[0] + jnp.sum((up * scaled).reshape(4, 8, width), axis=0), carry[1] + jnp.sum(up.reshape(4, 8, width), axis=0)
    nil = jnp.zeros((8, width), jnp.float32)
    gsum, ssum = lax.fori_loop(0, tok // 32, ln, (nil, nil))
    four = jnp.concatenate([jnp.sum(gsum, axis=0, keepdims=True), jnp.sum(ssum, axis=0, keepdims=True), sums2[...], jnp.zeros((4, width), jnp.float32)], axis=0)
    for j in range(16):
        sm[j % 2, j // 2] = four[:, 128 * j:128 * j + 128]
    for p in range(3):
        g = 16 * p + s
        sm[lax.rem(g // 3, 2), g // 6, pl.ds(4 + lax.rem(g, 3), 1)] = bias[:, 128 * p:128 * p + 128]
    def twin_small():
        return remote(sm.at[1 - c], smt, ssM, rsM, 0, sp.twin)
    twin_small().start()
    pump(t, t)
    twin_small().wait_recv()
    smc[...] = sm[c] + smt[...]
    def chip_small(j):
        return pltpu.make_async_remote_copy(src_ref=smc.at[j], dst_ref=smw.at[m], send_sem=ssW.at[j], recv_sem=rsW.at[m], device_id=chips[j], device_id_type=MESH)
    smw[m] = smc[m]
    for j in range(8):
        @pl.when(m != j)
        def _():
            chip_small(j).start()
    pump(t, t)
    for j in range(8):
        @pl.when(m != j)
        def _():
            pltpu.make_async_remote_copy(src_ref=smw.at[j], dst_ref=smw.at[j], send_sem=ssW.at[j], recv_sem=rsW.at[j], device_id=chips[j], device_id_type=MESH).wait_recv()
    smx[0] = jnp.sum(smw[...], axis=0)
    def row_small(d):
        return remote(smx.at[0], smx.at[d], ssX, rsX, d - 1, {"wt": lax.rem(w + d, 8)})
    for d in range(1, 8):
        row_small(d).start()
    for f in t:
        f()
    out_grad[...] = out_sum[...].T
    for b in range(6):
        ts, tw = source(b)
        @pl.when(no((ts == s) & (tw == w)))
        def _():
            pltpu.make_async_remote_copy(src_ref=qin.at[b], dst_ref=qin.at[b], send_sem=ssP.at[0, 0], recv_sem=rsP.at[b], device_id={"seq": ts, "wt": tw}, device_id_type=MESH).wait_recv()
    for i in range(2):
        for p in range(3):
            place(i, p, "wait")
    for b in range(6):
        qkv_grad[:, 128 * b:128 * b + 128] = qin[b].astype(jnp.float32).T
    for d in range(1, 8):
        row_small(d).wait()
    small[...] = jnp.sum(smx[...], axis=0)
    O.finish()
    qdone()
    Z.finish()
    T.finish()
    twin_small().wait_send()
    for j in range(8):
        @pl.when(m != j)
        def _():
            chip_small(j).wait_send()
    for d in range(1, 8):
        column(d, lax.rem(w + d, 8)).wait_send()

def last_part(cid, dproj, hw, rn, att, da, mgrad, x, gain, bias, sums2):
    tok, width = x.shape
    f, b16, f32, vm = jax.ShapeDtypeStruct, jnp.bfloat16, jnp.float32, pltpu.VMEM
    return pl.pallas_call(
        last_kernel,
        out_shape=(f((tok, width), b16), f((128, 256), f32), f((128, 768), f32), f((8, 128), f32)),
        in_specs=[VM, VM, ANY] + [VM] * 7, out_specs=(VM,) * 4,
        scratch_shapes=[vm(rn.shape, b16), vm((384, 16 * tok), b16), vm((16, tok, width), b16), vm((8, tok, width), b16), vm((7 * tok, width), b16), vm((tok, width), f32),
                        vm((8, tok, width), b16), vm((8, tok, 256), b16), vm((256, 8 * tok), b16), vm((8, 384, 256), b16), vm((7 * 384, 256), b16), vm((384, 256), f32),
                        vm((2, 3, 128, 128), b16), vm((6, 128, 128), b16), vm((16, 256, 128), b16), vm((8, 256, 128), b16), vm((7 * 256, 128), b16),
                        vm((2, 8, 8, 128), f32), vm((8, 8, 128), f32), vm((8, 8, 128), f32), vm((8, 8, 128), f32), vm((8, 8, 128), f32), vm((256, 128), f32)]
        + [dma(n) for n in (17, 17, 8, 8, 18, 18, 7, 7, 17, 17)] + [pltpu.SemaphoreType.DMA((2, 3)), dma(6), pltpu.SemaphoreType.DMA((2, 3))]
        + [dma(n) for n in (17, 17, 8, 8, 1, 1, 8, 8, 7, 7, 3)],
        compiler_params=params(cid), name="last",
    )(dproj, hw, rn, att, da, mgrad, x, gain, bias, sums2)
def params(cid):
    return pltpu.CompilerParams(collective_id=cid, has_side_effects=True, vmem_limit_bytes=56 * 2**20)

def dma(n):
    return pltpu.SemaphoreType.DMA((n,))

norm_eps = 1e-05
theta_base = 10000.0
ROT = 16
HEAD_DIM = 64


def rotary_angles(segment_row):
    rows = segment_row.shape[0]
    ends = [jnp.sum((segment_row < i).astype(jnp.int32)) for i in (1, 2)]
    start = jnp.where(segment_row == 0, 0, jnp.where(segment_row == 1, ends[0], ends[1]))
    offsets = (jnp.arange(rows, dtype=jnp.int32) - start).astype(jnp.float32)
    inv_freq = jnp.exp(jnp.arange(ROT // 2, dtype=jnp.float32) * (-2.0 * math.log(theta_base) / ROT))
    angles = inv_freq[:, None] * offsets[None, :]
    return start.reshape(1, rows), jnp.concatenate([jnp.cos(angles), jnp.sin(angles)], axis=0)


def per_device(layer_in, segment_ids, norm_one_gain, norm_one_shift, qkv_weight, qkv_bias, out_weight, norm_two_gain,
               norm_two_shift, gate_up_weight, down_weight, layer_grad):
    f32, bf16 = jnp.float32, jnp.bfloat16
    w = lax.axis_index("wt")
    tok, width = layer_in.shape[1:]
    rows = segment_ids.shape[1]
    hidden = down_weight.shape[0]
    upstream = layer_grad.reshape(tok, width)
    start, cs = rotary_angles(segment_ids.reshape(rows))
    bias = qkv_bias.reshape(48, 128)
    row_normed, head_weight, q, k, v, ot, lse, attended, out_all, all_up = front(
        0, layer_in.reshape(tok, width), norm_one_gain.reshape(1, width), norm_one_shift.reshape(1, width), qkv_weight, bias, cs, start, upstream, out_weight)
    out_all = out_all.reshape(width, width)
    middle, dh2, ffn_part, joined = middle_part(
        4, attended, layer_in.reshape(tok, width), out_all, norm_two_gain.reshape(1, width),
        norm_two_shift.reshape(1, width), all_up, gate_up_weight.transpose(1, 2, 0).reshape(2 * hidden, width), down_weight)
    middle_grad, da, dproj, bias_sum, sums_two, layer_out, gate_grad, down_grad = back_part(
        6, dh2, middle, upstream, norm_two_gain.reshape(1, width), out_all, q, k, v, start, ot, lse, cs, ffn_part, joined)
    layer_out = layer_out.reshape(1, tok, width)
    input_grad, out_grad, qkv_grad, small = last_part(
        9, dproj, head_weight, row_normed, attended, da, middle_grad, layer_in.reshape(tok, width), norm_one_gain.reshape(1, width), bias_sum, sums_two)
    gate_grad = gate_grad.reshape(2, hidden, 128).transpose(2, 0, 1)
    norms = lax.dynamic_slice_in_dim(small[:4], 16 * w, 16, 1)
    bias_grad = lax.dynamic_slice_in_dim(small[4:7].reshape(384), 48 * w, 48, 0)
    return (layer_out, input_grad.reshape(1, tok, width), norms[0], norms[1], qkv_grad, bias_grad, out_grad, norms[2], norms[3], gate_grad, down_grad)


def solution(mesh):
    both = P(("seq", "wt"))
    return jax.shard_map(
        per_device, mesh=mesh,
        in_specs=(P("wt", "seq", None), P("wt", None), P(), P(), P(None, "wt"), P(), P(None, "wt"), P(), P(), P(None, None, "wt"), P("wt", None), P("wt", "seq", None)),
        out_specs=(P("wt", "seq", None), P("wt", "seq", None), both, both, P("seq", "wt"), both, P("seq", "wt"), both, both, P("seq", None, "wt"), P("wt", "seq")),
        check_vma=False)
```
